32 devices in a mesh: rows: 8 (over z, core), expert: 4 (over y, x).
Axes of the slice: x: 2, y: 2, z: 4, core: 2. Of those that a mesh axis runs over, the one named last changes fastest.
Arguments:
- rows_in: float32 [32768, 256], P(('rows', 'expert')), may hold values from -6 to 6
- pred_grad: float32 [32768, 2], P(('rows', 'expert')), may hold values from -6 to 6
- lengths: int32 [256], replicated, may hold values from 1 to 200, 32768 in all
- session_type: int32 [256], replicated, may hold values from 0 to 31
- expert_in: bfloat16 [2, 16, 256, 256], P(None, 'expert'), may hold values from -0.375 to 0.375
- expert_in_bias: float32 [2, 16, 256], P(None, 'expert'), may hold values from -2 to 2
- expert_out: bfloat16 [2, 16, 256, 256], P(None, 'expert'), may hold values from -0.375 to 0.375
- expert_out_bias: float32 [2, 16, 256], P(None, 'expert'), may hold values from -2 to 2
- selector_logits: float32 [2, 32, 2, 4, 4], replicated, may hold values from -8 to 8, as said below
- selector_mix: float32 [2, 32, 2, 4], replicated, may hold values from -4 to 4
- tower_in: bfloat16 [2, 256, 128], replicated, may hold values from -0.375 to 0.375
- tower_bias: float32 [2, 128], replicated, may hold values from -2 to 2
- tower_out: float32 [2, 128], replicated, may hold values from -0.5 to 0.5
Outputs:
- predictions: float32 [32768, 2], P(('rows', 'expert'))
- rows_grad: float32 [32768, 256], P(('rows', 'expert'))
- expert_in_grad: float32 [2, 16, 256, 256], P(None, 'expert')
- expert_in_bias_grad: float32 [2, 16, 256], P(None, 'expert')
- expert_out_grad: float32 [2, 16, 256, 256], P(None, 'expert')
- expert_out_bias_grad: float32 [2, 16, 256], P(None, 'expert')
- logits_grad: float32 [2, 32, 2, 4, 4], replicated
- mix_grad: float32 [2, 32, 2, 4], replicated
- tower_in_grad: float32 [2, 256, 128], replicated
- tower_bias_grad: float32 [2, 128], replicated
- tower_out_grad: float32 [2, 128], replicated
The draws below stay inside these ranges and needn't reach their ends.
Inputs may be any that keep to these rules, and one draw needn't show every extreme that they name: The lengths sum to 32768. `selector_logits`: every logit has magnitude 6 to 8, except that in some selectors one bit, the same for all selectors of one layer and type, lies in [-3, 3]; all selectors of one layer and type reach experts of at most 4 pairs that differ in that bit, so a row has nonzero gate on at most 8 of the 16 experts of a layer and exactly zero gate on the others.
All inputs are finite; a program needn't handle non-finite values.
Results may differ from the reference program's by a relative error of at most 0.018.
Values may be sent and summed in bfloat16 or wider, within the bound.
No kernel may reach another device: no remote copies, remote signals or barrier semaphores. Data moves between devices by JAX's collectives and lax.ppermute only.
A program may use at most 192 MiB of HBM per device.

```python
import math
import jax
import jax.numpy as jnp
import numpy as np
from jax import lax

D = 256
H = 256
TOWER = 128
BITS = 4
EXPERTS = 16
SELECTORS = 4
TASKS = 2
LAYERS = 2
TYPES = 32
LONGEST = 200
ROWS = 32768
SESSIONS = 256


def draw_selector_logits(key, part):
    key = jax.random.fold_in(key, 7)
    layout_shape = (LAYERS, TYPES, TASKS, SELECTORS, BITS)
    pairing_count = 2 ** (BITS - 1)
    pick_key, rank_key, score_key, order_key, keep_key, side_key, size_key, free_key = jax.random.split(key, 8)
    free_bit = jax.random.randint(pick_key, (LAYERS, TYPES), 0, BITS)
    rank_keys = jax.random.split(rank_key, LAYERS)
    rank_positions = jax.vmap(lambda one_key: jax.random.permutation(one_key, pairing_count))(rank_keys).astype(jnp.int32)
    extra_credit = (pairing_count - 1 - rank_positions) * 250
    random_jitter = jax.random.randint(score_key, (LAYERS, TYPES, pairing_count), 0, 2400)
    score_values = (random_jitter + extra_credit[:, None, :]) * pairing_count + jnp.arange(pairing_count, dtype=jnp.int32)[None, None, :]
    chosen = lax.top_k(score_values, SELECTORS)[1].astype(jnp.int32)
    order_keys = jax.random.split(order_key, LAYERS * TYPES * TASKS)
    orders = jax.vmap(lambda one_key: jax.random.permutation(one_key, SELECTORS))(order_keys)
    orders = orders.reshape(LAYERS, TYPES, TASKS, SELECTORS).astype(jnp.int32)
    spread = jnp.broadcast_to(chosen[:, :, None, :], (LAYERS, TYPES, TASKS, SELECTORS))
    pairs = jnp.take_along_axis(spread, orders, axis=-1)
    bit_positions = jnp.arange(BITS, dtype=jnp.int32)
    chosen_bit = free_bit[:, :, None, None, None]
    other_index = bit_positions - (bit_positions > chosen_bit).astype(jnp.int32)
    other_index = jnp.maximum(other_index, 0)
    code_bit = pairs[..., None] // 2 ** other_index % 2
    signs = (code_bit * 2 - 1).astype(jnp.float32)
    is_free = chosen_bit == bit_positions
    saturate = jax.random.randint(keep_key, (LAYERS, TYPES, TASKS, SELECTORS, 1), 0, 2) == 1
    sides = (jax.random.randint(side_key, layout_shape, 0, 2) * 2 - 1).astype(jnp.float32)
    magnitude = jax.random.uniform(size_key, layout_shape, jnp.float32, 6.0, 8.0)
    far_value = signs * magnitude
    fixed_value = sides * magnitude
    near_value = jax.random.uniform(free_key, layout_shape, jnp.float32, -3.0, 3.0)
    return jnp.where(is_free, jnp.where(saturate, fixed_value, near_value), far_value)


def with_ends(array, own_key, least, high):
    spot = [jax.random.randint(jax.random.fold_in(own_key, axis), (), 0, length) for axis, length in enumerate(array.shape)]
    main_axis = array.shape.index(max(array.shape))
    beside = spot[:main_axis] + [(spot[main_axis] + 1) % array.shape[main_axis]] + spot[main_axis + 1:]
    return array.at[tuple(spot)].set(least).at[tuple(beside)].set(high)


def steps_of(stream_key, dims, pieces, low, top_value):
    loudness, own = 1.0, jax.random.fold_in(stream_key, 6)
    for axis_at, parts in pieces:
        steps = jnp.exp(jax.random.uniform(jax.random.fold_in(own, axis_at), (parts,), jnp.float32, low / len(pieces), top_value / len(pieces)))
        loudness = loudness * jnp.repeat(steps, dims[axis_at] // parts).reshape([-1 if axis == axis_at else 1 for axis in range(len(dims))])
    return loudness


def profile(count, total, bound, lean):
    loads = [(1 << 20) // math.isqrt(grade ** lean) + 1 for grade in range(2, count + 1)]
    rest, counts = total - bound - (count - 1), [1] * (count - 1)
    while rest > 0:
        free = [i for i in range(count - 1) if counts[i] < bound]
        whole, budget = sum([loads[i] for i in free]), rest
        for i in free:
            addition = min(bound - counts[i], max(1, budget * loads[i] // whole), rest)
            counts[i] = counts[i] + addition
            rest = rest - addition
    return np.array([bound] + counts)


def ragged(own_key, count, total, most, skew):
    if count == 2:
        one = jax.random.randint(own_key, (), max(1, total - most), min(most, total - 1) + 1)
        return jnp.stack([one, total - one])
    tallies = jnp.asarray(profile(count, total, most, skew), jnp.int32)
    couples = (count - 1) // 2
    giver, receiver = tallies[1:1 + 2 * couples:2], tallies[2:2 + 2 * couples:2]
    margin = jnp.minimum(giver - 1, most - receiver)
    passed = jax.random.randint(jax.random.fold_in(own_key, 1), (couples,), 0, 1 << 20) % (margin + 1)
    tallies = tallies.at[1:1 + 2 * couples:2].set(giver - passed).at[2:2 + 2 * couples:2].set(receiver + passed)
    return tallies[jax.random.permutation(jax.random.fold_in(own_key, 2), count)]


def scatter_about(key, shape, deviation, most, cuts=(), kind=jnp.bfloat16):
    gain = steps_of(key, shape, cuts, -0.22, 0.18) if cuts else 1.0
    array = jax.random.normal(key, shape, jnp.float32) * deviation * gain
    return jnp.minimum(jnp.maximum(array, -most), most).astype(kind)


def setup_inputs(seed: int = 0) -> dict:
    key_list = jax.random.split(jax.random.key(seed), 14)
    rows_in = scatter_about(key_list[0], (ROWS, D), 1.0, 6.0, ((0, 32),), jnp.float32)
    pred_grad = scatter_about(key_list[1], (ROWS, TASKS), 1.0, 6.0, ((0, 32),), jnp.float32)
    lengths = ragged(key_list[2], SESSIONS, ROWS, LONGEST, 0).astype(jnp.int32)
    session_type = with_ends(jax.random.randint(key_list[3], (SESSIONS,), 0, TYPES), jax.random.fold_in(key_list[3], 1), 0, TYPES - 1).astype(jnp.int32)
    expert_in = scatter_about(key_list[4], (LAYERS, EXPERTS, D, H), D ** -0.5, 0.375, ((1, 4),))
    expert_in_bias = scatter_about(key_list[5], (LAYERS, EXPERTS, H), 0.3, 2.0, ((1, 4),), jnp.float32)
    expert_out = scatter_about(key_list[6], (LAYERS, EXPERTS, H, D), H ** -0.5, 0.375, ((1, 4),))
    expert_out_bias = scatter_about(key_list[7], (LAYERS, EXPERTS, D), 0.3, 2.0, ((1, 4),), jnp.float32)
    selector_logits = draw_selector_logits(jax.random.fold_in(key_list[13], 71), 0)
    selector_mix = scatter_about(key_list[9], (LAYERS, TYPES, TASKS, SELECTORS), 1.0, 4.0, (), jnp.float32)
    tower_in = scatter_about(key_list[10], (TASKS, D, TOWER), D ** -0.5, 0.375)
    tower_bias = scatter_about(key_list[11], (TASKS, TOWER), 0.3, 2.0, (), jnp.float32)
    tower_out = scatter_about(key_list[12], (TASKS, TOWER), TOWER ** -0.5, 0.5, (), jnp.float32)
    return {"rows_in": rows_in, "pred_grad": pred_grad, "lengths": lengths, "session_type": session_type, "expert_in": expert_in, "expert_in_bias": expert_in_bias, "expert_out": expert_out, "expert_out_bias": expert_out_bias, "selector_logits": selector_logits, "selector_mix": selector_mix, "tower_in": tower_in, "tower_bias": tower_bias, "tower_out": tower_out}


@jax.custom_vjp
def low(v):
    return lax.optimization_barrier(v.astype(jnp.bfloat16)).astype(jnp.float32)

@jax.custom_vjp
def low_back(v):
    return v

def low_keep(v):
    return (low(v), None)

def low_pass(kept, grad):
    return (grad,)

def back_keep(v):
    return (v, None)

def back_low(kept, grad):
    return (low(grad),)
low.defvjp(low_keep, low_pass)
low_back.defvjp(back_keep, back_low)
SHARPNESS = 10.0
EXACT = lax.Precision.HIGHEST

def smooth_step(logit):
    cubic = -2.0 / SHARPNESS ** 3 * logit ** 3 + 1.5 / SHARPNESS * logit + 0.5
    return jnp.where(logit <= -SHARPNESS / 2, 0.0, jnp.where(logit >= SHARPNESS / 2, 1.0, cubic))

def gate_table(logits, mixing):
    width_bits = logits.shape[-1]
    numbers = jnp.arange(2 ** width_bits)
    powers = 2 ** jnp.arange(width_bits)
    bit_table = (numbers[:, None] // powers[None, :] % 2).astype(logits.dtype)
    stepped = smooth_step(logits)[..., None, :]
    factor = bit_table * stepped + (1.0 - bit_table) * (1.0 - stepped)
    reaches = jnp.prod(factor, axis=-1)
    shares = jax.nn.softmax(mixing, axis=-1)[..., None]
    return lax.optimization_barrier(jnp.sum(shares * reaches, axis=-2))

def experts_apply(stream, gate_rows, weight_in, bias_in, weight_out, bias_out):
    dispatched = low_back(jnp.broadcast_to(low(stream)[None], (EXPERTS,) + stream.shape))
    before = low_back(jnp.einsum('ebd,edh->ebh', dispatched, weight_in, precision=EXACT) + bias_in[:, None, :])
    hidden = low(jax.nn.gelu(before))
    expert_result = low_back(low(jnp.einsum('ebh,ehd->ebd', hidden, weight_out, precision=EXACT) + bias_out[:, None, :]))
    return jnp.einsum('bte,ebd->btd', low(gate_rows), expert_result, precision=EXACT)

def forward(params, row_block, type_block):
    weight_in, bias_in, weight_out, bias_out, logits, mixing, tower_w, tower_b, tower_v = params
    gate_values = gate_table(logits, mixing)
    type_hot = (type_block[:, None] == jnp.arange(TYPES, dtype=jnp.int32)[None, :]).astype(jnp.float32)
    stream = row_block
    blended = None
    for layer_at in range(LAYERS):
        gate_rows = jnp.einsum('bs,ste->bte', type_hot, gate_values[layer_at], precision=EXACT)
        blended = experts_apply(stream, gate_rows, weight_in[layer_at], bias_in[layer_at], weight_out[layer_at], bias_out[layer_at])
        if layer_at + 1 < LAYERS:
            stream = stream + lax.optimization_barrier(jnp.mean(blended, axis=1))
    closing = stream[:, None, :] + blended
    tower_input = low(closing)
    tower_before = low_back(jnp.einsum('btd,tdk->btk', tower_input, tower_w, precision=EXACT) + tower_b[None])
    return lax.optimization_barrier(jnp.sum(jax.nn.gelu(tower_before) * tower_v[None], axis=-1))

def reference(rows_in, pred_grad, lengths, session_type, expert_in, expert_in_bias, expert_out, expert_out_bias, selector_logits, selector_mix, tower_in, tower_bias, tower_out):
    row_type = jnp.repeat(session_type, lengths, total_repeat_length=ROWS).astype(jnp.int32)
    block_rows = math.gcd(ROWS, 2048)
    blocks = ROWS // block_rows
    params = (expert_in.astype(jnp.float32), expert_in_bias, expert_out.astype(jnp.float32), expert_out_bias, selector_logits, selector_mix, tower_in.astype(jnp.float32), tower_bias, tower_out)

    def forward_shift(totals, carried):
        row_block, type_block, cotangent = carried
        predicted, pullback = jax.vjp(lambda weights, inputs: forward(weights, inputs, type_block), params, row_block)
        weight_grads, input_grad = pullback(cotangent)
        totals = jax.tree.map(lambda running, added: running + added, totals, weight_grads)
        return (totals, (predicted, input_grad))
    initial = jax.tree.map(jnp.zeros_like, params)
    totals, (predicted, input_grad) = lax.scan(forward_shift, initial, (rows_in.reshape(blocks, block_rows, D), row_type.reshape(blocks, block_rows), pred_grad.reshape(blocks, block_rows, TASKS)))
    return (predicted.reshape(ROWS, TASKS), input_grad.reshape(ROWS, D), totals[0], totals[1], totals[2], totals[3], totals[4], totals[5], totals[6], totals[7], totals[8])
```

```python
import functools
import math

import jax
import jax.numpy as jnp
from jax import lax
from jax.experimental import pallas as pl
from jax.experimental.pallas import tpu as pltpu
from jax.sharding import PartitionSpec as P

SHARPNESS = 10.0
EXACT = lax.Precision.HIGHEST
bf16 = jnp.bfloat16
f32 = jnp.float32
INNER = math.sqrt(2.0 / math.pi)
CUBE = 0.044715 * INNER
TILE = 256
EXTRA = 16


def smooth_step(logit):
    cubic = -2.0 / SHARPNESS**3 * logit**3 + 1.5 / SHARPNESS * logit + 0.5
    return jnp.where(logit <= -SHARPNESS / 2, 0.0, jnp.where(logit >= SHARPNESS / 2, 1.0, cubic))


def smooth_slope(logit):
    slope = -6.0 / SHARPNESS**3 * logit**2 + 1.5 / SHARPNESS
    return jnp.where((logit > -SHARPNESS / 2) & (logit < SHARPNESS / 2), slope, 0.0)


def gate_parts(logits, mixing):
    bits = logits.shape[-1]
    experts = 2**bits
    bit_table = ((jnp.arange(experts)[:, None] >> jnp.arange(bits)[None, :]) & 1).astype(f32)
    stepped = smooth_step(logits)[..., None, :]
    factor = bit_table * stepped + (1.0 - bit_table) * (1.0 - stepped)
    reaches = jnp.prod(factor, axis=-1)
    shares = jax.nn.softmax(mixing, axis=-1)
    values = jnp.sum(shares[..., None] * reaches, axis=-2)
    slopes = []
    for bit in range(bits):
        others = jnp.prod(jnp.delete(factor, bit, axis=-1), axis=-1)
        sign = 2.0 * bit_table[:, bit] - 1.0
        slopes.append(
            (shares * smooth_slope(logits[..., bit]))[..., None] * sign * others
        )
    by_logit = jnp.stack(slopes, axis=-2)
    by_logit = by_logit.reshape(*by_logit.shape[:3], -1, experts)
    by_mix = shares[..., None] * (reaches - values[..., None, :])
    return values, jnp.concatenate([by_logit, by_mix], axis=-2)


def mm(a, b):
    return jnp.dot(a, b, preferred_element_type=f32)


def mm_nt(a, b):
    return lax.dot_general(a, b, (((1,), (1,)), ((), ())), preferred_element_type=f32)


def mm_tn(a, b):
    return lax.dot_general(a, b, (((0,), (0,)), ((), ())), preferred_element_type=f32)


def gelu_both(v):
    square = v * v
    bent = jnp.tanh(v * (INNER + CUBE * square))
    half = 0.5 * (1.0 + bent)
    value = v * half
    slope = half + 0.5 * v * (1.0 - bent * bent) * (INNER + 3.0 * CUBE * square)
    return value, slope


def gelu(v):
    bent = jnp.tanh(v * (INNER + CUBE * v * v))
    return 0.5 * v * (1.0 + bent)


def bias_rows(ref, at, width):
    rows = ref[at, 2 * width : 2 * width + EXTRA].astype(f32)
    return rows[0:1] + rows[1:2], rows[2:3] + rows[3:4]


def spot(pieces):
    return [(ref, at) for ref in pieces for at in range(ref.shape[0])]


def forward_kernel(columns, experts, tasks_out, fresh, with_tower, *refs):
    refs = list(refs)
    x_ref, gate_ref = refs[0], refs[1]
    at = 2
    if not fresh:
        sum_ref = refs[at]
        at += 1
    if with_tower:
        base_ref, pred_grad_ref, tower_in_ref, tower_bias_ref, tower_out_ref = refs[at : at + 5]
        at += 5
    outs = 6 if with_tower else 1
    weight_refs = refs[at : len(refs) - outs - (3 if with_tower else 0)]
    rest = refs[at + len(weight_refs) :]
    x_low = x_ref[...].astype(bf16)
    width = x_low.shape[1]
    gates = gate_ref[...]
    totals = [jnp.zeros(x_low.shape, f32) if fresh else sum_ref[t] for t in range(tasks_out)]
    for (ref, spot_at), column in zip(spot(weight_refs), columns):
        bias_in, bias_out = bias_rows(ref, spot_at, width)
        hidden = gelu(mm(x_low, ref[spot_at, 0:width]) + bias_in).astype(bf16)
        result = mm(hidden, ref[spot_at, width : 2 * width]) + bias_out
        result = result.astype(bf16).astype(f32)
        first, second = gates[:, column : column + 1], gates[:, experts + column : experts + column + 1]
        if tasks_out == 1:
            totals[0] += (0.5 * (first + second)) * result
        else:
            totals[0] += first * result
            totals[1] += second * result
    if not with_tower:
        out_ref = rest[0]
        for t in range(tasks_out):
            out_ref[t] = totals[t]
        return
    pred_ref, grad_ref, grad_low_sum_ref, in_grad_ref, bias_grad_ref, out_grad_ref = rest[:6]
    in_sum, bias_sum, out_sum = rest[6:]
    step = pl.program_id(0)

    @pl.when(step == 0)
    def _():
        in_sum[...] = jnp.zeros_like(in_sum)
        bias_sum[...] = jnp.zeros_like(bias_sum)
        out_sum[...] = jnp.zeros_like(out_sum)

    base = base_ref[0]
    summed = None
    predicted = []
    for t in range(tasks_out):
        closing_low = (base + totals[t]).astype(bf16)
        before = mm(closing_low, tower_in_ref[t]) + tower_bias_ref[t : t + 1]
        act, slope = gelu_both(before)
        vector = tower_out_ref[t : t + 1]
        predicted.append(jnp.sum(act * vector, axis=1, keepdims=True))
        cotangent = pred_grad_ref[:, t : t + 1]
        out_sum[t : t + 1] += jnp.sum(act * cotangent, axis=0, keepdims=True)
        before_grad = (slope * (cotangent * vector)).astype(bf16)
        bias_sum[t : t + 1] += jnp.sum(before_grad.astype(f32), axis=0, keepdims=True)
        in_sum[t] += mm_tn(closing_low, before_grad)
        closing_grad = mm_nt(before_grad, tower_in_ref[t])
        grad_ref[t] = closing_grad
        summed = closing_grad if summed is None else summed + closing_grad
    grad_low_sum_ref[0] = summed
    pred_ref[...] = jnp.concatenate(predicted, axis=1)

    @pl.when(step == pl.num_programs(0) - 1)
    def _():
        in_grad_ref[...] = in_sum[...]
        bias_grad_ref[...] = bias_sum[...]
        out_grad_ref[...] = out_sum[...]


def rows_spec(tile, shape):
    if len(shape) == 2:
        return pl.BlockSpec((tile, shape[1]), lambda i: (i, 0))
    return pl.BlockSpec((shape[0], tile, shape[2]), lambda i: (0, i, 0))


def whole_spec(shape):
    zeros = (0,) * len(shape)
    return pl.BlockSpec(shape, lambda i: zeros)


def params():
    return pltpu.CompilerParams(vmem_limit_bytes=56 * 2**20, dimension_semantics=("arbitrary",))


def forward_call(x, gates, total, pieces, columns, experts, tasks_out, tower=None):
    height, width = x.shape
    tile = min(TILE, height)
    count = sum(piece.shape[0] for piece in pieces)
    operands = [x, gates]
    specs = [rows_spec(tile, x.shape), rows_spec(tile, gates.shape)]
    if total is not None:
        operands.append(total)
        specs.append(rows_spec(tile, total.shape))
    summed = jax.ShapeDtypeStruct((tasks_out, height, width), f32)
    scratch = []
    if tower is None:
        outs, out_specs = summed, rows_spec(tile, summed.shape)
    else:
        base, pred_grad, tower_in, tower_bias, tower_out = tower
        operands += [base, pred_grad, tower_in, tower_bias, tower_out]
        specs += [rows_spec(tile, base.shape), rows_spec(tile, pred_grad.shape)]
        specs += [whole_spec(a.shape) for a in (tower_in, tower_bias, tower_out)]
        shapes = [pred_grad.shape, summed.shape, (1, height, width)]
        ends = [tower_in.shape, tower_bias.shape, tower_out.shape]
        outs = [jax.ShapeDtypeStruct(shape, f32) for shape in shapes + ends]
        out_specs = [rows_spec(tile, s) for s in shapes] + [whole_spec(s) for s in ends]
        scratch = [pltpu.VMEM(shape, f32) for shape in ends]
    operands += pieces
    specs += [whole_spec(piece.shape) for piece in pieces]
    return pl.pallas_call(
        functools.partial(
            forward_kernel, columns, experts, tasks_out, total is None, tower is not None
        ),
        grid=(height // tile,),
        out_shape=outs,
        in_specs=specs,
        out_specs=out_specs,
        scratch_shapes=scratch,
        compiler_params=params(),
        cost_estimate=pl.CostEstimate(
            flops=4 * count * height * width * width,
            bytes_accessed=count * 4 * width * width + 8 * height * width,
            transcendentals=count * height * width,
        ),
    )(*operands)


def backward_kernel(layout, experts, tasks, extra_rows, *refs):
    refs = list(refs)
    x_ref, gate_ref, type_ref, grad_ref, stream_ref, slope_ref, spread_ref, fold_ref = refs[:8]
    at = 8
    if extra_rows:
        extra_ref = refs[at]
        at += 1
    halves = 1 + max(half for _, half, _, _ in layout)
    weight_refs = refs[at : len(refs) - 1 - halves - 5]
    at += len(weight_refs)
    stream_out_ref = refs[at]
    out_refs = refs[at + 1 : at + 1 + halves]
    in_sum, out_sum, in_bias_sum, out_bias_sum, table_sum = refs[at + 1 + halves :]
    step = pl.program_id(0)

    @pl.when(step == 0)
    def _():
        for ref in (in_sum, out_sum, in_bias_sum, out_bias_sum, table_sum):
            ref[...] = jnp.zeros_like(ref)

    x_low = x_ref[...].astype(bf16)
    height, width = x_low.shape
    gates = gate_ref[...]
    grads = [grad_ref[t] for t in range(grad_ref.shape[0])]
    lone = len(grads) == 1
    if lone:
        grads = [grads[0] * (1.0 / tasks)]
    grad_low = [grad.astype(bf16) for grad in grads]
    lanes = lax.broadcasted_iota(jnp.int32, (height, tasks * experts), 1)
    gate_grad = jnp.zeros((height, tasks * experts), f32)
    stream = stream_ref[0]
    for slot, ((ref, spot_at), (column, _, _, _)) in enumerate(zip(spot(weight_refs), layout)):
        weight_in = ref[spot_at, 0:width]
        weight_out = ref[spot_at, width : 2 * width]
        bias_in, bias_out = bias_rows(ref, spot_at, width)
        value, slope = gelu_both(mm(x_low, weight_in) + bias_in)
        hidden = value.astype(bf16)
        gate = [gates[:, t * experts + column : t * experts + column + 1] for t in range(tasks)]
        if lone:
            scale = sum(gate[1:], gate[0])
            back = mm_nt(grad_low[0], weight_out)
            result_grad = (scale * grads[0]).astype(bf16)
            hidden_grad = scale * back
            dots = jnp.sum(hidden.astype(f32) * back + bias_out * grads[0], axis=1, keepdims=True)
            for t in range(tasks):
                gate_grad = jnp.where(lanes == t * experts + column, dots, gate_grad)
        else:
            result = (mm(hidden, weight_out) + bias_out).astype(bf16).astype(f32)
            blend = gate[0] * grads[0]
            for t in range(1, tasks):
                blend += gate[t] * grads[t]
            result_grad = blend.astype(bf16)
            hidden_grad = mm_nt(result_grad, weight_out)
            for t in range(tasks):
                dots = jnp.sum(result * grads[t], axis=1, keepdims=True)
                gate_grad = jnp.where(lanes == t * experts + column, dots, gate_grad)
        before_grad32 = slope * hidden_grad
        before_grad = before_grad32.astype(bf16)
        in_sum[slot] += mm_tn(x_low, before_grad)
        out_sum[slot] += mm_tn(hidden, result_grad)
        in_bias_sum[slot : slot + 1] += jnp.sum(before_grad.astype(f32), axis=0, keepdims=True)
        out_bias_sum[slot : slot + 1] += jnp.sum(result_grad.astype(f32), axis=0, keepdims=True)
        stream += mm_nt(before_grad, weight_in).astype(bf16).astype(f32)
    stream_out_ref[0] = stream
    high = gate_grad.astype(bf16)
    rest = (gate_grad - high.astype(f32)).astype(bf16)
    table_sum[...] += mm_tn(type_ref[...], high) + mm_tn(type_ref[...], rest)

    @pl.when(step == pl.num_programs(0) - 1)
    def _():
        spread = jnp.dot(table_sum[...], spread_ref[...], precision=EXACT, preferred_element_type=f32)
        small = jnp.dot(
            spread * slope_ref[...], fold_ref[...], precision=EXACT, preferred_element_type=f32
        ).astype(bf16)
        for out_ref in out_refs:
            out_ref[...] = jnp.zeros_like(out_ref)
        units = 1 + max(unit for _, _, _, unit in layout)
        stride = 2 * width + EXTRA
        groups = out_refs[0].shape[0]
        types, lanes_small = small.shape
        for half, out_ref in enumerate(out_refs):
            for group in range(groups):
                base = units * stride
                out_ref[group, base : base + types, 0:lanes_small] = small
                base += types
                if extra_rows:
                    out_ref[group, base : base + extra_rows] = extra_ref[half].astype(bf16)
        for slot, (_, half, group, unit) in enumerate(layout):
            base = unit * stride
            out_ref = out_refs[half]
            out_ref[group, base : base + width] = in_sum[slot].astype(bf16)
            out_ref[group, base + width : base + 2 * width] = out_sum[slot].astype(bf16)
            biases = jnp.concatenate(
                [in_bias_sum[slot : slot + 1], out_bias_sum[slot : slot + 1], jnp.zeros((EXTRA - 2, width), f32)]
            )
            out_ref[group, base + 2 * width : base + stride] = biases.astype(bf16)


def backward_call(x, gates, types, grad, stream, slopes, spread, fold, extra, pieces, layout, experts, tasks):
    height, width = x.shape
    tile = min(TILE, height)
    count = len(layout)
    halves = 1 + max(half for _, half, _, _ in layout)
    units = 1 + max(unit for _, _, _, unit in layout)
    groups = 1 + max(group for _, _, group, _ in layout)
    type_count = types.shape[1]
    extra_rows = 0 if extra is None else extra.shape[1]
    rows_out = units * (2 * width + EXTRA) + type_count + extra_rows
    operands = [x, gates, types, grad, stream, slopes, spread, fold]
    specs = [rows_spec(tile, a.shape) for a in (x, gates, types, grad, stream)]
    specs += [whole_spec(a.shape) for a in (slopes, spread, fold)]
    if extra is not None:
        operands.append(extra)
        specs.append(whole_spec(extra.shape))
    operands += pieces
    specs += [whole_spec(piece.shape) for piece in pieces]
    payload = jax.ShapeDtypeStruct((groups, rows_out, width), bf16)
    return pl.pallas_call(
        functools.partial(backward_kernel, layout, experts, tasks, extra_rows),
        grid=(height // tile,),
        out_shape=[jax.ShapeDtypeStruct(stream.shape, f32)] + [payload] * halves,
        in_specs=specs,
        out_specs=[rows_spec(tile, stream.shape)] + [whole_spec(payload.shape)] * halves,
        scratch_shapes=[
            pltpu.VMEM((count, width, width), f32),
            pltpu.VMEM((count, width, width), f32),
            pltpu.VMEM((count, width), f32),
            pltpu.VMEM((count, width), f32),
            pltpu.VMEM((type_count, tasks * experts), f32),
        ],
        compiler_params=params(),
        cost_estimate=pl.CostEstimate(
            flops=12 * count * height * width * width,
            bytes_accessed=count * 8 * width * width + 16 * height * width,
            transcendentals=count * height * width,
        ),
    )(*operands)


def flip(array, axis, bits):
    size = lax.axis_size(axis)
    return lax.ppermute(array, axis, [(i, i ^ bits) for i in range(size)])


def add_low(*arrays):
    level = [a.astype(f32) for a in arrays]
    while len(level) > 1:
        level = [level[i] + level[i + 1] for i in range(0, len(level), 2)]
    return level[0].astype(bf16)


def fetch(own, groups, halves):
    held = own.shape[0] // halves
    mine = own[:held]
    got = {0: [[own[:held]], [own[held:]]][:halves]}
    if groups == 4 and held == 2:
        by_x, by_y = flip(mine, "expert", 1), flip(mine, "expert", 2)
        far = [flip(by_x[:1], "expert", 2), flip(by_y[1:], "expert", 1)]
        arrived = {1: [by_x], 2: [by_y], 3: far}
    else:
        arrived = {ro: [flip(mine, "expert", ro)] for ro in range(1, groups)}
    for ro, parts in arrived.items():
        got[ro] = [parts]
        if halves == 2:
            got[ro].append([flip(part, "rows", 1) for part in parts])
    return got


def reduce_out(payloads, groups):
    if len(payloads) == 2:
        crossed = flip(payloads[1], "rows", 1)
    else:
        crossed = flip(payloads[0], "rows", 1)
    sums = [add_low(payloads[0][ro], crossed[ro]) for ro in range(groups)]
    arrived = [sums[0]] + [flip(sums[ro], "expert", ro) for ro in range(1, groups)]
    total = add_low(*arrived)
    step = 2
    while step < lax.axis_size("rows"):
        total = add_low(total, flip(total, "rows", step))
        step *= 2
    return total


def body(
    rows_in,
    pred_grad,
    lengths,
    session_type,
    expert_in,
    expert_in_bias,
    expert_out,
    expert_out_bias,
    selector_logits,
    selector_mix,
    tower_in,
    tower_bias,
    tower_out,
):
    height, width = rows_in.shape
    layers, owned = expert_in.shape[:2]
    type_count, tasks = selector_logits.shape[1:3]
    groups, shards = lax.axis_size("expert"), lax.axis_size("rows")
    experts = groups * owned
    halves = 2 if owned % 2 == 0 else 1
    held = owned // halves
    me, row_at = lax.axis_index("expert"), lax.axis_index("rows")
    core = row_at % 2 if halves == 2 else jnp.int32(0)

    own = []
    for layer_at in range(layers):
        biases = []
        for bias in (expert_in_bias[layer_at], expert_out_bias[layer_at]):
            high = bias.astype(bf16)
            biases += [high, (bias - high.astype(f32)).astype(bf16)]
        tail = jnp.stack(biases, axis=1)
        tail = jnp.pad(tail, ((0, 0), (0, EXTRA - tail.shape[1]), (0, 0)))
        whole = jnp.concatenate([expert_in[layer_at], expert_out[layer_at], tail], axis=1)
        if halves == 2:
            whole = jnp.where(core == 0, whole, jnp.roll(whole, held, axis=0))
        own.append(whole)
    weights = [fetch(own[layer_at], groups, halves) for layer_at in range(layers)]

    session_end = jnp.cumsum(lengths)
    position = (row_at * groups + me) * height + jnp.arange(height, dtype=jnp.int32)
    begun = (position[:, None] >= (session_end - lengths)[None, :]).astype(bf16)
    type_hot = (session_type[:, None] == jnp.arange(type_count, dtype=jnp.int32)[None, :]).astype(f32)
    change = (type_hot - jnp.pad(type_hot, ((1, 0), (0, 0)))[:-1]).astype(bf16)
    types = mm(begun, change).astype(bf16)
    gate_values, gate_slopes = gate_parts(selector_logits, selector_mix)
    by_place = jnp.arange(experts)
    order = (
        owned * (me ^ (by_place // owned))
        + held * (core ^ (by_place % owned // held))
        + by_place % held
    )
    gate_values = jnp.take(gate_values, order, axis=-1).astype(bf16)
    gate_slopes = jnp.take(gate_slopes, order, axis=-1)
    quantities = gate_slopes.shape[3]
    gates = [
        mm(types, gate_values[layer_at].reshape(type_count, tasks * experts))
        for layer_at in range(layers)
    ]
    lanes = quantities * tasks * experts
    slopes = [
        jnp.transpose(gate_slopes[layer_at], (0, 2, 1, 3)).reshape(type_count, lanes)
        for layer_at in range(layers)
    ]
    lane = jnp.arange(lanes)
    spread = (lane[None, :] % (tasks * experts) == jnp.arange(tasks * experts)[:, None]).astype(f32)
    target = (lane // experts % tasks) * quantities + lane // (tasks * experts)
    small_lanes = 128
    fold = (target[:, None] == jnp.arange(small_lanes)[None, :]).astype(f32)

    def column(ro, half, unit):
        return ro * owned + half * held + unit

    def all_of(layer_at, ros):
        pieces, columns = [], []
        for ro in ros:
            for half in range(halves):
                pieces += weights[layer_at][ro][half]
                columns += [column(ro, half, unit) for unit in range(held)]
        return pieces, tuple(columns)

    waves = [[0], list(range(1, max(2, groups - 1))), list(range(max(2, groups - 1), groups))]
    waves = [wave for wave in waves if wave]

    def forward(layer_at, x, tasks_out, tower=None):
        total = None
        for wave_at, ros in enumerate(waves):
            pieces, columns = all_of(layer_at, ros)
            last = wave_at == len(waves) - 1
            total = forward_call(
                x, gates[layer_at], total, pieces, columns, experts, tasks_out, tower if last else None
            )
        return total

    streams = [rows_in]
    for layer_at in range(layers - 1):
        streams.append(streams[-1] + forward(layer_at, streams[-1], 1)[0])
    tower = (streams[-1][None], pred_grad, tower_in, tower_bias, tower_out)
    predictions, grad, stream, tower_in_grad, tower_bias_grad, tower_out_grad = forward(
        layers - 1, streams[-1], tasks, tower
    )

    tower_rows = tower_in_grad.reshape(-1, width)
    if halves == 2:
        tower_rows = tower_rows.reshape(2, -1, width)
        tower_rows = jnp.where(core == 0, tower_rows, tower_rows[::-1])
    else:
        tower_rows = tower_rows[None]
    tower_small = jnp.concatenate([tower_bias_grad.reshape(-1, width), tower_out_grad.reshape(-1, width)])
    small_rows = -(-tower_small.shape[0] // EXTRA) * EXTRA
    tower_small = jnp.pad(tower_small, ((0, small_rows - tower_small.shape[0]), (0, 0)))
    extra = jnp.concatenate(
        [tower_rows, jnp.broadcast_to(tower_small[None], (halves, *tower_small.shape))], axis=1
    )

    def own_order(mine, other):
        if halves == 1:
            return [mine]
        return [jnp.where(core == 0, mine, other), jnp.where(core == 0, other, mine)]

    stride = 2 * width + EXTRA
    in_grad, out_grad, in_bias_grad, out_bias_grad, logits_grad, mix_grad = ([None] * layers for _ in range(6))
    for layer_at in reversed(range(layers)):
        parts = {}
        small = 0.0
        for unit in range(held):
            pieces, layout = [], []
            for ro in range(groups):
                for half in range(halves):
                    whole = weights[layer_at][ro][half]
                    pieces.append(whole[unit] if len(whole) > 1 else whole[0][unit : unit + 1])
                    layout.append((column(ro, half, unit), half, ro, 0))
            carried = extra if layer_at == layers - 1 and unit == 0 else None
            stream, *payloads = backward_call(
                streams[layer_at],
                gates[layer_at],
                types,
                grad,
                stream,
                slopes[layer_at],
                spread,
                fold,
                carried,
                pieces,
                tuple(layout),
                experts,
                tasks,
            )
            total = reduce_out(payloads, groups)
            other = flip(total, "rows", 1) if halves == 2 else None
            for half, array in enumerate(own_order(total, other)):
                parts[half * held + unit] = array[:stride]
            small = small + total[stride : stride + type_count].astype(f32)
            if carried is not None:
                both = jnp.concatenate(
                    [array[stride + type_count : stride + type_count + tower_rows.shape[1]] for array in own_order(total, other)]
                )
                tower_in_sum = both.astype(f32).reshape(tower_in.shape)
                ends = total[stride + type_count + tower_rows.shape[1] :].astype(f32)
                count = tower_bias.size // width
                tower_bias_sum = ends[:count].reshape(tower_bias.shape)
                tower_out_sum = ends[count : 2 * count].reshape(tower_out.shape)
        joined = jnp.stack([parts[k] for k in range(owned)]).astype(f32)
        in_grad[layer_at] = joined[:, :width]
        out_grad[layer_at] = joined[:, width : 2 * width]
        in_bias_grad[layer_at] = joined[:, 2 * width]
        out_bias_grad[layer_at] = joined[:, 2 * width + 1]
        small = small[:, : tasks * quantities].reshape(type_count, tasks, quantities)
        selectors, bits = selector_logits.shape[3:]
        logits_grad[layer_at] = small[:, :, : selectors * bits].reshape(type_count, tasks, selectors, bits)
        mix_grad[layer_at] = small[:, :, selectors * bits :]
        grad = stream
    return (
        predictions,
        stream[0],
        jnp.stack(in_grad),
        jnp.stack(in_bias_grad),
        jnp.stack(out_grad),
        jnp.stack(out_bias_grad),
        jnp.stack(logits_grad),
        jnp.stack(mix_grad),
        tower_in_sum,
        tower_bias_sum,
        tower_out_sum,
    )


def solution(mesh):
    in_specs = (
        P(("rows", "expert"), None),
        P(("rows", "expert"), None),
        P(),
        P(),
        P(None, "expert", None, None),
        P(None, "expert", None),
        P(None, "expert", None, None),
        P(None, "expert", None),
        P(),
        P(),
        P(),
        P(),
        P(),
    )
    out_specs = (
        P(("rows", "expert"), None),
        P(("rows", "expert"), None),
        P(None, "expert", None, None),
        P(None, "expert", None),
        P(None, "expert", None, None),
        P(None, "expert", None),
        P(),
        P(),
        P(),
        P(),
        P(),
    )
    return jax.shard_map(body, mesh=mesh, in_specs=in_specs, out_specs=out_specs, check_vma=False)
```

```python
import functools
import math

import jax
import jax.numpy as jnp
import numpy as np
from jax import lax
from jax.experimental import pallas as pl
from jax.experimental.pallas import tpu as pltpu
from jax.sharding import PartitionSpec as P

SHARPNESS = 10.0
EXACT = lax.Precision.HIGHEST
bf16 = jnp.bfloat16
f32 = jnp.float32
INNER = math.sqrt(2.0 / math.pi)
CUBE = 0.044715 * INNER
TILE = 1024
TOWER_TILE = 256
LANES = 128
EXTRA = 16


def mm(a, b):
    return jnp.dot(a, b, preferred_element_type=f32)


def mm_exact(a, b):
    return jnp.dot(a, b, precision=EXACT, preferred_element_type=f32)


def mm_nt(a, b):
    return lax.dot_general(a, b, (((1,), (1,)), ((), ())), preferred_element_type=f32)


def mm_tn(a, b):
    return lax.dot_general(a, b, (((0,), (0,)), ((), ())), preferred_element_type=f32)


def gelu_both(v):
    square = v * v
    half = 0.5 + 0.5 * jnp.tanh(v * (INNER + CUBE * square))
    value = v * half
    slope = half + value * (1.0 - half) * (2.0 * INNER + 6.0 * CUBE * square)
    return value, slope


def gelu_low(v):
    square = v * v
    half = 0.5 + 0.5 * jnp.tanh(v * (INNER + CUBE * square))
    value = (v * half).astype(bf16)
    bend = (2.0 * INNER + 6.0 * CUBE * square).astype(bf16)
    half = half.astype(bf16)
    return value, half + value * (1.0 - half) * bend


FAR = pl.BlockSpec(memory_space=pl.ANY)
NEAR = pl.BlockSpec(memory_space=pltpu.VMEM)
SCALARS = pl.BlockSpec(memory_space=pltpu.SMEM)


def kernel_params():
    return pltpu.CompilerParams(vmem_limit_bytes=58 * 2**20)


def whole_spec(shape):
    zeros = (0,) * len(shape)
    return pl.BlockSpec(shape, lambda i: zeros)


def prepare_kernel(sizes, place_ref, length_ref, kind_ref, logit_ref, mix_ref, spread_logit_ref, spread_mix_ref, *outs):
    owned, halves, held, selectors, bits, tasks = sizes
    type_ref, across_ref, slope_ref, *value_refs = outs
    height, type_count = type_ref.shape
    experts = 2**bits
    sessions = length_ref.shape[1]
    chunk = min(256, sessions)
    position = (place_ref[0] + lax.broadcasted_iota(jnp.int32, (height, 1), 0)).astype(f32)
    earlier = lax.broadcasted_iota(jnp.int32, (chunk, chunk), 0) < lax.broadcasted_iota(jnp.int32, (chunk, chunk), 1)
    earlier = jnp.where(earlier, 1.0, 0.0).astype(bf16)
    kinds = lax.broadcasted_iota(jnp.int32, (type_count, chunk), 0)
    before = jnp.zeros((1, 1), f32)
    types = jnp.zeros((height, type_count), f32)
    across = jnp.zeros((type_count, height), f32)
    for at in range(0, sessions, chunk):
        lengths = length_ref[:, at : at + chunk].astype(f32)
        begin = before + mm(jnp.broadcast_to(lengths.astype(bf16), (EXTRA, chunk)), earlier)[0:1]
        before += jnp.sum(lengths, axis=1, keepdims=True)
        member = jnp.where((position >= begin) & (position < begin + lengths), 1.0, 0.0).astype(bf16)
        of_type = jnp.where(kinds == kind_ref[:, at : at + chunk], 1.0, 0.0).astype(bf16)
        types += mm_nt(member, of_type)
        across += mm_nt(of_type, member)
    type_ref[...] = types.astype(bf16)
    across_ref[...] = across.astype(bf16)

    rows = logit_ref.shape[0]
    place = lax.broadcasted_iota(jnp.int32, (rows, LANES), 1) % experts
    expert = (
        owned * ((place // owned) ^ place_ref[1])
        + held * ((place % halves) ^ place_ref[2])
        + (place // halves) % held
    )
    logits = mm_exact(logit_ref[...], spread_logit_ref[...])
    mixes = mm_exact(mix_ref[...], spread_mix_ref[...])
    mixes = [mixes[:, k * LANES : (k + 1) * LANES] for k in range(selectors)]
    top = functools.reduce(jnp.maximum, mixes)
    shares = [jnp.exp(mix - top) for mix in mixes]
    whole = functools.reduce(jnp.add, shares)
    shares = [share / whole for share in shares]
    value = jnp.zeros((rows, LANES), f32)
    reaches = []
    for k in range(selectors):
        factors, signed = [], []
        for bit in range(bits):
            at = (k * bits + bit) * LANES
            logit = logits[:, at : at + LANES]
            cubic = (-2.0 / SHARPNESS**3) * logit * logit * logit + (1.5 / SHARPNESS) * logit + 0.5
            step = jnp.where(logit <= -SHARPNESS / 2, 0.0, jnp.where(logit >= SHARPNESS / 2, 1.0, cubic))
            slope = (-6.0 / SHARPNESS**3) * logit * logit + 1.5 / SHARPNESS
            slope = jnp.where((logit > -SHARPNESS / 2) & (logit < SHARPNESS / 2), slope, 0.0)
            on = (expert >> bit) & 1 == 1
            factors.append(jnp.where(on, step, 1.0 - step))
            signed.append(jnp.where(on, slope, -slope))
        reaches.append(functools.reduce(jnp.multiply, factors))
        value += shares[k] * reaches[k]
        for bit in range(bits):
            others = [factors[b] for b in range(bits) if b != bit]
            slope_ref[k * bits + bit] = shares[k] * signed[bit] * functools.reduce(jnp.multiply, others)
    for k in range(selectors):
        slope_ref[selectors * bits + k] = shares[k] * (reaches[k] - value)

    value = value.astype(bf16).astype(f32)
    for layer_at, ref in enumerate(value_refs):
        table = value[layer_at * type_count : (layer_at + 1) * type_count]
        columns = [table[:, t * experts : (t + 1) * experts] for t in range(tasks)]
        if layer_at < len(value_refs) - 1:
            columns = [functools.reduce(jnp.add, columns) / tasks]
        for pair in range(ref.shape[0]):
            lanes = []
            for half in range(halves):
                at = pair * halves + half
                lanes += [jnp.broadcast_to(c[:, at : at + 1], (type_count, LANES)) for c in columns]
            ref[pair] = jnp.concatenate(lanes, axis=1).astype(bf16)


def prepare_call(place, lengths, session_type, logits, mixing, height, sizes):
    owned, halves, held, selectors, bits, tasks = sizes
    layers, type_count = logits.shape[:2]
    experts = 2**bits
    rows = layers * type_count
    lane = np.arange(LANES)
    source = np.arange(tasks * selectors * bits)
    task, number = source // (selectors * bits), source % (selectors * bits)
    mine = (lane[None, :] // experts == task[:, None])[:, None, :]
    spread_logit = mine & (number[:, None, None] == np.arange(selectors * bits)[None, :, None])
    source = np.arange(tasks * selectors)
    mine = (lane[None, :] // experts == (source // selectors)[:, None])[:, None, :]
    spread_mix = mine & ((source % selectors)[:, None, None] == np.arange(selectors)[None, :, None])
    spread_logit = spread_logit.reshape(spread_logit.shape[0], -1).astype(np.float32)
    spread_mix = spread_mix.reshape(spread_mix.shape[0], -1).astype(np.float32)
    outs = [
        jax.ShapeDtypeStruct((height, type_count), bf16),
        jax.ShapeDtypeStruct((type_count, height), bf16),
        jax.ShapeDtypeStruct((selectors * (bits + 1), rows, LANES), f32),
    ]
    for layer_at in range(layers):
        each = tasks if layer_at == layers - 1 else 1
        outs.append(jax.ShapeDtypeStruct((experts // halves, type_count, halves * each * LANES), bf16))
    return pl.pallas_call(
        functools.partial(prepare_kernel, sizes),
        out_shape=outs,
        in_specs=[SCALARS] + [NEAR] * 6,
        out_specs=[NEAR] * len(outs),
        compiler_params=kernel_params(),
        cost_estimate=pl.CostEstimate(flops=2 * height * lengths.size * 64, bytes_accessed=2**21, transcendentals=2**16),
    )(
        place,
        lengths.reshape(1, -1),
        session_type.reshape(1, -1),
        logits.reshape(rows, -1),
        mixing.reshape(rows, -1),
        spread_logit,
        spread_mix,
    )


def bias_rows(weights, width):
    rows = weights[2 * width : 2 * width + EXTRA].astype(f32)
    return rows[0:1] + rows[1:2], rows[2:3] + rows[3:4]


def twice(a):
    return jnp.concatenate([a, a], axis=1)


def tiles(height, most):
    tile = min(most, height)
    return [pl.ds(at, tile) for at in range(0, height, tile)]


def joined(parts, axis):
    return parts[0] if len(parts) == 1 else jnp.concatenate(parts, axis=axis)


def gates_of(types, value_ref, count):
    gates = mm(types, value_ref[...]).astype(bf16)
    return [gates[:, at * LANES : (at + 1) * LANES] for at in range(count)]


def forward_step(weights, value_ref, x_low, type_ref, total_ref, biases, keep):
    height, width = x_low.shape
    kinds = total_ref.shape[0]
    bias_in, bias_out = zip(*(bias_rows(w, width) for w in weights))
    second = joined([w[width : 2 * width] for w in weights], 0)
    for rows in tiles(height, TILE):
        gates = gates_of(type_ref[rows], value_ref, len(weights) * kinds)
        scaled = [[] for _ in range(kinds)]
        for i, w in enumerate(weights):
            hidden, slope = gelu_low(mm(x_low[rows], w[0:width]) + bias_in[i])
            keep(i, rows, hidden, slope)
            for t in range(kinds):
                scaled[t].append(twice(gates[i * kinds + t]) * hidden)
        for t in range(kinds):
            total_ref[t, rows] += mm(joined(scaled[t], 1), second)
    for i in range(len(weights)):
        for t in range(kinds):
            at = (i * kinds + t) * LANES
            biases[t] += twice(value_ref[:, at : at + LANES].astype(f32)) * bias_out[i]


def forward_end(type_ref, total_ref, biases):
    for t in range(total_ref.shape[0]):
        high = biases[t].astype(bf16)
        rest = (biases[t] - high.astype(f32)).astype(bf16)
        for rows in tiles(total_ref.shape[1], TILE):
            total_ref[t, rows] += mm(type_ref[rows], high) + mm(type_ref[rows], rest)


def backward_start(x_low, type_across, low, across, share):
    width = x_low.shape[1]
    across[0:width] = x_low[...].T
    ones = lax.broadcasted_iota(jnp.int32, (EXTRA, x_low.shape[0]), 0) == 0
    across[width:] = jnp.where(ones, 1.0, 0.0).astype(bf16)
    for t in range(low.shape[0]):
        share[t] = mm(type_across[...], low[t])


def backward_step(weights, value_ref, hiddens, slopes, outs, pair, experts, type_ref, type_across, low, stream_ref, across, share, table, scratch):
    before_grads, result_grads, products = scratch
    kinds, height, width = low.shape
    count = len(weights)
    first = joined([w[0:width] for w in weights], 1)
    for rows in tiles(height, TILE):
        gates = [twice(gate) for gate in gates_of(type_ref[rows], value_ref, count * kinds)]
        befores = []
        for i, w in enumerate(weights):
            hidden, slope = hiddens[i][rows], slopes[i][rows]
            second = w[width : 2 * width]
            result_grad = gates[i * kinds] * low[0, rows]
            for t in range(1, kinds):
                result_grad += gates[i * kinds + t] * low[t, rows]
            if kinds == 1:
                hidden_grad = mm_nt(result_grad, second).astype(bf16)
                backs = [hidden_grad]
            else:
                backs = [mm_nt(low[t, rows], second).astype(bf16) for t in range(kinds)]
                hidden_grad = gates[i * kinds] * backs[0]
                for t in range(1, kinds):
                    hidden_grad += gates[i * kinds + t] * backs[t]
            for t in range(kinds):
                product = hidden * backs[t]
                at = (i * kinds + t) * LANES
                products[rows, at : at + LANES] = functools.reduce(
                    jnp.add, [product[:, lane : lane + LANES] for lane in range(0, width, LANES)]
                )
            before = slope * hidden_grad
            before_grads[i, rows] = before
            result_grads[i, rows] = result_grad
            befores.append(before)
        stream_ref[rows] += mm_nt(joined(befores, 1), first)
    sums = mm(type_across[...], products[...])
    lanes = lax.broadcasted_iota(jnp.int32, (type_ref.shape[1], LANES), 1)
    for i, w in enumerate(weights):
        _, bias_out = bias_rows(w, width)
        first_grad = mm(across[...], before_grads[i])
        outs[i][0:width] = first_grad[0:width].astype(bf16)
        outs[i][width : 2 * width] = mm_tn(hiddens[i][...], result_grads[i]).astype(bf16)
        out_bias = jnp.zeros((1, width), f32)
        place = pair * count + i
        for t in range(kinds):
            at = (i * kinds + t) * LANES
            gate = value_ref[:, at : at + LANES].astype(f32)
            out_bias += jnp.sum(twice(gate) * share[t], axis=0, keepdims=True)
            found = jnp.sum(sums[:, at : at + LANES], axis=1, keepdims=True)
            bias_part = jnp.sum(share[t] * bias_out, axis=1, keepdims=True)
            if kinds == 1:
                some = gate > 0.0
                found = jnp.where(some, 0.5 * found / jnp.where(some, gate, 1.0), 0.0)
                table[...] = jnp.where(lanes % experts == place, found + 0.5 * bias_part, table[...])
            else:
                table[...] = jnp.where(lanes == t * experts + place, found + bias_part, table[...])
        tail = jnp.concatenate([first_grad[width : width + 1], out_bias, jnp.zeros((EXTRA - 2, width), f32)])
        outs[i][2 * width : 2 * width + EXTRA] = tail.astype(bf16)


def through_gates(table, gate_slope_ref, experts, tasks):
    quantities, type_count = gate_slope_ref.shape[:2]
    lanes = lax.broadcasted_iota(jnp.int32, (type_count, LANES), 1)
    small = jnp.zeros((type_count, LANES), f32)
    for q in range(quantities):
        product = gate_slope_ref[q] * table[...]
        for t in range(tasks):
            part = jnp.sum(jnp.where(lanes // experts == t, product, 0.0), axis=1, keepdims=True)
            small = jnp.where(lanes == t * quantities + q, part, small)
    half = type_count // 2
    return jnp.concatenate([small[:half], small[half:]], axis=1).astype(bf16)


def fetch_weights(places, buffer, sems, each):
    step = pl.program_id(0)
    for of in range(len(places) // each):

        @pl.when(step == max(of - 1, 0))
        def _(of=of):
            for i, (ref, at) in enumerate(places[of * each : (of + 1) * each]):
                pltpu.make_async_copy(ref.at[at], buffer.at[of % 2, i], sems.at[of % 2, i]).start()

    slot = lax.rem(step, 2)
    for i in range(each):
        ref, at = places[0]
        pltpu.make_async_copy(ref.at[at], buffer.at[slot, i], sems.at[slot, i]).wait()
    return [buffer.at[slot, i] for i in range(each)]


def forward_kernel(places, pieces, each, first, *refs):
    refs = list(refs)
    take = lambda count: [refs.pop(0) for _ in range(count)]
    x_ref, type_ref, value_ref = take(3)
    if not first:
        total_ref, _, _ = take(3)
    weight_refs = take(pieces)
    out_ref, hidden_ref, slope_ref, x_low, biases, buffer, sems = take(7)
    step = pl.program_id(0)
    weights = fetch_weights([(weight_refs[piece], at) for piece, at in places], buffer, sems, each)

    @pl.when(step == 0)
    def _():
        x_low[...] = x_ref[...].astype(bf16)
        biases[...] = jnp.zeros_like(biases)
        out_ref[0] = x_ref[...] if first else total_ref[0]

    def keep(i, rows, hidden, slope):
        hidden_ref[0, i, rows] = hidden
        slope_ref[0, i, rows] = slope

    forward_step(weights, value_ref.at[0], x_low, type_ref, out_ref, biases, keep)

    @pl.when(step == pl.num_programs(0) - 1)
    def _():
        forward_end(type_ref, out_ref, biases)


def forward_call(x, types, values, total, stash, pieces, places, base):
    height, width = x.shape
    pairs, type_count, lanes = values.shape
    each = lanes // LANES
    operands = [x, types, values]
    specs = [whole_spec(x.shape), whole_spec(types.shape)]
    specs.append(pl.BlockSpec((1, type_count, lanes), lambda i: (base + i, 0, 0)))
    aliases = {}
    if total is not None:
        operands += [total, *stash]
        specs += [whole_spec(total.shape), FAR, FAR]
        aliases = {4: 1, 5: 2}
    summed = jax.ShapeDtypeStruct((1, height, width), f32)
    kept = jax.ShapeDtypeStruct((pairs, each, height, width), bf16)
    kept_spec = pl.BlockSpec((1, each, height, width), lambda i: (base + i, 0, 0, 0))
    number = len(places)
    results = pl.pallas_call(
        functools.partial(forward_kernel, places, len(pieces), each, total is None),
        grid=(number // each,),
        out_shape=[summed, kept, kept],
        in_specs=specs + [FAR] * len(pieces),
        out_specs=[whole_spec(summed.shape), kept_spec, kept_spec],
        scratch_shapes=[
            pltpu.VMEM((height, width), bf16),
            pltpu.VMEM((1, type_count, width), f32),
            pltpu.VMEM((2, each, *pieces[0].shape[1:]), bf16),
            pltpu.SemaphoreType.DMA((2, each)),
        ],
        input_output_aliases=aliases,
        compiler_params=kernel_params(),
        cost_estimate=pl.CostEstimate(
            flops=4 * number * height * width * width,
            bytes_accessed=number * (4 * width * width + 4 * height * width) + 8 * height * width,
            transcendentals=number * height * width,
        ),
    )(*operands, *pieces)
    return results[0], results[1:]


def middle_kernel(places, pieces, groups, halves, held, *refs):
    refs = list(refs)
    take = lambda count: [refs.pop(0) for _ in range(count)]
    place_ref, x_ref, type_ref, across_types_ref, value_ref, gate_slope_ref, pred_grad_ref = take(7)
    tower_in_ref, tower_bias_ref, tower_out_ref = take(3)
    weight_refs = take(pieces)
    pred_ref, stream_ref, small_ref, tower_small_ref, *tower_refs = take(4 + halves)
    out_refs = [take(halves) for _ in range(held)]
    x_low, weights, hidden_all, slope_all, total, biases, low, across, share, table = take(10)
    before_grads, result_grads, products, ready, in_grad, bias_grad, out_grad, load_sem, store_sem = take(9)
    height, width = x_ref.shape
    pairs = value_ref.shape[0]
    experts = pairs * halves
    tasks = total.shape[0]

    def load(pair, i, ref, at):
        return pltpu.make_async_copy(ref.at[at], weights.at[pair, i], load_sem.at[pair, i])

    for j, (piece, at) in enumerate(places):
        load(j // halves, j % halves, weight_refs[piece], at).start()
    x_low[...] = x_ref[...].astype(bf16)
    biases[...] = jnp.zeros_like(biases)
    for t in range(tasks):
        total[t] = x_ref[...]

    def forward_pair(pair, carry):
        for i in range(halves):
            load(pair, i, weight_refs[0], 0).wait()

        def keep(i, rows, hidden, slope):
            hidden_all[pair, i, rows] = hidden
            slope_all[pair, i, rows] = slope

        forward_step(
            [weights.at[pair, i] for i in range(halves)], value_ref.at[pair], x_low, type_ref, total, biases, keep
        )
        return carry

    lax.fori_loop(0, pairs, forward_pair, 0)
    forward_end(type_ref, total, biases)

    in_grad[...] = jnp.zeros_like(in_grad)
    bias_grad[...] = jnp.zeros_like(bias_grad)
    out_grad[...] = jnp.zeros_like(out_grad)
    for rows in tiles(height, TOWER_TILE):
        summed = None
        predicted = []
        for t in range(tasks):
            closing_low = total[t, rows].astype(bf16)
            act, slope = gelu_both(mm(closing_low, tower_in_ref[t]) + tower_bias_ref[t : t + 1])
            vector = tower_out_ref[t : t + 1]
            predicted.append(jnp.sum(act * vector, axis=1, keepdims=True))
            cotangent = pred_grad_ref[rows, t : t + 1]
            out_grad[t : t + 1] += jnp.sum(act * cotangent, axis=0, keepdims=True)
            before_grad = (slope * (cotangent * vector)).astype(bf16)
            bias_grad[t : t + 1] += jnp.sum(before_grad.astype(f32), axis=0, keepdims=True)
            in_grad[t] += mm_tn(closing_low, before_grad)
            closing_grad = mm_nt(before_grad, tower_in_ref[t])
            low[t, rows] = closing_grad.astype(bf16)
            summed = closing_grad if summed is None else summed + closing_grad
        stream_ref[rows] = summed
        pred_ref[rows] = jnp.concatenate(predicted, axis=1)
    narrow = in_grad.shape[2]
    for t in range(tasks):
        wide = jnp.concatenate([in_grad[t, : width * narrow // width], in_grad[t, width * narrow // width :]], axis=1)
        if halves == 2:

            @pl.when(place_ref[2] == t)
            def _(wide=wide):
                tower_refs[0][...] = wide.astype(bf16)

            @pl.when(place_ref[2] != t)
            def _(wide=wide):
                tower_refs[1][...] = wide.astype(bf16)

        else:
            tower_refs[0][t * wide.shape[0] : (t + 1) * wide.shape[0]] = wide.astype(bf16)
    ends = [jnp.concatenate([ref[0:1], ref[1:2]], axis=1) for ref in (bias_grad, out_grad)]
    tower_small_ref[...] = jnp.concatenate([*ends, jnp.zeros((EXTRA - 2, width), f32)]).astype(bf16)

    backward_start(x_low, across_types_ref, low, across, share)
    table[...] = jnp.zeros_like(table)

    def store(unit, group, half):
        pair = group * held + unit
        return pltpu.make_async_copy(ready.at[pair, half], out_refs[unit][half].at[group], store_sem.at[pair, half])

    for unit in range(held):

        def backward_group(group, carry, unit=unit):
            pair = group * held + unit
            backward_step(
                [weights.at[pair, i] for i in range(halves)],
                value_ref.at[pair],
                [hidden_all.at[pair, i] for i in range(halves)],
                [slope_all.at[pair, i] for i in range(halves)],
                [ready.at[pair, i] for i in range(halves)],
                pair,
                experts,
                type_ref,
                across_types_ref,
                low,
                stream_ref,
                across,
                share,
                table,
                (before_grads, result_grads, products),
            )
            for half in range(halves):
                store(unit, group, half).start()
            return carry

        lax.fori_loop(0, groups, backward_group, 0)
    small_ref[...] = through_gates(table, gate_slope_ref, experts, tasks)
    for unit in range(held):

        def drain(group, carry, unit=unit):
            for half in range(halves):
                store(unit, group, half).wait()
            return carry

        lax.fori_loop(0, groups, drain, 0)


def middle_call(place, x, types, across_types, values, gate_slopes, tower, pieces, places, groups, halves, held):
    height, width = x.shape
    pairs, type_count, lanes = values.shape
    pred_grad, tower_in, tower_bias, tower_out = tower
    tasks = tower_in.shape[0]
    stride = 2 * width + EXTRA
    experts = pairs * halves
    payload = jax.ShapeDtypeStruct((groups, stride, width), bf16)
    outs = [jax.ShapeDtypeStruct(shape, f32) for shape in (pred_grad.shape, (height, width))]
    outs.append(jax.ShapeDtypeStruct((type_count // 2, 2 * LANES), bf16))
    outs.append(jax.ShapeDtypeStruct((EXTRA, width), bf16))
    outs += [jax.ShapeDtypeStruct((tower_in.size // width // halves, width), bf16)] * halves
    near = len(outs)
    outs += [payload] * (halves * held)
    layer_at = gate_slopes.shape[1] // type_count - 1
    slope_spec = pl.BlockSpec((gate_slopes.shape[0], type_count, LANES), lambda i: (0, layer_at, 0))
    kept = pltpu.VMEM((pairs, halves, height, width), bf16)
    operands = [x, types, across_types, values, gate_slopes, *tower]
    specs = [whole_spec(a.shape) for a in operands]
    specs[4] = slope_spec
    return pl.pallas_call(
        functools.partial(middle_kernel, places, len(pieces), groups, halves, held),
        grid=(1,),
        out_shape=outs,
        in_specs=[SCALARS] + specs + [FAR] * len(pieces),
        out_specs=[whole_spec(out.shape) for out in outs[:near]] + [FAR] * (halves * held),
        scratch_shapes=[
            pltpu.VMEM((height, width), bf16),
            pltpu.VMEM((pairs, halves, stride, width), bf16),
            kept,
            kept,
            pltpu.VMEM((tasks, height, width), f32),
            pltpu.VMEM((tasks, type_count, width), f32),
            pltpu.VMEM((tasks, height, width), bf16),
            pltpu.VMEM((width + EXTRA, height), bf16),
            pltpu.VMEM((tasks, type_count, width), f32),
            pltpu.VMEM((type_count, LANES), f32),
            pltpu.VMEM((halves, height, width), bf16),
            pltpu.VMEM((halves, height, width), bf16),
            pltpu.VMEM((height, lanes), bf16),
            pltpu.VMEM((pairs, halves, stride, width), bf16),
            pltpu.VMEM(tower_in.shape, f32),
            pltpu.VMEM(tower_bias.shape, f32),
            pltpu.VMEM(tower_out.shape, f32),
            pltpu.SemaphoreType.DMA((pairs, halves)),
            pltpu.SemaphoreType.DMA((pairs, halves)),
        ],
        compiler_params=kernel_params(),
        cost_estimate=pl.CostEstimate(
            flops=14 * experts * height * width * width,
            bytes_accessed=experts * 8 * width * width + 16 * height * width,
            transcendentals=experts * height * width,
        ),
    )(place, *operands, *pieces)


def backward_kernel(places, pieces, each, held, unit, tasks, *refs):
    refs = list(refs)
    take = lambda count: [refs.pop(0) for _ in range(count)]
    x_ref, type_ref, across_types_ref, grad_ref, stream_ref, gate_slope_ref, value_ref, hidden_ref, slope_ref = take(9)
    weight_refs = take(pieces)
    stream_out_ref, small_ref = take(2)
    out_refs = take(each)
    x_low, across, low, share, table, before_grads, result_grads, products, buffer, sems = take(10)
    step = pl.program_id(0)
    groups = pl.num_programs(0)
    weights = fetch_weights([(weight_refs[piece], at) for piece, at in places], buffer, sems, each)

    @pl.when(step == 0)
    def _():
        x_low[...] = x_ref[...].astype(bf16)
        low[0] = grad_ref[...].astype(bf16)
        stream_out_ref[...] = stream_ref[...]
        table[...] = jnp.zeros_like(table)
        backward_start(x_low, across_types_ref, low, across, share)

    experts = len(places) * held
    backward_step(
        weights,
        value_ref.at[0],
        [hidden_ref.at[0, i] for i in range(each)],
        [slope_ref.at[0, i] for i in range(each)],
        [ref.at[0] for ref in out_refs],
        step * held + unit,
        experts,
        type_ref,
        across_types_ref,
        low,
        stream_out_ref,
        across,
        share,
        table,
        (before_grads, result_grads, products),
    )

    @pl.when(step == groups - 1)
    def _():
        small_ref[...] = through_gates(table, gate_slope_ref, experts, tasks)


def backward_call(x, types, across_types, grad, stream, gate_slopes, layer_at, values, stash, pieces, places, held, unit, tasks):
    height, width = x.shape
    pairs, type_count, lanes = values.shape
    each = lanes // LANES
    groups = pairs // held
    stride = 2 * width + EXTRA
    operands = [x, types, across_types, grad, stream, gate_slopes, values, *stash]
    specs = [whole_spec(a.shape) for a in operands[:5]]
    specs.append(pl.BlockSpec((gate_slopes.shape[0], type_count, LANES), lambda i: (0, layer_at, 0)))
    specs.append(pl.BlockSpec((1, type_count, lanes), lambda i: (i * held + unit, 0, 0)))
    specs += [pl.BlockSpec((1, each, height, width), lambda i: (i * held + unit, 0, 0, 0))] * 2
    payload = jax.ShapeDtypeStruct((groups, stride, width), bf16)
    small = jax.ShapeDtypeStruct((type_count // 2, 2 * LANES), bf16)
    number = groups * each
    return pl.pallas_call(
        functools.partial(backward_kernel, places, len(pieces), each, held, unit, tasks),
        grid=(groups,),
        out_shape=[jax.ShapeDtypeStruct(stream.shape, f32), small] + [payload] * each,
        in_specs=specs + [FAR] * len(pieces),
        out_specs=[whole_spec(stream.shape), whole_spec(small.shape)]
        + [pl.BlockSpec((1, stride, width), lambda i: (i, 0, 0))] * each,
        scratch_shapes=[
            pltpu.VMEM((height, width), bf16),
            pltpu.VMEM((width + EXTRA, height), bf16),
            pltpu.VMEM((1, height, width), bf16),
            pltpu.VMEM((1, type_count, width), f32),
            pltpu.VMEM((type_count, LANES), f32),
            pltpu.VMEM((each, height, width), bf16),
            pltpu.VMEM((each, height, width), bf16),
            pltpu.VMEM((height, lanes), bf16),
            pltpu.VMEM((2, each, stride, width), bf16),
            pltpu.SemaphoreType.DMA((2, each)),
        ],
        compiler_params=kernel_params(),
        cost_estimate=pl.CostEstimate(
            flops=8 * number * height * width * width,
            bytes_accessed=number * (8 * width * width + 4 * height * width) + 16 * height * width,
            transcendentals=0,
        ),
    )(*operands, *pieces)


def finish_kernel(layer_at, unit, held, halves, rows, first, *refs):
    refs = list(refs)
    take = lambda count: [refs.pop(0) for _ in range(count)]
    place_ref = take(1)[0]
    sources = take(halves)
    if not first:
        _, _, in_bias_ref, out_bias_ref = take(4)
    in_ref, out_ref, in_bias_out_ref, out_bias_out_ref, ready, sems = refs
    copies = []
    for half, source in enumerate(sources):
        where = held * (place_ref[2] ^ half) + unit
        for which, ref in enumerate((in_ref, out_ref)):
            ready[half, which] = source[which * rows : (which + 1) * rows].astype(f32)
            copy = pltpu.make_async_copy(ready.at[half, which], ref.at[layer_at, where], sems.at[half, which])
            copy.start()
            copies.append(copy)
    in_bias_out_ref[...] = jnp.zeros_like(in_bias_out_ref) if first else in_bias_ref[...]
    out_bias_out_ref[...] = jnp.zeros_like(out_bias_out_ref) if first else out_bias_ref[...]
    for half, source in enumerate(sources):
        where = held * (place_ref[2] ^ half) + unit
        tail = source[2 * rows : 2 * rows + EXTRA].astype(f32)
        in_bias_out_ref[layer_at, pl.ds(where, 1)] = tail[0:1]
        out_bias_out_ref[layer_at, pl.ds(where, 1)] = tail[1:2]
    for copy in copies:
        copy.wait()


def finish_call(place, sources, held_arrays, layer_at, unit, held, shape):
    halves = len(sources)
    rows, width = shape[2:]
    outs = [jax.ShapeDtypeStruct(shape, f32)] * 2
    outs += [jax.ShapeDtypeStruct((*shape[:2], width), f32)] * 2
    first = held_arrays is None
    aliases = {} if first else {1 + halves: 0, 2 + halves: 1}
    return pl.pallas_call(
        functools.partial(finish_kernel, layer_at, unit, held, halves, rows, first),
        out_shape=outs,
        in_specs=[SCALARS] + [NEAR] * halves + ([] if first else [FAR, FAR, NEAR, NEAR]),
        out_specs=[FAR, FAR, NEAR, NEAR],
        scratch_shapes=[
            pltpu.VMEM((halves, 2, rows, width), f32),
            pltpu.SemaphoreType.DMA((halves, 2)),
        ],
        input_output_aliases=aliases,
        compiler_params=kernel_params(),
        cost_estimate=pl.CostEstimate(flops=0, bytes_accessed=halves * 12 * rows * width, transcendentals=0),
    )(place, *sources, *([] if first else held_arrays))


def flip(array, axis, bits):
    size = lax.axis_size(axis)
    return lax.ppermute(array, axis, [(i, i ^ bits) for i in range(size)])


def add_low(*arrays):
    level = [a.astype(f32) for a in arrays]
    while len(level) > 1:
        level = [level[i] + level[i + 1] for i in range(0, len(level), 2)]
    return level[0].astype(bf16)


def after(arrays, others):
    return lax.optimization_barrier((arrays, others))[0]


def near(mine, groups):
    if groups == 4 and mine.shape[0] == 2:
        return {1: [flip(mine, "expert", 1)], 2: [flip(mine, "expert", 2)]}
    return {ro: [flip(mine, "expert", ro)] for ro in range(1, groups)}


def relay(arrived, groups, held):
    if groups == 4 and held == 2:
        return {3: [flip(arrived[1][0][:1], "expert", 2), flip(arrived[2][0][1:], "expert", 1)]}
    return {}


def crossed(parts, halves):
    return [] if halves == 1 else [flip(part, "rows", 1) for part in parts]


def scatter_start(sums, groups):
    return [sums[0]] + [flip(sums[ro], "expert", ro) for ro in range(1, groups)]


def body(
    rows_in,
    pred_grad,
    lengths,
    session_type,
    expert_in,
    expert_in_bias,
    expert_out,
    expert_out_bias,
    selector_logits,
    selector_mix,
    tower_in,
    tower_bias,
    tower_out,
):
    height, width = rows_in.shape
    layers, owned = expert_in.shape[:2]
    type_count, tasks = selector_logits.shape[1:3]
    selectors, bits = selector_logits.shape[3:]
    groups = lax.axis_size("expert")
    halves = 2 if owned % 2 == 0 else 1
    held = owned // halves
    stride = 2 * width + EXTRA
    me, row_at = lax.axis_index("expert"), lax.axis_index("rows")
    core = row_at % 2 if halves == 2 else jnp.int32(0)
    place = jnp.stack([(row_at * groups + me) * height, me, core]).astype(jnp.int32)

    def rows_of(layer_at, first):
        cut = lambda a: lax.dynamic_slice_in_dim(a[layer_at], first, held)
        tail = []
        for bias in (cut(expert_in_bias), cut(expert_out_bias)):
            high = bias.astype(bf16)
            tail += [high, (bias - high.astype(f32)).astype(bf16)]
        tail = jnp.pad(jnp.stack(tail, axis=1), ((0, 0), (0, EXTRA - len(tail)), (0, 0)))
        return jnp.concatenate([cut(expert_in), cut(expert_out), tail], axis=1)

    own = [[rows_of(layer_at, held * (core ^ half)) for half in range(halves)] for layer_at in range(layers)]
    sizes = (owned, halves, held, selectors, bits, tasks)
    types, across_types, gate_slopes, *values = prepare_call(
        place, lengths, session_type, selector_logits, selector_mix, height, sizes
    )

    def parts_of(got, across):
        pieces, places = [], {}
        for ro in got:
            spots = []
            for parts in (got[ro], across[ro]):
                here = []
                for part in parts:
                    here += [(len(pieces), at) for at in range(part.shape[0])]
                    pieces.append(part)
                if here:
                    spots.append(here)
            places[ro] = [[spots[half][unit] for half in range(halves)] for unit in range(held)]
        return pieces, places

    def pair_order(places, units):
        return tuple(spot for ro in sorted(places) for unit in units for spot in places[ro][unit])

    streams, stashes, weights = [rows_in], [], []
    for layer_at in range(layers):
        last = layer_at == layers - 1
        got = near(own[layer_at][0], groups)
        if layer_at == 0:
            got = after(got, types)
        far = relay(got, groups, held)
        across = {ro: crossed(got[ro], halves) for ro in got}
        if not last:
            own[layer_at + 1] = after(own[layer_at + 1], across)
        got = {0: own[layer_at][:1], **got}
        across[0] = own[layer_at][1:]
        if not last:
            pieces, places = parts_of(got, across)
            total, stash = forward_call(
                streams[-1], types, values[layer_at], None, None, pieces, pair_order(places, range(held)), 0
            )
            far = after(far, total)
        elif streams[1:]:
            far = after(far, streams[-1])
        far_across = {ro: crossed(far[ro], halves) for ro in far}
        if not last:
            if far:
                pieces, places = parts_of(far, far_across)
                base = held * min(far)
                order = pair_order(places, range(held))
                total, stash = forward_call(
                    streams[-1], types, values[layer_at], total, stash, pieces, order, base
                )
            streams.append(total[0])
            stashes.append(stash)
        weights.append(parts_of({**got, **far}, {**across, **far_across}))

    pieces, places = weights[-1]
    predictions, stream, small, tower_small, *rest = middle_call(
        place,
        streams[-1],
        types,
        across_types,
        values[-1],
        gate_slopes,
        (pred_grad, tower_in, tower_bias, tower_out),
        pieces,
        pair_order(places, range(held)),
        groups,
        halves,
        held,
    )
    tower_rows, rest = rest[:halves], rest[halves:]
    payloads = [rest[unit * halves : (unit + 1) * halves] for unit in range(held)]

    tower_tail = tower_rows[0]
    if halves == 2:
        tower_tail = add_low(tower_rows[0], flip(tower_rows[1], "rows", 1))
    tails = [[] for _ in range(held - 1)] + [[small, tower_small, tower_tail]]

    shards = lax.axis_size("rows")
    if shards == 8 and halves == 2:
        hops = [[(0, 1), (3, 2)], [(1, 2), (2, 1)], [(1, 0), (2, 3)]]
        hops = [[(2 * a + c, 2 * b + c) for a, b in hop for c in range(2)] for hop in hops]
    else:
        hops = [[(i, i ^ (2 << at)) for i in range(shards)] for at in range(shards.bit_length() - 2)]
    outer = (row_at < 2) | (row_at >= shards - 2)
    line = shards == 8 and halves == 2

    class Moving:
        def __init__(self, layer_at, unit, sums):
            self.layer_at, self.unit, self.sums, self.got, self.hops = layer_at, unit, sums, None, -1

        def ask(self, token):
            if self.got is None:
                self.got = scatter_start(after(self.sums, token), groups)
            elif self.hops < len(hops):
                total = after(self.total, token)
                self.got = [total, lax.ppermute(total, "rows", hops[self.hops])]
            else:
                self.got = [self.total] + ([flip(after(self.total, token), "rows", 1)] if halves == 2 else [])

        def add(self):
            if self.hops == len(hops):
                return True
            if line and self.hops == len(hops) - 1:
                self.total = jnp.where(outer, self.got[1], self.got[0])
            else:
                self.total = add_low(*self.got)
            self.hops += 1
            return False

    def arrive(entries, others):
        got, others = lax.optimization_barrier(([entry.got for entry in entries], others))
        for entry, what in zip(entries, got):
            entry.got = what
        ended = [entry for entry in entries if entry.add()]
        return ([entry.total for entry in entries], others), ended

    def core_received(payloads):
        return lax.optimization_barrier([flip(payload[-1], "rows", 1) for payload in payloads])

    def core_sums(payload, received, tails):
        if halves == 1:
            tails = [add_low(a, flip(a, "rows", 1)) for a in tails]
        return [
            jnp.concatenate([add_low(payload[0][ro], received[ro]), *tails], axis=0) for ro in range(groups)
        ]

    moving = []
    for unit, received in enumerate(core_received(payloads)):
        sums = core_sums(payloads[unit], received, tails[unit])
        stream = after(stream, sums)
        moving.append(Moving(layers - 1, unit, sums))
    moving[0].ask(())

    for layer_at in reversed(range(layers - 1)):
        pieces, places = weights[layer_at]
        fresh = []
        grad = stream
        for unit in range(held):
            stream, small, *payload = backward_call(
                streams[layer_at],
                types,
                across_types,
                grad,
                stream,
                gate_slopes,
                layer_at,
                values[layer_at],
                stashes[layer_at],
                pieces,
                pair_order(places, [unit]),
                held,
                unit,
                tasks,
            )
            beside = moving if unit == held - 1 else moving[: unit + 1]
            token, _ = arrive(beside, stream)
            stream = after(stream, token)
            if unit < held - 1:
                for entry in moving[: unit + 2]:
                    entry.ask(token)
            fresh.append((payload, small))
        received = core_received(after([payload for payload, _ in fresh], token))
        small = sum(part.astype(f32) for _, part in fresh).astype(bf16)
        for unit, (payload, _) in enumerate(fresh):
            sums = core_sums(payload, received[unit], [] if unit else [small])
            token = (token, sums)
            moving = moving + [Moving(layer_at, unit, sums)]

    arrays = None
    gate_grads = [0.0] * layers

    def finish(entry):
        nonlocal arrays, tower_bias_sum, tower_out_sum, tower_rows
        layer_at, unit, sources = entry.layer_at, entry.unit, entry.got
        arrays = finish_call(place, sources, arrays, layer_at, unit, held, expert_in.shape)
        if sources[0].shape[0] > stride:
            both = functools.reduce(jnp.add, [a[stride:].astype(f32) for a in sources])
            gate_grads[layer_at] = gate_grads[layer_at] + both[: type_count // 2]
            if layer_at == layers - 1:
                at = type_count // 2
                tower_bias_sum = both[at].reshape(tower_bias.shape)
                tower_out_sum = both[at + 1].reshape(tower_out.shape)
                tower_rows = [a[stride + at + EXTRA :].astype(f32) for a in sources]

    tower_bias_sum = tower_out_sum = tower_rows = None
    others = ()
    started = layers * held - held + 1
    while moving:
        for entry in moving[:started]:
            entry.ask(token)
        token, ended = arrive(moving[:started], others)
        moving = [entry for entry in moving if entry not in ended]
        started += 1 - len(ended)
        for entry in ended:
            finish(entry)
        others = (arrays, gate_grads, tower_rows) if ended else ()
    if halves == 2:
        tower_rows = [jnp.where(core == 0, *tower_rows), jnp.where(core == 0, *tower_rows[::-1])]
    wide = jnp.concatenate(tower_rows).reshape(tasks, -1, width)
    narrow = tower_in.shape[2]
    tower_in_sum = jnp.concatenate([wide[:, :, at : at + narrow] for at in range(0, width, narrow)], axis=1)
    quantities = selectors * (bits + 1)
    small = jnp.stack(gate_grads)
    small = jnp.concatenate([small[..., :LANES], small[..., LANES:]], axis=1)[..., : tasks * quantities]
    small = small.reshape(layers, type_count, tasks, quantities)
    logits_grad = small[..., : selectors * bits].reshape(selector_logits.shape)
    return (
        predictions,
        stream,
        arrays[0],
        arrays[2],
        arrays[1],
        arrays[3],
        logits_grad,
        small[..., selectors * bits :],
        tower_in_sum,
        tower_bias_sum,
        tower_out_sum,
    )


def solution(mesh):
    in_specs = (
        P(("rows", "expert"), None),
        P(("rows", "expert"), None),
        P(),
        P(),
        P(None, "expert", None, None),
        P(None, "expert", None),
        P(None, "expert", None, None),
        P(None, "expert", None),
        P(),
        P(),
        P(),
        P(),
        P(),
    )
    out_specs = (
        P(("rows", "expert"), None),
        P(("rows", "expert"), None),
        P(None, "expert", None, None),
        P(None, "expert", None),
        P(None, "expert", None, None),
        P(None, "expert", None),
        P(),
        P(),
        P(),
        P(),
        P(),
    )
    return jax.shard_map(body, mesh=mesh, in_specs=in_specs, out_specs=out_specs, check_vma=False)
```

```python
import functools
import math

import jax
import jax.numpy as jnp
import numpy as np
from jax import lax
from jax.experimental import pallas as pl
from jax.experimental.pallas import tpu as pltpu
from jax.sharding import PartitionSpec as P

SHARPNESS = 10.0
EXACT = lax.Precision.HIGHEST
bf16 = jnp.bfloat16
f32 = jnp.float32
INNER = math.sqrt(2.0 / math.pi)
CUBE = 0.044715 * INNER
TILE = 1024
TOWER_TILE = 256
LANES = 128
EXTRA = 16


def mm(a, b):
    return jnp.dot(a, b, preferred_element_type=f32)


def mm_exact(a, b):
    return jnp.dot(a, b, precision=EXACT, preferred_element_type=f32)


def mm_nt(a, b):
    return lax.dot_general(a, b, (((1,), (1,)), ((), ())), preferred_element_type=f32)


def mm_tn(a, b):
    return lax.dot_general(a, b, (((0,), (0,)), ((), ())), preferred_element_type=f32)


def gelu_both(v):
    square = v * v
    half = 0.5 + 0.5 * jnp.tanh(v * (INNER + CUBE * square))
    value = v * half
    slope = half + value * (1.0 - half) * (2.0 * INNER + 6.0 * CUBE * square)
    return value, slope


def gelu_low(v):
    bend = 2.0 * INNER + 8.0 * CUBE * (v * v)
    twice_share = 1.0 + jnp.tanh(v * bend)
    value = (v * twice_share).astype(bf16)
    bend, twice_share = bend.astype(bf16), twice_share.astype(bf16)
    rise = 3.0 * bend - 4.0 * INNER
    return value, twice_share + value * (2.0 - twice_share) * rise


FAR = pl.BlockSpec(memory_space=pl.ANY)
NEAR = pl.BlockSpec(memory_space=pltpu.VMEM)
SCALARS = pl.BlockSpec(memory_space=pltpu.SMEM)


def kernel_params():
    return pltpu.CompilerParams(vmem_limit_bytes=58 * 2**20)


def whole_spec(shape):
    zeros = (0,) * len(shape)
    return pl.BlockSpec(shape, lambda i: zeros)


def prepare_kernel(sizes, place_ref, length_ref, kind_ref, logit_ref, mix_ref, spread_logit_ref, spread_mix_ref, *outs):
    owned, halves, held, selectors, bits, tasks = sizes
    type_ref, across_ref, slope_ref, *value_refs = outs
    height, type_count = type_ref.shape
    experts = 2**bits
    sessions = length_ref.shape[1]
    chunk = min(256, sessions)
    position = (place_ref[0] + lax.broadcasted_iota(jnp.int32, (height, 1), 0)).astype(f32)
    earlier = lax.broadcasted_iota(jnp.int32, (chunk, chunk), 0) < lax.broadcasted_iota(jnp.int32, (chunk, chunk), 1)
    earlier = jnp.where(earlier, 1.0, 0.0).astype(bf16)
    kinds = lax.broadcasted_iota(jnp.int32, (type_count, chunk), 0)
    before = jnp.zeros((1, 1), f32)
    types = jnp.zeros((height, type_count), f32)
    across = jnp.zeros((type_count, height), f32)
    for at in range(0, sessions, chunk):
        lengths = length_ref[:, at : at + chunk].astype(f32)
        begin = before + mm(jnp.broadcast_to(lengths.astype(bf16), (EXTRA, chunk)), earlier)[0:1]
        before += jnp.sum(lengths, axis=1, keepdims=True)
        member = jnp.where((position >= begin) & (position < begin + lengths), 1.0, 0.0).astype(bf16)
        of_type = jnp.where(kinds == kind_ref[:, at : at + chunk], 1.0, 0.0).astype(bf16)
        types += mm_nt(member, of_type)
        across += mm_nt(of_type, member)
    type_ref[...] = types.astype(bf16)
    across_ref[...] = across.astype(bf16)

    rows = logit_ref.shape[0]
    place = lax.broadcasted_iota(jnp.int32, (rows, LANES), 1) % experts
    expert = (
        owned * ((place // owned) ^ place_ref[1])
        + held * ((place % halves) ^ place_ref[2])
        + (place // halves) % held
    )
    logits = mm_exact(logit_ref[...], spread_logit_ref[...])
    mixes = mm_exact(mix_ref[...], spread_mix_ref[...])
    mixes = [mixes[:, k * LANES : (k + 1) * LANES] for k in range(selectors)]
    top = functools.reduce(jnp.maximum, mixes)
    shares = [jnp.exp(mix - top) for mix in mixes]
    whole = functools.reduce(jnp.add, shares)
    shares = [share / whole for share in shares]
    value = jnp.zeros((rows, LANES), f32)
    reaches = []
    for k in range(selectors):
        factors, signed = [], []
        for bit in range(bits):
            at = (k * bits + bit) * LANES
            logit = logits[:, at : at + LANES]
            cubic = (-2.0 / SHARPNESS**3) * logit * logit * logit + (1.5 / SHARPNESS) * logit + 0.5
            step = jnp.where(logit <= -SHARPNESS / 2, 0.0, jnp.where(logit >= SHARPNESS / 2, 1.0, cubic))
            slope = (-6.0 / SHARPNESS**3) * logit * logit + 1.5 / SHARPNESS
            slope = jnp.where((logit > -SHARPNESS / 2) & (logit < SHARPNESS / 2), slope, 0.0)
            on = (expert >> bit) & 1 == 1
            factors.append(jnp.where(on, step, 1.0 - step))
            signed.append(jnp.where(on, slope, -slope))
        reaches.append(functools.reduce(jnp.multiply, factors))
        value += shares[k] * reaches[k]
        for bit in range(bits):
            others = [factors[b] for b in range(bits) if b != bit]
            slope_ref[k * bits + bit] = shares[k] * signed[bit] * functools.reduce(jnp.multiply, others)
    for k in range(selectors):
        slope_ref[selectors * bits + k] = shares[k] * (reaches[k] - value)

    value = value.astype(bf16).astype(f32)
    for layer_at, ref in enumerate(value_refs):
        table = value[layer_at * type_count : (layer_at + 1) * type_count]
        columns = [table[:, t * experts : (t + 1) * experts] for t in range(tasks)]
        if layer_at < len(value_refs) - 1:
            columns = [functools.reduce(jnp.add, columns) / tasks]
        for pair in range(ref.shape[0]):
            lanes = []
            for half in range(halves):
                at = pair * halves + half
                lanes += [jnp.broadcast_to(c[:, at : at + 1], (type_count, LANES)) for c in columns]
            ref[pair] = jnp.concatenate(lanes, axis=1).astype(bf16)


def prepare_call(place, lengths, session_type, logits, mixing, height, sizes):
    owned, halves, held, selectors, bits, tasks = sizes
    layers, type_count = logits.shape[:2]
    experts = 2**bits
    rows = layers * type_count
    lane = np.arange(LANES)
    source = np.arange(tasks * selectors * bits)
    task, number = source // (selectors * bits), source % (selectors * bits)
    mine = (lane[None, :] // experts == task[:, None])[:, None, :]
    spread_logit = mine & (number[:, None, None] == np.arange(selectors * bits)[None, :, None])
    source = np.arange(tasks * selectors)
    mine = (lane[None, :] // experts == (source // selectors)[:, None])[:, None, :]
    spread_mix = mine & ((source % selectors)[:, None, None] == np.arange(selectors)[None, :, None])
    spread_logit = spread_logit.reshape(spread_logit.shape[0], -1).astype(np.float32)
    spread_mix = spread_mix.reshape(spread_mix.shape[0], -1).astype(np.float32)
    outs = [
        jax.ShapeDtypeStruct((height, type_count), bf16),
        jax.ShapeDtypeStruct((type_count, height), bf16),
        jax.ShapeDtypeStruct((selectors * (bits + 1), rows, LANES), f32),
    ]
    for layer_at in range(layers):
        each = tasks if layer_at == layers - 1 else 1
        outs.append(jax.ShapeDtypeStruct((experts // halves, type_count, halves * each * LANES), bf16))
    return pl.pallas_call(
        functools.partial(prepare_kernel, sizes),
        out_shape=outs,
        in_specs=[SCALARS] + [NEAR] * 6,
        out_specs=[NEAR] * len(outs),
        compiler_params=kernel_params(),
        cost_estimate=pl.CostEstimate(flops=2 * height * lengths.size * 64, bytes_accessed=2**21, transcendentals=2**16),
    )(
        place,
        lengths.reshape(1, -1),
        session_type.reshape(1, -1),
        logits.reshape(rows, -1),
        mixing.reshape(rows, -1),
        spread_logit,
        spread_mix,
    )


def bias_rows(weights, width):
    rows = weights[2 * width : 2 * width + EXTRA].astype(f32)
    return rows[0:1] + rows[1:2], rows[2:3] + rows[3:4]


def twice(a):
    return jnp.concatenate([a, a], axis=1)


def tiles(height, most):
    tile = min(most, height)
    return [pl.ds(at, tile) for at in range(0, height, tile)]


def joined(parts, axis):
    return parts[0] if len(parts) == 1 else jnp.concatenate(parts, axis=axis)


def gates_of(types, value_ref, count):
    gates = mm(types, value_ref[...]).astype(bf16)
    return [gates[:, at * LANES : (at + 1) * LANES] for at in range(count)]


def forward_step(weights, value_ref, x_low, type_ref, total_ref, biases, keep, keep_gate=None):
    height, width = x_low.shape
    kinds = total_ref.shape[0]
    bias_in, bias_out = zip(*(bias_rows(w, width) for w in weights))
    second = joined([w[width : 2 * width] for w in weights], 0)
    for rows in tiles(height, TILE):
        gates = gates_of(type_ref[rows], value_ref, len(weights) * kinds)
        if keep_gate is not None:
            for at, gate in enumerate(gates):
                keep_gate(at, rows, gate)
        scaled = [[] for _ in range(kinds)]
        for i, w in enumerate(weights):
            hidden, slope = gelu_low(mm(x_low[rows], w[0:width]) + bias_in[i])
            keep(i, rows, hidden, slope)
            for t in range(kinds):
                scaled[t].append(twice(gates[i * kinds + t]) * hidden)
        for t in range(kinds):
            total_ref[t, rows] += mm(joined(scaled[t], 1), second)
    for i in range(len(weights)):
        for t in range(kinds):
            at = (i * kinds + t) * LANES
            biases[t] += twice(value_ref[:, at : at + LANES].astype(f32)) * bias_out[i]


def forward_end(type_ref, total_ref, biases):
    for t in range(total_ref.shape[0]):
        high = biases[t].astype(bf16)
        rest = (biases[t] - high.astype(f32)).astype(bf16)
        for rows in tiles(total_ref.shape[1], TILE):
            total_ref[t, rows] += mm(type_ref[rows], high) + mm(type_ref[rows], rest)


def backward_start(x_low, type_across, low, across, share):
    width = x_low.shape[1]
    across[0:width] = x_low[...].T
    ones = lax.broadcasted_iota(jnp.int32, (EXTRA, x_low.shape[0]), 0) == 0
    across[width:] = jnp.where(ones, 1.0, 0.0).astype(bf16)
    for t in range(low.shape[0]):
        share[t] = mm(type_across[...], low[t])


def backward_step(weights, value_ref, hiddens, slopes, outs, pair, experts, type_ref, type_across, low, stream_ref, across, share, table, scratch, kept_gates=None):
    before_grads, result_grads, products = scratch
    kinds, height, width = low.shape
    count = len(weights)
    first = joined([w[0:width] for w in weights], 1)
    for rows in tiles(height, TILE):
        if kept_gates is None:
            gates = gates_of(type_ref[rows], value_ref, count * kinds)
        else:
            gates = [kept_gates[at, rows] for at in range(count * kinds)]
        gates = [twice(gate) for gate in gates]
        befores = []
        for i, w in enumerate(weights):
            hidden, slope = hiddens[i][rows], slopes[i][rows]
            second = w[width : 2 * width]
            result_grad = gates[i * kinds] * low[0, rows]
            for t in range(1, kinds):
                result_grad += gates[i * kinds + t] * low[t, rows]
            if kinds == 1:
                hidden_grad = mm_nt(result_grad, second).astype(bf16)
                backs = [hidden_grad]
            else:
                backs = [mm_nt(low[t, rows], second).astype(bf16) for t in range(kinds)]
                hidden_grad = gates[i * kinds] * backs[0]
                for t in range(1, kinds):
                    hidden_grad += gates[i * kinds + t] * backs[t]
            for t in range(kinds):
                product = hidden * backs[t]
                at = (i * kinds + t) * LANES
                products[rows, at : at + LANES] = functools.reduce(
                    jnp.add, [product[:, lane : lane + LANES] for lane in range(0, width, LANES)]
                )
            before = slope * hidden_grad
            before_grads[i, rows] = before
            result_grads[i, rows] = result_grad
            befores.append(before)
        stream_ref[rows] += mm_nt(joined(befores, 1), first)
    sums = mm(type_across[...], products[...])
    lanes = lax.broadcasted_iota(jnp.int32, (type_ref.shape[1], LANES), 1)
    for i, w in enumerate(weights):
        _, bias_out = bias_rows(w, width)
        first_grad = 0.5 * mm(across[...], before_grads[i])
        outs[i][0:width] = first_grad[0:width].astype(bf16)
        outs[i][width : 2 * width] = mm_tn(hiddens[i][...], result_grads[i]).astype(bf16)
        out_bias = jnp.zeros((1, width), f32)
        place = pair * count + i
        for t in range(kinds):
            at = (i * kinds + t) * LANES
            gate = value_ref[:, at : at + LANES].astype(f32)
            out_bias += jnp.sum(twice(gate) * share[t], axis=0, keepdims=True)
            found = jnp.sum(sums[:, at : at + LANES], axis=1, keepdims=True)
            bias_part = jnp.sum(share[t] * bias_out, axis=1, keepdims=True)
            if kinds == 1:
                some = gate > 0.0
                found = jnp.where(some, 0.5 * found / jnp.where(some, gate, 1.0), 0.0)
                table[...] = jnp.where(lanes % experts == place, found + 0.5 * bias_part, table[...])
            else:
                table[...] = jnp.where(lanes == t * experts + place, found + bias_part, table[...])
        tail = jnp.concatenate([first_grad[width : width + 1], out_bias, jnp.zeros((EXTRA - 2, width), f32)])
        outs[i][2 * width : 2 * width + EXTRA] = tail.astype(bf16)


def through_gates(table, gate_slope_ref, experts, tasks):
    quantities, type_count = gate_slope_ref.shape[:2]
    lanes = lax.broadcasted_iota(jnp.int32, (type_count, LANES), 1)
    small = jnp.zeros((type_count, LANES), f32)
    for q in range(quantities):
        product = gate_slope_ref[q] * table[...]
        for t in range(tasks):
            part = jnp.sum(jnp.where(lanes // experts == t, product, 0.0), axis=1, keepdims=True)
            small = jnp.where(lanes == t * quantities + q, part, small)
    half = type_count // 2
    return jnp.concatenate([small[:half], small[half:]], axis=1).astype(bf16)


def store_copies(ready, pair, held, out_refs, sems):
    group, unit = pair // held, lax.rem(pair, held)
    copies = [(None, pltpu.make_async_copy(ready.at[0], out_refs[0].at[group, unit], sems.at[0]))]
    for at, ref in enumerate(out_refs[1:]):
        copies.append((group == at, pltpu.make_async_copy(ready.at[1], ref.at[unit], sems.at[1])))
    return copies


def for_each(copies, act):
    for condition, copy in copies:
        if condition is None:
            act(copy)
        else:
            pl.when(condition)(functools.partial(act, copy))


def start(copy):
    copy.start()


def wait(copy):
    copy.wait()


def fetch_weights(places, buffer, sems, each):
    step = pl.program_id(0)
    for of in range(len(places) // each):

        @pl.when(step == max(of - 1, 0))
        def _(of=of):
            for i, (ref, at) in enumerate(places[of * each : (of + 1) * each]):
                pltpu.make_async_copy(ref.at[at], buffer.at[of % 2, i], sems.at[of % 2, i]).start()

    slot = lax.rem(step, 2)
    for i in range(each):
        ref, at = places[0]
        pltpu.make_async_copy(ref.at[at], buffer.at[slot, i], sems.at[slot, i]).wait()
    return [buffer.at[slot, i] for i in range(each)]


def forward_kernel(places, pieces, each, first, *refs):
    refs = list(refs)
    take = lambda count: [refs.pop(0) for _ in range(count)]
    x_ref, type_ref, value_ref = take(3)
    if not first:
        total_ref, _, _ = take(3)
    weight_refs = take(pieces)
    out_ref, hidden_ref, slope_ref, x_low, biases, buffer, sems = take(7)
    step = pl.program_id(0)
    weights = fetch_weights([(weight_refs[piece], at) for piece, at in places], buffer, sems, each)

    @pl.when(step == 0)
    def _():
        x_low[...] = x_ref[...].astype(bf16)
        biases[...] = jnp.zeros_like(biases)
        out_ref[0] = x_ref[...] if first else total_ref[0]

    def keep(i, rows, hidden, slope):
        hidden_ref[0, i, rows] = hidden
        slope_ref[0, i, rows] = slope

    forward_step(weights, value_ref.at[0], x_low, type_ref, out_ref, biases, keep)

    @pl.when(step == pl.num_programs(0) - 1)
    def _():
        forward_end(type_ref, out_ref, biases)


def forward_call(x, types, values, total, stash, pieces, places, base):
    height, width = x.shape
    pairs, type_count, lanes = values.shape
    each = lanes // LANES
    operands = [x, types, values]
    specs = [whole_spec(x.shape), whole_spec(types.shape)]
    specs.append(pl.BlockSpec((1, type_count, lanes), lambda i: (base + i, 0, 0)))
    aliases = {}
    if total is not None:
        operands += [total, *stash]
        specs += [whole_spec(total.shape), FAR, FAR]
        aliases = {4: 1, 5: 2}
    summed = jax.ShapeDtypeStruct((1, height, width), f32)
    kept = jax.ShapeDtypeStruct((pairs, each, height, width), bf16)
    kept_spec = pl.BlockSpec((1, each, height, width), lambda i: (base + i, 0, 0, 0))
    number = len(places)
    results = pl.pallas_call(
        functools.partial(forward_kernel, places, len(pieces), each, total is None),
        grid=(number // each,),
        out_shape=[summed, kept, kept],
        in_specs=specs + [FAR] * len(pieces),
        out_specs=[whole_spec(summed.shape), kept_spec, kept_spec],
        scratch_shapes=[
            pltpu.VMEM((height, width), bf16),
            pltpu.VMEM((1, type_count, width), f32),
            pltpu.VMEM((2, each, *pieces[0].shape[1:]), bf16),
            pltpu.SemaphoreType.DMA((2, each)),
        ],
        input_output_aliases=aliases,
        compiler_params=kernel_params(),
        cost_estimate=pl.CostEstimate(
            flops=4 * number * height * width * width,
            bytes_accessed=number * (4 * width * width + 4 * height * width) + 8 * height * width,
            transcendentals=number * height * width,
        ),
    )(*operands, *pieces)
    return results[0], results[1:]


def middle_kernel(places, pieces, groups, halves, held, *refs):
    refs = list(refs)
    take = lambda count: [refs.pop(0) for _ in range(count)]
    place_ref, x_ref, type_ref, across_types_ref, value_ref, gate_slope_ref, pred_grad_ref = take(7)
    tower_in_ref, tower_bias_ref, tower_out_ref = take(3)
    weight_refs = take(pieces)
    pred_ref, stream_ref, small_ref, *tower_refs = take(3 + halves)
    out_refs = take(1 + groups * (halves - 1))
    x_low, weights, hidden_all, slope_all, gates_all, total, biases, low, across, share, table = take(11)
    before_grads, result_grads, products, ready, in_grad, bias_grad, out_grad, load_sem, store_sem = take(9)
    height, width = x_ref.shape
    pairs = value_ref.shape[0]
    experts = pairs * halves
    tasks = total.shape[0]

    def load(pair, i, ref, at):
        return pltpu.make_async_copy(ref.at[at], weights.at[pair, i], load_sem.at[pair, i])

    for j, (piece, at) in enumerate(places):
        load(j // halves, j % halves, weight_refs[piece], at).start()
    x_low[...] = x_ref[...].astype(bf16)
    biases[...] = jnp.zeros_like(biases)
    for t in range(tasks):
        total[t] = x_ref[...]

    def forward_pair(pair, carry):
        for i in range(halves):
            load(pair, i, weight_refs[0], 0).wait()

        def keep(i, rows, hidden, slope):
            hidden_all[pair, i, rows] = hidden
            slope_all[pair, i, rows] = slope

        def keep_gate(at, rows, gate):
            gates_all[pair, at, rows] = gate

        forward_step(
            [weights.at[pair, i] for i in range(halves)],
            value_ref.at[pair],
            x_low,
            type_ref,
            total,
            biases,
            keep,
            keep_gate,
        )
        return carry

    lax.fori_loop(0, pairs, forward_pair, 0)
    forward_end(type_ref, total, biases)

    in_grad[...] = jnp.zeros_like(in_grad)
    bias_grad[...] = jnp.zeros_like(bias_grad)
    out_grad[...] = jnp.zeros_like(out_grad)
    for rows in tiles(height, TOWER_TILE):
        summed = None
        predicted = []
        for t in range(tasks):
            closing_low = total[t, rows].astype(bf16)
            act, slope = gelu_both(mm(closing_low, tower_in_ref[t]) + tower_bias_ref[t : t + 1])
            vector = tower_out_ref[t : t + 1]
            predicted.append(jnp.sum(act * vector, axis=1, keepdims=True))
            cotangent = pred_grad_ref[rows, t : t + 1]
            out_grad[t : t + 1] += jnp.sum(act * cotangent, axis=0, keepdims=True)
            before_grad = (slope * (cotangent * vector)).astype(bf16)
            bias_grad[t : t + 1] += jnp.sum(before_grad.astype(f32), axis=0, keepdims=True)
            in_grad[t] += mm_tn(closing_low, before_grad)
            closing_grad = mm_nt(before_grad, tower_in_ref[t])
            low[t, rows] = closing_grad.astype(bf16)
            summed = closing_grad if summed is None else summed + closing_grad
        stream_ref[rows] = summed
        pred_ref[rows] = jnp.concatenate(predicted, axis=1)
    narrow = in_grad.shape[2]
    for t in range(tasks):
        wide = jnp.concatenate([in_grad[t, : width * narrow // width], in_grad[t, width * narrow // width :]], axis=1)
        if halves == 2:

            @pl.when(place_ref[2] == t)
            def _(wide=wide):
                tower_refs[0][...] = wide.astype(bf16)

            @pl.when(place_ref[2] != t)
            def _(wide=wide):
                tower_refs[1][...] = wide.astype(bf16)

        else:
            tower_refs[0][t * wide.shape[0] : (t + 1) * wide.shape[0]] = wide.astype(bf16)
    ends = [jnp.concatenate([ref[0:1], ref[1:2]], axis=1) for ref in (bias_grad, out_grad)]
    tower_small = jnp.concatenate([*ends, jnp.zeros((EXTRA - 2, width), f32)]).astype(bf16)

    backward_start(x_low, across_types_ref, low, across, share)
    table[...] = jnp.zeros_like(table)

    def stores(pair):
        return store_copies(ready.at[pair], pair, held, out_refs, store_sem.at[pair])

    def backward_pair(pair, carry):
        backward_step(
            [weights.at[pair, i] for i in range(halves)],
            value_ref.at[pair],
            [hidden_all.at[pair, i] for i in range(halves)],
            [slope_all.at[pair, i] for i in range(halves)],
            [ready.at[pair, i] for i in range(halves)],
            pair,
            experts,
            type_ref,
            across_types_ref,
            low,
            stream_ref,
            across,
            share,
            table,
            (before_grads, result_grads, products),
            gates_all.at[pair],
        )
        for_each(stores(pair), start)
        return carry

    lax.fori_loop(0, pairs, backward_pair, 0)
    small_ref[...] = jnp.concatenate([through_gates(table, gate_slope_ref, experts, tasks), tower_small])

    def drain(pair, carry):
        for_each(stores(pair), wait)
        return carry

    lax.fori_loop(0, pairs, drain, 0)


def middle_call(place, x, types, across_types, values, gate_slopes, tower, pieces, places, groups, halves, held):
    height, width = x.shape
    pairs, type_count, lanes = values.shape
    pred_grad, tower_in, tower_bias, tower_out = tower
    tasks = tower_in.shape[0]
    stride = 2 * width + EXTRA
    experts = pairs * halves
    outs = [jax.ShapeDtypeStruct(shape, f32) for shape in (pred_grad.shape, (height, width))]
    outs.append(jax.ShapeDtypeStruct((type_count // 2 + EXTRA, 2 * LANES), bf16))
    outs += [jax.ShapeDtypeStruct((tower_in.size // width // halves, width), bf16)] * halves
    near = len(outs)
    outs.append(jax.ShapeDtypeStruct((groups, held, stride, width), bf16))
    outs += [jax.ShapeDtypeStruct((held, stride, width), bf16)] * (groups * (halves - 1))
    layer_at = gate_slopes.shape[1] // type_count - 1
    slope_spec = pl.BlockSpec((gate_slopes.shape[0], type_count, LANES), lambda i: (0, layer_at, 0))
    kept = pltpu.VMEM((pairs, halves, height, width), bf16)
    operands = [x, types, across_types, values, gate_slopes, *tower]
    specs = [whole_spec(a.shape) for a in operands]
    specs[4] = slope_spec
    return pl.pallas_call(
        functools.partial(middle_kernel, places, len(pieces), groups, halves, held),
        grid=(1,),
        out_shape=outs,
        in_specs=[SCALARS] + specs + [FAR] * len(pieces),
        out_specs=[whole_spec(out.shape) for out in outs[:near]] + [FAR] * (len(outs) - near),
        scratch_shapes=[
            pltpu.VMEM((height, width), bf16),
            pltpu.VMEM((pairs, halves, stride, width), bf16),
            kept,
            kept,
            pltpu.VMEM((pairs, halves * tasks, height, LANES), bf16),
            pltpu.VMEM((tasks, height, width), f32),
            pltpu.VMEM((tasks, type_count, width), f32),
            pltpu.VMEM((tasks, height, width), bf16),
            pltpu.VMEM((width + EXTRA, height), bf16),
            pltpu.VMEM((tasks, type_count, width), f32),
            pltpu.VMEM((type_count, LANES), f32),
            pltpu.VMEM((halves, height, width), bf16),
            pltpu.VMEM((halves, height, width), bf16),
            pltpu.VMEM((height, lanes), bf16),
            pltpu.VMEM((pairs, halves, stride, width), bf16),
            pltpu.VMEM(tower_in.shape, f32),
            pltpu.VMEM(tower_bias.shape, f32),
            pltpu.VMEM(tower_out.shape, f32),
            pltpu.SemaphoreType.DMA((pairs, halves)),
            pltpu.SemaphoreType.DMA((pairs, halves)),
        ],
        compiler_params=kernel_params(),
        cost_estimate=pl.CostEstimate(
            flops=14 * experts * height * width * width,
            bytes_accessed=experts * 8 * width * width + 16 * height * width,
            transcendentals=experts * height * width,
        ),
    )(place, *operands, *pieces)


def backward_kernel(places, pieces, each, held, tasks, *refs):
    refs = list(refs)
    take = lambda count: [refs.pop(0) for _ in range(count)]
    x_ref, type_ref, across_types_ref, stream_ref, gate_slope_ref, value_ref, hidden_ref, slope_ref = take(8)
    weight_refs = take(pieces)
    stream_out_ref, small_ref = take(2)
    out_refs = take(1 + len(places) // each // held * (each - 1))
    x_low, across, low, share, table, before_grads, result_grads, products, buffer, ready, sems, store_sem = take(12)
    step = pl.program_id(0)
    slot = lax.rem(step, 2)
    experts = len(places)
    weights = fetch_weights([(weight_refs[piece], at) for piece, at in places], buffer, sems, each)

    @pl.when(step == 0)
    def _():
        x_low[...] = x_ref[...].astype(bf16)
        low[0] = stream_ref[...].astype(bf16)
        stream_out_ref[...] = stream_ref[...]
        table[...] = jnp.zeros_like(table)
        backward_start(x_low, across_types_ref, low, across, share)

    def stores(pair):
        at = lax.rem(pair, 2)
        return store_copies(ready.at[at], pair, held, out_refs, store_sem.at[at])

    @pl.when(step >= 2)
    def _():
        for_each(stores(step - 2), wait)

    backward_step(
        weights,
        value_ref.at[0],
        [hidden_ref.at[0, i] for i in range(each)],
        [slope_ref.at[0, i] for i in range(each)],
        [ready.at[slot, i] for i in range(each)],
        step,
        experts,
        type_ref,
        across_types_ref,
        low,
        stream_out_ref,
        across,
        share,
        table,
        (before_grads, result_grads, products),
    )

    for_each(stores(step), start)

    @pl.when(step == pl.num_programs(0) - 1)
    def _():
        small_ref[...] = through_gates(table, gate_slope_ref, experts, tasks)
        for_each(stores(step - 1), wait)
        for_each(stores(step), wait)


def backward_call(x, types, across_types, stream, gate_slopes, layer_at, values, stash, pieces, places, held, tasks):
    height, width = x.shape
    pairs, type_count, lanes = values.shape
    each = lanes // LANES
    groups = pairs // held
    stride = 2 * width + EXTRA
    operands = [x, types, across_types, stream, gate_slopes, values, *stash]
    specs = [whole_spec(a.shape) for a in operands[:4]]
    specs.append(pl.BlockSpec((gate_slopes.shape[0], type_count, LANES), lambda i: (0, layer_at, 0)))
    specs.append(pl.BlockSpec((1, type_count, lanes), lambda i: (i, 0, 0)))
    specs += [pl.BlockSpec((1, each, height, width), lambda i: (i, 0, 0, 0))] * 2
    mine = jax.ShapeDtypeStruct((groups, held, stride, width), bf16)
    others = [jax.ShapeDtypeStruct((held, stride, width), bf16)] * (groups * (each - 1))
    small = jax.ShapeDtypeStruct((type_count // 2, 2 * LANES), bf16)
    number = pairs * each
    return pl.pallas_call(
        functools.partial(backward_kernel, places, len(pieces), each, held, tasks),
        grid=(pairs,),
        out_shape=[jax.ShapeDtypeStruct(stream.shape, f32), small, mine, *others],
        in_specs=specs + [FAR] * len(pieces),
        out_specs=[whole_spec(stream.shape), whole_spec(small.shape)] + [FAR] * (1 + len(others)),
        scratch_shapes=[
            pltpu.VMEM((height, width), bf16),
            pltpu.VMEM((width + EXTRA, height), bf16),
            pltpu.VMEM((1, height, width), bf16),
            pltpu.VMEM((1, type_count, width), f32),
            pltpu.VMEM((type_count, LANES), f32),
            pltpu.VMEM((each, height, width), bf16),
            pltpu.VMEM((each, height, width), bf16),
            pltpu.VMEM((height, lanes), bf16),
            pltpu.VMEM((2, each, stride, width), bf16),
            pltpu.VMEM((2, each, stride, width), bf16),
            pltpu.SemaphoreType.DMA((2, each)),
            pltpu.SemaphoreType.DMA((2, each)),
        ],
        compiler_params=kernel_params(),
        cost_estimate=pl.CostEstimate(
            flops=8 * number * height * width * width,
            bytes_accessed=number * (8 * width * width + 4 * height * width) + 16 * height * width,
            transcendentals=0,
        ),
    )(*operands, *pieces)


def finish_kernel(names, held, rows, first, *refs):
    place_ref, *refs = refs
    sources, refs = refs[: len(names)], refs[len(names) :]
    in_ref, out_ref, in_bias_out_ref, out_bias_out_ref, ready, sems = refs[-6:]
    in_bias_out_ref[...] = jnp.zeros_like(in_bias_out_ref) if first else refs[2][...]
    out_bias_out_ref[...] = jnp.zeros_like(out_bias_out_ref) if first else refs[3][...]
    copies = []
    for at, ((layer_at, half), source) in enumerate(zip(names, sources)):
        for unit in range(held):
            base = unit * (2 * rows + EXTRA)
            where = held * (place_ref[2] ^ half) + unit
            for which, ref in enumerate((in_ref, out_ref)):
                begin = base + which * rows
                ready[at, unit, which] = source[begin : begin + rows].astype(f32)
                copy = pltpu.make_async_copy(
                    ready.at[at, unit, which], ref.at[layer_at, where], sems.at[at, unit, which]
                )
                copy.start()
                copies.append(copy)
            tail = source[base + 2 * rows : base + 2 * rows + EXTRA].astype(f32)
            in_bias_out_ref[layer_at, pl.ds(where, 1)] = tail[0:1]
            out_bias_out_ref[layer_at, pl.ds(where, 1)] = tail[1:2]
    for copy in copies:
        copy.wait()


def finish_call(place, named, held_arrays, held, shape):
    rows, width = shape[2:]
    names, sources = tuple(named), list(named.values())
    outs = [jax.ShapeDtypeStruct(shape, f32)] * 2
    outs += [jax.ShapeDtypeStruct((*shape[:2], width), f32)] * 2
    first = held_arrays is None
    number = len(names)
    return pl.pallas_call(
        functools.partial(finish_kernel, names, held, rows, first),
        out_shape=outs,
        in_specs=[SCALARS] + [NEAR] * number + ([] if first else [FAR, FAR, NEAR, NEAR]),
        out_specs=[FAR, FAR, NEAR, NEAR],
        scratch_shapes=[
            pltpu.VMEM((number, held, 2, rows, width), f32),
            pltpu.SemaphoreType.DMA((number, held, 2)),
        ],
        input_output_aliases={} if first else {1 + number: 0, 2 + number: 1},
        compiler_params=kernel_params(),
        cost_estimate=pl.CostEstimate(flops=0, bytes_accessed=number * held * 12 * rows * width, transcendentals=0),
    )(place, *sources, *([] if first else held_arrays))


def flip(array, axis, bits):
    size = lax.axis_size(axis)
    return lax.ppermute(array, axis, [(i, i ^ bits) for i in range(size)])


def add_low(*arrays):
    level = [a.astype(f32) for a in arrays]
    while len(level) > 1:
        level = [level[i] + level[i + 1] for i in range(0, len(level), 2)]
    return level[0].astype(bf16)


def after(arrays, others):
    return lax.optimization_barrier((arrays, others))[0]


def near(mine, groups):
    if groups == 4 and mine.shape[0] == 2:
        return {1: [flip(mine, "expert", 1)], 2: [flip(mine, "expert", 2)]}
    return {ro: [flip(mine, "expert", ro)] for ro in range(1, groups)}


def relay(arrived, groups, held):
    if groups == 4 and held == 2:
        return {3: [flip(arrived[1][0][:1], "expert", 2), flip(arrived[2][0][1:], "expert", 1)]}
    return {}


def crossed(parts, halves):
    return [] if halves == 1 else [flip(part, "rows", 1) for part in parts]


def body(
    rows_in,
    pred_grad,
    lengths,
    session_type,
    expert_in,
    expert_in_bias,
    expert_out,
    expert_out_bias,
    selector_logits,
    selector_mix,
    tower_in,
    tower_bias,
    tower_out,
):
    height, width = rows_in.shape
    layers, owned = expert_in.shape[:2]
    type_count, tasks = selector_logits.shape[1:3]
    selectors, bits = selector_logits.shape[3:]
    groups = lax.axis_size("expert")
    halves = 2 if owned % 2 == 0 else 1
    held = owned // halves
    stride = 2 * width + EXTRA
    me, row_at = lax.axis_index("expert"), lax.axis_index("rows")
    core = row_at % 2 if halves == 2 else jnp.int32(0)
    place = jnp.stack([(row_at * groups + me) * height, me, core]).astype(jnp.int32)

    def rows_of(layer_at, first):
        cut = lambda a: lax.dynamic_slice_in_dim(a[layer_at], first, held)
        half = lambda a: a * jnp.asarray(0.5, a.dtype)
        tail = []
        for bias in (half(cut(expert_in_bias)), cut(expert_out_bias)):
            high = bias.astype(bf16)
            tail += [high, (bias - high.astype(f32)).astype(bf16)]
        tail = jnp.pad(jnp.stack(tail, axis=1), ((0, 0), (0, EXTRA - len(tail)), (0, 0)))
        return jnp.concatenate([half(cut(expert_in)), cut(expert_out), tail], axis=1)

    own = [[rows_of(layer_at, held * (core ^ half)) for half in range(halves)] for layer_at in range(layers)]
    sizes = (owned, halves, held, selectors, bits, tasks)
    types, across_types, gate_slopes, *values = prepare_call(
        place, lengths, session_type, selector_logits, selector_mix, height, sizes
    )

    def parts_of(got, across):
        pieces, places = [], {}
        for ro in got:
            spots = []
            for parts in (got[ro], across[ro]):
                here = []
                for part in parts:
                    here += [(len(pieces), at) for at in range(part.shape[0])]
                    pieces.append(part)
                if here:
                    spots.append(here)
            places[ro] = [[spots[half][unit] for half in range(halves)] for unit in range(held)]
        return pieces, places

    def pair_order(places, units):
        return tuple(spot for ro in sorted(places) for unit in units for spot in places[ro][unit])

    streams, stashes, weights = [rows_in], [], []
    for layer_at in range(layers):
        last = layer_at == layers - 1
        got = near(own[layer_at][0], groups)
        if layer_at == 0:
            got = after(got, types)
        far = relay(got, groups, held)
        across = {ro: crossed(got[ro], halves) for ro in got}
        if not last:
            own[layer_at + 1] = after(own[layer_at + 1], across)
        got = {0: own[layer_at][:1], **got}
        across[0] = own[layer_at][1:]
        if not last:
            pieces, places = parts_of(got, across)
            total, stash = forward_call(
                streams[-1], types, values[layer_at], None, None, pieces, pair_order(places, range(held)), 0
            )
            far = after(far, total)
        elif streams[1:]:
            far = after(far, streams[-1])
        far_across = {ro: crossed(far[ro], halves) for ro in far}
        if not last:
            if far:
                pieces, places = parts_of(far, far_across)
                base = held * min(far)
                order = pair_order(places, range(held))
                total, stash = forward_call(
                    streams[-1], types, values[layer_at], total, stash, pieces, order, base
                )
            streams.append(total[0])
            stashes.append(stash)
        weights.append(parts_of({**got, **far}, {**across, **far_across}))

    pieces, places = weights[-1]
    predictions, stream, small, *rest = middle_call(
        place,
        streams[-1],
        types,
        across_types,
        values[-1],
        gate_slopes,
        (pred_grad, tower_in, tower_bias, tower_out),
        pieces,
        pair_order(places, range(held)),
        groups,
        halves,
        held,
    )
    tower_rows, payload = rest[:halves], rest[halves:]

    shards = lax.axis_size("rows")
    paired = shards > 2
    hops = ["share"] + [4 << at for at in range(shards.bit_length() - 3)] + ["join"] if paired else []
    upper = (row_at & 2) > 0

    class Moving:
        def __init__(self, layer_at, payload, small, end=None):
            self.layer_at, self.mine, self.end = layer_at, payload[0], [] if end is None else [end]
            self.others = payload[1:] or [payload[0][ro] for ro in range(groups)]
            self.small = small
            self.got = [flip(part, "rows", 1) for part in [self.small, *self.others[1:]]]
            self.total, self.sums, self.hops = None, None, -2

        def ask(self, token):
            if self.hops == -1:
                sums, own = after((self.sums, self.others[0]), token)
                self.got = [flip(own, "rows", 1)] + [flip(sums[ro], "expert", ro) for ro in range(1, groups)]
                return
            total = after(self.total, token)
            if self.hops == len(hops):
                self.got = [total] + ([flip(total, "rows", 1)] if halves == 2 else [])
            elif hops[self.hops] == "share":
                cut = total.shape[0] // 2
                self.got = [
                    jnp.where(upper, total[cut:], total[:cut]),
                    flip(jnp.where(upper, total[:cut], total[cut:]), "rows", 2),
                ]
            else:
                self.got = [total, flip(total, "rows", 2 if hops[self.hops] == "join" else hops[self.hops])]

        def core_sum(self, ro, received):
            rows = add_low(self.mine[ro], received).reshape(held * stride, width)
            return jnp.concatenate([rows, self.small, *self.end])

        def add(self):
            if self.hops == len(hops):
                return True
            if self.hops == -2:
                self.small = add_low(self.small, self.got[0])
                self.sums = {ro: self.core_sum(ro, self.got[ro]) for ro in range(1, groups)}
            elif self.hops == -1:
                self.total = add_low(self.core_sum(0, self.got[0]), *self.got[1:])
            elif hops[self.hops] != "join":
                self.total = add_low(*self.got)
            else:
                here, there = self.got
                self.total = jnp.concatenate([jnp.where(upper, there, here), jnp.where(upper, here, there)])
            self.hops += 1
            return False

    def arrive(entries, others):
        got, others = lax.optimization_barrier(([entry.got for entry in entries], others))
        for entry, what in zip(entries, got):
            entry.got = what
        ended = [entry for entry in entries if entry.add()]
        return ([entry.sums if entry.total is None else entry.total for entry in entries], others), ended

    tower_tail = tower_rows[0]
    if halves == 2:
        tower_tail = add_low(tower_rows[0], flip(tower_rows[1], "rows", 1))
    moving = [Moving(layers - 1, payload, small, tower_tail)]
    token, _ = arrive(moving, ())
    stream = after(stream, token)
    for layer_at in reversed(range(layers - 1)):
        for entry in moving:
            entry.ask(token)
        pieces, places = weights[layer_at]
        stream, small, *payload = backward_call(
            streams[layer_at],
            types,
            across_types,
            stream,
            gate_slopes,
            layer_at,
            values[layer_at],
            stashes[layer_at],
            pieces,
            pair_order(places, range(held)),
            held,
            tasks,
        )
        token, _ = arrive(moving, stream)
        moving.append(Moving(layer_at, payload, small))
        token, _ = arrive(moving[-1:], token)

    whole = {}
    while moving:
        for entry in moving:
            entry.ask(token)
        for entry in [entry for entry in moving if entry.hops == len(hops)]:
            moving.remove(entry)
            whole[entry.layer_at] = entry.got
        if moving:
            token, _ = arrive(moving, ())
    first = {(layer_at, 0): got[0] for layer_at, got in whole.items()}
    if halves == 2:
        first.update({(layer_at, 1): got[1] for layer_at, got in whole.items() if layer_at > 0})
    arrays = finish_call(place, first, None, held, expert_in.shape)
    ends = {layer_at: got[0][held * stride :].astype(f32) for layer_at, got in whole.items()}
    gate_grads = [ends[layer_at][: type_count // 2] for layer_at in range(layers)]
    end = ends[layers - 1]
    at = type_count // 2
    tower_bias_sum = end[at].reshape(tower_bias.shape)
    tower_out_sum = end[at + 1].reshape(tower_out.shape)
    at = held * stride + at + EXTRA
    tower_rows = [array[at:].astype(f32) for array in whole[layers - 1]]
    if halves == 2:
        tower_rows = [jnp.where(core == 0, *tower_rows), jnp.where(core == 0, *tower_rows[::-1])]
    wide = jnp.concatenate(tower_rows).reshape(tasks, -1, width)
    narrow = tower_in.shape[2]
    tower_in_sum = jnp.concatenate([wide[:, :, at : at + narrow] for at in range(0, width, narrow)], axis=1)
    quantities = selectors * (bits + 1)
    small = jnp.stack(gate_grads)
    small = jnp.concatenate([small[..., :LANES], small[..., LANES:]], axis=1)[..., : tasks * quantities]
    small = small.reshape(layers, type_count, tasks, quantities)
    logits_grad = small[..., : selectors * bits].reshape(selector_logits.shape)
    smalls = (logits_grad, small[..., selectors * bits :], tower_in_sum, tower_bias_sum, tower_out_sum)
    if halves == 2:
        last, (arrays, smalls) = lax.optimization_barrier((whole[0][1], (arrays, smalls)))
        arrays = finish_call(place, {(0, 1): last}, arrays, held, expert_in.shape)
    return (
        predictions,
        stream,
        arrays[0],
        arrays[2],
        arrays[1],
        arrays[3],
        *smalls,
    )


def solution(mesh):
    in_specs = (
        P(("rows", "expert"), None),
        P(("rows", "expert"), None),
        P(),
        P(),
        P(None, "expert", None, None),
        P(None, "expert", None),
        P(None, "expert", None, None),
        P(None, "expert", None),
        P(),
        P(),
        P(),
        P(),
        P(),
    )
    out_specs = (
        P(("rows", "expert"), None),
        P(("rows", "expert"), None),
        P(None, "expert", None, None),
        P(None, "expert", None),
        P(None, "expert", None, None),
        P(None, "expert", None),
        P(),
        P(),
        P(),
        P(),
        P(),
    )
    return jax.shard_map(body, mesh=mesh, in_specs=in_specs, out_specs=out_specs, check_vma=False)
```

```python
import functools
import math

import jax
import jax.numpy as jnp
import numpy as np
from jax import lax
from jax.experimental import pallas as pl
from jax.experimental.pallas import tpu as pltpu
from jax.sharding import PartitionSpec as P

SHARPNESS = 10.0
EXACT = lax.Precision.HIGHEST
bf16 = jnp.bfloat16
f32 = jnp.float32
INNER = math.sqrt(2.0 / math.pi)
CUBE = 0.044715 * INNER
TILE = 1024
TOWER_TILE = 512
LANES = 128
EXTRA = 16


def mm(a, b):
    return jnp.dot(a, b, preferred_element_type=f32)


def mm_exact(a, b):
    return jnp.dot(a, b, precision=EXACT, preferred_element_type=f32)


def mm_nt(a, b):
    return lax.dot_general(a, b, (((1,), (1,)), ((), ())), preferred_element_type=f32)


def mm_tn(a, b):
    return lax.dot_general(a, b, (((0,), (0,)), ((), ())), preferred_element_type=f32)


def gelu_both(v):
    square = v * v
    half = 0.5 + 0.5 * jnp.tanh(v * (INNER + CUBE * square))
    value = v * half
    slope = half + value * (1.0 - half) * (2.0 * INNER + 6.0 * CUBE * square)
    return value, slope


def gelu_low(v):
    bend = 2.0 * INNER + 8.0 * CUBE * (v * v)
    twice_share = 1.0 + jnp.tanh(v * bend)
    value = (v * twice_share).astype(bf16)
    bend, twice_share = bend.astype(bf16), twice_share.astype(bf16)
    rise = 3.0 * bend - 4.0 * INNER
    return value, twice_share + value * (2.0 - twice_share) * rise


FAR = pl.BlockSpec(memory_space=pl.ANY)
NEAR = pl.BlockSpec(memory_space=pltpu.VMEM)
SCALARS = pl.BlockSpec(memory_space=pltpu.SMEM)


def kernel_params():
    return pltpu.CompilerParams(vmem_limit_bytes=58 * 2**20)


def whole_spec(shape):
    zeros = (0,) * len(shape)
    return pl.BlockSpec(shape, lambda i: zeros)


def prepare_kernel(sizes, place_ref, length_ref, kind_ref, logit_ref, mix_ref, spread_logit_ref, spread_mix_ref, *outs):
    owned, halves, held, selectors, bits, tasks = sizes
    type_ref, across_ref, slope_ref, *value_refs = outs
    height, type_count = type_ref.shape
    experts = 2**bits
    sessions = length_ref.shape[1]
    chunk = min(256, sessions)
    position = (place_ref[0] + lax.broadcasted_iota(jnp.int32, (height, 1), 0)).astype(f32)
    earlier = lax.broadcasted_iota(jnp.int32, (chunk, chunk), 0) < lax.broadcasted_iota(jnp.int32, (chunk, chunk), 1)
    earlier = jnp.where(earlier, 1.0, 0.0).astype(bf16)
    kinds = lax.broadcasted_iota(jnp.int32, (type_count, chunk), 0)
    before = jnp.zeros((1, 1), f32)
    types = jnp.zeros((height, type_count), f32)
    across = jnp.zeros((type_count, height), f32)
    for at in range(0, sessions, chunk):
        lengths = length_ref[:, at : at + chunk].astype(f32)
        begin = before + mm(jnp.broadcast_to(lengths.astype(bf16), (EXTRA, chunk)), earlier)[0:1]
        before += jnp.sum(lengths, axis=1, keepdims=True)
        member = jnp.where((position >= begin) & (position < begin + lengths), 1.0, 0.0).astype(bf16)
        of_type = jnp.where(kinds == kind_ref[:, at : at + chunk], 1.0, 0.0).astype(bf16)
        types += mm_nt(member, of_type)
        across += mm_nt(of_type, member)
    type_ref[...] = types.astype(bf16)
    across_ref[...] = across.astype(bf16)

    rows = logit_ref.shape[0]
    place = lax.broadcasted_iota(jnp.int32, (rows, LANES), 1) % experts
    expert = (
        owned * ((place // owned) ^ place_ref[1])
        + held * ((place % halves) ^ place_ref[2])
        + (place // halves) % held
    )
    logits = mm_exact(logit_ref[...], spread_logit_ref[...])
    mixes = mm_exact(mix_ref[...], spread_mix_ref[...])
    mixes = [mixes[:, k * LANES : (k + 1) * LANES] for k in range(selectors)]
    top = functools.reduce(jnp.maximum, mixes)
    shares = [jnp.exp(mix - top) for mix in mixes]
    whole = functools.reduce(jnp.add, shares)
    shares = [share / whole for share in shares]
    value = jnp.zeros((rows, LANES), f32)
    reaches = []
    for k in range(selectors):
        factors, signed = [], []
        for bit in range(bits):
            at = (k * bits + bit) * LANES
            logit = logits[:, at : at + LANES]
            cubic = (-2.0 / SHARPNESS**3) * logit * logit * logit + (1.5 / SHARPNESS) * logit + 0.5
            step = jnp.where(logit <= -SHARPNESS / 2, 0.0, jnp.where(logit >= SHARPNESS / 2, 1.0, cubic))
            slope = (-6.0 / SHARPNESS**3) * logit * logit + 1.5 / SHARPNESS
            slope = jnp.where((logit > -SHARPNESS / 2) & (logit < SHARPNESS / 2), slope, 0.0)
            on = (expert >> bit) & 1 == 1
            factors.append(jnp.where(on, step, 1.0 - step))
            signed.append(jnp.where(on, slope, -slope))
        reaches.append(functools.reduce(jnp.multiply, factors))
        value += shares[k] * reaches[k]
        for bit in range(bits):
            others = [factors[b] for b in range(bits) if b != bit]
            slope_ref[k * bits + bit] = shares[k] * signed[bit] * functools.reduce(jnp.multiply, others)
    for k in range(selectors):
        slope_ref[selectors * bits + k] = shares[k] * (reaches[k] - value)

    value = value.astype(bf16).astype(f32)
    for layer_at, ref in enumerate(value_refs):
        table = value[layer_at * type_count : (layer_at + 1) * type_count]
        columns = [table[:, t * experts : (t + 1) * experts] for t in range(tasks)]
        if layer_at < len(value_refs) - 1:
            columns = [functools.reduce(jnp.add, columns) / tasks]
        for pair in range(ref.shape[0]):
            lanes = []
            for half in range(halves):
                at = pair * halves + half
                lanes += [jnp.broadcast_to(c[:, at : at + 1], (type_count, LANES)) for c in columns]
            ref[pair] = jnp.concatenate(lanes, axis=1).astype(bf16)


def prepare_call(place, lengths, session_type, logits, mixing, height, sizes):
    owned, halves, held, selectors, bits, tasks = sizes
    layers, type_count = logits.shape[:2]
    experts = 2**bits
    rows = layers * type_count
    lane = np.arange(LANES)
    source = np.arange(tasks * selectors * bits)
    task, number = source // (selectors * bits), source % (selectors * bits)
    mine = (lane[None, :] // experts == task[:, None])[:, None, :]
    spread_logit = mine & (number[:, None, None] == np.arange(selectors * bits)[None, :, None])
    source = np.arange(tasks * selectors)
    mine = (lane[None, :] // experts == (source // selectors)[:, None])[:, None, :]
    spread_mix = mine & ((source % selectors)[:, None, None] == np.arange(selectors)[None, :, None])
    spread_logit = spread_logit.reshape(spread_logit.shape[0], -1).astype(np.float32)
    spread_mix = spread_mix.reshape(spread_mix.shape[0], -1).astype(np.float32)
    outs = [
        jax.ShapeDtypeStruct((height, type_count), bf16),
        jax.ShapeDtypeStruct((type_count, height), bf16),
        jax.ShapeDtypeStruct((selectors * (bits + 1), rows, LANES), f32),
    ]
    for layer_at in range(layers):
        each = tasks if layer_at == layers - 1 else 1
        outs.append(jax.ShapeDtypeStruct((experts // halves, type_count, halves * each * LANES), bf16))
    return pl.pallas_call(
        functools.partial(prepare_kernel, sizes),
        out_shape=outs,
        in_specs=[SCALARS] + [NEAR] * 6,
        out_specs=[NEAR] * len(outs),
        compiler_params=kernel_params(),
        cost_estimate=pl.CostEstimate(flops=2 * height * lengths.size * 64, bytes_accessed=2**21, transcendentals=2**16),
    )(
        place,
        lengths.reshape(1, -1),
        session_type.reshape(1, -1),
        logits.reshape(rows, -1),
        mixing.reshape(rows, -1),
        spread_logit,
        spread_mix,
    )


def bias_rows(weights, width):
    rows = weights[2 * width : 2 * width + EXTRA].astype(f32)
    return rows[0:1] + rows[1:2], rows[2:3] + rows[3:4]


def twice(a):
    return jnp.concatenate([a, a], axis=1)


def tiles(height, most):
    tile = min(most, height)
    return [pl.ds(at, tile) for at in range(0, height, tile)]


def joined(parts, axis):
    return parts[0] if len(parts) == 1 else jnp.concatenate(parts, axis=axis)


def gates_of(types, value_ref, count):
    gates = mm(types, value_ref[...]).astype(bf16)
    return [gates[:, at * LANES : (at + 1) * LANES] for at in range(count)]


def forward_step(weights, value_ref, x_low, type_ref, total_ref, biases, keep, keep_gate=None, keep_result=None):
    height, width = x_low.shape
    kinds = total_ref.shape[0]
    bias_in, bias_out = zip(*(bias_rows(w, width) for w in weights))
    second = joined([w[width : 2 * width] for w in weights], 0)
    for rows in tiles(height, TILE):
        gates = gates_of(type_ref[rows], value_ref, len(weights) * kinds)
        if keep_gate is not None:
            for at, gate in enumerate(gates):
                keep_gate(at, rows, gate)
        scaled = [[] for _ in range(kinds)]
        for i, w in enumerate(weights):
            hidden, slope = gelu_low(mm(x_low[rows], w[0:width]) + bias_in[i])
            keep(i, rows, hidden, slope)
            if keep_result is not None:
                result = mm(hidden, w[width : 2 * width]).astype(bf16)
                keep_result(i, rows, result)
            for t in range(kinds):
                scaled[t].append(twice(gates[i * kinds + t]) * (hidden if keep_result is None else result))
        for t in range(kinds):
            if keep_result is None:
                total_ref[t, rows] += mm(joined(scaled[t], 1), second)
            else:
                total_ref[t, rows] += functools.reduce(jnp.add, scaled[t]).astype(f32)
    for i in range(len(weights)):
        for t in range(kinds):
            at = (i * kinds + t) * LANES
            biases[t] += twice(value_ref[:, at : at + LANES].astype(f32)) * bias_out[i]


def forward_end(type_ref, total_ref, biases):
    for t in range(total_ref.shape[0]):
        high = biases[t].astype(bf16)
        rest = (biases[t] - high.astype(f32)).astype(bf16)
        for rows in tiles(total_ref.shape[1], TILE):
            total_ref[t, rows] += mm(twice(type_ref[rows]), jnp.concatenate([high, rest], axis=0))


def backward_start(x_low, type_across, low, across, share):
    width = x_low.shape[1]
    across[0:width] = x_low[...].T
    ones = lax.broadcasted_iota(jnp.int32, (EXTRA, x_low.shape[0]), 0) == 0
    across[width:] = jnp.where(ones, 1.0, 0.0).astype(bf16)
    for t in range(low.shape[0]):
        share[t] = mm(type_across[...], low[t])


def backward_step(weights, value_ref, hiddens, slopes, outs, pair, experts, type_ref, type_across, low, stream_ref, across, share, table, scratch, kept_gates=None, results=None, dots=None):
    before_grads, result_grads, products = scratch
    kinds, height, width = low.shape
    count = len(weights)
    first = joined([w[0:width] for w in weights], 1)
    for rows in tiles(height, TILE):
        if kept_gates is None:
            gates = gates_of(type_ref[rows], value_ref, count * kinds)
        else:
            gates = [kept_gates[at, rows] for at in range(count * kinds)]
        gates = [twice(gate) for gate in gates]
        befores = []
        for i, w in enumerate(weights):
            hidden, slope = hiddens[i][rows], slopes[i][rows]
            second = w[width : 2 * width]
            result_grad = gates[i * kinds] * low[0, rows]
            for t in range(1, kinds):
                result_grad += gates[i * kinds + t] * low[t, rows]
            hidden_grad = mm_nt(result_grad, second).astype(bf16)
            for t in range(kinds):
                product = hidden * hidden_grad if results is None else results[i][rows] * low[t, rows]
                product = functools.reduce(
                    jnp.add, [product[:, lane : lane + LANES] for lane in range(0, width, LANES)]
                )
                if dots is None:
                    at = (i * kinds + t) * LANES
                    products[rows, at : at + LANES] = product
                else:
                    found = jnp.sum(product.astype(f32), axis=1, keepdims=True)
                    lanes = lax.broadcasted_iota(jnp.int32, (1, LANES), 1)
                    dots[rows] = jnp.where(lanes == t * experts + pair * count + i, found, dots[rows])
            before = slope * hidden_grad
            before_grads[i, rows] = before
            result_grads[i, rows] = result_grad
            befores.append(before)
        stream_ref[rows] += mm_nt(joined(befores, 1), first)
    sums = None if dots is not None else mm(type_across[...], products[...])
    lanes = lax.broadcasted_iota(jnp.int32, (type_ref.shape[1], LANES), 1)
    for i, w in enumerate(weights):
        _, bias_out = bias_rows(w, width)
        first_grad = 0.5 * mm(across[...], before_grads[i])
        outs[i][0:width] = first_grad[0:width].astype(bf16)
        outs[i][width : 2 * width] = mm_tn(hiddens[i][...], result_grads[i]).astype(bf16)
        out_bias = jnp.zeros((1, width), f32)
        place = pair * count + i
        for t in range(kinds):
            at = (i * kinds + t) * LANES
            gate = value_ref[:, at : at + LANES].astype(f32)
            out_bias += jnp.sum(twice(gate) * share[t], axis=0, keepdims=True)
            found = 0.0 if sums is None else jnp.sum(sums[:, at : at + LANES], axis=1, keepdims=True)
            bias_part = jnp.sum(share[t] * bias_out, axis=1, keepdims=True)
            if kinds == 1:
                some = gate > 0.0
                found = jnp.where(some, 0.5 * found / jnp.where(some, gate, 1.0), 0.0)
                table[...] = jnp.where(lanes % experts == place, found + 0.5 * bias_part, table[...])
            else:
                table[...] = jnp.where(lanes == t * experts + place, found + bias_part, table[...])
        tail = jnp.concatenate([first_grad[width : width + 1], out_bias, jnp.zeros((EXTRA - 2, width), f32)])
        outs[i][2 * width : 2 * width + EXTRA] = tail.astype(bf16)


def through_gates(table, gate_slope_ref, experts, tasks):
    quantities, type_count = gate_slope_ref.shape[:2]
    lanes = lax.broadcasted_iota(jnp.int32, (type_count, LANES), 1)
    small = jnp.zeros((type_count, LANES), f32)
    for q in range(quantities):
        product = gate_slope_ref[q] * table[...]
        for t in range(tasks):
            part = jnp.sum(jnp.where(lanes // experts == t, product, 0.0), axis=1, keepdims=True)
            small = jnp.where(lanes == t * quantities + q, part, small)
    half = type_count // 2
    return jnp.concatenate([small[:half], small[half:]], axis=1).astype(bf16)


def store_copies(ready, pair, held, out_refs, sems):
    group, unit = pair // held, lax.rem(pair, held)
    rows = pl.ds(pl.multiple_of(unit * ready.shape[1], EXTRA), ready.shape[1])
    copies = [(None, pltpu.make_async_copy(ready.at[0], out_refs[0].at[group, rows], sems.at[0]))]
    for at, ref in enumerate(out_refs[1:]):
        copies.append((group == at, pltpu.make_async_copy(ready.at[1], ref.at[rows], sems.at[1])))
    return copies


def end_copies(ends, out_refs, sems):
    rows = out_refs[0].shape[1]
    last = pl.ds(rows - ends.shape[1], ends.shape[1])
    groups = out_refs[0].shape[0]
    copies = [pltpu.make_async_copy(ends.at[0], out_refs[0].at[at, last], sems.at[0, at]) for at in range(groups)]
    copies += [
        pltpu.make_async_copy(ends.at[1], ref.at[last], sems.at[1, at]) for at, ref in enumerate(out_refs[1:])
    ]
    return [(None, copy) for copy in copies]


def for_each(copies, act):
    for condition, copy in copies:
        if condition is None:
            act(copy)
        else:
            pl.when(condition)(functools.partial(act, copy))


def start(copy):
    copy.start()


def wait(copy):
    copy.wait()


def fetch_weights(places, buffer, sems, each):
    step = pl.program_id(0)
    for of in range(len(places) // each):

        @pl.when(step == max(of - 1, 0))
        def _(of=of):
            for i, (ref, at) in enumerate(places[of * each : (of + 1) * each]):
                pltpu.make_async_copy(ref.at[at], buffer.at[of % 2, i], sems.at[of % 2, i]).start()

    slot = lax.rem(step, 2)
    for i in range(each):
        ref, at = places[0]
        pltpu.make_async_copy(ref.at[at], buffer.at[slot, i], sems.at[slot, i]).wait()
    return [buffer.at[slot, i] for i in range(each)]


def forward_kernel(places, pieces, each, first, *refs):
    refs = list(refs)
    take = lambda count: [refs.pop(0) for _ in range(count)]
    x_ref, type_ref, value_ref = take(3)
    if not first:
        total_ref, _, _ = take(3)
    weight_refs = take(pieces)
    out_ref, hidden_ref, slope_ref, x_low, biases, buffer, sems = take(7)
    step = pl.program_id(0)
    weights = fetch_weights([(weight_refs[piece], at) for piece, at in places], buffer, sems, each)

    @pl.when(step == 0)
    def _():
        x_low[...] = x_ref[...].astype(bf16)
        biases[...] = jnp.zeros_like(biases)
        out_ref[0] = x_ref[...] if first else total_ref[0]

    def keep(i, rows, hidden, slope):
        hidden_ref[0, i, rows] = hidden
        slope_ref[0, i, rows] = slope

    forward_step(weights, value_ref.at[0], x_low, type_ref, out_ref, biases, keep)

    @pl.when(step == pl.num_programs(0) - 1)
    def _():
        forward_end(type_ref, out_ref, biases)


def forward_call(x, types, values, total, stash, pieces, places, base):
    height, width = x.shape
    pairs, type_count, lanes = values.shape
    each = lanes // LANES
    operands = [x, types, values]
    specs = [whole_spec(x.shape), whole_spec(types.shape)]
    specs.append(pl.BlockSpec((1, type_count, lanes), lambda i: (base + i, 0, 0)))
    aliases = {}
    if total is not None:
        operands += [total, *stash]
        specs += [whole_spec(total.shape), FAR, FAR]
        aliases = {4: 1, 5: 2}
    summed = jax.ShapeDtypeStruct((1, height, width), f32)
    kept = jax.ShapeDtypeStruct((pairs, each, height, width), bf16)
    kept_spec = pl.BlockSpec((1, each, height, width), lambda i: (base + i, 0, 0, 0))
    number = len(places)
    results = pl.pallas_call(
        functools.partial(forward_kernel, places, len(pieces), each, total is None),
        grid=(number // each,),
        out_shape=[summed, kept, kept],
        in_specs=specs + [FAR] * len(pieces),
        out_specs=[whole_spec(summed.shape), kept_spec, kept_spec],
        scratch_shapes=[
            pltpu.VMEM((height, width), bf16),
            pltpu.VMEM((1, type_count, width), f32),
            pltpu.VMEM((2, each, *pieces[0].shape[1:]), bf16),
            pltpu.SemaphoreType.DMA((2, each)),
        ],
        input_output_aliases=aliases,
        compiler_params=kernel_params(),
        cost_estimate=pl.CostEstimate(
            flops=4 * number * height * width * width,
            bytes_accessed=number * (4 * width * width + 4 * height * width) + 8 * height * width,
            transcendentals=number * height * width,
        ),
    )(*operands, *pieces)
    return results[0], results[1:]


def middle_kernel(places, pieces, groups, halves, held, *refs):
    refs = list(refs)
    take = lambda count: [refs.pop(0) for _ in range(count)]
    place_ref, x_ref, type_ref, across_types_ref, value_ref, gate_slope_ref, pred_grad_ref = take(7)
    tower_in_ref, tower_bias_ref, tower_out_ref = take(3)
    weight_refs = take(pieces)
    pred_ref, stream_ref = take(2)
    out_refs = take(1 + groups * (halves - 1))
    x_low, weights, hidden_all, slope_all, result_all, gates_all, total, biases, low, across, share, table = take(12)
    before_grads, result_grads, dots, cotangents, ready, ends, in_grad, bias_grad, out_grad, load_sem, store_sem, end_sem = take(12)
    height, width = x_ref.shape
    pairs = value_ref.shape[0]
    experts = pairs * halves
    tasks = total.shape[0]

    def load(pair, i, ref, at):
        return pltpu.make_async_copy(ref.at[at], weights.at[pair, i], load_sem.at[pair, i])

    for j, (piece, at) in enumerate(places):
        load(j // halves, j % halves, weight_refs[piece], at).start()
    x_low[...] = x_ref[...].astype(bf16)
    biases[...] = jnp.zeros_like(biases)
    for t in range(tasks):
        total[t] = x_ref[...]

    def forward_pair(pair, carry):
        for i in range(halves):
            load(pair, i, weight_refs[0], 0).wait()

        def keep(i, rows, hidden, slope):
            hidden_all[pair, i, rows] = hidden
            slope_all[pair, i, rows] = slope

        def keep_gate(at, rows, gate):
            gates_all[pair, at, rows] = gate

        def keep_result(i, rows, result):
            result_all[pair, i, rows] = result

        forward_step(
            [weights.at[pair, i] for i in range(halves)],
            value_ref.at[pair],
            x_low,
            type_ref,
            total,
            biases,
            keep,
            keep_gate,
            keep_result,
        )
        return carry

    lax.fori_loop(0, pairs, forward_pair, 0)
    forward_end(type_ref, total, biases)

    cotangents[...] = jnp.concatenate(
        [pred_grad_ref[...], jnp.zeros((cotangents.shape[1] - tasks, height), f32)]
    ).T
    in_grad[...] = jnp.zeros_like(in_grad)
    bias_grad[...] = jnp.zeros_like(bias_grad)
    out_grad[...] = jnp.zeros_like(out_grad)
    for rows in tiles(height, TOWER_TILE):
        summed = None
        predicted = []
        for t in range(tasks):
            closing_low = total[t, rows].astype(bf16)
            act, slope = gelu_both(mm(closing_low, tower_in_ref[t]) + tower_bias_ref[t : t + 1])
            vector = tower_out_ref[t : t + 1]
            predicted.append(jnp.sum(act * vector, axis=1, keepdims=True))
            cotangent = cotangents[rows, t : t + 1]
            out_grad[t : t + 1] += jnp.sum(act * cotangent, axis=0, keepdims=True)
            before_grad = (slope * (cotangent * vector)).astype(bf16)
            bias_grad[t : t + 1] += jnp.sum(before_grad.astype(f32), axis=0, keepdims=True)
            in_grad[t] += mm_tn(closing_low, before_grad)
            closing_grad = mm_nt(before_grad, tower_in_ref[t])
            low[t, rows] = closing_grad.astype(bf16)
            summed = closing_grad if summed is None else summed + closing_grad
        stream_ref[rows] = summed
        blank = jnp.zeros((predicted[0].shape[0], cotangents.shape[1] - tasks), f32)
        pred_ref[:, rows] = jnp.concatenate([*predicted, blank], axis=1).T[0:tasks]
    narrow = in_grad.shape[2]
    tall = width * narrow // width
    begin = type_ref.shape[1] // 2 + EXTRA
    for t in range(tasks):
        wide = jnp.concatenate([in_grad[t, :tall], in_grad[t, tall:]], axis=1).astype(bf16)
        if halves == 2:
            ends[place_ref[2] ^ t, begin:] = wide
        else:
            ends[0, begin + t * tall : begin + (t + 1) * tall] = wide
    vectors = [jnp.concatenate([ref[0:1], ref[1:2]], axis=1) for ref in (bias_grad, out_grad)]
    vectors = jnp.concatenate([*vectors, jnp.zeros((EXTRA - 2, width), f32)]).astype(bf16)
    for half in range(halves):
        ends[half, begin - EXTRA : begin] = vectors

    backward_start(x_low, across_types_ref, low, across, share)
    table[...] = jnp.zeros_like(table)
    dots[...] = jnp.zeros_like(dots)

    def stores(pair):
        return store_copies(ready.at[pair], pair, held, out_refs, store_sem.at[pair])

    def backward_pair(pair, carry):
        backward_step(
            [weights.at[pair, i] for i in range(halves)],
            value_ref.at[pair],
            [hidden_all.at[pair, i] for i in range(halves)],
            [slope_all.at[pair, i] for i in range(halves)],
            [ready.at[pair, i] for i in range(halves)],
            pair,
            experts,
            type_ref,
            across_types_ref,
            low,
            stream_ref,
            across,
            share,
            table,
            (before_grads, result_grads, None),
            gates_all.at[pair],
            [result_all.at[pair, i] for i in range(halves)],
            dots,
        )
        for_each(stores(pair), start)
        return carry

    lax.fori_loop(0, pairs, backward_pair, 0)
    high = dots[...].astype(bf16)
    rest = (dots[...] - high.astype(f32)).astype(bf16)
    table[...] += mm(across_types_ref[...], high) + mm(across_types_ref[...], rest)
    small = through_gates(table, gate_slope_ref, experts, tasks)
    for half in range(halves):
        ends[half, 0 : small.shape[0]] = small
    for_each(end_copies(ends, out_refs, end_sem), start)

    def drain(pair, carry):
        for_each(stores(pair), wait)
        return carry

    lax.fori_loop(0, pairs, drain, 0)
    for_each(end_copies(ends, out_refs, end_sem), wait)


def middle_call(place, x, types, across_types, values, gate_slopes, tower, pieces, places, groups, halves, held):
    height, width = x.shape
    pairs, type_count, lanes = values.shape
    pred_grad, tower_in, tower_bias, tower_out = tower
    tasks = tower_in.shape[0]
    stride = 2 * width + EXTRA
    experts = pairs * halves
    outs = [jax.ShapeDtypeStruct(shape, f32) for shape in (pred_grad.shape, (height, width))]
    near = len(outs)
    end_rows = type_count // 2 + EXTRA + tower_in.size // width // halves
    rows = held * stride + end_rows
    outs.append(jax.ShapeDtypeStruct((groups, rows, width), bf16))
    outs += [jax.ShapeDtypeStruct((rows, width), bf16)] * (groups * (halves - 1))
    layer_at = gate_slopes.shape[1] // type_count - 1
    slope_spec = pl.BlockSpec((gate_slopes.shape[0], type_count, LANES), lambda i: (0, layer_at, 0))
    kept = pltpu.VMEM((pairs, halves, height, width), bf16)
    operands = [x, types, across_types, values, gate_slopes, *tower]
    specs = [whole_spec(a.shape) for a in operands]
    specs[4] = slope_spec
    return pl.pallas_call(
        functools.partial(middle_kernel, places, len(pieces), groups, halves, held),
        grid=(1,),
        out_shape=outs,
        in_specs=[SCALARS] + specs + [FAR] * len(pieces),
        out_specs=[whole_spec(out.shape) for out in outs[:near]] + [FAR] * (len(outs) - near),
        scratch_shapes=[
            pltpu.VMEM((height, width), bf16),
            pltpu.VMEM((pairs, halves, stride, width), bf16),
            kept,
            kept,
            kept,
            pltpu.VMEM((pairs, halves * tasks, height, LANES), bf16),
            pltpu.VMEM((tasks, height, width), f32),
            pltpu.VMEM((tasks, type_count, width), f32),
            pltpu.VMEM((tasks, height, width), bf16),
            pltpu.VMEM((width + EXTRA, height), bf16),
            pltpu.VMEM((tasks, type_count, width), f32),
            pltpu.VMEM((type_count, LANES), f32),
            pltpu.VMEM((halves, height, width), bf16),
            pltpu.VMEM((halves, height, width), bf16),
            pltpu.VMEM((height, LANES), f32),
            pltpu.VMEM((height, LANES), f32),
            pltpu.VMEM((pairs, halves, stride, width), bf16),
            pltpu.VMEM((halves, end_rows, width), bf16),
            pltpu.VMEM(tower_in.shape, f32),
            pltpu.VMEM(tower_bias.shape, f32),
            pltpu.VMEM(tower_out.shape, f32),
            pltpu.SemaphoreType.DMA((pairs, halves)),
            pltpu.SemaphoreType.DMA((pairs, halves)),
            pltpu.SemaphoreType.DMA((halves, groups)),
        ],
        compiler_params=kernel_params(),
        cost_estimate=pl.CostEstimate(
            flops=14 * experts * height * width * width,
            bytes_accessed=experts * 8 * width * width + 16 * height * width,
            transcendentals=experts * height * width,
        ),
    )(place, *operands, *pieces)


def backward_kernel(places, pieces, each, held, tasks, *refs):
    refs = list(refs)
    take = lambda count: [refs.pop(0) for _ in range(count)]
    x_ref, type_ref, across_types_ref, stream_ref, gate_slope_ref, value_ref, hidden_ref, slope_ref = take(8)
    weight_refs = take(pieces)
    stream_out_ref = take(1)[0]
    out_refs = take(1 + len(places) // each // held * (each - 1))
    x_low, across, low, share, table, before_grads, result_grads, products, buffer, ready, ends = take(11)
    sems, store_sem, end_sem = take(3)
    step = pl.program_id(0)
    slot = lax.rem(step, 2)
    experts = len(places)
    weights = fetch_weights([(weight_refs[piece], at) for piece, at in places], buffer, sems, each)

    @pl.when(step == 0)
    def _():
        x_low[...] = x_ref[...].astype(bf16)
        low[0] = stream_ref[...].astype(bf16)
        stream_out_ref[...] = stream_ref[...]
        table[...] = jnp.zeros_like(table)
        backward_start(x_low, across_types_ref, low, across, share)

    def stores(pair):
        at = lax.rem(pair, 2)
        return store_copies(ready.at[at], pair, held, out_refs, store_sem.at[at])

    @pl.when(step >= 2)
    def _():
        for_each(stores(step - 2), wait)

    backward_step(
        weights,
        value_ref.at[0],
        [hidden_ref.at[0, i] for i in range(each)],
        [slope_ref.at[0, i] for i in range(each)],
        [ready.at[slot, i] for i in range(each)],
        step,
        experts,
        type_ref,
        across_types_ref,
        low,
        stream_out_ref,
        across,
        share,
        table,
        (before_grads, result_grads, products),
    )

    for_each(stores(step), start)

    @pl.when(step == pl.num_programs(0) - 1)
    def _():
        small = through_gates(table, gate_slope_ref, experts, tasks)
        for half in range(each):
            ends[half] = small
        for_each(end_copies(ends, out_refs, end_sem), start)
        for_each(stores(step - 1), wait)
        for_each(stores(step), wait)
        for_each(end_copies(ends, out_refs, end_sem), wait)


def backward_call(x, types, across_types, stream, gate_slopes, layer_at, values, stash, pieces, places, held, tasks):
    height, width = x.shape
    pairs, type_count, lanes = values.shape
    each = lanes // LANES
    groups = pairs // held
    stride = 2 * width + EXTRA
    operands = [x, types, across_types, stream, gate_slopes, values, *stash]
    specs = [whole_spec(a.shape) for a in operands[:4]]
    specs.append(pl.BlockSpec((gate_slopes.shape[0], type_count, LANES), lambda i: (0, layer_at, 0)))
    specs.append(pl.BlockSpec((1, type_count, lanes), lambda i: (i, 0, 0)))
    specs += [pl.BlockSpec((1, each, height, width), lambda i: (i, 0, 0, 0))] * 2
    rows = held * stride + type_count // 2
    mine = jax.ShapeDtypeStruct((groups, rows, width), bf16)
    others = [jax.ShapeDtypeStruct((rows, width), bf16)] * (groups * (each - 1))
    number = pairs * each
    return pl.pallas_call(
        functools.partial(backward_kernel, places, len(pieces), each, held, tasks),
        grid=(pairs,),
        out_shape=[jax.ShapeDtypeStruct(stream.shape, f32), mine, *others],
        in_specs=specs + [FAR] * len(pieces),
        out_specs=[whole_spec(stream.shape)] + [FAR] * (1 + len(others)),
        scratch_shapes=[
            pltpu.VMEM((height, width), bf16),
            pltpu.VMEM((width + EXTRA, height), bf16),
            pltpu.VMEM((1, height, width), bf16),
            pltpu.VMEM((1, type_count, width), f32),
            pltpu.VMEM((type_count, LANES), f32),
            pltpu.VMEM((each, height, width), bf16),
            pltpu.VMEM((each, height, width), bf16),
            pltpu.VMEM((height, lanes), bf16),
            pltpu.VMEM((2, each, stride, width), bf16),
            pltpu.VMEM((2, each, stride, width), bf16),
            pltpu.VMEM((each, type_count // 2, width), bf16),
            pltpu.SemaphoreType.DMA((2, each)),
            pltpu.SemaphoreType.DMA((2, each)),
            pltpu.SemaphoreType.DMA((each, groups)),
        ],
        compiler_params=kernel_params(),
        cost_estimate=pl.CostEstimate(
            flops=8 * number * height * width * width,
            bytes_accessed=number * (8 * width * width + 4 * height * width) + 16 * height * width,
            transcendentals=0,
        ),
    )(*operands, *pieces)


def finish_kernel(names, held, rows, first, *refs):
    place_ref, *refs = refs
    sources, refs = refs[: len(names)], refs[len(names) :]
    in_ref, out_ref, in_bias_out_ref, out_bias_out_ref, ready, sems = refs[-6:]
    in_bias_out_ref[...] = jnp.zeros_like(in_bias_out_ref) if first else refs[2][...]
    out_bias_out_ref[...] = jnp.zeros_like(out_bias_out_ref) if first else refs[3][...]
    copies = []
    for at, ((layer_at, half), source) in enumerate(zip(names, sources)):
        for unit in range(held):
            base = unit * (2 * rows + EXTRA)
            where = held * (place_ref[2] ^ half) + unit
            for which, ref in enumerate((in_ref, out_ref)):
                begin = base + which * rows
                ready[at, unit, which] = source[begin : begin + rows].astype(f32)
                copy = pltpu.make_async_copy(
                    ready.at[at, unit, which], ref.at[layer_at, where], sems.at[at, unit, which]
                )
                copy.start()
                copies.append(copy)
            tail = source[base + 2 * rows : base + 2 * rows + EXTRA].astype(f32)
            in_bias_out_ref[layer_at, pl.ds(where, 1)] = tail[0:1]
            out_bias_out_ref[layer_at, pl.ds(where, 1)] = tail[1:2]
    for copy in copies:
        copy.wait()


def finish_call(place, named, held_arrays, held, shape):
    rows, width = shape[2:]
    names, sources = tuple(named), list(named.values())
    outs = [jax.ShapeDtypeStruct(shape, f32)] * 2
    outs += [jax.ShapeDtypeStruct((*shape[:2], width), f32)] * 2
    first = held_arrays is None
    number = len(names)
    return pl.pallas_call(
        functools.partial(finish_kernel, names, held, rows, first),
        out_shape=outs,
        in_specs=[SCALARS] + [NEAR] * number + ([] if first else [FAR, FAR, NEAR, NEAR]),
        out_specs=[FAR, FAR, NEAR, NEAR],
        scratch_shapes=[
            pltpu.VMEM((number, held, 2, rows, width), f32),
            pltpu.SemaphoreType.DMA((number, held, 2)),
        ],
        input_output_aliases={} if first else {1 + number: 0, 2 + number: 1},
        compiler_params=kernel_params(),
        cost_estimate=pl.CostEstimate(flops=0, bytes_accessed=number * held * 12 * rows * width, transcendentals=0),
    )(place, *sources, *([] if first else held_arrays))


def flip(array, axis, bits):
    size = lax.axis_size(axis)
    return lax.ppermute(array, axis, [(i, i ^ bits) for i in range(size)])


def add_low(*arrays):
    level = [a.astype(f32) for a in arrays]
    while len(level) > 1:
        level = [level[i] + level[i + 1] for i in range(0, len(level), 2)]
    return level[0].astype(bf16)


def after(arrays, others):
    return lax.optimization_barrier((arrays, others))[0]


def near(mine, groups):
    if groups == 4 and mine.shape[0] == 2:
        return {1: [flip(mine, "expert", 1)], 2: [flip(mine, "expert", 2)]}
    return {ro: [flip(mine, "expert", ro)] for ro in range(1, groups)}


def relay(arrived, groups, held):
    if groups == 4 and held == 2:
        return {3: [flip(arrived[1][0][:1], "expert", 2), flip(arrived[2][0][1:], "expert", 1)]}
    return {}


def crossed(parts, halves):
    return [] if halves == 1 else [flip(part, "rows", 1) for part in parts]


def body(
    rows_in,
    pred_grad,
    lengths,
    session_type,
    expert_in,
    expert_in_bias,
    expert_out,
    expert_out_bias,
    selector_logits,
    selector_mix,
    tower_in,
    tower_bias,
    tower_out,
):
    height, width = rows_in.shape
    layers, owned = expert_in.shape[:2]
    type_count, tasks = selector_logits.shape[1:3]
    selectors, bits = selector_logits.shape[3:]
    groups = lax.axis_size("expert")
    halves = 2 if owned % 2 == 0 else 1
    held = owned // halves
    stride = 2 * width + EXTRA
    me, row_at = lax.axis_index("expert"), lax.axis_index("rows")
    core = row_at % 2 if halves == 2 else jnp.int32(0)
    place = jnp.stack([(row_at * groups + me) * height, me, core]).astype(jnp.int32)

    def rows_of(layer_at, first):
        cut = lambda a: lax.dynamic_slice_in_dim(a[layer_at], first, held)
        half = lambda a: a * jnp.asarray(0.5, a.dtype)
        tail = []
        for bias in (half(cut(expert_in_bias)), cut(expert_out_bias)):
            high = bias.astype(bf16)
            tail += [high, (bias - high.astype(f32)).astype(bf16)]
        tail = jnp.pad(jnp.stack(tail, axis=1), ((0, 0), (0, EXTRA - len(tail)), (0, 0)))
        return jnp.concatenate([half(cut(expert_in)), cut(expert_out), tail], axis=1)

    own = [[rows_of(layer_at, held * (core ^ half)) for half in range(halves)] for layer_at in range(layers)]
    sizes = (owned, halves, held, selectors, bits, tasks)
    types, across_types, gate_slopes, *values = prepare_call(
        place, lengths, session_type, selector_logits, selector_mix, height, sizes
    )

    def parts_of(got, across):
        pieces, places = [], {}
        for ro in got:
            spots = []
            for parts in (got[ro], across[ro]):
                here = []
                for part in parts:
                    here += [(len(pieces), at) for at in range(part.shape[0])]
                    pieces.append(part)
                if here:
                    spots.append(here)
            places[ro] = [[spots[half][unit] for half in range(halves)] for unit in range(held)]
        return pieces, places

    def pair_order(places, units):
        return tuple(spot for ro in sorted(places) for unit in units for spot in places[ro][unit])

    streams, stashes, weights = [rows_in], [], []
    for layer_at in range(layers):
        last = layer_at == layers - 1
        got = near(own[layer_at][0], groups)
        if layer_at == 0:
            got = after(got, (types, own[0][1:], own[1:]))
        far = relay(got, groups, held)
        across = {ro: crossed(got[ro], halves) for ro in got}
        if not last:
            own[layer_at + 1][0] = after(own[layer_at + 1][0], got)
        got = {0: own[layer_at][:1], **got}
        across[0] = own[layer_at][1:]
        if not last:
            pieces, places = parts_of(got, across)
            total, stash = forward_call(
                streams[-1], types, values[layer_at], None, None, pieces, pair_order(places, range(held)), 0
            )
            far = after(far, total)
        elif streams[1:]:
            far = after(far, streams[-1])
        far_across = {ro: crossed(far[ro], halves) for ro in far}
        if not last:
            if far:
                pieces, places = parts_of(far, far_across)
                base = held * min(far)
                order = pair_order(places, range(held))
                total, stash = forward_call(
                    streams[-1], types, values[layer_at], total, stash, pieces, order, base
                )
            streams.append(total[0])
            stashes.append(stash)
        weights.append(parts_of({**got, **far}, {**across, **far_across}))

    pieces, places = weights[-1]
    predictions, stream, *payload = middle_call(
        place,
        streams[-1],
        types,
        across_types,
        values[-1],
        gate_slopes,
        (pred_grad.T, tower_in, tower_bias, tower_out),
        pieces,
        pair_order(places, range(held)),
        groups,
        halves,
        held,
    )

    shards = lax.axis_size("rows")
    paired = shards > 2
    hops = ["share"] + [4 << at for at in range(shards.bit_length() - 3)] + ["join"] if paired else []
    upper = (row_at & 2) > 0

    class Moving:
        def __init__(self, layer_at, payload):
            self.layer_at, self.mine = layer_at, payload[0]
            self.others = payload[1:] or [payload[0][ro] for ro in range(groups)]
            self.got = [flip(part, "rows", 1) for part in self.others[1:]]
            self.total, self.sums, self.hops = None, None, -2

        def ask(self, token):
            if self.hops == -1:
                sums, own = after((self.sums, self.others[0]), token)
                self.got = [flip(own, "rows", 1)] + [flip(sums[ro], "expert", ro) for ro in range(1, groups)]
                return
            total = after(self.total, token)
            if self.hops == len(hops):
                self.got = [total] + ([flip(total, "rows", 1)] if halves == 2 else [])
            elif hops[self.hops] == "share":
                cut = total.shape[0] // 2
                self.got = [
                    jnp.where(upper, total[cut:], total[:cut]),
                    flip(jnp.where(upper, total[:cut], total[cut:]), "rows", 2),
                ]
            else:
                self.got = [total, flip(total, "rows", 2 if hops[self.hops] == "join" else hops[self.hops])]

        def add(self):
            if self.hops == len(hops):
                return True
            if self.hops == -2:
                self.sums = {ro: add_low(self.mine[ro], self.got[ro - 1]) for ro in range(1, groups)}
            elif self.hops == -1:
                self.total = add_low(add_low(self.mine[0], self.got[0]), *self.got[1:])
            elif hops[self.hops] != "join":
                self.total = add_low(*self.got)
            else:
                here, there = self.got
                self.total = jnp.concatenate([jnp.where(upper, there, here), jnp.where(upper, here, there)])
            self.hops += 1
            return False

    def arrive(entries, others):
        got, others = lax.optimization_barrier(([entry.got for entry in entries], others))
        for entry, what in zip(entries, got):
            entry.got = what
        ended = [entry for entry in entries if entry.add()]
        return ([entry.sums if entry.total is None else entry.total for entry in entries], others), ended

    moving = [Moving(layers - 1, payload)]
    token, _ = arrive(moving, ())
    stream = after(stream, token)
    for layer_at in reversed(range(layers - 1)):
        for entry in moving:
            entry.ask(token)
        pieces, places = weights[layer_at]
        stream, *payload = backward_call(
            streams[layer_at],
            types,
            across_types,
            stream,
            gate_slopes,
            layer_at,
            values[layer_at],
            stashes[layer_at],
            pieces,
            pair_order(places, range(held)),
            held,
            tasks,
        )
        token, _ = arrive(moving, stream)
        moving.append(Moving(layer_at, payload))
        token, _ = arrive(moving[-1:], token)

    whole = {}
    arrays, tower_sums = None, ()

    def ask(*entries):
        nonlocal arrays, tower_sums
        for entry in entries:
            entry.ask(token)
        for entry in entries:
            if entry.hops < len(hops):
                continue
            moving.remove(entry)
            layer_at, got = entry.layer_at, entry.got
            whole[layer_at] = got
            if layer_at == layers - 1:
                end = got[0][held * stride + type_count // 2 :].astype(f32)
                tower_rows = [array[held * stride + type_count // 2 + EXTRA :].astype(f32) for array in got]
                if halves == 2:
                    tower_rows = [jnp.where(core == 0, *tower_rows), jnp.where(core == 0, *tower_rows[::-1])]
                wide = jnp.concatenate(tower_rows).reshape(tasks, -1, width)
                narrow = tower_in.shape[2]
                parts = [wide[:, :, at : at + narrow] for at in range(0, width, narrow)]
                tower_sums = (
                    jnp.concatenate(parts, axis=1),
                    end[0].reshape(tower_bias.shape),
                    end[1].reshape(tower_out.shape),
                )
            if moving:
                sources = {(layer_at, half): array for half, array in enumerate(got)}
                arrays = finish_call(place, sources, arrays, held, expert_in.shape)

    if layers == 2 and len(hops) == 3:
        later, earlier = moving
        ask(earlier, later)
        token, _ = arrive([later], ())
        ask(later)
        token, _ = arrive([earlier, later], ())
        ask(earlier)
        token, _ = arrive([earlier], ())
        ask(earlier, later)
        token, _ = arrive([earlier, later], ())
    while moving:
        ask(*moving)
        if moving:
            token, _ = arrive(moving, (arrays, tower_sums))
    gate_grads = [whole[layer_at][0][held * stride :][: type_count // 2].astype(f32) for layer_at in range(layers)]
    quantities = selectors * (bits + 1)
    small = jnp.stack(gate_grads)
    small = jnp.concatenate([small[..., :LANES], small[..., LANES:]], axis=1)[..., : tasks * quantities]
    small = small.reshape(layers, type_count, tasks, quantities)
    logits_grad = small[..., : selectors * bits].reshape(selector_logits.shape)
    smalls = (logits_grad, small[..., selectors * bits :], *tower_sums)
    got, (arrays, smalls) = lax.optimization_barrier((whole[0], (arrays, smalls)))
    arrays = finish_call(place, {(0, half): array for half, array in enumerate(got)}, arrays, held, expert_in.shape)
    return (
        predictions.T,
        stream,
        arrays[0],
        arrays[2],
        arrays[1],
        arrays[3],
        *smalls,
    )


def solution(mesh):
    in_specs = (
        P(("rows", "expert"), None),
        P(("rows", "expert"), None),
        P(),
        P(),
        P(None, "expert", None, None),
        P(None, "expert", None),
        P(None, "expert", None, None),
        P(None, "expert", None),
        P(),
        P(),
        P(),
        P(),
        P(),
    )
    out_specs = (
        P(("rows", "expert"), None),
        P(("rows", "expert"), None),
        P(None, "expert", None, None),
        P(None, "expert", None),
        P(None, "expert", None, None),
        P(None, "expert", None),
        P(),
        P(),
        P(),
        P(),
        P(),
    )
    return jax.shard_map(body, mesh=mesh, in_specs=in_specs, out_specs=out_specs, check_vma=False)
```

```python
import functools
import math

import jax
import jax.numpy as jnp
import numpy as np
from jax import lax
from jax.experimental import pallas as pl
from jax.experimental.pallas import tpu as pltpu
from jax.sharding import PartitionSpec as P

SHARPNESS = 10.0
EXACT = lax.Precision.HIGHEST
bf16 = jnp.bfloat16
f32 = jnp.float32
INNER = math.sqrt(2.0 / math.pi)
CUBE = 0.044715 * INNER
TILE = 1024
TOWER_TILE = 512
LANES = 128
EXTRA = 16


def mm(a, b):
    return jnp.dot(a, b, preferred_element_type=f32)


def mm_exact(a, b):
    return jnp.dot(a, b, precision=EXACT, preferred_element_type=f32)


def mm_nt(a, b):
    return lax.dot_general(a, b, (((1,), (1,)), ((), ())), preferred_element_type=f32)


def mm_tn(a, b):
    return lax.dot_general(a, b, (((0,), (0,)), ((), ())), preferred_element_type=f32)


def gelu_both(v):
    square = v * v
    half = 0.5 + 0.5 * jnp.tanh(v * (INNER + CUBE * square))
    value = v * half
    slope = half + value * (1.0 - half) * (2.0 * INNER + 6.0 * CUBE * square)
    return value, slope


def gelu_parts(v):
    bend = 2.0 * INNER + 8.0 * CUBE * (v * v)
    twice_share = 1.0 + jnp.tanh(v * bend)
    return v * twice_share, bend, twice_share


def gelu_slope(value, bend, twice_share):
    rise = 3.0 * bend - 4.0 * INNER
    return twice_share + value * (2.0 - twice_share) * rise


FAR = pl.BlockSpec(memory_space=pl.ANY)
NEAR = pl.BlockSpec(memory_space=pltpu.VMEM)
SCALARS = pl.BlockSpec(memory_space=pltpu.SMEM)


def kernel_params():
    return pltpu.CompilerParams(vmem_limit_bytes=58 * 2**20)


def whole_spec(shape):
    zeros = (0,) * len(shape)
    return pl.BlockSpec(shape, lambda i: zeros)


def prepare_kernel(sizes, place_ref, length_ref, kind_ref, logit_ref, mix_ref, spread_logit_ref, spread_mix_ref, *outs):
    owned, halves, held, selectors, bits, tasks = sizes
    type_ref, across_ref, slope_ref, *value_refs = outs
    height, type_count = type_ref.shape
    experts = 2**bits
    sessions = length_ref.shape[1]
    chunk = min(256, sessions)
    position = (place_ref[0] + lax.broadcasted_iota(jnp.int32, (height, 1), 0)).astype(f32)
    earlier = lax.broadcasted_iota(jnp.int32, (chunk, chunk), 0) < lax.broadcasted_iota(jnp.int32, (chunk, chunk), 1)
    earlier = jnp.where(earlier, 1.0, 0.0).astype(bf16)
    kinds = lax.broadcasted_iota(jnp.int32, (type_count, chunk), 0)
    before = jnp.zeros((1, 1), f32)
    types = jnp.zeros((height, type_count), f32)
    across = jnp.zeros((type_count, height), f32)
    for at in range(0, sessions, chunk):
        lengths = length_ref[:, at : at + chunk].astype(f32)
        begin = before + mm(jnp.broadcast_to(lengths.astype(bf16), (EXTRA, chunk)), earlier)[0:1]
        before += jnp.sum(lengths, axis=1, keepdims=True)
        member = jnp.where((position >= begin) & (position < begin + lengths), 1.0, 0.0).astype(bf16)
        of_type = jnp.where(kinds == kind_ref[:, at : at + chunk], 1.0, 0.0).astype(bf16)
        types += mm_nt(member, of_type)
        across += mm_nt(of_type, member)
    type_ref[...] = types.astype(bf16)
    across_ref[...] = across.astype(bf16)

    rows = logit_ref.shape[0]
    place = lax.broadcasted_iota(jnp.int32, (rows, LANES), 1) % experts
    expert = (
        owned * ((place // owned) ^ place_ref[1])
        + held * ((place % halves) ^ place_ref[2])
        + (place // halves) % held
    )
    logits = mm_exact(logit_ref[...], spread_logit_ref[...])
    mixes = mm_exact(mix_ref[...], spread_mix_ref[...])
    mixes = [mixes[:, k * LANES : (k + 1) * LANES] for k in range(selectors)]
    top = functools.reduce(jnp.maximum, mixes)
    shares = [jnp.exp(mix - top) for mix in mixes]
    whole = functools.reduce(jnp.add, shares)
    shares = [share / whole for share in shares]
    value = jnp.zeros((rows, LANES), f32)
    reaches = []
    for k in range(selectors):
        factors, signed = [], []
        for bit in range(bits):
            at = (k * bits + bit) * LANES
            logit = logits[:, at : at + LANES]
            cubic = (-2.0 / SHARPNESS**3) * logit * logit * logit + (1.5 / SHARPNESS) * logit + 0.5
            step = jnp.where(logit <= -SHARPNESS / 2, 0.0, jnp.where(logit >= SHARPNESS / 2, 1.0, cubic))
            slope = (-6.0 / SHARPNESS**3) * logit * logit + 1.5 / SHARPNESS
            slope = jnp.where((logit > -SHARPNESS / 2) & (logit < SHARPNESS / 2), slope, 0.0)
            on = (expert >> bit) & 1 == 1
            factors.append(jnp.where(on, step, 1.0 - step))
            signed.append(jnp.where(on, slope, -slope))
        reaches.append(functools.reduce(jnp.multiply, factors))
        value += shares[k] * reaches[k]
        for bit in range(bits):
            others = [factors[b] for b in range(bits) if b != bit]
            slope_ref[k * bits + bit] = shares[k] * signed[bit] * functools.reduce(jnp.multiply, others)
    for k in range(selectors):
        slope_ref[selectors * bits + k] = shares[k] * (reaches[k] - value)

    value = value.astype(bf16).astype(f32)
    for layer_at, ref in enumerate(value_refs):
        table = value[layer_at * type_count : (layer_at + 1) * type_count]
        columns = [table[:, t * experts : (t + 1) * experts] for t in range(tasks)]
        if layer_at < len(value_refs) - 1:
            columns = [functools.reduce(jnp.add, columns) / tasks]
        for pair in range(ref.shape[0]):
            lanes = []
            for half in range(halves):
                at = pair * halves + half
                lanes += [jnp.broadcast_to(c[:, at : at + 1], (type_count, LANES)) for c in columns]
            ref[pair] = jnp.concatenate(lanes, axis=1).astype(bf16)


def prepare_call(place, lengths, session_type, logits, mixing, height, sizes):
    owned, halves, held, selectors, bits, tasks = sizes
    layers, type_count = logits.shape[:2]
    experts = 2**bits
    rows = layers * type_count
    lane = np.arange(LANES)
    source = np.arange(tasks * selectors * bits)
    task, number = source // (selectors * bits), source % (selectors * bits)
    mine = (lane[None, :] // experts == task[:, None])[:, None, :]
    spread_logit = mine & (number[:, None, None] == np.arange(selectors * bits)[None, :, None])
    source = np.arange(tasks * selectors)
    mine = (lane[None, :] // experts == (source // selectors)[:, None])[:, None, :]
    spread_mix = mine & ((source % selectors)[:, None, None] == np.arange(selectors)[None, :, None])
    spread_logit = spread_logit.reshape(spread_logit.shape[0], -1).astype(np.float32)
    spread_mix = spread_mix.reshape(spread_mix.shape[0], -1).astype(np.float32)
    outs = [
        jax.ShapeDtypeStruct((height, type_count), bf16),
        jax.ShapeDtypeStruct((type_count, height), bf16),
        jax.ShapeDtypeStruct((selectors * (bits + 1), rows, LANES), f32),
    ]
    for layer_at in range(layers):
        each = tasks if layer_at == layers - 1 else 1
        outs.append(jax.ShapeDtypeStruct((experts // halves, type_count, halves * each * LANES), bf16))
    return pl.pallas_call(
        functools.partial(prepare_kernel, sizes),
        out_shape=outs,
        in_specs=[SCALARS] + [NEAR] * 6,
        out_specs=[NEAR] * len(outs),
        compiler_params=kernel_params(),
        cost_estimate=pl.CostEstimate(flops=2 * height * lengths.size * 64, bytes_accessed=2**21, transcendentals=2**16),
    )(
        place,
        lengths.reshape(1, -1),
        session_type.reshape(1, -1),
        logits.reshape(rows, -1),
        mixing.reshape(rows, -1),
        spread_logit,
        spread_mix,
    )


def bias_rows(weights, width):
    rows = weights[2 * width : 2 * width + EXTRA].astype(f32)
    return rows[0:1] + rows[1:2], rows[2:3] + rows[3:4]


def twice(a):
    return jnp.concatenate([a, a], axis=1)


def tiles(height, most):
    tile = min(most, height)
    return [pl.ds(at, tile) for at in range(0, height, tile)]


def joined(parts, axis):
    return parts[0] if len(parts) == 1 else jnp.concatenate(parts, axis=axis)


def gates_of(types, value_ref, count):
    gates = mm(types, value_ref[...]).astype(bf16)
    return [gates[:, at * LANES : (at + 1) * LANES] for at in range(count)]


def forward_step(weights, value_ref, x_low, type_ref, total_ref, biases, keep, keep_gate=None, keep_result=None):
    height, width = x_low.shape
    kinds = total_ref.shape[0]
    bias_in, bias_out = zip(*(bias_rows(w, width) for w in weights))
    second = joined([w[width : 2 * width] for w in weights], 0)
    for rows in tiles(height, TILE):
        gates = gates_of(type_ref[rows], value_ref, len(weights) * kinds)
        if keep_gate is not None:
            for at, gate in enumerate(gates):
                keep_gate(at, rows, gate)
        scaled = [[] for _ in range(kinds)]
        for i, w in enumerate(weights):
            before = mm(x_low[rows], w[0:width]) + bias_in[i]
            hidden, bend, twice_share = gelu_parts(before)
            hidden = hidden.astype(bf16)
            keep(i, rows, hidden, gelu_slope(hidden, bend.astype(bf16), twice_share.astype(bf16)))
            if keep_result is not None:
                result = mm(hidden, w[width : 2 * width]).astype(bf16)
                keep_result(i, rows, result)
            for t in range(kinds):
                scaled[t].append(twice(gates[i * kinds + t]) * (hidden if keep_result is None else result))
        for t in range(kinds):
            if keep_result is None:
                total_ref[t, rows] += mm(joined(scaled[t], 1), second)
            else:
                total_ref[t, rows] += functools.reduce(jnp.add, scaled[t]).astype(f32)
    for i in range(len(weights)):
        for t in range(kinds):
            at = (i * kinds + t) * LANES
            biases[t] += twice(value_ref[:, at : at + LANES].astype(f32)) * bias_out[i]


def forward_end(type_ref, total_ref, biases):
    for t in range(total_ref.shape[0]):
        high = biases[t].astype(bf16)
        rest = (biases[t] - high.astype(f32)).astype(bf16)
        for rows in tiles(total_ref.shape[1], TILE):
            total_ref[t, rows] += mm(twice(type_ref[rows]), jnp.concatenate([high, rest], axis=0))


def backward_start(x_low, type_across, low, across, share):
    width = x_low.shape[1]
    across[0:width] = x_low[...].T
    ones = lax.broadcasted_iota(jnp.int32, (EXTRA, x_low.shape[0]), 0) == 0
    across[width:] = jnp.where(ones, 1.0, 0.0).astype(bf16)
    for t in range(low.shape[0]):
        share[t] = mm(type_across[...], low[t])


def backward_step(weights, value_ref, hiddens, slopes, outs, pair, experts, type_ref, type_across, low, stream_ref, across, share, table, scratch, kept_gates=None, results=None, dots=None):
    before_grads, result_grads, products = scratch
    kinds, height, width = low.shape
    count = len(weights)
    first = joined([w[0:width] for w in weights], 1)
    for rows in tiles(height, TILE):
        if kept_gates is None:
            gates = gates_of(type_ref[rows], value_ref, count * kinds)
        else:
            gates = [kept_gates[at, rows] for at in range(count * kinds)]
        gates = [twice(gate) for gate in gates]
        befores = []
        for i, w in enumerate(weights):
            hidden, slope = hiddens[i][rows], slopes[i][rows]
            second = w[width : 2 * width]
            result_grad = gates[i * kinds] * low[0, rows]
            for t in range(1, kinds):
                result_grad += gates[i * kinds + t] * low[t, rows]
            hidden_grad = mm_nt(result_grad, second).astype(bf16)
            for t in range(kinds):
                product = hidden * hidden_grad if results is None else results[i][rows] * low[t, rows]
                product = functools.reduce(
                    jnp.add, [product[:, lane : lane + LANES] for lane in range(0, width, LANES)]
                )
                if dots is None:
                    at = (i * kinds + t) * LANES
                    products[rows, at : at + LANES] = product
                else:
                    found = jnp.sum(product.astype(f32), axis=1, keepdims=True)
                    lanes = lax.broadcasted_iota(jnp.int32, (1, LANES), 1)
                    dots[rows] = jnp.where(lanes == t * experts + pair * count + i, found, dots[rows])
            before = slope * hidden_grad
            before_grads[i, rows] = before
            result_grads[i, rows] = result_grad
            befores.append(before)
        stream_ref[rows] += mm_nt(joined(befores, 1), first)
    sums = None if dots is not None else mm(type_across[...], products[...])
    lanes = lax.broadcasted_iota(jnp.int32, (type_ref.shape[1], LANES), 1)
    for i, w in enumerate(weights):
        _, bias_out = bias_rows(w, width)
        first_grad = 0.5 * mm(across[...], before_grads[i])
        outs[i][0:width] = first_grad[0:width].astype(bf16)
        outs[i][width : 2 * width] = mm_tn(hiddens[i][...], result_grads[i]).astype(bf16)
        out_bias = jnp.zeros((1, width), f32)
        place = pair * count + i
        for t in range(kinds):
            at = (i * kinds + t) * LANES
            gate = value_ref[:, at : at + LANES].astype(f32)
            out_bias += jnp.sum(twice(gate) * share[t], axis=0, keepdims=True)
            found = 0.0 if sums is None else jnp.sum(sums[:, at : at + LANES], axis=1, keepdims=True)
            bias_part = jnp.sum(share[t] * bias_out, axis=1, keepdims=True)
            if kinds == 1:
                some = gate > 0.0
                found = jnp.where(some, 0.5 * found / jnp.where(some, gate, 1.0), 0.0)
                table[...] = jnp.where(lanes % experts == place, found + 0.5 * bias_part, table[...])
            else:
                table[...] = jnp.where(lanes == t * experts + place, found + bias_part, table[...])
        tail = jnp.concatenate([first_grad[width : width + 1], out_bias, jnp.zeros((EXTRA - 2, width), f32)])
        outs[i][2 * width : 2 * width + EXTRA] = tail.astype(bf16)


def through_gates(table, gate_slope_ref, experts, tasks):
    quantities, type_count = gate_slope_ref.shape[:2]
    lanes = lax.broadcasted_iota(jnp.int32, (type_count, LANES), 1)
    small = jnp.zeros((type_count, LANES), f32)
    for q in range(quantities):
        product = gate_slope_ref[q] * table[...]
        for t in range(tasks):
            part = jnp.sum(jnp.where(lanes // experts == t, product, 0.0), axis=1, keepdims=True)
            small = jnp.where(lanes == t * quantities + q, part, small)
    half = type_count // 2
    return jnp.concatenate([small[:half], small[half:]], axis=1).astype(bf16)


def store_copies(ready, pair, held, out_refs, sems):
    group, unit = pair // held, lax.rem(pair, held)
    rows = pl.ds(pl.multiple_of(unit * ready.shape[1], EXTRA), ready.shape[1])
    copies = [(None, pltpu.make_async_copy(ready.at[0], out_refs[0].at[group, rows], sems.at[0]))]
    for at, ref in enumerate(out_refs[1:]):
        copies.append((group == at, pltpu.make_async_copy(ready.at[1], ref.at[rows], sems.at[1])))
    return copies


def end_copies(ends, out_refs, sems):
    rows = out_refs[0].shape[1]
    last = pl.ds(rows - ends.shape[1], ends.shape[1])
    groups = out_refs[0].shape[0]
    copies = [pltpu.make_async_copy(ends.at[0], out_refs[0].at[at, last], sems.at[0, at]) for at in range(groups)]
    copies += [
        pltpu.make_async_copy(ends.at[1], ref.at[last], sems.at[1, at]) for at, ref in enumerate(out_refs[1:])
    ]
    return [(None, copy) for copy in copies]


def for_each(copies, act):
    for condition, copy in copies:
        if condition is None:
            act(copy)
        else:
            pl.when(condition)(functools.partial(act, copy))


def start(copy):
    copy.start()


def wait(copy):
    copy.wait()


def fetch_weights(places, buffer, sems, each):
    step = pl.program_id(0)
    for of in range(len(places) // each):

        @pl.when(step == max(of - 1, 0))
        def _(of=of):
            for i, (ref, at) in enumerate(places[of * each : (of + 1) * each]):
                pltpu.make_async_copy(ref.at[at], buffer.at[of % 2, i], sems.at[of % 2, i]).start()

    slot = lax.rem(step, 2)
    for i in range(each):
        ref, at = places[0]
        pltpu.make_async_copy(ref.at[at], buffer.at[slot, i], sems.at[slot, i]).wait()
    return [buffer.at[slot, i] for i in range(each)]


def forward_kernel(places, pieces, each, first, *refs):
    refs = list(refs)
    take = lambda count: [refs.pop(0) for _ in range(count)]
    x_ref, type_ref, value_ref = take(3)
    if not first:
        total_ref, _, _ = take(3)
    weight_refs = take(pieces)
    out_ref, hidden_ref, slope_ref, x_low, biases, buffer, sems = take(7)
    step = pl.program_id(0)
    weights = fetch_weights([(weight_refs[piece], at) for piece, at in places], buffer, sems, each)

    @pl.when(step == 0)
    def _():
        x_low[...] = x_ref[...].astype(bf16)
        biases[...] = jnp.zeros_like(biases)
        out_ref[0] = x_ref[...] if first else total_ref[0]

    def keep(i, rows, hidden, slope):
        hidden_ref[0, i, rows] = hidden
        slope_ref[0, i, rows] = slope

    forward_step(weights, value_ref.at[0], x_low, type_ref, out_ref, biases, keep)

    @pl.when(step == pl.num_programs(0) - 1)
    def _():
        forward_end(type_ref, out_ref, biases)


def forward_call(x, types, values, total, stash, pieces, places, base):
    height, width = x.shape
    pairs, type_count, lanes = values.shape
    each = lanes // LANES
    operands = [x, types, values]
    specs = [whole_spec(x.shape), whole_spec(types.shape)]
    specs.append(pl.BlockSpec((1, type_count, lanes), lambda i: (base + i, 0, 0)))
    aliases = {}
    if total is not None:
        operands += [total, *stash]
        specs += [whole_spec(total.shape), FAR, FAR]
        aliases = {4: 1, 5: 2}
    summed = jax.ShapeDtypeStruct((1, height, width), f32)
    kept = jax.ShapeDtypeStruct((pairs, each, height, width), bf16)
    kept_spec = pl.BlockSpec((1, each, height, width), lambda i: (base + i, 0, 0, 0))
    number = len(places)
    results = pl.pallas_call(
        functools.partial(forward_kernel, places, len(pieces), each, total is None),
        grid=(number // each,),
        out_shape=[summed, kept, kept],
        in_specs=specs + [FAR] * len(pieces),
        out_specs=[whole_spec(summed.shape), kept_spec, kept_spec],
        scratch_shapes=[
            pltpu.VMEM((height, width), bf16),
            pltpu.VMEM((1, type_count, width), f32),
            pltpu.VMEM((2, each, *pieces[0].shape[1:]), bf16),
            pltpu.SemaphoreType.DMA((2, each)),
        ],
        input_output_aliases=aliases,
        compiler_params=kernel_params(),
        cost_estimate=pl.CostEstimate(
            flops=4 * number * height * width * width,
            bytes_accessed=number * (4 * width * width + 4 * height * width) + 8 * height * width,
            transcendentals=number * height * width,
        ),
    )(*operands, *pieces)
    return results[0], results[1:]


def middle_kernel(places, pieces, groups, halves, held, *refs):
    refs = list(refs)
    take = lambda count: [refs.pop(0) for _ in range(count)]
    place_ref, x_ref, type_ref, across_types_ref, value_ref, gate_slope_ref, pred_grad_ref = take(7)
    tower_in_ref, tower_bias_ref, tower_out_ref = take(3)
    weight_refs = take(pieces)
    pred_ref, stream_ref = take(2)
    out_refs = take(1 + groups * (halves - 1))
    x_low, weights, hidden_all, slope_all, result_all, gates_all, total, biases, low, across, share, table = take(12)
    before_grads, result_grads, dots, cotangents, ready, ends, in_grad, bias_grad, out_grad, load_sem, store_sem, end_sem = take(12)
    height, width = x_ref.shape
    pairs = value_ref.shape[0]
    experts = pairs * halves
    tasks = total.shape[0]

    def load(pair, i, ref, at):
        return pltpu.make_async_copy(ref.at[at], weights.at[pair, i], load_sem.at[pair, i])

    for j, (piece, at) in enumerate(places):
        load(j // halves, j % halves, weight_refs[piece], at).start()
    x_low[...] = x_ref[...].astype(bf16)
    biases[...] = jnp.zeros_like(biases)
    for t in range(tasks):
        total[t] = x_ref[...]

    def forward_pair(pair, carry):
        for i in range(halves):
            load(pair, i, weight_refs[0], 0).wait()

        def keep(i, rows, hidden, slope):
            hidden_all[pair, i, rows] = hidden
            slope_all[pair, i, rows] = slope

        def keep_gate(at, rows, gate):
            gates_all[pair, at, rows] = gate

        def keep_result(i, rows, result):
            result_all[pair, i, rows] = result

        forward_step(
            [weights.at[pair, i] for i in range(halves)],
            value_ref.at[pair],
            x_low,
            type_ref,
            total,
            biases,
            keep,
            keep_gate,
            keep_result,
        )
        return carry

    lax.fori_loop(0, pairs, forward_pair, 0)
    forward_end(type_ref, total, biases)

    cotangents[...] = jnp.concatenate(
        [pred_grad_ref[...], jnp.zeros((cotangents.shape[1] - tasks, height), f32)]
    ).T
    in_grad[...] = jnp.zeros_like(in_grad)
    bias_grad[...] = jnp.zeros_like(bias_grad)
    out_grad[...] = jnp.zeros_like(out_grad)
    for rows in tiles(height, TOWER_TILE):
        summed = None
        predicted = []
        for t in range(tasks):
            closing_low = total[t, rows].astype(bf16)
            act, slope = gelu_both(mm(closing_low, tower_in_ref[t]) + tower_bias_ref[t : t + 1])
            vector = tower_out_ref[t : t + 1]
            predicted.append(jnp.sum(act * vector, axis=1, keepdims=True))
            cotangent = cotangents[rows, t : t + 1]
            out_grad[t : t + 1] += jnp.sum(act * cotangent, axis=0, keepdims=True)
            before_grad = (slope * (cotangent * vector)).astype(bf16)
            bias_grad[t : t + 1] += jnp.sum(before_grad.astype(f32), axis=0, keepdims=True)
            in_grad[t] += mm_tn(closing_low, before_grad)
            closing_grad = mm_nt(before_grad, tower_in_ref[t])
            low[t, rows] = closing_grad.astype(bf16)
            summed = closing_grad if summed is None else summed + closing_grad
        stream_ref[rows] = summed
        blank = jnp.zeros((predicted[0].shape[0], cotangents.shape[1] - tasks), f32)
        pred_ref[:, rows] = jnp.concatenate([*predicted, blank], axis=1).T[0:tasks]
    narrow = in_grad.shape[2]
    tall = width * narrow // width
    begin = type_ref.shape[1] // 2 + EXTRA
    for t in range(tasks):
        wide = jnp.concatenate([in_grad[t, :tall], in_grad[t, tall:]], axis=1).astype(bf16)
        if halves == 2:
            ends[place_ref[2] ^ t, begin:] = wide
        else:
            ends[0, begin + t * tall : begin + (t + 1) * tall] = wide
    vectors = [jnp.concatenate([ref[0:1], ref[1:2]], axis=1) for ref in (bias_grad, out_grad)]
    vectors = jnp.concatenate([*vectors, jnp.zeros((EXTRA - 2, width), f32)]).astype(bf16)
    for half in range(halves):
        ends[half, begin - EXTRA : begin] = vectors

    backward_start(x_low, across_types_ref, low, across, share)
    table[...] = jnp.zeros_like(table)
    dots[...] = jnp.zeros_like(dots)

    def stores(pair):
        return store_copies(ready.at[pair], pair, held, out_refs, store_sem.at[pair])

    def backward_pair(pair, carry):
        backward_step(
            [weights.at[pair, i] for i in range(halves)],
            value_ref.at[pair],
            [hidden_all.at[pair, i] for i in range(halves)],
            [slope_all.at[pair, i] for i in range(halves)],
            [ready.at[pair, i] for i in range(halves)],
            pair,
            experts,
            type_ref,
            across_types_ref,
            low,
            stream_ref,
            across,
            share,
            table,
            (before_grads, result_grads, None),
            gates_all.at[pair],
            [result_all.at[pair, i] for i in range(halves)],
            dots,
        )
        for_each(stores(pair), start)
        return carry

    lax.fori_loop(0, pairs, backward_pair, 0)
    high = dots[...].astype(bf16)
    rest = (dots[...] - high.astype(f32)).astype(bf16)
    table[...] += mm(across_types_ref[...], high) + mm(across_types_ref[...], rest)
    small = through_gates(table, gate_slope_ref, experts, tasks)
    for half in range(halves):
        ends[half, 0 : small.shape[0]] = small
    for_each(end_copies(ends, out_refs, end_sem), start)

    def drain(pair, carry):
        for_each(stores(pair), wait)
        return carry

    lax.fori_loop(0, pairs, drain, 0)
    for_each(end_copies(ends, out_refs, end_sem), wait)


def middle_call(place, x, types, across_types, values, gate_slopes, tower, pieces, places, groups, halves, held):
    height, width = x.shape
    pairs, type_count, lanes = values.shape
    pred_grad, tower_in, tower_bias, tower_out = tower
    tasks = tower_in.shape[0]
    stride = 2 * width + EXTRA
    experts = pairs * halves
    outs = [jax.ShapeDtypeStruct(shape, f32) for shape in (pred_grad.shape, (height, width))]
    near = len(outs)
    end_rows = type_count // 2 + EXTRA + tower_in.size // width // halves
    rows = held * stride + end_rows
    outs.append(jax.ShapeDtypeStruct((groups, rows, width), bf16))
    outs += [jax.ShapeDtypeStruct((rows, width), bf16)] * (groups * (halves - 1))
    layer_at = gate_slopes.shape[1] // type_count - 1
    slope_spec = pl.BlockSpec((gate_slopes.shape[0], type_count, LANES), lambda i: (0, layer_at, 0))
    kept = pltpu.VMEM((pairs, halves, height, width), bf16)
    operands = [x, types, across_types, values, gate_slopes, *tower]
    specs = [whole_spec(a.shape) for a in operands]
    specs[4] = slope_spec
    return pl.pallas_call(
        functools.partial(middle_kernel, places, len(pieces), groups, halves, held),
        grid=(1,),
        out_shape=outs,
        in_specs=[SCALARS] + specs + [FAR] * len(pieces),
        out_specs=[whole_spec(out.shape) for out in outs[:near]] + [FAR] * (len(outs) - near),
        scratch_shapes=[
            pltpu.VMEM((height, width), bf16),
            pltpu.VMEM((pairs, halves, stride, width), bf16),
            kept,
            kept,
            kept,
            pltpu.VMEM((pairs, halves * tasks, height, LANES), bf16),
            pltpu.VMEM((tasks, height, width), f32),
            pltpu.VMEM((tasks, type_count, width), f32),
            pltpu.VMEM((tasks, height, width), bf16),
            pltpu.VMEM((width + EXTRA, height), bf16),
            pltpu.VMEM((tasks, type_count, width), f32),
            pltpu.VMEM((type_count, LANES), f32),
            pltpu.VMEM((halves, height, width), bf16),
            pltpu.VMEM((halves, height, width), bf16),
            pltpu.VMEM((height, LANES), f32),
            pltpu.VMEM((height, LANES), f32),
            pltpu.VMEM((pairs, halves, stride, width), bf16),
            pltpu.VMEM((halves, end_rows, width), bf16),
            pltpu.VMEM(tower_in.shape, f32),
            pltpu.VMEM(tower_bias.shape, f32),
            pltpu.VMEM(tower_out.shape, f32),
            pltpu.SemaphoreType.DMA((pairs, halves)),
            pltpu.SemaphoreType.DMA((pairs, halves)),
            pltpu.SemaphoreType.DMA((halves, groups)),
        ],
        compiler_params=kernel_params(),
        cost_estimate=pl.CostEstimate(
            flops=14 * experts * height * width * width,
            bytes_accessed=experts * 8 * width * width + 16 * height * width,
            transcendentals=experts * height * width,
        ),
    )(place, *operands, *pieces)


def backward_kernel(places, pieces, each, held, tasks, *refs):
    refs = list(refs)
    take = lambda count: [refs.pop(0) for _ in range(count)]
    x_ref, type_ref, across_types_ref, stream_ref, gate_slope_ref, value_ref, hidden_ref, slope_ref = take(8)
    weight_refs = take(pieces)
    stream_out_ref = take(1)[0]
    out_refs = take(1 + len(places) // each // held * (each - 1))
    x_low, across, low, share, table, before_grads, result_grads, products, buffer, ready, ends = take(11)
    sems, store_sem, end_sem = take(3)
    step = pl.program_id(0)
    slot = lax.rem(step, 2)
    experts = len(places)
    weights = fetch_weights([(weight_refs[piece], at) for piece, at in places], buffer, sems, each)

    @pl.when(step == 0)
    def _():
        x_low[...] = x_ref[...].astype(bf16)
        low[0] = stream_ref[...].astype(bf16)
        stream_out_ref[...] = stream_ref[...]
        table[...] = jnp.zeros_like(table)
        backward_start(x_low, across_types_ref, low, across, share)

    def stores(pair):
        at = lax.rem(pair, 2)
        return store_copies(ready.at[at], pair, held, out_refs, store_sem.at[at])

    @pl.when(step >= 2)
    def _():
        for_each(stores(step - 2), wait)

    backward_step(
        weights,
        value_ref.at[0],
        [hidden_ref.at[0, i] for i in range(each)],
        [slope_ref.at[0, i] for i in range(each)],
        [ready.at[slot, i] for i in range(each)],
        step,
        experts,
        type_ref,
        across_types_ref,
        low,
        stream_out_ref,
        across,
        share,
        table,
        (before_grads, result_grads, products),
    )

    for_each(stores(step), start)

    @pl.when(step == pl.num_programs(0) - 1)
    def _():
        small = through_gates(table, gate_slope_ref, experts, tasks)
        for half in range(each):
            ends[half] = small
        for_each(end_copies(ends, out_refs, end_sem), start)
        for_each(stores(step - 1), wait)
        for_each(stores(step), wait)
        for_each(end_copies(ends, out_refs, end_sem), wait)


def backward_call(x, types, across_types, stream, gate_slopes, layer_at, values, stash, pieces, places, held, tasks):
    height, width = x.shape
    pairs, type_count, lanes = values.shape
    each = lanes // LANES
    groups = pairs // held
    stride = 2 * width + EXTRA
    operands = [x, types, across_types, stream, gate_slopes, values, *stash]
    specs = [whole_spec(a.shape) for a in operands[:4]]
    specs.append(pl.BlockSpec((gate_slopes.shape[0], type_count, LANES), lambda i: (0, layer_at, 0)))
    specs.append(pl.BlockSpec((1, type_count, lanes), lambda i: (i, 0, 0)))
    specs += [pl.BlockSpec((1, each, height, width), lambda i: (i, 0, 0, 0))] * 2
    rows = held * stride + type_count // 2
    mine = jax.ShapeDtypeStruct((groups, rows, width), bf16)
    others = [jax.ShapeDtypeStruct((rows, width), bf16)] * (groups * (each - 1))
    number = pairs * each
    return pl.pallas_call(
        functools.partial(backward_kernel, places, len(pieces), each, held, tasks),
        grid=(pairs,),
        out_shape=[jax.ShapeDtypeStruct(stream.shape, f32), mine, *others],
        in_specs=specs + [FAR] * len(pieces),
        out_specs=[whole_spec(stream.shape)] + [FAR] * (1 + len(others)),
        scratch_shapes=[
            pltpu.VMEM((height, width), bf16),
            pltpu.VMEM((width + EXTRA, height), bf16),
            pltpu.VMEM((1, height, width), bf16),
            pltpu.VMEM((1, type_count, width), f32),
            pltpu.VMEM((type_count, LANES), f32),
            pltpu.VMEM((each, height, width), bf16),
            pltpu.VMEM((each, height, width), bf16),
            pltpu.VMEM((height, lanes), bf16),
            pltpu.VMEM((2, each, stride, width), bf16),
            pltpu.VMEM((2, each, stride, width), bf16),
            pltpu.VMEM((each, type_count // 2, width), bf16),
            pltpu.SemaphoreType.DMA((2, each)),
            pltpu.SemaphoreType.DMA((2, each)),
            pltpu.SemaphoreType.DMA((each, groups)),
        ],
        compiler_params=kernel_params(),
        cost_estimate=pl.CostEstimate(
            flops=8 * number * height * width * width,
            bytes_accessed=number * (8 * width * width + 4 * height * width) + 16 * height * width,
            transcendentals=0,
        ),
    )(*operands, *pieces)


def finish_kernel(names, held, rows, first, *refs):
    place_ref, *refs = refs
    sources, refs = refs[: len(names)], refs[len(names) :]
    in_ref, out_ref, in_bias_out_ref, out_bias_out_ref, ready, sems = refs[-6:]
    in_bias_out_ref[...] = jnp.zeros_like(in_bias_out_ref) if first else refs[2][...]
    out_bias_out_ref[...] = jnp.zeros_like(out_bias_out_ref) if first else refs[3][...]
    copies = []
    for at, ((layer_at, half), source) in enumerate(zip(names, sources)):
        for unit in range(held):
            base = unit * (2 * rows + EXTRA)
            where = held * (place_ref[2] ^ half) + unit
            for which, ref in enumerate((in_ref, out_ref)):
                begin = base + which * rows
                ready[at, unit, which] = source[begin : begin + rows].astype(f32)
                copy = pltpu.make_async_copy(
                    ready.at[at, unit, which], ref.at[layer_at, where], sems.at[at, unit, which]
                )
                copy.start()
                copies.append(copy)
            tail = source[base + 2 * rows : base + 2 * rows + EXTRA].astype(f32)
            in_bias_out_ref[layer_at, pl.ds(where, 1)] = tail[0:1]
            out_bias_out_ref[layer_at, pl.ds(where, 1)] = tail[1:2]
    for copy in copies:
        copy.wait()


def finish_call(place, named, held_arrays, held, shape):
    rows, width = shape[2:]
    names, sources = tuple(named), list(named.values())
    outs = [jax.ShapeDtypeStruct(shape, f32)] * 2
    outs += [jax.ShapeDtypeStruct((*shape[:2], width), f32)] * 2
    first = held_arrays is None
    number = len(names)
    return pl.pallas_call(
        functools.partial(finish_kernel, names, held, rows, first),
        out_shape=outs,
        in_specs=[SCALARS] + [NEAR] * number + ([] if first else [FAR, FAR, NEAR, NEAR]),
        out_specs=[FAR, FAR, NEAR, NEAR],
        scratch_shapes=[
            pltpu.VMEM((number, held, 2, rows, width), f32),
            pltpu.SemaphoreType.DMA((number, held, 2)),
        ],
        input_output_aliases={} if first else {1 + number: 0, 2 + number: 1},
        compiler_params=kernel_params(),
        cost_estimate=pl.CostEstimate(flops=0, bytes_accessed=number * held * 12 * rows * width, transcendentals=0),
    )(place, *sources, *([] if first else held_arrays))


def flip(array, axis, bits):
    size = lax.axis_size(axis)
    return lax.ppermute(array, axis, [(i, i ^ bits) for i in range(size)])


def add_low(*arrays):
    level = [a.astype(f32) for a in arrays]
    while len(level) > 1:
        level = [level[i] + level[i + 1] for i in range(0, len(level), 2)]
    return level[0].astype(bf16)


def after(arrays, others):
    return lax.optimization_barrier((arrays, others))[0]


def near(mine, groups):
    if groups == 4 and mine.shape[0] == 2:
        return {1: [flip(mine, "expert", 1)], 2: [flip(mine, "expert", 2)]}
    return {ro: [flip(mine, "expert", ro)] for ro in range(1, groups)}


def relay(arrived, groups, held):
    if groups == 4 and held == 2:
        return {3: [flip(arrived[1][0][:1], "expert", 2), flip(arrived[2][0][1:], "expert", 1)]}
    return {}


def crossed(parts, halves):
    return [] if halves == 1 else [flip(part, "rows", 1) for part in parts]


def body(
    rows_in,
    pred_grad,
    lengths,
    session_type,
    expert_in,
    expert_in_bias,
    expert_out,
    expert_out_bias,
    selector_logits,
    selector_mix,
    tower_in,
    tower_bias,
    tower_out,
):
    height, width = rows_in.shape
    layers, owned = expert_in.shape[:2]
    type_count, tasks = selector_logits.shape[1:3]
    selectors, bits = selector_logits.shape[3:]
    groups = lax.axis_size("expert")
    halves = 2 if owned % 2 == 0 else 1
    held = owned // halves
    stride = 2 * width + EXTRA
    me, row_at = lax.axis_index("expert"), lax.axis_index("rows")
    core = row_at % 2 if halves == 2 else jnp.int32(0)
    place = jnp.stack([(row_at * groups + me) * height, me, core]).astype(jnp.int32)

    def rows_of(layer_at, first):
        cut = lambda a: lax.dynamic_slice(a, (layer_at, first) + (0,) * (a.ndim - 2), (1, held) + a.shape[2:])[0]
        half = lambda a: a * jnp.asarray(0.5, a.dtype)
        tail = []
        for bias in (half(cut(expert_in_bias)), cut(expert_out_bias)):
            high = bias.astype(bf16)
            tail += [high, (bias - high.astype(f32)).astype(bf16)]
        tail = jnp.pad(jnp.stack(tail, axis=1), ((0, 0), (0, EXTRA - len(tail)), (0, 0)))
        return jnp.concatenate([half(cut(expert_in)), cut(expert_out), tail], axis=1)

    first = rows_of(0, held * core)
    asked = near(first, groups)
    sizes = (owned, halves, held, selectors, bits, tasks)
    types, across_types, gate_slopes, *values = prepare_call(
        place, lengths, session_type, selector_logits, selector_mix, height, sizes
    )

    later = after((expert_in, expert_in_bias, expert_out, expert_out_bias), types)
    expert_in, expert_in_bias, expert_out, expert_out_bias = later
    own = [[rows_of(layer_at, held * (core ^ half)) for half in range(halves)] for layer_at in range(layers)]
    own[0][0] = first

    def parts_of(got, across):
        pieces, places = [], {}
        for ro in got:
            spots = []
            for parts in (got[ro], across[ro]):
                here = []
                for part in parts:
                    here += [(len(pieces), at) for at in range(part.shape[0])]
                    pieces.append(part)
                if here:
                    spots.append(here)
            places[ro] = [[spots[half][unit] for half in range(halves)] for unit in range(held)]
        return pieces, places

    def pair_order(places, units):
        return tuple(spot for ro in sorted(places) for unit in units for spot in places[ro][unit])

    streams, stashes, weights = [rows_in], [], []
    for layer_at in range(layers):
        last = layer_at == layers - 1
        got = near(own[layer_at][0], groups) if layer_at else after(asked, (types, own[0][1:], own[1:]))
        far = relay(got, groups, held)
        across = {ro: crossed(got[ro], halves) for ro in got}
        if not last:
            pass
        got = {0: own[layer_at][:1], **got}
        across[0] = own[layer_at][1:]
        if not last:
            pieces, places = parts_of(got, across)
            total, stash = forward_call(
                streams[-1], types, values[layer_at], None, None, pieces, pair_order(places, range(held)), 0
            )
            far = after(far, total)
        elif streams[1:]:
            far = after(far, streams[-1])
        far_across = {ro: crossed(far[ro], halves) for ro in far}
        if not last:
            if far:
                pieces, places = parts_of(far, far_across)
                base = held * min(far)
                order = pair_order(places, range(held))
                total, stash = forward_call(
                    streams[-1], types, values[layer_at], total, stash, pieces, order, base
                )
            streams.append(total[0])
            stashes.append(stash)
        weights.append(parts_of({**got, **far}, {**across, **far_across}))

    pieces, places = weights[-1]
    predictions, stream, *payload = middle_call(
        place,
        streams[-1],
        types,
        across_types,
        values[-1],
        gate_slopes,
        (pred_grad.T, tower_in, tower_bias, tower_out),
        pieces,
        pair_order(places, range(held)),
        groups,
        halves,
        held,
    )

    shards = lax.axis_size("rows")
    paired = shards > 2
    hops = ["share"] + [4 << at for at in range(shards.bit_length() - 3)] + ["join"] if paired else []
    upper = (row_at & 2) > 0

    class Moving:
        def __init__(self, layer_at, payload):
            self.layer_at, self.mine = layer_at, payload[0]
            self.others = payload[1:] or [payload[0][ro] for ro in range(groups)]
            self.got = [flip(part, "rows", 1) for part in self.others[1:]]
            self.total, self.sums, self.hops = None, None, -2

        def ask(self, token):
            if self.hops == -1:
                sums, own = after((self.sums, self.others[0]), token)
                self.got = [flip(own, "rows", 1)] + [flip(sums[ro], "expert", ro) for ro in range(1, groups)]
                return
            total = after(self.total, token)
            if self.hops == len(hops):
                self.got = [total] + ([flip(total, "rows", 1)] if halves == 2 else [])
            elif hops[self.hops] == "share":
                cut = total.shape[0] // 2
                self.got = [
                    jnp.where(upper, total[cut:], total[:cut]),
                    flip(jnp.where(upper, total[:cut], total[cut:]), "rows", 2),
                ]
            else:
                self.got = [total, flip(total, "rows", 2 if hops[self.hops] == "join" else hops[self.hops])]

        def add(self):
            if self.hops == len(hops):
                return True
            if self.hops == -2:
                self.sums = {ro: add_low(self.mine[ro], self.got[ro - 1]) for ro in range(1, groups)}
            elif self.hops == -1:
                self.total = add_low(add_low(self.mine[0], self.got[0]), *self.got[1:])
            elif hops[self.hops] != "join":
                self.total = add_low(*self.got)
            else:
                here, there = self.got
                self.total = jnp.concatenate([jnp.where(upper, there, here), jnp.where(upper, here, there)])
            self.hops += 1
            return False

    def arrive(entries, others):
        got, others = lax.optimization_barrier(([entry.got for entry in entries], others))
        for entry, what in zip(entries, got):
            entry.got = what
        ended = [entry for entry in entries if entry.add()]
        return ([entry.sums if entry.total is None else entry.total for entry in entries], others), ended

    moving = [Moving(layers - 1, payload)]
    token, _ = arrive(moving, ())
    stream = after(stream, token)
    for layer_at in reversed(range(layers - 1)):
        for entry in moving:
            entry.ask(token)
        pieces, places = weights[layer_at]
        stream, *payload = backward_call(
            streams[layer_at],
            types,
            across_types,
            stream,
            gate_slopes,
            layer_at,
            values[layer_at],
            stashes[layer_at],
            pieces,
            pair_order(places, range(held)),
            held,
            tasks,
        )
        token, _ = arrive(moving, stream)
        moving.append(Moving(layer_at, payload))
        token, _ = arrive(moving[-1:], token)

    whole = {}
    arrays, tower_sums = None, ()

    def ask(*entries):
        nonlocal arrays, tower_sums
        for entry in entries:
            entry.ask(token)
        for entry in entries:
            if entry.hops < len(hops):
                continue
            moving.remove(entry)
            layer_at, got = entry.layer_at, entry.got
            whole[layer_at] = got
            if layer_at == layers - 1:
                end = got[0][held * stride + type_count // 2 :].astype(f32)
                tower_rows = [array[held * stride + type_count // 2 + EXTRA :].astype(f32) for array in got]
                if halves == 2:
                    tower_rows = [jnp.where(core == 0, *tower_rows), jnp.where(core == 0, *tower_rows[::-1])]
                wide = jnp.concatenate(tower_rows).reshape(tasks, -1, width)
                narrow = tower_in.shape[2]
                parts = [wide[:, :, at : at + narrow] for at in range(0, width, narrow)]
                tower_sums = (
                    jnp.concatenate(parts, axis=1),
                    end[0].reshape(tower_bias.shape),
                    end[1].reshape(tower_out.shape),
                )
            if moving:
                sources = {(layer_at, half): array for half, array in enumerate(got)}
                arrays = finish_call(place, sources, arrays, held, expert_in.shape)

    if layers == 2 and len(hops) == 3:
        later, earlier = moving
        ask(earlier, later)
        token, _ = arrive([later], ())
        ask(later)
        token, _ = arrive([earlier, later], ())
        ask(earlier)
        token, _ = arrive([earlier], ())
        ask(earlier, later)
        token, _ = arrive([earlier, later], ())
    while moving:
        ask(*moving)
        if moving:
            token, _ = arrive(moving, (arrays, tower_sums))
    gate_grads = [whole[layer_at][0][held * stride :][: type_count // 2].astype(f32) for layer_at in range(layers)]
    quantities = selectors * (bits + 1)
    small = jnp.stack(gate_grads)
    small = jnp.concatenate([small[..., :LANES], small[..., LANES:]], axis=1)[..., : tasks * quantities]
    small = small.reshape(layers, type_count, tasks, quantities)
    logits_grad = small[..., : selectors * bits].reshape(selector_logits.shape)
    smalls = (logits_grad, small[..., selectors * bits :], *tower_sums)
    got, (arrays, smalls) = lax.optimization_barrier((whole[0], (arrays, smalls)))
    arrays = finish_call(place, {(0, half): array for half, array in enumerate(got)}, arrays, held, expert_in.shape)
    return (
        predictions.T,
        stream,
        arrays[0],
        arrays[2],
        arrays[1],
        arrays[3],
        *smalls,
    )


def solution(mesh):
    in_specs = (
        P(("rows", "expert"), None),
        P(("rows", "expert"), None),
        P(),
        P(),
        P(None, "expert", None, None),
        P(None, "expert", None),
        P(None, "expert", None, None),
        P(None, "expert", None),
        P(),
        P(),
        P(),
        P(),
        P(),
    )
    out_specs = (
        P(("rows", "expert"), None),
        P(("rows", "expert"), None),
        P(None, "expert", None, None),
        P(None, "expert", None),
        P(None, "expert", None, None),
        P(None, "expert", None),
        P(),
        P(),
        P(),
        P(),
        P(),
    )
    return jax.shard_map(body, mesh=mesh, in_specs=in_specs, out_specs=out_specs, check_vma=False)
```

```python
import functools
import math

import jax
import jax.numpy as jnp
import numpy as np
from jax import lax
from jax.experimental import pallas as pl
from jax.experimental.pallas import tpu as pltpu
from jax.sharding import PartitionSpec as P

SHARPNESS = 10.0
EXACT = lax.Precision.HIGHEST
bf16 = jnp.bfloat16
f32 = jnp.float32
INNER = math.sqrt(2.0 / math.pi)
CUBE = 0.044715 * INNER
TILE = 1024
TOWER_TILE = 512
LANES = 128
EXTRA = 16


def mm(a, b):
    return jnp.dot(a, b, preferred_element_type=f32)


def mm_exact(a, b):
    return jnp.dot(a, b, precision=EXACT, preferred_element_type=f32)


def mm_nt(a, b):
    return lax.dot_general(a, b, (((1,), (1,)), ((), ())), preferred_element_type=f32)


def mm_tn(a, b):
    return lax.dot_general(a, b, (((0,), (0,)), ((), ())), preferred_element_type=f32)


def gelu_both(v):
    square = v * v
    half = 0.5 + 0.5 * jnp.tanh(v * (INNER + CUBE * square))
    value = v * half
    slope = half + value * (1.0 - half) * (2.0 * INNER + 6.0 * CUBE * square)
    return value, slope


def gelu_parts(v):
    bend = 2.0 * INNER + 8.0 * CUBE * (v * v)
    twice_share = 1.0 + jnp.tanh(v * bend)
    return v * twice_share, bend, twice_share


def gelu_slope(value, bend, twice_share):
    rise = 3.0 * bend - 4.0 * INNER
    return twice_share + value * (2.0 - twice_share) * rise


FAR = pl.BlockSpec(memory_space=pl.ANY)
NEAR = pl.BlockSpec(memory_space=pltpu.VMEM)
SCALARS = pl.BlockSpec(memory_space=pltpu.SMEM)


def kernel_params(mebibytes):
    return pltpu.CompilerParams(vmem_limit_bytes=mebibytes * 2**20)


def whole_spec(shape):
    zeros = (0,) * len(shape)
    return pl.BlockSpec(shape, lambda i: zeros)


def prepare_kernel(sizes, place_ref, length_ref, kind_ref, logit_ref, mix_ref, spread_logit_ref, spread_mix_ref, *outs):
    owned, halves, held, selectors, bits, tasks = sizes
    type_ref, across_ref, slope_ref, *value_refs = outs
    height, type_count = type_ref.shape
    experts = 2**bits
    sessions = length_ref.shape[1]
    chunk = min(256, sessions)
    position = (place_ref[0] + lax.broadcasted_iota(jnp.int32, (height, 1), 0)).astype(f32)
    earlier = lax.broadcasted_iota(jnp.int32, (chunk, chunk), 0) < lax.broadcasted_iota(jnp.int32, (chunk, chunk), 1)
    earlier = jnp.where(earlier, 1.0, 0.0).astype(bf16)
    kinds = lax.broadcasted_iota(jnp.int32, (type_count, chunk), 0)
    before = jnp.zeros((1, 1), f32)
    types = jnp.zeros((height, type_count), f32)
    across = jnp.zeros((type_count, height), f32)
    for at in range(0, sessions, chunk):
        lengths = length_ref[:, at : at + chunk].astype(f32)
        begin = before + mm(jnp.broadcast_to(lengths.astype(bf16), (EXTRA, chunk)), earlier)[0:1]
        before += jnp.sum(lengths, axis=1, keepdims=True)
        member = jnp.where((position >= begin) & (position < begin + lengths), 1.0, 0.0).astype(bf16)
        of_type = jnp.where(kinds == kind_ref[:, at : at + chunk], 1.0, 0.0).astype(bf16)
        types += mm_nt(member, of_type)
        across += mm_nt(of_type, member)
    type_ref[...] = types.astype(bf16)
    across_ref[...] = across.astype(bf16)

    rows = logit_ref.shape[0]
    place = lax.broadcasted_iota(jnp.int32, (rows, LANES), 1) % experts
    expert = (
        owned * ((place // owned) ^ place_ref[1])
        + held * ((place % halves) ^ place_ref[2])
        + (place // halves) % held
    )
    logits = mm_exact(logit_ref[...], spread_logit_ref[...])
    mixes = mm_exact(mix_ref[...], spread_mix_ref[...])
    mixes = [mixes[:, k * LANES : (k + 1) * LANES] for k in range(selectors)]
    top = functools.reduce(jnp.maximum, mixes)
    shares = [jnp.exp(mix - top) for mix in mixes]
    whole = functools.reduce(jnp.add, shares)
    shares = [share / whole for share in shares]
    value = jnp.zeros((rows, LANES), f32)
    reaches = []
    for k in range(selectors):
        factors, signed = [], []
        for bit in range(bits):
            at = (k * bits + bit) * LANES
            logit = logits[:, at : at + LANES]
            cubic = (-2.0 / SHARPNESS**3) * logit * logit * logit + (1.5 / SHARPNESS) * logit + 0.5
            step = jnp.where(logit <= -SHARPNESS / 2, 0.0, jnp.where(logit >= SHARPNESS / 2, 1.0, cubic))
            slope = (-6.0 / SHARPNESS**3) * logit * logit + 1.5 / SHARPNESS
            slope = jnp.where((logit > -SHARPNESS / 2) & (logit < SHARPNESS / 2), slope, 0.0)
            on = (expert >> bit) & 1 == 1
            factors.append(jnp.where(on, step, 1.0 - step))
            signed.append(jnp.where(on, slope, -slope))
        reaches.append(functools.reduce(jnp.multiply, factors))
        value += shares[k] * reaches[k]
        for bit in range(bits):
            others = [factors[b] for b in range(bits) if b != bit]
            slope_ref[k * bits + bit] = shares[k] * signed[bit] * functools.reduce(jnp.multiply, others)
    for k in range(selectors):
        slope_ref[selectors * bits + k] = shares[k] * (reaches[k] - value)

    value = value.astype(bf16).astype(f32)
    for layer_at, ref in enumerate(value_refs):
        table = value[layer_at * type_count : (layer_at + 1) * type_count]
        columns = [table[:, t * experts : (t + 1) * experts] for t in range(tasks)]
        if layer_at < len(value_refs) - 1:
            columns = [functools.reduce(jnp.add, columns) / tasks]
        for pair in range(ref.shape[0]):
            lanes = []
            for half in range(halves):
                at = pair * halves + half
                lanes += [jnp.broadcast_to(c[:, at : at + 1], (type_count, LANES)) for c in columns]
            ref[pair] = jnp.concatenate(lanes, axis=1).astype(bf16)


def prepare_call(place, lengths, session_type, logits, mixing, height, sizes):
    owned, halves, held, selectors, bits, tasks = sizes
    layers, type_count = logits.shape[:2]
    experts = 2**bits
    rows = layers * type_count
    lane = np.arange(LANES)
    source = np.arange(tasks * selectors * bits)
    task, number = source // (selectors * bits), source % (selectors * bits)
    mine = (lane[None, :] // experts == task[:, None])[:, None, :]
    spread_logit = mine & (number[:, None, None] == np.arange(selectors * bits)[None, :, None])
    source = np.arange(tasks * selectors)
    mine = (lane[None, :] // experts == (source // selectors)[:, None])[:, None, :]
    spread_mix = mine & ((source % selectors)[:, None, None] == np.arange(selectors)[None, :, None])
    spread_logit = spread_logit.reshape(spread_logit.shape[0], -1).astype(np.float32)
    spread_mix = spread_mix.reshape(spread_mix.shape[0], -1).astype(np.float32)
    outs = [
        jax.ShapeDtypeStruct((height, type_count), bf16),
        jax.ShapeDtypeStruct((type_count, height), bf16),
        jax.ShapeDtypeStruct((selectors * (bits + 1), rows, LANES), f32),
    ]
    for layer_at in range(layers):
        each = tasks if layer_at == layers - 1 else 1
        outs.append(jax.ShapeDtypeStruct((experts // halves, type_count, halves * each * LANES), bf16))
    return pl.pallas_call(
        functools.partial(prepare_kernel, sizes),
        out_shape=outs,
        in_specs=[SCALARS] + [NEAR] * 6,
        out_specs=[NEAR] * len(outs),
        compiler_params=kernel_params(58),
        cost_estimate=pl.CostEstimate(flops=2 * height * lengths.size * 64, bytes_accessed=2**21, transcendentals=2**16),
    )(
        place,
        lengths.reshape(1, -1),
        session_type.reshape(1, -1),
        logits.reshape(rows, -1),
        mixing.reshape(rows, -1),
        spread_logit,
        spread_mix,
    )


def bias_rows(weights, width):
    rows = weights[2 * width : 2 * width + EXTRA].astype(f32)
    return rows[0:1] + rows[1:2], rows[2:3] + rows[3:4]


def twice(a):
    return jnp.concatenate([a, a], axis=1)


def tiles(height, most):
    tile = min(most, height)
    return [pl.ds(at, tile) for at in range(0, height, tile)]


def joined(parts, axis):
    return parts[0] if len(parts) == 1 else jnp.concatenate(parts, axis=axis)


def gates_of(types, value_ref, count):
    gates = mm(types, value_ref[...]).astype(bf16)
    return [gates[:, at * LANES : (at + 1) * LANES] for at in range(count)]


def forward_step(weights, value_ref, x_low, type_ref, total_ref, biases, keep, keep_gate=None, keep_result=None):
    height, width = x_low.shape
    kinds = total_ref.shape[0]
    bias_in, bias_out = zip(*(bias_rows(w, width) for w in weights))
    second = joined([w[width : 2 * width] for w in weights], 0)
    for rows in tiles(height, TILE):
        gates = gates_of(type_ref[rows], value_ref, len(weights) * kinds)
        if keep_gate is not None:
            for at, gate in enumerate(gates):
                keep_gate(at, rows, gate)
        scaled = [[] for _ in range(kinds)]
        for i, w in enumerate(weights):
            before = mm(x_low[rows], w[0:width]) + bias_in[i]
            hidden, bend, twice_share = gelu_parts(before)
            hidden = hidden.astype(bf16)
            keep(i, rows, hidden, gelu_slope(hidden, bend.astype(bf16), twice_share.astype(bf16)))
            if keep_result is not None:
                result = mm(hidden, w[width : 2 * width]).astype(bf16)
                keep_result(i, rows, result)
            for t in range(kinds):
                scaled[t].append(twice(gates[i * kinds + t]) * (hidden if keep_result is None else result))
        for t in range(kinds):
            if keep_result is None:
                total_ref[t, rows] += mm(joined(scaled[t], 1), second)
            else:
                total_ref[t, rows] += functools.reduce(jnp.add, scaled[t]).astype(f32)
    for i in range(len(weights)):
        for t in range(kinds):
            at = (i * kinds + t) * LANES
            biases[t] += twice(value_ref[:, at : at + LANES].astype(f32)) * bias_out[i]


def forward_end(type_ref, total_ref, biases):
    for t in range(total_ref.shape[0]):
        high = biases[t].astype(bf16)
        rest = (biases[t] - high.astype(f32)).astype(bf16)
        for rows in tiles(total_ref.shape[1], TILE):
            total_ref[t, rows] += mm(twice(type_ref[rows]), jnp.concatenate([high, rest], axis=0))


def backward_start(x_low, type_across, low, across, share):
    width = x_low.shape[1]
    across[0:width] = x_low[...].T
    ones = lax.broadcasted_iota(jnp.int32, (EXTRA, x_low.shape[0]), 0) == 0
    across[width:] = jnp.where(ones, 1.0, 0.0).astype(bf16)
    for t in range(low.shape[0]):
        share[t] = mm(type_across[...], low[t])


def backward_step(weights, value_ref, hiddens, slopes, outs, pair, experts, type_ref, type_across, low, stream_ref, across, share, table, scratch, kept_gates=None, results=None, dots=None, gate_lanes=None):
    before_grads, result_grads = scratch
    kinds, height, width = low.shape
    count = len(weights)
    first = joined([w[0:width] for w in weights], 1)
    for rows in tiles(height, TILE):
        if kept_gates is None:
            gates = gates_of(type_ref[rows], value_ref, count * kinds)
        else:
            gates = [kept_gates[at, rows] for at in range(count * kinds)]
        gates = [twice(gate) for gate in gates]
        befores = []
        for i, w in enumerate(weights):
            hidden, slope = hiddens[i][rows], slopes[i][rows]
            second = w[width : 2 * width]
            result_grad = gates[i * kinds] * low[0, rows]
            for t in range(1, kinds):
                result_grad += gates[i * kinds + t] * low[t, rows]
            hidden_grad = mm_nt(result_grad, second).astype(bf16)
            for t in range(kinds):
                product = hidden * hidden_grad if results is None else results[i][rows] * low[t, rows]
                product = functools.reduce(
                    jnp.add, [product[:, lane : lane + LANES] for lane in range(0, width, LANES)]
                )
                found = jnp.sum(product.astype(f32), axis=1, keepdims=True)
                lanes = lax.broadcasted_iota(jnp.int32, (1, LANES), 1)
                place = pair * count + i
                chosen = lanes % experts == place if kinds == 1 else lanes == t * experts + place
                dots[rows] = jnp.where(chosen, found, dots[rows])
            before = slope * hidden_grad
            before_grads[i, rows] = before
            result_grads[i, rows] = result_grad
            befores.append(before)
        stream_ref[rows] += mm_nt(joined(befores, 1), first)
    lanes = lax.broadcasted_iota(jnp.int32, (type_ref.shape[1], LANES), 1)
    for i, w in enumerate(weights):
        _, bias_out = bias_rows(w, width)
        first_grad = 0.5 * mm(across[...], before_grads[i])
        outs[i][0:width] = first_grad[0:width].astype(bf16)
        outs[i][width : 2 * width] = mm_tn(hiddens[i][...], result_grads[i]).astype(bf16)
        out_bias = jnp.zeros((1, width), f32)
        place = pair * count + i
        for t in range(kinds):
            at = (i * kinds + t) * LANES
            gate = value_ref[:, at : at + LANES].astype(f32)
            out_bias += jnp.sum(twice(gate) * share[t], axis=0, keepdims=True)
            bias_part = jnp.sum(share[t] * bias_out, axis=1, keepdims=True)
            if kinds == 1:
                table[...] = jnp.where(lanes % experts == place, 0.5 * bias_part, table[...])
                gate_lanes[...] = jnp.where(lanes % experts == place, gate, gate_lanes[...])
            else:
                table[...] = jnp.where(lanes == t * experts + place, bias_part, table[...])
        tail = jnp.concatenate([first_grad[width : width + 1], out_bias, jnp.zeros((EXTRA - 2, width), f32)])
        outs[i][2 * width : 2 * width + EXTRA] = tail.astype(bf16)


def by_type(type_across, dots):
    high = dots[...].astype(bf16)
    rest = (dots[...] - high.astype(f32)).astype(bf16)
    return mm(type_across[...], high) + mm(type_across[...], rest)


def through_gates(table, gate_slope_ref, experts, tasks):
    quantities, type_count = gate_slope_ref.shape[:2]
    lanes = lax.broadcasted_iota(jnp.int32, (type_count, LANES), 1)
    small = jnp.zeros((type_count, LANES), f32)
    for q in range(quantities):
        product = gate_slope_ref[q] * table[...]
        for t in range(tasks):
            part = jnp.sum(jnp.where(lanes // experts == t, product, 0.0), axis=1, keepdims=True)
            small = jnp.where(lanes == t * quantities + q, part, small)
    half = type_count // 2
    return jnp.concatenate([small[:half], small[half:]], axis=1).astype(bf16)


def store_copies(ready, pair, held, out_refs, sems):
    group, unit = pair // held, lax.rem(pair, held)
    rows = pl.ds(pl.multiple_of(unit * ready.shape[1], EXTRA), ready.shape[1])
    copies = [(None, pltpu.make_async_copy(ready.at[0], out_refs[0].at[group, rows], sems.at[0]))]
    for at, ref in enumerate(out_refs[1:]):
        copies.append((group == at, pltpu.make_async_copy(ready.at[1], ref.at[rows], sems.at[1])))
    return copies


def end_copies(ends, out_refs, sems):
    rows = out_refs[0].shape[1]
    last = pl.ds(rows - ends.shape[1], ends.shape[1])
    groups = out_refs[0].shape[0]
    copies = [pltpu.make_async_copy(ends.at[0], out_refs[0].at[at, last], sems.at[0, at]) for at in range(groups)]
    copies += [
        pltpu.make_async_copy(ends.at[1], ref.at[last], sems.at[1, at]) for at, ref in enumerate(out_refs[1:])
    ]
    return [(None, copy) for copy in copies]


def for_each(copies, act):
    for condition, copy in copies:
        if condition is None:
            act(copy)
        else:
            pl.when(condition)(functools.partial(act, copy))


def start(copy):
    copy.start()


def wait(copy):
    copy.wait()


def fetch_weights(places, buffer, sems, each):
    step = pl.program_id(0)
    for of in range(len(places) // each):

        @pl.when(step == max(of - 1, 0))
        def _(of=of):
            for i, (ref, at) in enumerate(places[of * each : (of + 1) * each]):
                pltpu.make_async_copy(ref.at[at], buffer.at[of % 2, i], sems.at[of % 2, i]).start()

    slot = lax.rem(step, 2)
    for i in range(each):
        ref, at = places[0]
        pltpu.make_async_copy(ref.at[at], buffer.at[slot, i], sems.at[slot, i]).wait()
    return [buffer.at[slot, i] for i in range(each)]


def forward_kernel(places, pieces, each, first, *refs):
    refs = list(refs)
    take = lambda count: [refs.pop(0) for _ in range(count)]
    x_ref, type_ref, value_ref = take(3)
    if not first:
        total_ref, _, _ = take(3)
    weight_refs = take(pieces)
    out_ref, hidden_ref, slope_ref, x_low, biases, buffer, sems = take(7)
    step = pl.program_id(0)
    weights = fetch_weights([(weight_refs[piece], at) for piece, at in places], buffer, sems, each)

    @pl.when(step == 0)
    def _():
        x_low[...] = x_ref[...].astype(bf16)
        biases[...] = jnp.zeros_like(biases)
        out_ref[0] = x_ref[...] if first else total_ref[0]

    def keep(i, rows, hidden, slope):
        hidden_ref[0, i, rows] = hidden
        slope_ref[0, i, rows] = slope

    forward_step(weights, value_ref.at[0], x_low, type_ref, out_ref, biases, keep)

    @pl.when(step == pl.num_programs(0) - 1)
    def _():
        forward_end(type_ref, out_ref, biases)


def forward_call(x, types, values, total, stash, pieces, places, base):
    height, width = x.shape
    pairs, type_count, lanes = values.shape
    each = lanes // LANES
    operands = [x, types, values]
    specs = [whole_spec(x.shape), whole_spec(types.shape)]
    specs.append(pl.BlockSpec((1, type_count, lanes), lambda i: (base + i, 0, 0)))
    aliases = {}
    if total is not None:
        operands += [total, *stash]
        specs += [whole_spec(total.shape), FAR, FAR]
        aliases = {4: 1, 5: 2}
    summed = jax.ShapeDtypeStruct((1, height, width), f32)
    kept = jax.ShapeDtypeStruct((pairs, each, height, width), bf16)
    kept_spec = pl.BlockSpec((1, each, height, width), lambda i: (base + i, 0, 0, 0))
    number = len(places)
    results = pl.pallas_call(
        functools.partial(forward_kernel, places, len(pieces), each, total is None),
        grid=(number // each,),
        out_shape=[summed, kept, kept],
        in_specs=specs + [FAR] * len(pieces),
        out_specs=[whole_spec(summed.shape), kept_spec, kept_spec],
        scratch_shapes=[
            pltpu.VMEM((height, width), bf16),
            pltpu.VMEM((1, type_count, width), f32),
            pltpu.VMEM((2, each, *pieces[0].shape[1:]), bf16),
            pltpu.SemaphoreType.DMA((2, each)),
        ],
        input_output_aliases=aliases,
        compiler_params=kernel_params(58),
        cost_estimate=pl.CostEstimate(
            flops=4 * number * height * width * width,
            bytes_accessed=number * (4 * width * width + 4 * height * width) + 8 * height * width,
            transcendentals=number * height * width,
        ),
    )(*operands, *pieces)
    return results[0], results[1:]


def middle_kernel(places, pieces, groups, halves, held, *refs):
    refs = list(refs)
    take = lambda count: [refs.pop(0) for _ in range(count)]
    place_ref, x_ref, type_ref, across_types_ref, value_ref, gate_slope_ref, pred_grad_ref = take(7)
    tower_in_ref, tower_bias_ref, tower_out_ref = take(3)
    weight_refs = take(pieces)
    pred_ref, stream_ref = take(2)
    out_refs = take(1 + (groups - 1) * (halves - 1))
    left_refs = take(7)
    x_low, weights, hidden_all, slope_all, result_all, gates_all, total, biases, low, across, share, table = take(12)
    before_grads, result_grads, dots, cotangents, ready, ends, in_grad, bias_grad, out_grad, load_sem, store_sem, end_sem, left_sem = take(13)
    height, width = x_ref.shape
    pairs = value_ref.shape[0]
    experts = pairs * halves
    tasks = total.shape[0]

    def load(pair, i, ref, at):
        return pltpu.make_async_copy(ref.at[at], weights.at[pair, i], load_sem.at[pair, i])

    for j, (piece, at) in enumerate(places):
        load(j // halves, j % halves, weight_refs[piece], at).start()
    x_low[...] = x_ref[...].astype(bf16)
    biases[...] = jnp.zeros_like(biases)
    for t in range(tasks):
        total[t] = x_ref[...]

    def forward_pair(pair, carry):
        for i in range(halves):
            load(pair, i, weight_refs[0], 0).wait()

        def keep(i, rows, hidden, slope):
            hidden_all[pair, i, rows] = hidden
            slope_all[pair, i, rows] = slope

        def keep_gate(at, rows, gate):
            gates_all[pair, at, rows] = gate

        def keep_result(i, rows, result):
            result_all[pair, i, rows] = result

        forward_step(
            [weights.at[pair, i] for i in range(halves)],
            value_ref.at[pair],
            x_low,
            type_ref,
            total,
            biases,
            keep,
            keep_gate,
            keep_result,
        )
        return carry

    lax.fori_loop(0, pairs, forward_pair, 0)
    forward_end(type_ref, total, biases)

    def left(at, source):
        return pltpu.make_async_copy(source, left_refs[at], left_sem.at[at])

    own = [kept.at[0:held] for kept in (hidden_all, slope_all, result_all)]
    for at, source in enumerate(own):
        left(at, source).start()

    cotangents[...] = jnp.concatenate(
        [pred_grad_ref[...], jnp.zeros((cotangents.shape[1] - tasks, height), f32)]
    ).T
    in_grad[...] = jnp.zeros_like(in_grad)
    bias_grad[...] = jnp.zeros_like(bias_grad)
    out_grad[...] = jnp.zeros_like(out_grad)
    for rows in tiles(height, TOWER_TILE):
        summed = None
        predicted = []
        for t in range(tasks):
            closing_low = total[t, rows].astype(bf16)
            act, slope = gelu_both(mm(closing_low, tower_in_ref[t]) + tower_bias_ref[t : t + 1])
            vector = tower_out_ref[t : t + 1]
            predicted.append(jnp.sum(act * vector, axis=1, keepdims=True))
            cotangent = cotangents[rows, t : t + 1]
            out_grad[t : t + 1] += jnp.sum(act * cotangent, axis=0, keepdims=True)
            before_grad = (slope * (cotangent * vector)).astype(bf16)
            bias_grad[t : t + 1] += jnp.sum(before_grad.astype(f32), axis=0, keepdims=True)
            in_grad[t] += mm_tn(closing_low, before_grad)
            closing_grad = mm_nt(before_grad, tower_in_ref[t])
            low[t, rows] = closing_grad.astype(bf16)
            summed = closing_grad if summed is None else summed + closing_grad
        stream_ref[rows] = summed
        blank = jnp.zeros((predicted[0].shape[0], cotangents.shape[1] - tasks), f32)
        pred_ref[:, rows] = jnp.concatenate([*predicted, blank], axis=1).T[0:tasks]
    narrow = in_grad.shape[2]
    tall = width * narrow // width
    begin = type_ref.shape[1] // 2 + EXTRA
    for t in range(tasks):
        wide = jnp.concatenate([in_grad[t, :tall], in_grad[t, tall:]], axis=1).astype(bf16)
        if halves == 2:
            ends[place_ref[2] ^ t, begin:] = wide
        else:
            ends[0, begin + t * tall : begin + (t + 1) * tall] = wide
    vectors = [jnp.concatenate([ref[0:1], ref[1:2]], axis=1) for ref in (bias_grad, out_grad)]
    vectors = jnp.concatenate([*vectors, jnp.zeros((EXTRA - 2, width), f32)]).astype(bf16)
    for half in range(halves):
        ends[half, begin - EXTRA : begin] = vectors

    left(3, low).start()
    backward_start(x_low, across_types_ref, low, across, share)
    left(4, across).start()
    left(5, share).start()
    table[...] = jnp.zeros_like(table)
    dots[...] = jnp.zeros_like(dots)

    def stores(pair):
        return store_copies(ready.at[pair], pair - held, held, out_refs, store_sem.at[pair])

    def backward_pair(pair, carry):
        backward_step(
            [weights.at[pair, i] for i in range(halves)],
            value_ref.at[pair],
            [hidden_all.at[pair, i] for i in range(halves)],
            [slope_all.at[pair, i] for i in range(halves)],
            [ready.at[pair, i] for i in range(halves)],
            pair,
            experts,
            type_ref,
            across_types_ref,
            low,
            stream_ref,
            across,
            share,
            table,
            (before_grads, result_grads),
            gates_all.at[pair],
            [result_all.at[pair, i] for i in range(halves)],
            dots,
        )
        for_each(stores(pair), start)
        return carry

    lax.fori_loop(held, pairs, backward_pair, 0)
    table[...] += by_type(across_types_ref, dots)
    small = through_gates(table, gate_slope_ref, experts, tasks)
    for half in range(halves):
        ends[half, 0 : small.shape[0]] = small
    left(6, ends).start()
    for_each(end_copies(ends, out_refs, end_sem), start)

    def drain(pair, carry):
        for_each(stores(pair), wait)
        return carry

    lax.fori_loop(held, pairs, drain, 0)
    for_each(end_copies(ends, out_refs, end_sem), wait)
    for at, source in enumerate([*own, low, across, share, ends]):
        left(at, source).wait()


def middle_call(place, x, types, across_types, values, gate_slopes, tower, pieces, places, groups, halves, held):
    height, width = x.shape
    pairs, type_count, lanes = values.shape
    pred_grad, tower_in, tower_bias, tower_out = tower
    tasks = tower_in.shape[0]
    stride = 2 * width + EXTRA
    experts = pairs * halves
    outs = [jax.ShapeDtypeStruct(shape, f32) for shape in (pred_grad.shape, (height, width))]
    near = len(outs)
    end_rows = type_count // 2 + EXTRA + tower_in.size // width // halves
    rows = held * stride + end_rows
    outs.append(jax.ShapeDtypeStruct((groups - 1, rows, width), bf16))
    outs += [jax.ShapeDtypeStruct((rows, width), bf16)] * ((groups - 1) * (halves - 1))
    outs += [jax.ShapeDtypeStruct((held, halves, height, width), bf16)] * 3
    outs.append(jax.ShapeDtypeStruct((tasks, height, width), bf16))
    outs.append(jax.ShapeDtypeStruct((width + EXTRA, height), bf16))
    outs.append(jax.ShapeDtypeStruct((tasks, type_count, width), f32))
    outs.append(jax.ShapeDtypeStruct((halves, end_rows, width), bf16))
    layer_at = gate_slopes.shape[1] // type_count - 1
    slope_spec = pl.BlockSpec((gate_slopes.shape[0], type_count, LANES), lambda i: (0, layer_at, 0))
    kept = pltpu.VMEM((pairs, halves, height, width), bf16)
    operands = [x, types, across_types, values, gate_slopes, *tower]
    specs = [whole_spec(a.shape) for a in operands]
    specs[4] = slope_spec
    return pl.pallas_call(
        functools.partial(middle_kernel, places, len(pieces), groups, halves, held),
        grid=(1,),
        out_shape=outs,
        in_specs=[SCALARS] + specs + [FAR] * len(pieces),
        out_specs=[whole_spec(out.shape) for out in outs[:near]] + [FAR] * (len(outs) - near),
        scratch_shapes=[
            pltpu.VMEM((height, width), bf16),
            pltpu.VMEM((pairs, halves, stride, width), bf16),
            kept,
            kept,
            kept,
            pltpu.VMEM((pairs, halves * tasks, height, LANES), bf16),
            pltpu.VMEM((tasks, height, width), f32),
            pltpu.VMEM((tasks, type_count, width), f32),
            pltpu.VMEM((tasks, height, width), bf16),
            pltpu.VMEM((width + EXTRA, height), bf16),
            pltpu.VMEM((tasks, type_count, width), f32),
            pltpu.VMEM((type_count, LANES), f32),
            pltpu.VMEM((halves, height, width), bf16),
            pltpu.VMEM((halves, height, width), bf16),
            pltpu.VMEM((height, LANES), f32),
            pltpu.VMEM((height, LANES), f32),
            pltpu.VMEM((pairs, halves, stride, width), bf16),
            pltpu.VMEM((halves, end_rows, width), bf16),
            pltpu.VMEM(tower_in.shape, f32),
            pltpu.VMEM(tower_bias.shape, f32),
            pltpu.VMEM(tower_out.shape, f32),
            pltpu.SemaphoreType.DMA((pairs, halves)),
            pltpu.SemaphoreType.DMA((pairs, halves)),
            pltpu.SemaphoreType.DMA((halves, groups)),
            pltpu.SemaphoreType.DMA((7,)),
        ],
        compiler_params=kernel_params(58),
        cost_estimate=pl.CostEstimate(
            flops=14 * experts * height * width * width,
            bytes_accessed=experts * 8 * width * width + 16 * height * width,
            transcendentals=experts * height * width,
        ),
    )(place, *operands, *pieces)


def backward_kernel(places, pieces, each, held, tasks, *refs):
    refs = list(refs)
    take = lambda count: [refs.pop(0) for _ in range(count)]
    x_ref, type_ref, across_types_ref, stream_ref, gate_slope_ref, value_ref, hidden_ref, slope_ref = take(8)
    last_value_ref, last_low_ref, last_across_ref, last_share_ref, last_end_ref = take(5)
    last_refs, last_weight_refs = take(3), take(each)
    weight_refs = take(pieces)
    stream_out_ref = take(1)[0]
    groups = len(places) // each // held
    out_refs = take(1 + groups * (each - 1))
    last_out_refs = take(each)
    x_low, across, low, share, table, before_grads, result_grads, gate_lanes, buffer, ready, ends = take(11)
    x_wide, gate_slopes, last_table, dots, kept, last_weights, last_ready = take(7)
    sems, store_sem, end_sem, last_sem, last_store_sem, late_sem = take(6)
    step = pl.program_id(0)
    slot = lax.rem(step, 2)
    experts = len(places)
    types = type_ref.shape[1]
    stride = buffer.shape[2]
    scratch = (before_grads, result_grads)
    weights = fetch_weights([(weight_refs[piece], at) for piece, at in places], buffer, sems, each)

    late = [
        (None, pltpu.make_async_copy(source, target, late_sem.at[at]))
        for at, (source, target) in enumerate(((x_ref, x_wide), (gate_slope_ref, gate_slopes)))
    ]

    def last_loads(unit):
        copies = [
            pltpu.make_async_copy(last_refs[which].at[unit], kept.at[which, unit], last_sem.at[unit, which])
            for which in range(3)
        ]
        for half in range(each):
            source, sem = last_weight_refs[half].at[unit], last_sem.at[unit, 3 + half]
            copies.append(pltpu.make_async_copy(source, last_weights.at[unit, half], sem))
        return [(None, copy) for copy in copies]

    def last_stores():
        copies = []
        for half, ref in enumerate(last_out_refs):
            for unit in range(held):
                rows = pl.ds(unit * stride, stride)
                copies.append(
                    pltpu.make_async_copy(last_ready.at[unit, half], ref.at[rows], last_store_sem.at[half, unit])
                )
            rows = pl.ds(held * stride, last_end_ref.shape[1])
            copies.append(pltpu.make_async_copy(last_end_ref.at[half], ref.at[rows], last_store_sem.at[half, held]))
        return [(None, copy) for copy in copies]

    @pl.when(step == 0)
    def _():
        for unit in range(held):
            for_each(last_loads(unit), start)
        for_each(late, start)
        stream_out_ref[...] = stream_ref[...]
        last_table[...] = jnp.zeros_like(last_table)
        dots[...] = jnp.zeros_like(dots)

        def last_pair(unit, carry):
            for_each(last_loads(unit), wait)
            backward_step(
                [last_weights.at[unit, i] for i in range(each)],
                last_value_ref.at[unit],
                [kept.at[0, unit, i] for i in range(each)],
                [kept.at[1, unit, i] for i in range(each)],
                [last_ready.at[unit, i] for i in range(each)],
                unit,
                experts,
                type_ref,
                across_types_ref,
                last_low_ref,
                stream_out_ref,
                last_across_ref,
                last_share_ref,
                last_table,
                scratch,
                None,
                [kept.at[2, unit, i] for i in range(each)],
                dots,
            )
            return carry

        lax.fori_loop(0, held, last_pair, 0)
        for_each(last_stores(), start)
        last_table[...] += by_type(across_types_ref, dots)
        dots[...] = jnp.zeros_like(dots)
        for_each(late[:1], wait)
        x_low[...] = x_wide[...].astype(bf16)
        low[0] = stream_out_ref[...].astype(bf16)
        table[...] = jnp.zeros_like(table)
        gate_lanes[...] = jnp.zeros_like(gate_lanes)
        backward_start(x_low, across_types_ref, low, across, share)

    def stores(pair):
        at = lax.rem(pair, 2)
        return store_copies(ready.at[at], pair, held, out_refs, store_sem.at[at])

    @pl.when(step >= 2)
    def _():
        for_each(stores(step - 2), wait)

    backward_step(
        weights,
        value_ref.at[0],
        [hidden_ref.at[0, i] for i in range(each)],
        [slope_ref.at[0, i] for i in range(each)],
        [ready.at[slot, i] for i in range(each)],
        step,
        experts,
        type_ref,
        across_types_ref,
        low,
        stream_out_ref,
        across,
        share,
        table,
        scratch,
        None,
        None,
        dots,
        gate_lanes,
    )

    for_each(stores(step), start)

    @pl.when(step == pl.num_programs(0) - 1)
    def _():
        for_each(late[1:], wait)
        gate = gate_lanes[...]
        found = 0.5 * by_type(across_types_ref, dots) / jnp.where(gate > 0.0, gate, 1.0)
        table[...] += jnp.where(gate > 0.0, found, 0.0)
        both = ((table, 0), (last_table, types))
        small = [through_gates(part, gate_slopes.at[:, pl.ds(at, types)], experts, tasks) for part, at in both]
        for half in range(each):
            ends[half] = jnp.concatenate(small)
        for_each(end_copies(ends, out_refs, end_sem), start)
        for_each(stores(step - 1), wait)
        for_each(stores(step), wait)
        for_each(end_copies(ends, out_refs, end_sem), wait)
        for_each(last_stores(), wait)


def backward_call(x, types, across_types, stream, gate_slopes, values, stash, pieces, places, held, tasks, last):
    height, width = x.shape
    pairs, type_count, lanes = values.shape
    each = lanes // LANES
    groups = pairs // held
    stride = 2 * width + EXTRA
    last_values, last_weights, *last_kept, last_low, last_across, last_share, last_ends = last
    operands = [x, types, across_types, stream, gate_slopes, values, *stash]
    specs = [FAR, *[whole_spec(a.shape) for a in operands[1:4]], FAR]
    specs.append(pl.BlockSpec((1, type_count, lanes), lambda i: (i, 0, 0)))
    specs += [pl.BlockSpec((1, each, height, width), lambda i: (i, 0, 0, 0))] * 2
    near = [last_low, last_across, last_share, last_ends]
    operands += [last_values, *near, *last_kept, *last_weights]
    specs.append(pl.BlockSpec((held, *last_values.shape[1:]), lambda i: (0, 0, 0)))
    specs += [whole_spec(a.shape) for a in near]
    specs += [FAR] * (len(last_kept) + each)
    rows = held * stride + type_count
    mine = jax.ShapeDtypeStruct((groups, rows, width), bf16)
    others = [jax.ShapeDtypeStruct((rows, width), bf16)] * (groups * (each - 1))
    others += [jax.ShapeDtypeStruct((held * stride + last_ends.shape[1], width), bf16)] * each
    number = pairs * each
    return pl.pallas_call(
        functools.partial(backward_kernel, places, len(pieces), each, held, tasks),
        grid=(pairs,),
        out_shape=[jax.ShapeDtypeStruct(stream.shape, f32), mine, *others],
        in_specs=specs + [FAR] * len(pieces),
        out_specs=[whole_spec(stream.shape)] + [FAR] * (1 + len(others)),
        scratch_shapes=[
            pltpu.VMEM((height, width), bf16),
            pltpu.VMEM((width + EXTRA, height), bf16),
            pltpu.VMEM((1, height, width), bf16),
            pltpu.VMEM((1, type_count, width), f32),
            pltpu.VMEM((type_count, LANES), f32),
            pltpu.VMEM((each, height, width), bf16),
            pltpu.VMEM((each, height, width), bf16),
            pltpu.VMEM((type_count, LANES), f32),
            pltpu.VMEM((2, each, stride, width), bf16),
            pltpu.VMEM((2, each, stride, width), bf16),
            pltpu.VMEM((each, type_count, width), bf16),
            pltpu.VMEM((height, width), f32),
            pltpu.VMEM(gate_slopes.shape, f32),
            pltpu.VMEM((type_count, LANES), f32),
            pltpu.VMEM((height, LANES), f32),
            pltpu.VMEM((3, held, each, height, width), bf16),
            pltpu.VMEM((held, each, stride, width), bf16),
            pltpu.VMEM((held, each, stride, width), bf16),
            pltpu.SemaphoreType.DMA((2, each)),
            pltpu.SemaphoreType.DMA((2, each)),
            pltpu.SemaphoreType.DMA((each, groups)),
            pltpu.SemaphoreType.DMA((held, 3 + each)),
            pltpu.SemaphoreType.DMA((each, held + 1)),
            pltpu.SemaphoreType.DMA((2,)),
        ],
        compiler_params=kernel_params(58),
        cost_estimate=pl.CostEstimate(
            flops=10 * number * height * width * width,
            bytes_accessed=number * (8 * width * width + 4 * height * width) + 16 * height * width,
            transcendentals=0,
        ),
    )(*operands, *pieces)


def finish_kernel(names, held, rows, first, *refs):
    place_ref, *refs = refs
    sources, refs = refs[: len(names)], refs[len(names) :]
    in_ref, out_ref, in_bias_out_ref, out_bias_out_ref, ready, sems = refs[-6:]
    in_bias_out_ref[...] = jnp.zeros_like(in_bias_out_ref) if first else refs[2][...]
    out_bias_out_ref[...] = jnp.zeros_like(out_bias_out_ref) if first else refs[3][...]
    copies = []
    for at, ((layer_at, half), source) in enumerate(zip(names, sources)):
        for unit in range(held):
            base = unit * (2 * rows + EXTRA)
            where = held * (place_ref[2] ^ half) + unit
            for which, ref in enumerate((in_ref, out_ref)):
                begin = base + which * rows
                ready[at, unit, which] = source[begin : begin + rows].astype(f32)
                copy = pltpu.make_async_copy(
                    ready.at[at, unit, which], ref.at[layer_at, where], sems.at[at, unit, which]
                )
                copy.start()
                copies.append(copy)
            tail = source[base + 2 * rows : base + 2 * rows + EXTRA].astype(f32)
            in_bias_out_ref[layer_at, pl.ds(where, 1)] = tail[0:1]
            out_bias_out_ref[layer_at, pl.ds(where, 1)] = tail[1:2]
    for copy in copies:
        copy.wait()


def finish_call(place, named, held_arrays, held, shape):
    rows, width = shape[2:]
    names, sources = tuple(named), list(named.values())
    outs = [jax.ShapeDtypeStruct(shape, f32)] * 2
    outs += [jax.ShapeDtypeStruct((*shape[:2], width), f32)] * 2
    first = held_arrays is None
    number = len(names)
    return pl.pallas_call(
        functools.partial(finish_kernel, names, held, rows, first),
        out_shape=outs,
        in_specs=[SCALARS] + [NEAR] * number + ([] if first else [FAR, FAR, NEAR, NEAR]),
        out_specs=[FAR, FAR, NEAR, NEAR],
        scratch_shapes=[
            pltpu.VMEM((number, held, 2, rows, width), f32),
            pltpu.SemaphoreType.DMA((number, held, 2)),
        ],
        input_output_aliases={} if first else {1 + number: 0, 2 + number: 1},
        compiler_params=kernel_params(12),
        cost_estimate=pl.CostEstimate(flops=0, bytes_accessed=number * held * 12 * rows * width, transcendentals=0),
    )(place, *sources, *([] if first else held_arrays))


def flip(array, axis, bits):
    size = lax.axis_size(axis)
    return lax.ppermute(array, axis, [(i, i ^ bits) for i in range(size)])


def add_low(*arrays):
    level = [a.astype(f32) for a in arrays]
    while len(level) > 1:
        level = [level[i] + level[i + 1] for i in range(0, len(level), 2)]
    return level[0].astype(bf16)


def after(arrays, others):
    return lax.optimization_barrier((arrays, others))[0]


def near(mine, groups):
    if groups == 4 and mine.shape[0] == 2:
        return {1: [flip(mine, "expert", 1)], 2: [flip(mine, "expert", 2)]}
    return {ro: [flip(mine, "expert", ro)] for ro in range(1, groups)}


def relay(arrived, groups, held):
    if groups == 4 and held == 2:
        return {3: [flip(arrived[1][0][:1], "expert", 2), flip(arrived[2][0][1:], "expert", 1)]}
    return {}


def crossed(parts, halves):
    return [] if halves == 1 else [flip(part, "rows", 1) for part in parts]


def body(
    rows_in,
    pred_grad,
    lengths,
    session_type,
    expert_in,
    expert_in_bias,
    expert_out,
    expert_out_bias,
    selector_logits,
    selector_mix,
    tower_in,
    tower_bias,
    tower_out,
):
    height, width = rows_in.shape
    layers, owned = expert_in.shape[:2]
    type_count, tasks = selector_logits.shape[1:3]
    selectors, bits = selector_logits.shape[3:]
    groups = lax.axis_size("expert")
    halves = 2 if owned % 2 == 0 else 1
    held = owned // halves
    stride = 2 * width + EXTRA
    me, row_at = lax.axis_index("expert"), lax.axis_index("rows")
    core = row_at % 2 if halves == 2 else jnp.int32(0)
    place = jnp.stack([(row_at * groups + me) * height, me, core]).astype(jnp.int32)

    def rows_of(layer_at, first):
        cut = lambda a: lax.dynamic_slice(a, (layer_at, first) + (0,) * (a.ndim - 2), (1, held) + a.shape[2:])[0]
        half = lambda a: a * jnp.asarray(0.5, a.dtype)
        tail = []
        for bias in (half(cut(expert_in_bias)), cut(expert_out_bias)):
            high = bias.astype(bf16)
            tail += [high, (bias - high.astype(f32)).astype(bf16)]
        tail = jnp.pad(jnp.stack(tail, axis=1), ((0, 0), (0, EXTRA - len(tail)), (0, 0)))
        return jnp.concatenate([half(cut(expert_in)), cut(expert_out), tail], axis=1)

    first = rows_of(0, held * core)
    asked = near(first, groups)
    sizes = (owned, halves, held, selectors, bits, tasks)
    types, across_types, gate_slopes, *values = prepare_call(
        place, lengths, session_type, selector_logits, selector_mix, height, sizes
    )

    later = after((expert_in, expert_in_bias, expert_out, expert_out_bias), types)
    expert_in, expert_in_bias, expert_out, expert_out_bias = later
    own = [[rows_of(layer_at, held * (core ^ half)) for half in range(halves)] for layer_at in range(layers)]
    own[0][0] = first

    def parts_of(got, across):
        pieces, places = [], {}
        for ro in got:
            spots = []
            for parts in (got[ro], across[ro]):
                here = []
                for part in parts:
                    here += [(len(pieces), at) for at in range(part.shape[0])]
                    pieces.append(part)
                if here:
                    spots.append(here)
            places[ro] = [[spots[half][unit] for half in range(halves)] for unit in range(held)]
        return pieces, places

    def pair_order(places, units):
        return tuple(spot for ro in sorted(places) for unit in units for spot in places[ro][unit])

    streams, stashes, weights = [rows_in], [], []
    for layer_at in range(layers):
        last = layer_at == layers - 1
        got = near(own[layer_at][0], groups) if layer_at else after(asked, (types, own[0][1:], own[1:]))
        far = relay(got, groups, held)
        across = {ro: crossed(got[ro], halves) for ro in got}
        got = {0: own[layer_at][:1], **got}
        across[0] = own[layer_at][1:]
        if not last:
            pieces, places = parts_of(got, across)
            total, stash = forward_call(
                streams[-1], types, values[layer_at], None, None, pieces, pair_order(places, range(held)), 0
            )
            far = after(far, total)
        elif streams[1:]:
            far = after(far, streams[-1])
        far_across = {ro: crossed(far[ro], halves) for ro in far}
        if not last:
            if far:
                pieces, places = parts_of(far, far_across)
                base = held * min(far)
                order = pair_order(places, range(held))
                total, stash = forward_call(
                    streams[-1], types, values[layer_at], total, stash, pieces, order, base
                )
            streams.append(total[0])
            stashes.append(stash)
        weights.append(parts_of({**got, **far}, {**across, **far_across}))

    pieces, places = weights[-1]
    predictions, stream, *payload = middle_call(
        place,
        streams[-1],
        types,
        across_types,
        values[-1],
        gate_slopes,
        (pred_grad.T, tower_in, tower_bias, tower_out),
        pieces,
        pair_order(places, range(held)),
        groups,
        halves,
        held,
    )

    shards = lax.axis_size("rows")
    paired = shards > 2
    hops = ["share"] + [4 << at for at in range(shards.bit_length() - 3)] + ["join"] if paired else []
    upper = (row_at & 2) > 0

    class Moving:
        def __init__(self, layer_at, mine, others):
            self.layer_at, self.mine, self.own = layer_at, mine, None
            self.got = [flip(part, "rows", 1) for part in others]
            self.sums, self.parts, self.total, self.hops = None, None, None, -2

        def ask(self, token):
            if self.hops == -1:
                sums, own = after((self.sums, self.own), token)
                ros = range(1, groups) if self.parts is None else ()
                self.got = [flip(sums[ro - 1], "expert", ro) for ro in ros]
                self.got += [] if own is None else [flip(own[1], "rows", 1)]
                return
            total = after(self.total, token)
            if self.hops == len(hops):
                self.got = [total] + ([flip(total, "rows", 1)] if halves == 2 else [])
            elif hops[self.hops] == "share":
                cut = total.shape[0] // 2
                self.got = [
                    jnp.where(upper, total[cut:], total[:cut]),
                    flip(jnp.where(upper, total[:cut], total[cut:]), "rows", 2),
                ]
            else:
                self.got = [total, flip(total, "rows", 2 if hops[self.hops] == "join" else hops[self.hops])]

        def add(self):
            if self.hops == -2:
                self.sums = [add_low(*pair) for pair in zip(self.mine, self.got)]
            elif self.hops == -1:
                got = self.got
                if self.parts is None:
                    self.parts = []
                    while len(got) >= 1 << len(self.parts) and (1 << len(self.parts)) < groups:
                        size = 1 << len(self.parts)
                        level, got = got[:size], got[size:]
                        while len(level) > 1:
                            level = [add_low(*level[i : i + 2]) for i in range(0, len(level), 2)]
                        self.parts += level
                if self.own is None:
                    return
                self.total = functools.reduce(add_low, self.parts, add_low(self.own[0], got[0]))
            elif hops[self.hops] != "join":
                self.total = add_low(*self.got)
            else:
                here, there = self.got
                self.total = jnp.concatenate([jnp.where(upper, there, here), jnp.where(upper, here, there)])
            self.hops += 1

    def arrive(entries, others):
        got, others = lax.optimization_barrier(([entry.got for entry in entries], others))
        for entry, what in zip(entries, got):
            entry.got = what
            entry.add()
        there = [[x for x in (entry.total, entry.parts, entry.sums) if x is not None][0] for entry in entries]
        return there, others

    assert layers == 2
    mine, left = payload[0], payload[-7:]
    mine = [mine[ro] for ro in range(groups - 1)]
    later = Moving(1, mine, payload[1:-7] or mine)
    token = arrive([later], ())
    stream = after(stream, token)
    later.ask(token)
    pieces, places = weights[0]
    stream, mine, *others = backward_call(
        streams[0],
        types,
        across_types,
        stream,
        gate_slopes,
        values[0],
        stashes[0],
        pieces,
        pair_order(places, range(held)),
        held,
        tasks,
        (values[1], own[1], *left),
    )
    token = arrive([later], stream)
    others, last_own = others[:-halves], others[-halves:]
    mine = [mine[ro] for ro in range(groups)]
    others = others or mine
    earlier = Moving(0, mine[1:], others[1:])
    earlier.own = (mine[0], others[0])
    later.own = (last_own[0], last_own[-1])
    later.ask(())
    token = arrive([earlier, later], token)
    moving = [later, earlier]

    whole = {}
    arrays, tower_sums = None, ()

    def ask(*entries):
        nonlocal arrays, tower_sums
        for entry in entries:
            entry.ask(token)
        for entry in entries:
            if entry.hops < len(hops):
                continue
            moving.remove(entry)
            layer_at, got = entry.layer_at, entry.got
            whole[layer_at] = got
            if layer_at == layers - 1:
                end = got[0][held * stride + type_count // 2 :].astype(f32)
                tower_rows = [array[held * stride + type_count // 2 + EXTRA :].astype(f32) for array in got]
                if halves == 2:
                    tower_rows = [jnp.where(core == 0, *tower_rows), jnp.where(core == 0, *tower_rows[::-1])]
                wide = jnp.concatenate(tower_rows).reshape(tasks, -1, width)
                narrow = tower_in.shape[2]
                parts = [wide[:, :, at : at + narrow] for at in range(0, width, narrow)]
                tower_sums = (
                    jnp.concatenate(parts, axis=1),
                    end[0].reshape(tower_bias.shape),
                    end[1].reshape(tower_out.shape),
                )
            if moving:
                sources = {(layer_at, half): array for half, array in enumerate(got)}
                arrays = finish_call(place, sources, arrays, held, expert_in.shape)

    if len(hops) == 3:
        ask(earlier, later)
        token = arrive([later], ())
        ask(later)
        token = arrive([earlier, later], ())
        ask(earlier)
        token = arrive([earlier], ())
        ask(earlier, later)
        token = arrive([earlier, later], ())
    while moving:
        ask(*moving)
        if moving:
            token = arrive(moving, (arrays, tower_sums))
    ends = [whole[layer_at][0][held * stride : held * stride + type_count].astype(f32) for layer_at in range(layers)]
    cut = type_count // 2
    gate_grads = [ends[0][:cut], ends[1][:cut] + ends[0][cut:]]
    quantities = selectors * (bits + 1)
    small = jnp.stack(gate_grads)
    small = jnp.concatenate([small[..., :LANES], small[..., LANES:]], axis=1)[..., : tasks * quantities]
    small = small.reshape(layers, type_count, tasks, quantities)
    logits_grad = small[..., : selectors * bits].reshape(selector_logits.shape)
    smalls = (logits_grad, small[..., selectors * bits :], *tower_sums)
    got, (arrays, smalls) = lax.optimization_barrier((whole[0], (arrays, smalls)))
    arrays = finish_call(place, {(0, half): array for half, array in enumerate(got)}, arrays, held, expert_in.shape)
    return (
        predictions.T,
        stream,
        arrays[0],
        arrays[2],
        arrays[1],
        arrays[3],
        *smalls,
    )


def solution(mesh):
    in_specs = (
        P(("rows", "expert"), None),
        P(("rows", "expert"), None),
        P(),
        P(),
        P(None, "expert", None, None),
        P(None, "expert", None),
        P(None, "expert", None, None),
        P(None, "expert", None),
        P(),
        P(),
        P(),
        P(),
        P(),
    )
    out_specs = (
        P(("rows", "expert"), None),
        P(("rows", "expert"), None),
        P(None, "expert", None, None),
        P(None, "expert", None),
        P(None, "expert", None, None),
        P(None, "expert", None),
        P(),
        P(),
        P(),
        P(),
        P(),
    )
    return jax.shard_map(body, mesh=mesh, in_specs=in_specs, out_specs=out_specs, check_vma=False)
```

```python
import functools
import math

import jax
import jax.numpy as jnp
import numpy as np
from jax import lax
from jax.experimental import pallas as pl
from jax.experimental.pallas import tpu as pltpu
from jax.sharding import PartitionSpec as P

SHARPNESS = 10.0
EXACT = lax.Precision.HIGHEST
bf16 = jnp.bfloat16
f32 = jnp.float32
INNER = math.sqrt(2.0 / math.pi)
CUBE = 0.044715 * INNER
TILE = 1024
TOWER_TILE = 512
LANES = 128
EXTRA = 16


def mm(a, b):
    return jnp.dot(a, b, preferred_element_type=f32)


def mm_exact(a, b):
    return jnp.dot(a, b, precision=EXACT, preferred_element_type=f32)


def mm_nt(a, b):
    return lax.dot_general(a, b, (((1,), (1,)), ((), ())), preferred_element_type=f32)


def mm_tn(a, b):
    return lax.dot_general(a, b, (((0,), (0,)), ((), ())), preferred_element_type=f32)


def gelu_both(v):
    square = v * v
    half = 0.5 + 0.5 * jnp.tanh(v * (INNER + CUBE * square))
    value = v * half
    slope = half + value * (1.0 - half) * (2.0 * INNER + 6.0 * CUBE * square)
    return value, slope


def gelu_parts(v):
    bend = 2.0 * INNER + 8.0 * CUBE * (v * v)
    twice_share = 1.0 + jnp.tanh(v * bend)
    return v * twice_share, bend, twice_share


def gelu_slope(value, bend, twice_share):
    rise = 3.0 * bend - 4.0 * INNER
    return twice_share + value * (2.0 - twice_share) * rise


FAR = pl.BlockSpec(memory_space=pl.ANY)
NEAR = pl.BlockSpec(memory_space=pltpu.VMEM)
SCALARS = pl.BlockSpec(memory_space=pltpu.SMEM)


def kernel_params(mebibytes):
    return pltpu.CompilerParams(vmem_limit_bytes=mebibytes * 2**20)


def whole_spec(shape):
    zeros = (0,) * len(shape)
    return pl.BlockSpec(shape, lambda i: zeros)


def prepare_kernel(sizes, place_ref, length_ref, kind_ref, logit_ref, mix_ref, spread_logit_ref, spread_mix_ref, *outs):
    owned, halves, held, selectors, bits, tasks = sizes
    type_ref, across_ref, slope_ref, *value_refs = outs
    height, type_count = type_ref.shape
    experts = 2**bits
    sessions = length_ref.shape[1]
    chunk = min(256, sessions)
    position = (place_ref[0] + lax.broadcasted_iota(jnp.int32, (height, 1), 0)).astype(f32)
    earlier = lax.broadcasted_iota(jnp.int32, (chunk, chunk), 0) < lax.broadcasted_iota(jnp.int32, (chunk, chunk), 1)
    earlier = jnp.where(earlier, 1.0, 0.0).astype(bf16)
    kinds = lax.broadcasted_iota(jnp.int32, (type_count, chunk), 0)
    before = jnp.zeros((1, 1), f32)
    types = jnp.zeros((height, type_count), f32)
    across = jnp.zeros((type_count, height), f32)
    for at in range(0, sessions, chunk):
        lengths = length_ref[:, at : at + chunk].astype(f32)
        begin = before + mm(jnp.broadcast_to(lengths.astype(bf16), (EXTRA, chunk)), earlier)[0:1]
        before += jnp.sum(lengths, axis=1, keepdims=True)
        member = jnp.where((position >= begin) & (position < begin + lengths), 1.0, 0.0).astype(bf16)
        of_type = jnp.where(kinds == kind_ref[:, at : at + chunk], 1.0, 0.0).astype(bf16)
        types += mm_nt(member, of_type)
        across += mm_nt(of_type, member)
    type_ref[...] = types.astype(bf16)
    across_ref[...] = across.astype(bf16)

    rows = logit_ref.shape[0]
    place = lax.broadcasted_iota(jnp.int32, (rows, LANES), 1) % experts
    expert = (
        owned * ((place // owned) ^ place_ref[1])
        + held * ((place % halves) ^ place_ref[2])
        + (place // halves) % held
    )
    logits = mm_exact(logit_ref[...], spread_logit_ref[...])
    mixes = mm_exact(mix_ref[...], spread_mix_ref[...])
    mixes = [mixes[:, k * LANES : (k + 1) * LANES] for k in range(selectors)]
    top = functools.reduce(jnp.maximum, mixes)
    shares = [jnp.exp(mix - top) for mix in mixes]
    whole = functools.reduce(jnp.add, shares)
    shares = [share / whole for share in shares]
    value = jnp.zeros((rows, LANES), f32)
    reaches = []
    for k in range(selectors):
        factors, signed = [], []
        for bit in range(bits):
            at = (k * bits + bit) * LANES
            logit = logits[:, at : at + LANES]
            cubic = (-2.0 / SHARPNESS**3) * logit * logit * logit + (1.5 / SHARPNESS) * logit + 0.5
            step = jnp.where(logit <= -SHARPNESS / 2, 0.0, jnp.where(logit >= SHARPNESS / 2, 1.0, cubic))
            slope = (-6.0 / SHARPNESS**3) * logit * logit + 1.5 / SHARPNESS
            slope = jnp.where((logit > -SHARPNESS / 2) & (logit < SHARPNESS / 2), slope, 0.0)
            on = (expert >> bit) & 1 == 1
            factors.append(jnp.where(on, step, 1.0 - step))
            signed.append(jnp.where(on, slope, -slope))
        reaches.append(functools.reduce(jnp.multiply, factors))
        value += shares[k] * reaches[k]
        for bit in range(bits):
            others = [factors[b] for b in range(bits) if b != bit]
            slope_ref[k * bits + bit] = shares[k] * signed[bit] * functools.reduce(jnp.multiply, others)
    for k in range(selectors):
        slope_ref[selectors * bits + k] = shares[k] * (reaches[k] - value)

    value = value.astype(bf16).astype(f32)
    for layer_at, ref in enumerate(value_refs):
        table = value[layer_at * type_count : (layer_at + 1) * type_count]
        columns = [table[:, t * experts : (t + 1) * experts] for t in range(tasks)]
        if layer_at < len(value_refs) - 1:
            columns = [functools.reduce(jnp.add, columns) / tasks]
        for pair in range(ref.shape[0]):
            lanes = []
            for half in range(halves):
                at = pair * halves + half
                lanes += [jnp.broadcast_to(c[:, at : at + 1], (type_count, LANES)) for c in columns]
            ref[pair] = jnp.concatenate(lanes, axis=1).astype(bf16)


def prepare_call(place, lengths, session_type, logits, mixing, height, sizes):
    owned, halves, held, selectors, bits, tasks = sizes
    layers, type_count = logits.shape[:2]
    experts = 2**bits
    rows = layers * type_count
    lane = np.arange(LANES)
    source = np.arange(tasks * selectors * bits)
    task, number = source // (selectors * bits), source % (selectors * bits)
    mine = (lane[None, :] // experts == task[:, None])[:, None, :]
    spread_logit = mine & (number[:, None, None] == np.arange(selectors * bits)[None, :, None])
    source = np.arange(tasks * selectors)
    mine = (lane[None, :] // experts == (source // selectors)[:, None])[:, None, :]
    spread_mix = mine & ((source % selectors)[:, None, None] == np.arange(selectors)[None, :, None])
    spread_logit = spread_logit.reshape(spread_logit.shape[0], -1).astype(np.float32)
    spread_mix = spread_mix.reshape(spread_mix.shape[0], -1).astype(np.float32)
    outs = [
        jax.ShapeDtypeStruct((height, type_count), bf16),
        jax.ShapeDtypeStruct((type_count, height), bf16),
        jax.ShapeDtypeStruct((selectors * (bits + 1), rows, LANES), f32),
    ]
    for layer_at in range(layers):
        each = tasks if layer_at == layers - 1 else 1
        outs.append(jax.ShapeDtypeStruct((experts // halves, type_count, halves * each * LANES), bf16))
    return pl.pallas_call(
        functools.partial(prepare_kernel, sizes),
        out_shape=outs,
        in_specs=[SCALARS] + [NEAR] * 6,
        out_specs=[NEAR] * len(outs),
        compiler_params=kernel_params(58),
        cost_estimate=pl.CostEstimate(flops=2 * height * lengths.size * 64, bytes_accessed=2**21, transcendentals=2**16),
    )(
        place,
        lengths.reshape(1, -1),
        session_type.reshape(1, -1),
        logits.reshape(rows, -1),
        mixing.reshape(rows, -1),
        spread_logit,
        spread_mix,
    )


def bias_rows(weights, width):
    rows = weights[2 * width : 2 * width + EXTRA].astype(f32)
    return rows[0:1] + rows[1:2], rows[2:3] + rows[3:4]


def twice(a):
    return jnp.concatenate([a, a], axis=1)


def tiles(height, most):
    tile = min(most, height)
    return [pl.ds(at, tile) for at in range(0, height, tile)]


def joined(parts, axis):
    return parts[0] if len(parts) == 1 else jnp.concatenate(parts, axis=axis)


def gates_of(types, value_ref, count):
    gates = mm(types, value_ref[...]).astype(bf16)
    return [gates[:, at * LANES : (at + 1) * LANES] for at in range(count)]


def forward_step(weights, value_ref, x_low, type_ref, total_ref, biases, keep, keep_gate=None, keep_result=None):
    height, width = x_low.shape
    kinds = total_ref.shape[0]
    bias_in, bias_out = zip(*(bias_rows(w, width) for w in weights))
    second = joined([w[width : 2 * width] for w in weights], 0)
    for rows in tiles(height, TILE):
        gates = gates_of(type_ref[rows], value_ref, len(weights) * kinds)
        if keep_gate is not None:
            for at, gate in enumerate(gates):
                keep_gate(at, rows, gate)
        scaled = [[] for _ in range(kinds)]
        for i, w in enumerate(weights):
            before = mm(x_low[rows], w[0:width]) + bias_in[i]
            hidden, bend, twice_share = gelu_parts(before)
            hidden = hidden.astype(bf16)
            keep(i, rows, hidden, gelu_slope(hidden, bend.astype(bf16), twice_share.astype(bf16)))
            if keep_result is not None:
                result = mm(hidden, w[width : 2 * width]).astype(bf16)
                keep_result(i, rows, result)
            for t in range(kinds):
                scaled[t].append(twice(gates[i * kinds + t]) * (hidden if keep_result is None else result))
        for t in range(kinds):
            if keep_result is None:
                total_ref[t, rows] += mm(joined(scaled[t], 1), second)
            else:
                total_ref[t, rows] += functools.reduce(jnp.add, scaled[t]).astype(f32)
    for i in range(len(weights)):
        for t in range(kinds):
            at = (i * kinds + t) * LANES
            biases[t] += twice(value_ref[:, at : at + LANES].astype(f32)) * bias_out[i]


def forward_end(type_ref, total_ref, biases):
    for t in range(total_ref.shape[0]):
        high = biases[t].astype(bf16)
        rest = (biases[t] - high.astype(f32)).astype(bf16)
        for rows in tiles(total_ref.shape[1], TILE):
            total_ref[t, rows] += mm(twice(type_ref[rows]), jnp.concatenate([high, rest], axis=0))


def backward_start(x_low, type_across, low, across, share):
    width = x_low.shape[1]
    across[0:width] = x_low[...].T
    ones = lax.broadcasted_iota(jnp.int32, (EXTRA, x_low.shape[0]), 0) == 0
    across[width:] = jnp.where(ones, 1.0, 0.0).astype(bf16)
    for t in range(low.shape[0]):
        share[t] = mm(type_across[...], low[t])


def backward_step(weights, value_ref, hiddens, slopes, outs, pair, experts, type_ref, type_across, low, stream_ref, across, share, table, scratch, kept_gates=None, results=None, dots=None, gate_lanes=None):
    before_grads, result_grads = scratch
    kinds, height, width = low.shape
    count = len(weights)
    first = joined([w[0:width] for w in weights], 1)
    for rows in tiles(height, TILE):
        if kept_gates is None:
            gates = gates_of(type_ref[rows], value_ref, count * kinds)
        else:
            gates = [kept_gates[at, rows] for at in range(count * kinds)]
        gates = [twice(gate) for gate in gates]
        befores = []
        for i, w in enumerate(weights):
            hidden, slope = hiddens[i][rows], slopes[i][rows]
            second = w[width : 2 * width]
            result_grad = gates[i * kinds] * low[0, rows]
            for t in range(1, kinds):
                result_grad += gates[i * kinds + t] * low[t, rows]
            hidden_grad = mm_nt(result_grad, second).astype(bf16)
            for t in range(kinds):
                product = hidden * hidden_grad if results is None else results[i][rows] * low[t, rows]
                product = functools.reduce(
                    jnp.add, [product[:, lane : lane + LANES] for lane in range(0, width, LANES)]
                )
                found = jnp.sum(product.astype(f32), axis=1, keepdims=True)
                lanes = lax.broadcasted_iota(jnp.int32, (1, LANES), 1)
                place = pair * count + i
                chosen = lanes % experts == place if kinds == 1 else lanes == t * experts + place
                dots[rows] = jnp.where(chosen, found, dots[rows])
            before = slope * hidden_grad
            before_grads[i, rows] = before
            result_grads[i, rows] = result_grad
            befores.append(before)
        stream_ref[rows] += mm_nt(joined(befores, 1), first)
    lanes = lax.broadcasted_iota(jnp.int32, (type_ref.shape[1], LANES), 1)
    for i, w in enumerate(weights):
        _, bias_out = bias_rows(w, width)
        first_grad = 0.5 * mm(across[...], before_grads[i])
        outs[i][0:width] = first_grad[0:width].astype(bf16)
        outs[i][width : 2 * width] = mm_tn(hiddens[i][...], result_grads[i]).astype(bf16)
        out_bias = jnp.zeros((1, width), f32)
        place = pair * count + i
        for t in range(kinds):
            at = (i * kinds + t) * LANES
            gate = value_ref[:, at : at + LANES].astype(f32)
            out_bias += jnp.sum(twice(gate) * share[t], axis=0, keepdims=True)
            bias_part = jnp.sum(share[t] * bias_out, axis=1, keepdims=True)
            if kinds == 1:
                table[...] = jnp.where(lanes % experts == place, 0.5 * bias_part, table[...])
                gate_lanes[...] = jnp.where(lanes % experts == place, gate, gate_lanes[...])
            else:
                table[...] = jnp.where(lanes == t * experts + place, bias_part, table[...])
        tail = jnp.concatenate([first_grad[width : width + 1], out_bias, jnp.zeros((EXTRA - 2, width), f32)])
        outs[i][2 * width : 2 * width + EXTRA] = tail.astype(bf16)


def by_type(type_across, dots):
    high = dots[...].astype(bf16)
    rest = (dots[...] - high.astype(f32)).astype(bf16)
    return mm(type_across[...], high) + mm(type_across[...], rest)


def through_gates(table, gate_slope_ref, experts, tasks):
    quantities, type_count = gate_slope_ref.shape[:2]
    lanes = lax.broadcasted_iota(jnp.int32, (type_count, LANES), 1)
    small = jnp.zeros((type_count, LANES), f32)
    for q in range(quantities):
        product = gate_slope_ref[q] * table[...]
        for t in range(tasks):
            part = jnp.sum(jnp.where(lanes // experts == t, product, 0.0), axis=1, keepdims=True)
            small = jnp.where(lanes == t * quantities + q, part, small)
    half = type_count // 2
    return jnp.concatenate([small[:half], small[half:]], axis=1).astype(bf16)


def store_copies(ready, pair, held, out_refs, sems):
    group, unit = pair // held, lax.rem(pair, held)
    rows = pl.ds(pl.multiple_of(unit * ready.shape[1], EXTRA), ready.shape[1])
    copies = [(None, pltpu.make_async_copy(ready.at[0], out_refs[0].at[group, rows], sems.at[0]))]
    for at, ref in enumerate(out_refs[1:]):
        copies.append((group == at, pltpu.make_async_copy(ready.at[1], ref.at[rows], sems.at[1])))
    return copies


def end_copies(ends, out_refs, sems):
    rows = out_refs[0].shape[1]
    last = pl.ds(rows - ends.shape[1], ends.shape[1])
    groups = out_refs[0].shape[0]
    copies = [pltpu.make_async_copy(ends.at[0], out_refs[0].at[at, last], sems.at[0, at]) for at in range(groups)]
    copies += [
        pltpu.make_async_copy(ends.at[1], ref.at[last], sems.at[1, at]) for at, ref in enumerate(out_refs[1:])
    ]
    return [(None, copy) for copy in copies]


def for_each(copies, act):
    for condition, copy in copies:
        if condition is None:
            act(copy)
        else:
            pl.when(condition)(functools.partial(act, copy))


def start(copy):
    copy.start()


def wait(copy):
    copy.wait()


def fetch_weights(places, buffer, sems, each):
    step = pl.program_id(0)
    for of in range(len(places) // each):

        @pl.when(step == max(of - 1, 0))
        def _(of=of):
            for i, (ref, at) in enumerate(places[of * each : (of + 1) * each]):
                pltpu.make_async_copy(ref.at[at], buffer.at[of % 2, i], sems.at[of % 2, i]).start()

    slot = lax.rem(step, 2)
    for i in range(each):
        ref, at = places[0]
        pltpu.make_async_copy(ref.at[at], buffer.at[slot, i], sems.at[slot, i]).wait()
    return [buffer.at[slot, i] for i in range(each)]


def forward_kernel(places, pieces, each, first, *refs):
    refs = list(refs)
    take = lambda count: [refs.pop(0) for _ in range(count)]
    x_ref, type_ref, value_ref = take(3)
    if not first:
        total_ref, _, _ = take(3)
    weight_refs = take(pieces)
    out_ref, hidden_ref, slope_ref, x_low, biases, buffer, sems = take(7)
    step = pl.program_id(0)
    weights = fetch_weights([(weight_refs[piece], at) for piece, at in places], buffer, sems, each)

    @pl.when(step == 0)
    def _():
        x_low[...] = x_ref[...].astype(bf16)
        biases[...] = jnp.zeros_like(biases)
        out_ref[0] = x_ref[...] if first else total_ref[0]

    def keep(i, rows, hidden, slope):
        hidden_ref[0, i, rows] = hidden
        slope_ref[0, i, rows] = slope

    forward_step(weights, value_ref.at[0], x_low, type_ref, out_ref, biases, keep)

    @pl.when(step == pl.num_programs(0) - 1)
    def _():
        forward_end(type_ref, out_ref, biases)


def forward_call(x, types, values, total, stash, pieces, places, base):
    height, width = x.shape
    pairs, type_count, lanes = values.shape
    each = lanes // LANES
    operands = [x, types, values]
    specs = [whole_spec(x.shape), whole_spec(types.shape)]
    specs.append(pl.BlockSpec((1, type_count, lanes), lambda i: (base + i, 0, 0)))
    aliases = {}
    if total is not None:
        operands += [total, *stash]
        specs += [whole_spec(total.shape), FAR, FAR]
        aliases = {4: 1, 5: 2}
    summed = jax.ShapeDtypeStruct((1, height, width), f32)
    kept = jax.ShapeDtypeStruct((pairs, each, height, width), bf16)
    kept_spec = pl.BlockSpec((1, each, height, width), lambda i: (base + i, 0, 0, 0))
    number = len(places)
    results = pl.pallas_call(
        functools.partial(forward_kernel, places, len(pieces), each, total is None),
        grid=(number // each,),
        out_shape=[summed, kept, kept],
        in_specs=specs + [whole_spec(piece.shape) for piece in pieces],
        out_specs=[whole_spec(summed.shape), kept_spec, kept_spec],
        scratch_shapes=[
            pltpu.VMEM((height, width), bf16),
            pltpu.VMEM((1, type_count, width), f32),
            pltpu.VMEM((2, each, *pieces[0].shape[1:]), bf16),
            pltpu.SemaphoreType.DMA((2, each)),
        ],
        input_output_aliases=aliases,
        compiler_params=kernel_params(58),
        cost_estimate=pl.CostEstimate(
            flops=4 * number * height * width * width,
            bytes_accessed=number * (4 * width * width + 4 * height * width) + 8 * height * width,
            transcendentals=number * height * width,
        ),
    )(*operands, *pieces)
    return results[0], results[1:]


def middle_kernel(places, pieces, groups, halves, held, *refs):
    refs = list(refs)
    take = lambda count: [refs.pop(0) for _ in range(count)]
    place_ref, x_ref, type_ref, across_types_ref, value_ref, gate_slope_ref, pred_grad_ref = take(7)
    tower_in_ref, tower_bias_ref, tower_out_ref = take(3)
    weight_refs = take(pieces)
    pred_ref, stream_ref = take(2)
    out_refs = take(1 + (groups - 1) * (halves - 1))
    left_refs = take(7)
    x_low, weights, hidden_all, slope_all, result_all, gates_all, total, biases, low, across, share, table = take(12)
    before_grads, result_grads, dots, cotangents, ready, ends, in_grad, bias_grad, out_grad, load_sem, store_sem, end_sem, left_sem = take(13)
    height, width = x_ref.shape
    pairs = value_ref.shape[0]
    experts = pairs * halves
    tasks = total.shape[0]

    def load(pair, i, ref, at):
        return pltpu.make_async_copy(ref.at[at], weights.at[pair, i], load_sem.at[pair, i])

    for j, (piece, at) in enumerate(places):
        load(j // halves, j % halves, weight_refs[piece], at).start()
    x_low[...] = x_ref[...].astype(bf16)
    biases[...] = jnp.zeros_like(biases)
    for t in range(tasks):
        total[t] = x_ref[...]

    def forward_pair(pair, carry):
        for i in range(halves):
            load(pair, i, weight_refs[0], 0).wait()

        def keep(i, rows, hidden, slope):
            hidden_all[pair, i, rows] = hidden
            slope_all[pair, i, rows] = slope

        def keep_gate(at, rows, gate):
            gates_all[pair, at, rows] = gate

        def keep_result(i, rows, result):
            result_all[pair, i, rows] = result

        forward_step(
            [weights.at[pair, i] for i in range(halves)],
            value_ref.at[pair],
            x_low,
            type_ref,
            total,
            biases,
            keep,
            keep_gate,
            keep_result,
        )
        return carry

    lax.fori_loop(0, pairs, forward_pair, 0)
    forward_end(type_ref, total, biases)

    def left(at, source):
        return pltpu.make_async_copy(source, left_refs[at], left_sem.at[at])

    own = [kept.at[0:held] for kept in (hidden_all, slope_all, result_all)]
    for at, source in enumerate(own):
        left(at, source).start()

    cotangents[...] = jnp.concatenate(
        [pred_grad_ref[...], jnp.zeros((cotangents.shape[1] - tasks, height), f32)]
    ).T
    in_grad[...] = jnp.zeros_like(in_grad)
    bias_grad[...] = jnp.zeros_like(bias_grad)
    out_grad[...] = jnp.zeros_like(out_grad)
    for rows in tiles(height, TOWER_TILE):
        summed = None
        predicted = []
        for t in range(tasks):
            closing_low = total[t, rows].astype(bf16)
            act, slope = gelu_both(mm(closing_low, tower_in_ref[t]) + tower_bias_ref[t : t + 1])
            vector = tower_out_ref[t : t + 1]
            predicted.append(jnp.sum(act * vector, axis=1, keepdims=True))
            cotangent = cotangents[rows, t : t + 1]
            out_grad[t : t + 1] += jnp.sum(act * cotangent, axis=0, keepdims=True)
            before_grad = (slope * (cotangent * vector)).astype(bf16)
            bias_grad[t : t + 1] += jnp.sum(before_grad.astype(f32), axis=0, keepdims=True)
            in_grad[t] += mm_tn(closing_low, before_grad)
            closing_grad = mm_nt(before_grad, tower_in_ref[t])
            low[t, rows] = closing_grad.astype(bf16)
            summed = closing_grad if summed is None else summed + closing_grad
        stream_ref[rows] = summed
        blank = jnp.zeros((predicted[0].shape[0], cotangents.shape[1] - tasks), f32)
        pred_ref[:, rows] = jnp.concatenate([*predicted, blank], axis=1).T[0:tasks]
    narrow = in_grad.shape[2]
    tall = width * narrow // width
    begin = type_ref.shape[1] // 2 + EXTRA
    for t in range(tasks):
        wide = jnp.concatenate([in_grad[t, :tall], in_grad[t, tall:]], axis=1).astype(bf16)
        if halves == 2:
            ends[place_ref[2] ^ t, begin:] = wide
        else:
            ends[0, begin + t * tall : begin + (t + 1) * tall] = wide
    vectors = [jnp.concatenate([ref[0:1], ref[1:2]], axis=1) for ref in (bias_grad, out_grad)]
    vectors = jnp.concatenate([*vectors, jnp.zeros((EXTRA - 2, width), f32)]).astype(bf16)
    for half in range(halves):
        ends[half, begin - EXTRA : begin] = vectors

    left(3, low).start()
    backward_start(x_low, across_types_ref, low, across, share)
    left(4, across).start()
    left(5, share).start()
    table[...] = jnp.zeros_like(table)
    dots[...] = jnp.zeros_like(dots)

    def stores(pair):
        return store_copies(ready.at[pair], pair - held, held, out_refs, store_sem.at[pair])

    def backward_pair(pair, carry):
        backward_step(
            [weights.at[pair, i] for i in range(halves)],
            value_ref.at[pair],
            [hidden_all.at[pair, i] for i in range(halves)],
            [slope_all.at[pair, i] for i in range(halves)],
            [ready.at[pair, i] for i in range(halves)],
            pair,
            experts,
            type_ref,
            across_types_ref,
            low,
            stream_ref,
            across,
            share,
            table,
            (before_grads, result_grads),
            gates_all.at[pair],
            [result_all.at[pair, i] for i in range(halves)],
            dots,
        )
        for_each(stores(pair), start)
        return carry

    lax.fori_loop(held, pairs, backward_pair, 0)
    table[...] += by_type(across_types_ref, dots)
    small = through_gates(table, gate_slope_ref, experts, tasks)
    for half in range(halves):
        ends[half, 0 : small.shape[0]] = small
    left(6, ends).start()
    for_each(end_copies(ends, out_refs, end_sem), start)

    def drain(pair, carry):
        for_each(stores(pair), wait)
        return carry

    lax.fori_loop(held, pairs, drain, 0)
    for_each(end_copies(ends, out_refs, end_sem), wait)
    for at, source in enumerate([*own, low, across, share, ends]):
        left(at, source).wait()


def middle_call(place, x, types, across_types, values, gate_slopes, tower, pieces, places, groups, halves, held):
    height, width = x.shape
    pairs, type_count, lanes = values.shape
    pred_grad, tower_in, tower_bias, tower_out = tower
    tasks = tower_in.shape[0]
    stride = 2 * width + EXTRA
    experts = pairs * halves
    outs = [jax.ShapeDtypeStruct(shape, f32) for shape in (pred_grad.shape, (height, width))]
    near = len(outs)
    end_rows = type_count // 2 + EXTRA + tower_in.size // width // halves
    rows = held * stride + end_rows
    outs.append(jax.ShapeDtypeStruct((groups - 1, rows, width), bf16))
    outs += [jax.ShapeDtypeStruct((rows, width), bf16)] * ((groups - 1) * (halves - 1))
    outs += [jax.ShapeDtypeStruct((held, halves, height, width), bf16)] * 3
    outs.append(jax.ShapeDtypeStruct((tasks, height, width), bf16))
    outs.append(jax.ShapeDtypeStruct((width + EXTRA, height), bf16))
    outs.append(jax.ShapeDtypeStruct((tasks, type_count, width), f32))
    outs.append(jax.ShapeDtypeStruct((halves, end_rows, width), bf16))
    layer_at = gate_slopes.shape[1] // type_count - 1
    slope_spec = pl.BlockSpec((gate_slopes.shape[0], type_count, LANES), lambda i: (0, layer_at, 0))
    kept = pltpu.VMEM((pairs, halves, height, width), bf16)
    operands = [x, types, across_types, values, gate_slopes, *tower]
    specs = [whole_spec(a.shape) for a in operands]
    specs[4] = slope_spec
    return pl.pallas_call(
        functools.partial(middle_kernel, places, len(pieces), groups, halves, held),
        grid=(1,),
        out_shape=outs,
        in_specs=[SCALARS] + specs + [FAR] * len(pieces),
        out_specs=[whole_spec(out.shape) for out in outs[:near]] + [FAR] * (len(outs) - near),
        scratch_shapes=[
            pltpu.VMEM((height, width), bf16),
            pltpu.VMEM((pairs, halves, stride, width), bf16),
            kept,
            kept,
            kept,
            pltpu.VMEM((pairs, halves * tasks, height, LANES), bf16),
            pltpu.VMEM((tasks, height, width), f32),
            pltpu.VMEM((tasks, type_count, width), f32),
            pltpu.VMEM((tasks, height, width), bf16),
            pltpu.VMEM((width + EXTRA, height), bf16),
            pltpu.VMEM((tasks, type_count, width), f32),
            pltpu.VMEM((type_count, LANES), f32),
            pltpu.VMEM((halves, height, width), bf16),
            pltpu.VMEM((halves, height, width), bf16),
            pltpu.VMEM((height, LANES), f32),
            pltpu.VMEM((height, LANES), f32),
            pltpu.VMEM((pairs, halves, stride, width), bf16),
            pltpu.VMEM((halves, end_rows, width), bf16),
            pltpu.VMEM(tower_in.shape, f32),
            pltpu.VMEM(tower_bias.shape, f32),
            pltpu.VMEM(tower_out.shape, f32),
            pltpu.SemaphoreType.DMA((pairs, halves)),
            pltpu.SemaphoreType.DMA((pairs, halves)),
            pltpu.SemaphoreType.DMA((halves, groups)),
            pltpu.SemaphoreType.DMA((7,)),
        ],
        compiler_params=kernel_params(58),
        cost_estimate=pl.CostEstimate(
            flops=14 * experts * height * width * width,
            bytes_accessed=experts * 8 * width * width + 16 * height * width,
            transcendentals=experts * height * width,
        ),
    )(place, *operands, *pieces)


def backward_kernel(places, pieces, each, held, tasks, *refs):
    refs = list(refs)
    take = lambda count: [refs.pop(0) for _ in range(count)]
    x_ref, type_ref, across_types_ref, stream_ref, gate_slope_ref, value_ref, hidden_ref, slope_ref = take(8)
    last_value_ref, last_low_ref, last_across_ref, last_share_ref, last_end_ref = take(5)
    last_refs, last_weight_refs = take(3), take(each)
    weight_refs = take(pieces)
    stream_out_ref = take(1)[0]
    groups = len(places) // each // held
    out_refs = take(1 + groups * (each - 1))
    last_out_refs = take(each)
    x_low, across, low, share, table, before_grads, result_grads, gate_lanes, buffer, ready, ends = take(11)
    x_wide, gate_slopes, last_table, dots, kept, last_weights, last_ready = take(7)
    sems, store_sem, end_sem, last_sem, last_store_sem, late_sem = take(6)
    step = pl.program_id(0)
    slot = lax.rem(step, 2)
    experts = len(places)
    types = type_ref.shape[1]
    stride = buffer.shape[2]
    scratch = (before_grads, result_grads)
    weights = fetch_weights([(weight_refs[piece], at) for piece, at in places], buffer, sems, each)

    late = [
        (None, pltpu.make_async_copy(source, target, late_sem.at[at]))
        for at, (source, target) in enumerate(((x_ref, x_wide), (gate_slope_ref, gate_slopes)))
    ]

    def last_loads(unit):
        copies = [
            pltpu.make_async_copy(last_refs[which].at[unit], kept.at[which, unit], last_sem.at[unit, which])
            for which in range(3)
        ]
        for half in range(each):
            source, sem = last_weight_refs[half].at[unit], last_sem.at[unit, 3 + half]
            copies.append(pltpu.make_async_copy(source, last_weights.at[unit, half], sem))
        return [(None, copy) for copy in copies]

    def last_stores():
        copies = []
        for half, ref in enumerate(last_out_refs):
            for unit in range(held):
                rows = pl.ds(unit * stride, stride)
                copies.append(
                    pltpu.make_async_copy(last_ready.at[unit, half], ref.at[rows], last_store_sem.at[half, unit])
                )
            rows = pl.ds(held * stride, last_end_ref.shape[1])
            copies.append(pltpu.make_async_copy(last_end_ref.at[half], ref.at[rows], last_store_sem.at[half, held]))
        return [(None, copy) for copy in copies]

    @pl.when(step == 0)
    def _():
        for unit in range(held):
            for_each(last_loads(unit), start)
        for_each(late, start)
        stream_out_ref[...] = stream_ref[...]
        last_table[...] = jnp.zeros_like(last_table)
        dots[...] = jnp.zeros_like(dots)

        def last_pair(unit, carry):
            for_each(last_loads(unit), wait)
            backward_step(
                [last_weights.at[unit, i] for i in range(each)],
                last_value_ref.at[unit],
                [kept.at[0, unit, i] for i in range(each)],
                [kept.at[1, unit, i] for i in range(each)],
                [last_ready.at[unit, i] for i in range(each)],
                unit,
                experts,
                type_ref,
                across_types_ref,
                last_low_ref,
                stream_out_ref,
                last_across_ref,
                last_share_ref,
                last_table,
                scratch,
                None,
                [kept.at[2, unit, i] for i in range(each)],
                dots,
            )
            return carry

        lax.fori_loop(0, held, last_pair, 0)
        for_each(last_stores(), start)
        last_table[...] += by_type(across_types_ref, dots)
        dots[...] = jnp.zeros_like(dots)
        for_each(late[:1], wait)
        x_low[...] = x_wide[...].astype(bf16)
        low[0] = stream_out_ref[...].astype(bf16)
        table[...] = jnp.zeros_like(table)
        gate_lanes[...] = jnp.zeros_like(gate_lanes)
        backward_start(x_low, across_types_ref, low, across, share)

    def stores(pair):
        at = lax.rem(pair, 2)
        return store_copies(ready.at[at], pair, held, out_refs, store_sem.at[at])

    @pl.when(step >= 2)
    def _():
        for_each(stores(step - 2), wait)

    backward_step(
        weights,
        value_ref.at[0],
        [hidden_ref.at[0, i] for i in range(each)],
        [slope_ref.at[0, i] for i in range(each)],
        [ready.at[slot, i] for i in range(each)],
        step,
        experts,
        type_ref,
        across_types_ref,
        low,
        stream_out_ref,
        across,
        share,
        table,
        scratch,
        None,
        None,
        dots,
        gate_lanes,
    )

    for_each(stores(step), start)

    @pl.when(step == pl.num_programs(0) - 1)
    def _():
        for_each(late[1:], wait)
        gate = gate_lanes[...]
        found = 0.5 * by_type(across_types_ref, dots) / jnp.where(gate > 0.0, gate, 1.0)
        table[...] += jnp.where(gate > 0.0, found, 0.0)
        both = ((table, 0), (last_table, types))
        small = [through_gates(part, gate_slopes.at[:, pl.ds(at, types)], experts, tasks) for part, at in both]
        for half in range(each):
            ends[half] = jnp.concatenate(small)
        for_each(end_copies(ends, out_refs, end_sem), start)
        for_each(stores(step - 1), wait)
        for_each(stores(step), wait)
        for_each(end_copies(ends, out_refs, end_sem), wait)
        for_each(last_stores(), wait)


def backward_call(x, types, across_types, stream, gate_slopes, values, stash, pieces, places, held, tasks, last):
    height, width = x.shape
    pairs, type_count, lanes = values.shape
    each = lanes // LANES
    groups = pairs // held
    stride = 2 * width + EXTRA
    last_values, last_weights, *last_kept, last_low, last_across, last_share, last_ends = last
    operands = [x, types, across_types, stream, gate_slopes, values, *stash]
    specs = [FAR, *[whole_spec(a.shape) for a in operands[1:4]], FAR]
    specs.append(pl.BlockSpec((1, type_count, lanes), lambda i: (i, 0, 0)))
    specs += [pl.BlockSpec((1, each, height, width), lambda i: (i, 0, 0, 0))] * 2
    near = [last_low, last_across, last_share, last_ends]
    operands += [last_values, *near, *last_kept, *last_weights]
    specs.append(pl.BlockSpec((held, *last_values.shape[1:]), lambda i: (0, 0, 0)))
    specs += [whole_spec(a.shape) for a in near]
    specs += [FAR] * (len(last_kept) + each)
    rows = held * stride + type_count
    mine = jax.ShapeDtypeStruct((groups, rows, width), bf16)
    others = [jax.ShapeDtypeStruct((rows, width), bf16)] * (groups * (each - 1))
    others += [jax.ShapeDtypeStruct((held * stride + last_ends.shape[1], width), bf16)] * each
    number = pairs * each
    return pl.pallas_call(
        functools.partial(backward_kernel, places, len(pieces), each, held, tasks),
        grid=(pairs,),
        out_shape=[jax.ShapeDtypeStruct(stream.shape, f32), mine, *others],
        in_specs=specs + [FAR] * len(pieces),
        out_specs=[whole_spec(stream.shape)] + [FAR] * (1 + len(others)),
        scratch_shapes=[
            pltpu.VMEM((height, width), bf16),
            pltpu.VMEM((width + EXTRA, height), bf16),
            pltpu.VMEM((1, height, width), bf16),
            pltpu.VMEM((1, type_count, width), f32),
            pltpu.VMEM((type_count, LANES), f32),
            pltpu.VMEM((each, height, width), bf16),
            pltpu.VMEM((each, height, width), bf16),
            pltpu.VMEM((type_count, LANES), f32),
            pltpu.VMEM((2, each, stride, width), bf16),
            pltpu.VMEM((2, each, stride, width), bf16),
            pltpu.VMEM((each, type_count, width), bf16),
            pltpu.VMEM((height, width), f32),
            pltpu.VMEM(gate_slopes.shape, f32),
            pltpu.VMEM((type_count, LANES), f32),
            pltpu.VMEM((height, LANES), f32),
            pltpu.VMEM((3, held, each, height, width), bf16),
            pltpu.VMEM((held, each, stride, width), bf16),
            pltpu.VMEM((held, each, stride, width), bf16),
            pltpu.SemaphoreType.DMA((2, each)),
            pltpu.SemaphoreType.DMA((2, each)),
            pltpu.SemaphoreType.DMA((each, groups)),
            pltpu.SemaphoreType.DMA((held, 3 + each)),
            pltpu.SemaphoreType.DMA((each, held + 1)),
            pltpu.SemaphoreType.DMA((2,)),
        ],
        compiler_params=kernel_params(58),
        cost_estimate=pl.CostEstimate(
            flops=10 * number * height * width * width,
            bytes_accessed=number * (8 * width * width + 4 * height * width) + 16 * height * width,
            transcendentals=0,
        ),
    )(*operands, *pieces)


def finish_kernel(names, held, rows, first, *refs):
    place_ref, *refs = refs
    sources, refs = refs[: len(names)], refs[len(names) :]
    in_ref, out_ref, in_bias_out_ref, out_bias_out_ref, ready, sems = refs[-6:]
    in_bias_out_ref[...] = jnp.zeros_like(in_bias_out_ref) if first else refs[2][...]
    out_bias_out_ref[...] = jnp.zeros_like(out_bias_out_ref) if first else refs[3][...]
    copies = []
    for at, ((layer_at, half), source) in enumerate(zip(names, sources)):
        for unit in range(held):
            base = unit * (2 * rows + EXTRA)
            where = held * (place_ref[2] ^ half) + unit
            for which, ref in enumerate((in_ref, out_ref)):
                begin = base + which * rows
                ready[at, unit, which] = source[begin : begin + rows].astype(f32)
                copy = pltpu.make_async_copy(
                    ready.at[at, unit, which], ref.at[layer_at, where], sems.at[at, unit, which]
                )
                copy.start()
                copies.append(copy)
            tail = source[base + 2 * rows : base + 2 * rows + EXTRA].astype(f32)
            in_bias_out_ref[layer_at, pl.ds(where, 1)] = tail[0:1]
            out_bias_out_ref[layer_at, pl.ds(where, 1)] = tail[1:2]
    for copy in copies:
        copy.wait()


def finish_call(place, named, held_arrays, held, shape):
    rows, width = shape[2:]
    names, sources = tuple(named), list(named.values())
    outs = [jax.ShapeDtypeStruct(shape, f32)] * 2
    outs += [jax.ShapeDtypeStruct((*shape[:2], width), f32)] * 2
    first = held_arrays is None
    number = len(names)
    return pl.pallas_call(
        functools.partial(finish_kernel, names, held, rows, first),
        out_shape=outs,
        in_specs=[SCALARS] + [NEAR] * number + ([] if first else [FAR, FAR, NEAR, NEAR]),
        out_specs=[FAR, FAR, NEAR, NEAR],
        scratch_shapes=[
            pltpu.VMEM((number, held, 2, rows, width), f32),
            pltpu.SemaphoreType.DMA((number, held, 2)),
        ],
        input_output_aliases={} if first else {1 + number: 0, 2 + number: 1},
        compiler_params=kernel_params(12),
        cost_estimate=pl.CostEstimate(flops=0, bytes_accessed=number * held * 12 * rows * width, transcendentals=0),
    )(place, *sources, *([] if first else held_arrays))


def flip(array, axis, bits):
    size = lax.axis_size(axis)
    return lax.ppermute(array, axis, [(i, i ^ bits) for i in range(size)])


def add_low(*arrays):
    level = [a.astype(f32) for a in arrays]
    while len(level) > 1:
        level = [level[i] + level[i + 1] for i in range(0, len(level), 2)]
    return level[0].astype(bf16)


def after(arrays, others):
    return lax.optimization_barrier((arrays, others))[0]


def near(mine, groups):
    if groups == 4 and mine.shape[0] == 2:
        return {1: [flip(mine, "expert", 1)], 2: [flip(mine, "expert", 2)]}
    return {ro: [flip(mine, "expert", ro)] for ro in range(1, groups)}


def relay(arrived, groups, held):
    if groups == 4 and held == 2:
        return {3: [flip(arrived[1][0][:1], "expert", 2), flip(arrived[2][0][1:], "expert", 1)]}
    return {}


def crossed(parts, halves):
    return [] if halves == 1 else [flip(part, "rows", 1) for part in parts]


def body(
    rows_in,
    pred_grad,
    lengths,
    session_type,
    expert_in,
    expert_in_bias,
    expert_out,
    expert_out_bias,
    selector_logits,
    selector_mix,
    tower_in,
    tower_bias,
    tower_out,
):
    height, width = rows_in.shape
    layers, owned = expert_in.shape[:2]
    type_count, tasks = selector_logits.shape[1:3]
    selectors, bits = selector_logits.shape[3:]
    groups = lax.axis_size("expert")
    halves = 2 if owned % 2 == 0 else 1
    held = owned // halves
    stride = 2 * width + EXTRA
    me, row_at = lax.axis_index("expert"), lax.axis_index("rows")
    core = row_at % 2 if halves == 2 else jnp.int32(0)
    place = jnp.stack([(row_at * groups + me) * height, me, core]).astype(jnp.int32)

    def rows_of(layer_at, first):
        cut = lambda a: lax.dynamic_slice(a, (layer_at, first) + (0,) * (a.ndim - 2), (1, held) + a.shape[2:])[0]
        half = lambda a: a * jnp.asarray(0.5, a.dtype)
        tail = []
        for bias in (half(cut(expert_in_bias)), cut(expert_out_bias)):
            high = bias.astype(bf16)
            tail += [high, (bias - high.astype(f32)).astype(bf16)]
        tail = jnp.pad(jnp.stack(tail, axis=1), ((0, 0), (0, EXTRA - len(tail)), (0, 0)))
        return jnp.concatenate([half(cut(expert_in)), cut(expert_out), tail], axis=1)

    first = rows_of(0, held * core)
    asked = near(first, groups)
    sizes = (owned, halves, held, selectors, bits, tasks)
    types, across_types, gate_slopes, *values = prepare_call(
        place, lengths, session_type, selector_logits, selector_mix, height, sizes
    )

    later = after((expert_in, expert_in_bias, expert_out, expert_out_bias), types)
    expert_in, expert_in_bias, expert_out, expert_out_bias = later
    own = [[rows_of(layer_at, held * (core ^ half)) for half in range(halves)] for layer_at in range(layers)]
    own[0][0] = first

    def parts_of(got, across):
        pieces, places = [], {}
        for ro in got:
            spots = []
            for parts in (got[ro], across[ro]):
                here = []
                for part in parts:
                    here += [(len(pieces), at) for at in range(part.shape[0])]
                    pieces.append(part)
                if here:
                    spots.append(here)
            places[ro] = [[spots[half][unit] for half in range(halves)] for unit in range(held)]
        return pieces, places

    def pair_order(places, units):
        return tuple(spot for ro in sorted(places) for unit in units for spot in places[ro][unit])

    streams, stashes, weights = [rows_in], [], []
    for layer_at in range(layers):
        last = layer_at == layers - 1
        got = near(own[layer_at][0], groups) if layer_at else after(asked, (types, own[0][1:], own[1:]))
        far = relay(got, groups, held)
        across = {ro: crossed(got[ro], halves) for ro in got}
        got = {0: own[layer_at][:1], **got}
        across[0] = own[layer_at][1:]
        if not last:
            pieces, places = parts_of(got, across)
            total, stash = forward_call(
                streams[-1], types, values[layer_at], None, None, pieces, pair_order(places, range(held)), 0
            )
            far = after(far, total)
        elif streams[1:]:
            far = after(far, streams[-1])
        far_across = {ro: crossed(far[ro], halves) for ro in far}
        if not last:
            if far:
                pieces, places = parts_of(far, far_across)
                base = held * min(far)
                order = pair_order(places, range(held))
                total, stash = forward_call(
                    streams[-1], types, values[layer_at], total, stash, pieces, order, base
                )
            streams.append(total[0])
            stashes.append(stash)
        weights.append(parts_of({**got, **far}, {**across, **far_across}))

    pieces, places = weights[-1]
    predictions, stream, *payload = middle_call(
        place,
        streams[-1],
        types,
        across_types,
        values[-1],
        gate_slopes,
        (pred_grad.T, tower_in, tower_bias, tower_out),
        pieces,
        pair_order(places, range(held)),
        groups,
        halves,
        held,
    )

    shards = lax.axis_size("rows")
    paired = shards > 2
    hops = ["share"] + [4 << at for at in range(shards.bit_length() - 3)] + ["join"] if paired else []
    upper = (row_at & 2) > 0

    class Moving:
        def __init__(self, layer_at, mine, others):
            self.layer_at, self.mine, self.own = layer_at, mine, None
            self.got = [flip(part, "rows", 1) for part in others]
            self.sums, self.parts, self.total, self.hops = None, None, None, -2

        def ask(self, token):
            if self.hops == -1:
                sums, own = after((self.sums, self.own), token)
                ros = range(1, groups) if self.parts is None else ()
                self.got = [flip(sums[ro - 1], "expert", ro) for ro in ros]
                self.got += [] if own is None else [flip(own[1], "rows", 1)]
                return
            total = after(self.total, token)
            if self.hops == len(hops):
                self.got = [total] + ([flip(total, "rows", 1)] if halves == 2 else [])
            elif hops[self.hops] == "share":
                cut = total.shape[0] // 2
                self.got = [
                    jnp.where(upper, total[cut:], total[:cut]),
                    flip(jnp.where(upper, total[:cut], total[cut:]), "rows", 2),
                ]
            else:
                self.got = [total, flip(total, "rows", 2 if hops[self.hops] == "join" else hops[self.hops])]

        def add(self):
            if self.hops == -2:
                self.sums = [add_low(*pair) for pair in zip(self.mine, self.got)]
            elif self.hops == -1:
                got = self.got
                if self.parts is None:
                    self.parts = []
                    while len(got) >= 1 << len(self.parts) and (1 << len(self.parts)) < groups:
                        size = 1 << len(self.parts)
                        level, got = got[:size], got[size:]
                        while len(level) > 1:
                            level = [add_low(*level[i : i + 2]) for i in range(0, len(level), 2)]
                        self.parts += level
                if self.own is None:
                    return
                self.total = functools.reduce(add_low, self.parts, add_low(self.own[0], got[0]))
            elif hops[self.hops] != "join":
                self.total = add_low(*self.got)
            else:
                here, there = self.got
                self.total = jnp.concatenate([jnp.where(upper, there, here), jnp.where(upper, here, there)])
            self.hops += 1

    def arrive(entries, others):
        got, others = lax.optimization_barrier(([entry.got for entry in entries], others))
        for entry, what in zip(entries, got):
            entry.got = what
            entry.add()
        there = [[x for x in (entry.total, entry.parts, entry.sums) if x is not None][0] for entry in entries]
        return there, others

    assert layers == 2
    mine, left = payload[0], payload[-7:]
    mine = [mine[ro] for ro in range(groups - 1)]
    later = Moving(1, mine, payload[1:-7] or mine)
    token = arrive([later], ())
    stream = after(stream, token)
    later.ask(token)
    pieces, places = weights[0]
    stream, mine, *others = backward_call(
        streams[0],
        types,
        across_types,
        stream,
        gate_slopes,
        values[0],
        stashes[0],
        pieces,
        pair_order(places, range(held)),
        held,
        tasks,
        (values[1], own[1], *left),
    )
    token = arrive([later], stream)
    others, last_own = others[:-halves], others[-halves:]
    mine = [mine[ro] for ro in range(groups)]
    others = others or mine
    earlier = Moving(0, mine[1:], others[1:])
    earlier.own = (mine[0], others[0])
    later.own = (last_own[0], last_own[-1])
    later.ask(())
    token = arrive([earlier, later], token)
    moving = [later, earlier]

    whole = {}
    arrays, tower_sums = None, ()

    def ask(*entries):
        nonlocal arrays, tower_sums
        for entry in entries:
            entry.ask(token)
        for entry in entries:
            if entry.hops < len(hops):
                continue
            moving.remove(entry)
            layer_at, got = entry.layer_at, entry.got
            whole[layer_at] = got
            if layer_at == layers - 1:
                end = got[0][held * stride + type_count // 2 :].astype(f32)
                tower_rows = [array[held * stride + type_count // 2 + EXTRA :].astype(f32) for array in got]
                if halves == 2:
                    tower_rows = [jnp.where(core == 0, *tower_rows), jnp.where(core == 0, *tower_rows[::-1])]
                wide = jnp.concatenate(tower_rows).reshape(tasks, -1, width)
                narrow = tower_in.shape[2]
                parts = [wide[:, :, at : at + narrow] for at in range(0, width, narrow)]
                tower_sums = (
                    jnp.concatenate(parts, axis=1),
                    end[0].reshape(tower_bias.shape),
                    end[1].reshape(tower_out.shape),
                )
            if moving:
                sources = {(layer_at, half): array for half, array in enumerate(got)}
                arrays = finish_call(place, sources, arrays, held, expert_in.shape)

    if len(hops) == 3:
        ask(earlier, later)
        token = arrive([later], ())
        ask(later)
        token = arrive([earlier, later], ())
        ask(earlier)
        token = arrive([earlier], ())
        ask(earlier, later)
        token = arrive([earlier, later], ())
    while moving:
        ask(*moving)
        if moving:
            token = arrive(moving, (arrays, tower_sums))
    ends = [whole[layer_at][0][held * stride : held * stride + type_count].astype(f32) for layer_at in range(layers)]
    cut = type_count // 2
    gate_grads = [ends[0][:cut], ends[1][:cut] + ends[0][cut:]]
    quantities = selectors * (bits + 1)
    small = jnp.stack(gate_grads)
    small = jnp.concatenate([small[..., :LANES], small[..., LANES:]], axis=1)[..., : tasks * quantities]
    small = small.reshape(layers, type_count, tasks, quantities)
    logits_grad = small[..., : selectors * bits].reshape(selector_logits.shape)
    smalls = (logits_grad, small[..., selectors * bits :], *tower_sums)
    got, (arrays, smalls) = lax.optimization_barrier((whole[0], (arrays, smalls)))
    arrays = finish_call(place, {(0, half): array for half, array in enumerate(got)}, arrays, held, expert_in.shape)
    return (
        predictions.T,
        stream,
        arrays[0],
        arrays[2],
        arrays[1],
        arrays[3],
        *smalls,
    )


def solution(mesh):
    in_specs = (
        P(("rows", "expert"), None),
        P(("rows", "expert"), None),
        P(),
        P(),
        P(None, "expert", None, None),
        P(None, "expert", None),
        P(None, "expert", None, None),
        P(None, "expert", None),
        P(),
        P(),
        P(),
        P(),
        P(),
    )
    out_specs = (
        P(("rows", "expert"), None),
        P(("rows", "expert"), None),
        P(None, "expert", None, None),
        P(None, "expert", None),
        P(None, "expert", None, None),
        P(None, "expert", None),
        P(),
        P(),
        P(),
        P(),
        P(),
    )
    return jax.shard_map(body, mesh=mesh, in_specs=in_specs, out_specs=out_specs, check_vma=False)
```

```python
import functools
import math

import jax
import jax.numpy as jnp
import numpy as np
from jax import lax
from jax.experimental import pallas as pl
from jax.experimental.pallas import tpu as pltpu
from jax.sharding import PartitionSpec as P

SHARPNESS = 10.0
EXACT = lax.Precision.HIGHEST
bf16 = jnp.bfloat16
f32 = jnp.float32
INNER = math.sqrt(2.0 / math.pi)
CUBE = 0.044715 * INNER
TILE = 1024
TOWER_TILE = 512
LANES = 128
EXTRA = 16


def mm(a, b):
    return jnp.dot(a, b, preferred_element_type=f32)


def mm_exact(a, b):
    return jnp.dot(a, b, precision=EXACT, preferred_element_type=f32)


def mm_nt(a, b):
    return lax.dot_general(a, b, (((1,), (1,)), ((), ())), preferred_element_type=f32)


def mm_tn(a, b):
    return lax.dot_general(a, b, (((0,), (0,)), ((), ())), preferred_element_type=f32)


def gelu_both(v):
    square = v * v
    half = 0.5 + 0.5 * jnp.tanh(v * (INNER + CUBE * square))
    value = v * half
    slope = half + value * (1.0 - half) * (2.0 * INNER + 6.0 * CUBE * square)
    return value, slope


def gelu_parts(v):
    bend = 2.0 * INNER + 8.0 * CUBE * (v * v)
    twice_share = 1.0 + jnp.tanh(v * bend)
    return v * twice_share, bend, twice_share


def gelu_slope(value, bend, twice_share):
    rise = 3.0 * bend - 4.0 * INNER
    return twice_share + value * (2.0 - twice_share) * rise


FAR = pl.BlockSpec(memory_space=pl.ANY)
NEAR = pl.BlockSpec(memory_space=pltpu.VMEM)
SCALARS = pl.BlockSpec(memory_space=pltpu.SMEM)


def kernel_params(mebibytes):
    return pltpu.CompilerParams(vmem_limit_bytes=mebibytes * 2**20)


def whole_spec(shape):
    zeros = (0,) * len(shape)
    return pl.BlockSpec(shape, lambda i: zeros)


def prepare_kernel(sizes, place_ref, length_ref, kind_ref, logit_ref, mix_ref, spread_logit_ref, spread_mix_ref, *outs):
    owned, halves, held, selectors, bits, tasks = sizes
    type_ref, across_ref, slope_ref, *value_refs = outs
    height, type_count = type_ref.shape
    experts = 2**bits
    sessions = length_ref.shape[1]
    chunk = min(256, sessions)
    position = (place_ref[0] + lax.broadcasted_iota(jnp.int32, (height, 1), 0)).astype(f32)
    earlier = lax.broadcasted_iota(jnp.int32, (chunk, chunk), 0) < lax.broadcasted_iota(jnp.int32, (chunk, chunk), 1)
    earlier = jnp.where(earlier, 1.0, 0.0).astype(bf16)
    kinds = lax.broadcasted_iota(jnp.int32, (type_count, chunk), 0)
    before = jnp.zeros((1, 1), f32)
    types = jnp.zeros((height, type_count), f32)
    across = jnp.zeros((type_count, height), f32)
    for at in range(0, sessions, chunk):
        lengths = length_ref[:, at : at + chunk].astype(f32)
        begin = before + mm(jnp.broadcast_to(lengths.astype(bf16), (EXTRA, chunk)), earlier)[0:1]
        before += jnp.sum(lengths, axis=1, keepdims=True)
        member = jnp.where((position >= begin) & (position < begin + lengths), 1.0, 0.0).astype(bf16)
        of_type = jnp.where(kinds == kind_ref[:, at : at + chunk], 1.0, 0.0).astype(bf16)
        types += mm_nt(member, of_type)
        across += mm_nt(of_type, member)
    type_ref[...] = types.astype(bf16)
    across_ref[...] = across.astype(bf16)

    rows = logit_ref.shape[0]
    place = lax.broadcasted_iota(jnp.int32, (rows, LANES), 1) % experts
    expert = (
        owned * ((place // owned) ^ place_ref[1])
        + held * ((place % halves) ^ place_ref[2])
        + (place // halves) % held
    )
    logits = mm_exact(logit_ref[...], spread_logit_ref[...])
    mixes = mm_exact(mix_ref[...], spread_mix_ref[...])
    mixes = [mixes[:, k * LANES : (k + 1) * LANES] for k in range(selectors)]
    top = functools.reduce(jnp.maximum, mixes)
    shares = [jnp.exp(mix - top) for mix in mixes]
    whole = functools.reduce(jnp.add, shares)
    shares = [share / whole for share in shares]
    value = jnp.zeros((rows, LANES), f32)
    reaches = []
    for k in range(selectors):
        factors, signed = [], []
        for bit in range(bits):
            at = (k * bits + bit) * LANES
            logit = logits[:, at : at + LANES]
            cubic = (-2.0 / SHARPNESS**3) * logit * logit * logit + (1.5 / SHARPNESS) * logit + 0.5
            step = jnp.where(logit <= -SHARPNESS / 2, 0.0, jnp.where(logit >= SHARPNESS / 2, 1.0, cubic))
            slope = (-6.0 / SHARPNESS**3) * logit * logit + 1.5 / SHARPNESS
            slope = jnp.where((logit > -SHARPNESS / 2) & (logit < SHARPNESS / 2), slope, 0.0)
            on = (expert >> bit) & 1 == 1
            factors.append(jnp.where(on, step, 1.0 - step))
            signed.append(jnp.where(on, slope, -slope))
        reaches.append(functools.reduce(jnp.multiply, factors))
        value += shares[k] * reaches[k]
        for bit in range(bits):
            others = [factors[b] for b in range(bits) if b != bit]
            slope_ref[k * bits + bit] = shares[k] * signed[bit] * functools.reduce(jnp.multiply, others)
    for k in range(selectors):
        slope_ref[selectors * bits + k] = shares[k] * (reaches[k] - value)

    value = value.astype(bf16).astype(f32)
    for layer_at, ref in enumerate(value_refs):
        table = value[layer_at * type_count : (layer_at + 1) * type_count]
        columns = [table[:, t * experts : (t + 1) * experts] for t in range(tasks)]
        if layer_at < len(value_refs) - 1:
            columns = [functools.reduce(jnp.add, columns) / tasks]
        for pair in range(ref.shape[0]):
            lanes = []
            for half in range(halves):
                at = pair * halves + half
                lanes += [jnp.broadcast_to(c[:, at : at + 1], (type_count, LANES)) for c in columns]
            ref[pair] = jnp.concatenate(lanes, axis=1).astype(bf16)


def prepare_call(place, lengths, session_type, logits, mixing, height, sizes):
    owned, halves, held, selectors, bits, tasks = sizes
    layers, type_count = logits.shape[:2]
    experts = 2**bits
    rows = layers * type_count
    lane = np.arange(LANES)
    source = np.arange(tasks * selectors * bits)
    task, number = source // (selectors * bits), source % (selectors * bits)
    mine = (lane[None, :] // experts == task[:, None])[:, None, :]
    spread_logit = mine & (number[:, None, None] == np.arange(selectors * bits)[None, :, None])
    source = np.arange(tasks * selectors)
    mine = (lane[None, :] // experts == (source // selectors)[:, None])[:, None, :]
    spread_mix = mine & ((source % selectors)[:, None, None] == np.arange(selectors)[None, :, None])
    spread_logit = spread_logit.reshape(spread_logit.shape[0], -1).astype(np.float32)
    spread_mix = spread_mix.reshape(spread_mix.shape[0], -1).astype(np.float32)
    outs = [
        jax.ShapeDtypeStruct((height, type_count), bf16),
        jax.ShapeDtypeStruct((type_count, height), bf16),
        jax.ShapeDtypeStruct((selectors * (bits + 1), rows, LANES), f32),
    ]
    for layer_at in range(layers):
        each = tasks if layer_at == layers - 1 else 1
        outs.append(jax.ShapeDtypeStruct((experts // halves, type_count, halves * each * LANES), bf16))
    return pl.pallas_call(
        functools.partial(prepare_kernel, sizes),
        out_shape=outs,
        in_specs=[SCALARS] + [NEAR] * 6,
        out_specs=[NEAR] * len(outs),
        compiler_params=kernel_params(58),
        cost_estimate=pl.CostEstimate(flops=2 * height * lengths.size * 64, bytes_accessed=2**21, transcendentals=2**16),
    )(
        place,
        lengths.reshape(1, -1),
        session_type.reshape(1, -1),
        logits.reshape(rows, -1),
        mixing.reshape(rows, -1),
        spread_logit,
        spread_mix,
    )


def bias_rows(weights, width):
    rows = weights[2 * width : 2 * width + EXTRA].astype(f32)
    return rows[0:1] + rows[1:2], rows[2:3] + rows[3:4]


def twice(a):
    return jnp.concatenate([a, a], axis=1)


def tiles(height, most):
    tile = min(most, height)
    return [pl.ds(at, tile) for at in range(0, height, tile)]


def joined(parts, axis):
    return parts[0] if len(parts) == 1 else jnp.concatenate(parts, axis=axis)


def gates_of(types, value_ref, count):
    gates = mm(types, value_ref[...]).astype(bf16)
    return [gates[:, at * LANES : (at + 1) * LANES] for at in range(count)]


def forward_step(weights, value_ref, x_low, type_ref, total_ref, biases, keep, keep_gate=None, keep_result=None):
    height, width = x_low.shape
    kinds = total_ref.shape[0]
    bias_in, bias_out = zip(*(bias_rows(w, width) for w in weights))
    second = joined([w[width : 2 * width] for w in weights], 0)
    for rows in tiles(height, TILE):
        gates = gates_of(type_ref[rows], value_ref, len(weights) * kinds)
        if keep_gate is not None:
            for at, gate in enumerate(gates):
                keep_gate(at, rows, gate)
        scaled = [[] for _ in range(kinds)]
        for i, w in enumerate(weights):
            before = mm(x_low[rows], w[0:width]) + bias_in[i]
            hidden, bend, twice_share = gelu_parts(before)
            hidden = hidden.astype(bf16)
            keep(i, rows, hidden, gelu_slope(hidden, bend.astype(bf16), twice_share.astype(bf16)))
            if keep_result is not None:
                result = mm(hidden, w[width : 2 * width]).astype(bf16)
                keep_result(i, rows, result)
            for t in range(kinds):
                scaled[t].append(twice(gates[i * kinds + t]) * (hidden if keep_result is None else result))
        for t in range(kinds):
            if keep_result is None:
                total_ref[t, rows] += mm(joined(scaled[t], 1), second)
            else:
                total_ref[t, rows] += functools.reduce(jnp.add, scaled[t]).astype(f32)
    for i in range(len(weights)):
        for t in range(kinds):
            at = (i * kinds + t) * LANES
            biases[t] += twice(value_ref[:, at : at + LANES].astype(f32)) * bias_out[i]


def forward_end(type_ref, total_ref, biases):
    for t in range(total_ref.shape[0]):
        high = biases[t].astype(bf16)
        rest = (biases[t] - high.astype(f32)).astype(bf16)
        for rows in tiles(total_ref.shape[1], TILE):
            total_ref[t, rows] += mm(twice(type_ref[rows]), jnp.concatenate([high, rest], axis=0))


def backward_start(x_low, type_across, low, across, share):
    width = x_low.shape[1]
    across[0:width] = x_low[...].T
    ones = lax.broadcasted_iota(jnp.int32, (EXTRA, x_low.shape[0]), 0) == 0
    across[width:] = jnp.where(ones, 1.0, 0.0).astype(bf16)
    for t in range(low.shape[0]):
        share[t] = mm(type_across[...], low[t])


def backward_step(weights, value_ref, hiddens, slopes, outs, pair, experts, type_ref, type_across, low, stream_ref, across, share, table, scratch, kept_gates=None, results=None, dots=None, gate_lanes=None):
    before_grads, result_grads = scratch
    kinds, height, width = low.shape
    count = len(weights)
    first = joined([w[0:width] for w in weights], 1)
    for rows in tiles(height, TILE):
        if kept_gates is None:
            gates = gates_of(type_ref[rows], value_ref, count * kinds)
        else:
            gates = [kept_gates[at, rows] for at in range(count * kinds)]
        gates = [twice(gate) for gate in gates]
        befores = []
        for i, w in enumerate(weights):
            hidden, slope = hiddens[i][rows], slopes[i][rows]
            second = w[width : 2 * width]
            result_grad = gates[i * kinds] * low[0, rows]
            for t in range(1, kinds):
                result_grad += gates[i * kinds + t] * low[t, rows]
            hidden_grad = mm_nt(result_grad, second).astype(bf16)
            for t in range(kinds):
                product = hidden * hidden_grad if results is None else results[i][rows] * low[t, rows]
                product = functools.reduce(
                    jnp.add, [product[:, lane : lane + LANES] for lane in range(0, width, LANES)]
                )
                found = jnp.sum(product.astype(f32), axis=1, keepdims=True)
                lanes = lax.broadcasted_iota(jnp.int32, (1, LANES), 1)
                place = pair * count + i
                chosen = lanes % experts == place if kinds == 1 else lanes == t * experts + place
                dots[rows] = jnp.where(chosen, found, dots[rows])
            before = slope * hidden_grad
            before_grads[i, rows] = before
            result_grads[i, rows] = result_grad
            befores.append(before)
        stream_ref[rows] += mm_nt(joined(befores, 1), first)
    lanes = lax.broadcasted_iota(jnp.int32, (type_ref.shape[1], LANES), 1)
    for i, w in enumerate(weights):
        _, bias_out = bias_rows(w, width)
        first_grad = 0.5 * mm(across[...], before_grads[i])
        outs[i][0:width] = first_grad[0:width].astype(bf16)
        outs[i][width : 2 * width] = mm_tn(hiddens[i][...], result_grads[i]).astype(bf16)
        out_bias = jnp.zeros((1, width), f32)
        place = pair * count + i
        for t in range(kinds):
            at = (i * kinds + t) * LANES
            gate = value_ref[:, at : at + LANES].astype(f32)
            out_bias += jnp.sum(twice(gate) * share[t], axis=0, keepdims=True)
            bias_part = jnp.sum(share[t] * bias_out, axis=1, keepdims=True)
            if kinds == 1:
                table[...] = jnp.where(lanes % experts == place, 0.5 * bias_part, table[...])
                gate_lanes[...] = jnp.where(lanes % experts == place, gate, gate_lanes[...])
            else:
                table[...] = jnp.where(lanes == t * experts + place, bias_part, table[...])
        tail = jnp.concatenate([first_grad[width : width + 1], out_bias, jnp.zeros((EXTRA - 2, width), f32)])
        outs[i][2 * width : 2 * width + EXTRA] = tail.astype(bf16)


def by_type(type_across, dots):
    high = dots[...].astype(bf16)
    rest = (dots[...] - high.astype(f32)).astype(bf16)
    return mm(type_across[...], high) + mm(type_across[...], rest)


def through_gates(table, gate_slope_ref, experts, tasks):
    quantities, type_count = gate_slope_ref.shape[:2]
    lanes = lax.broadcasted_iota(jnp.int32, (type_count, LANES), 1)
    small = jnp.zeros((type_count, LANES), f32)
    for q in range(quantities):
        product = gate_slope_ref[q] * table[...]
        for t in range(tasks):
            part = jnp.sum(jnp.where(lanes // experts == t, product, 0.0), axis=1, keepdims=True)
            small = jnp.where(lanes == t * quantities + q, part, small)
    half = type_count // 2
    return jnp.concatenate([small[:half], small[half:]], axis=1).astype(bf16)


def store_copies(ready, pair, held, out_refs, sems):
    group, unit = pair // held, lax.rem(pair, held)
    rows = pl.ds(pl.multiple_of(unit * ready.shape[1], EXTRA), ready.shape[1])
    copies = [(None, pltpu.make_async_copy(ready.at[0], out_refs[0].at[group, rows], sems.at[0]))]
    for at, ref in enumerate(out_refs[1:]):
        copies.append((group == at, pltpu.make_async_copy(ready.at[1], ref.at[rows], sems.at[1])))
    return copies


def end_copies(ends, out_refs, sems):
    rows = out_refs[0].shape[1]
    last = pl.ds(rows - ends.shape[1], ends.shape[1])
    groups = out_refs[0].shape[0]
    copies = [pltpu.make_async_copy(ends.at[0], out_refs[0].at[at, last], sems.at[0, at]) for at in range(groups)]
    copies += [
        pltpu.make_async_copy(ends.at[1], ref.at[last], sems.at[1, at]) for at, ref in enumerate(out_refs[1:])
    ]
    return [(None, copy) for copy in copies]


def for_each(copies, act):
    for condition, copy in copies:
        if condition is None:
            act(copy)
        else:
            pl.when(condition)(functools.partial(act, copy))


def start(copy):
    copy.start()


def wait(copy):
    copy.wait()


def fetch_weights(places, buffer, sems, each):
    step = pl.program_id(0)
    for of in range(len(places) // each):

        @pl.when(step == max(of - 1, 0))
        def _(of=of):
            for i, (ref, at) in enumerate(places[of * each : (of + 1) * each]):
                pltpu.make_async_copy(ref.at[at], buffer.at[of % 2, i], sems.at[of % 2, i]).start()

    slot = lax.rem(step, 2)
    for i in range(each):
        ref, at = places[0]
        pltpu.make_async_copy(ref.at[at], buffer.at[slot, i], sems.at[slot, i]).wait()
    return [buffer.at[slot, i] for i in range(each)]


def forward_kernel(places, pieces, each, first, *refs):
    refs = list(refs)
    take = lambda count: [refs.pop(0) for _ in range(count)]
    x_ref, type_ref, value_ref = take(3)
    if not first:
        total_ref, _, _ = take(3)
    weight_refs = take(pieces)
    out_ref, hidden_ref, slope_ref, x_low, biases, buffer, sems = take(7)
    step = pl.program_id(0)
    weights = fetch_weights([(weight_refs[piece], at) for piece, at in places], buffer, sems, each)

    @pl.when(step == 0)
    def _():
        x_low[...] = x_ref[...].astype(bf16)
        biases[...] = jnp.zeros_like(biases)
        out_ref[0] = x_ref[...] if first else total_ref[0]

    def keep(i, rows, hidden, slope):
        hidden_ref[0, i, rows] = hidden
        slope_ref[0, i, rows] = slope

    forward_step(weights, value_ref.at[0], x_low, type_ref, out_ref, biases, keep)

    @pl.when(step == pl.num_programs(0) - 1)
    def _():
        forward_end(type_ref, out_ref, biases)


def forward_call(x, types, values, total, stash, pieces, places, base):
    height, width = x.shape
    pairs, type_count, lanes = values.shape
    each = lanes // LANES
    operands = [x, types, values]
    specs = [whole_spec(x.shape), whole_spec(types.shape)]
    specs.append(pl.BlockSpec((1, type_count, lanes), lambda i: (base + i, 0, 0)))
    aliases = {}
    if total is not None:
        operands += [total, *stash]
        specs += [whole_spec(total.shape), FAR, FAR]
        aliases = {4: 1, 5: 2}
    summed = jax.ShapeDtypeStruct((1, height, width), f32)
    kept = jax.ShapeDtypeStruct((pairs, each, height, width), bf16)
    kept_spec = pl.BlockSpec((1, each, height, width), lambda i: (base + i, 0, 0, 0))
    number = len(places)
    results = pl.pallas_call(
        functools.partial(forward_kernel, places, len(pieces), each, total is None),
        grid=(number // each,),
        out_shape=[summed, kept, kept],
        in_specs=specs + [whole_spec(piece.shape) for piece in pieces],
        out_specs=[whole_spec(summed.shape), kept_spec, kept_spec],
        scratch_shapes=[
            pltpu.VMEM((height, width), bf16),
            pltpu.VMEM((1, type_count, width), f32),
            pltpu.VMEM((2, each, *pieces[0].shape[1:]), bf16),
            pltpu.SemaphoreType.DMA((2, each)),
        ],
        input_output_aliases=aliases,
        compiler_params=kernel_params(58),
        cost_estimate=pl.CostEstimate(
            flops=4 * number * height * width * width,
            bytes_accessed=number * (4 * width * width + 4 * height * width) + 8 * height * width,
            transcendentals=number * height * width,
        ),
    )(*operands, *pieces)
    return results[0], results[1:]


def middle_kernel(places, pieces, groups, halves, held, *refs):
    refs = list(refs)
    take = lambda count: [refs.pop(0) for _ in range(count)]
    place_ref, x_ref, type_ref, across_types_ref, value_ref, gate_slope_ref, pred_grad_ref = take(7)
    tower_in_ref, tower_bias_ref, tower_out_ref = take(3)
    weight_refs = take(pieces)
    pred_ref, stream_ref = take(2)
    out_refs = take(1 + (groups - 1) * (halves - 1))
    left_refs = take(7)
    x_low, weights, hidden_all, slope_all, result_all, gates_all, total, biases, low, across, share, table = take(12)
    before_grads, result_grads, dots, cotangents, ready, ends, in_grad, bias_grad, out_grad, load_sem, store_sem, end_sem, left_sem = take(13)
    height, width = x_ref.shape
    pairs = value_ref.shape[0]
    experts = pairs * halves
    tasks = total.shape[0]

    def load(pair, i, ref, at):
        return pltpu.make_async_copy(ref.at[at], weights.at[pair, i], load_sem.at[pair, i])

    for j, (piece, at) in enumerate(places):
        load(j // halves, j % halves, weight_refs[piece], at).start()
    x_low[...] = x_ref[...].astype(bf16)
    biases[...] = jnp.zeros_like(biases)
    for t in range(tasks):
        total[t] = x_ref[...]

    def forward_pair(pair, carry):
        for i in range(halves):
            load(pair, i, weight_refs[0], 0).wait()

        def keep(i, rows, hidden, slope):
            hidden_all[pair, i, rows] = hidden
            slope_all[pair, i, rows] = slope

        def keep_gate(at, rows, gate):
            gates_all[pair, at, rows] = gate

        def keep_result(i, rows, result):
            result_all[pair, i, rows] = result

        forward_step(
            [weights.at[pair, i] for i in range(halves)],
            value_ref.at[pair],
            x_low,
            type_ref,
            total,
            biases,
            keep,
            keep_gate,
            keep_result,
        )
        return carry

    lax.fori_loop(0, pairs, forward_pair, 0)
    forward_end(type_ref, total, biases)

    def left(at, source):
        return pltpu.make_async_copy(source, left_refs[at], left_sem.at[at])

    own = [kept.at[0:held] for kept in (hidden_all, slope_all, result_all)]
    for at, source in enumerate(own):
        left(at, source).start()

    cotangents[...] = jnp.concatenate(
        [pred_grad_ref[...], jnp.zeros((cotangents.shape[1] - tasks, height), f32)]
    ).T
    in_grad[...] = jnp.zeros_like(in_grad)
    bias_grad[...] = jnp.zeros_like(bias_grad)
    out_grad[...] = jnp.zeros_like(out_grad)
    for rows in tiles(height, TOWER_TILE):
        summed = None
        predicted = []
        for t in range(tasks):
            closing_low = total[t, rows].astype(bf16)
            act, slope = gelu_both(mm(closing_low, tower_in_ref[t]) + tower_bias_ref[t : t + 1])
            vector = tower_out_ref[t : t + 1]
            predicted.append(jnp.sum(act * vector, axis=1, keepdims=True))
            cotangent = cotangents[rows, t : t + 1]
            out_grad[t : t + 1] += jnp.sum(act * cotangent, axis=0, keepdims=True)
            before_grad = (slope * (cotangent * vector)).astype(bf16)
            bias_grad[t : t + 1] += jnp.sum(before_grad.astype(f32), axis=0, keepdims=True)
            in_grad[t] += mm_tn(closing_low, before_grad)
            closing_grad = mm_nt(before_grad, tower_in_ref[t])
            low[t, rows] = closing_grad.astype(bf16)
            summed = closing_grad if summed is None else summed + closing_grad
        stream_ref[rows] = summed
        blank = jnp.zeros((predicted[0].shape[0], cotangents.shape[1] - tasks), f32)
        pred_ref[:, rows] = jnp.concatenate([*predicted, blank], axis=1).T[0:tasks]
    narrow = in_grad.shape[2]
    tall = width * narrow // width
    begin = type_ref.shape[1] // 2 + EXTRA
    for t in range(tasks):
        wide = jnp.concatenate([in_grad[t, :tall], in_grad[t, tall:]], axis=1).astype(bf16)
        if halves == 2:
            ends[place_ref[2] ^ t, begin:] = wide
        else:
            ends[0, begin + t * tall : begin + (t + 1) * tall] = wide
    vectors = [jnp.concatenate([ref[0:1], ref[1:2]], axis=1) for ref in (bias_grad, out_grad)]
    vectors = jnp.concatenate([*vectors, jnp.zeros((EXTRA - 2, width), f32)]).astype(bf16)
    for half in range(halves):
        ends[half, begin - EXTRA : begin] = vectors

    left(3, low).start()
    backward_start(x_low, across_types_ref, low, across, share)
    left(4, across).start()
    left(5, share).start()
    table[...] = jnp.zeros_like(table)
    dots[...] = jnp.zeros_like(dots)

    def stores(pair):
        return store_copies(ready.at[pair], pair - held, held, out_refs, store_sem.at[pair])

    def backward_pair(pair, carry):
        backward_step(
            [weights.at[pair, i] for i in range(halves)],
            value_ref.at[pair],
            [hidden_all.at[pair, i] for i in range(halves)],
            [slope_all.at[pair, i] for i in range(halves)],
            [ready.at[pair, i] for i in range(halves)],
            pair,
            experts,
            type_ref,
            across_types_ref,
            low,
            stream_ref,
            across,
            share,
            table,
            (before_grads, result_grads),
            gates_all.at[pair],
            [result_all.at[pair, i] for i in range(halves)],
            dots,
        )
        for_each(stores(pair), start)
        return carry

    lax.fori_loop(held, pairs, backward_pair, 0)
    table[...] += by_type(across_types_ref, dots)
    small = through_gates(table, gate_slope_ref, experts, tasks)
    for half in range(halves):
        ends[half, 0 : small.shape[0]] = small
    left(6, ends).start()
    for_each(end_copies(ends, out_refs, end_sem), start)

    def drain(pair, carry):
        for_each(stores(pair), wait)
        return carry

    lax.fori_loop(held, pairs, drain, 0)
    for_each(end_copies(ends, out_refs, end_sem), wait)
    for at, source in enumerate([*own, low, across, share, ends]):
        left(at, source).wait()


def middle_call(place, x, types, across_types, values, gate_slopes, tower, pieces, places, groups, halves, held):
    height, width = x.shape
    pairs, type_count, lanes = values.shape
    pred_grad, tower_in, tower_bias, tower_out = tower
    tasks = tower_in.shape[0]
    stride = 2 * width + EXTRA
    experts = pairs * halves
    outs = [jax.ShapeDtypeStruct(shape, f32) for shape in (pred_grad.shape, (height, width))]
    near = len(outs)
    end_rows = type_count // 2 + EXTRA + tower_in.size // width // halves
    rows = held * stride + end_rows
    outs.append(jax.ShapeDtypeStruct((groups - 1, rows, width), bf16))
    outs += [jax.ShapeDtypeStruct((rows, width), bf16)] * ((groups - 1) * (halves - 1))
    outs += [jax.ShapeDtypeStruct((held, halves, height, width), bf16)] * 3
    outs.append(jax.ShapeDtypeStruct((tasks, height, width), bf16))
    outs.append(jax.ShapeDtypeStruct((width + EXTRA, height), bf16))
    outs.append(jax.ShapeDtypeStruct((tasks, type_count, width), f32))
    outs.append(jax.ShapeDtypeStruct((halves, end_rows, width), bf16))
    layer_at = gate_slopes.shape[1] // type_count - 1
    slope_spec = pl.BlockSpec((gate_slopes.shape[0], type_count, LANES), lambda i: (0, layer_at, 0))
    kept = pltpu.VMEM((pairs, halves, height, width), bf16)
    operands = [x, types, across_types, values, gate_slopes, *tower]
    specs = [whole_spec(a.shape) for a in operands]
    specs[4] = slope_spec
    return pl.pallas_call(
        functools.partial(middle_kernel, places, len(pieces), groups, halves, held),
        grid=(1,),
        out_shape=outs,
        in_specs=[SCALARS] + specs + [whole_spec(a.shape) for a in pieces[:halves]] + [FAR] * (len(pieces) - halves),
        out_specs=[whole_spec(out.shape) for out in outs[:near]] + [FAR] * (len(outs) - near),
        scratch_shapes=[
            pltpu.VMEM((height, width), bf16),
            pltpu.VMEM((pairs, halves, stride, width), bf16),
            kept,
            kept,
            kept,
            pltpu.VMEM((pairs, halves * tasks, height, LANES), bf16),
            pltpu.VMEM((tasks, height, width), f32),
            pltpu.VMEM((tasks, type_count, width), f32),
            pltpu.VMEM((tasks, height, width), bf16),
            pltpu.VMEM((width + EXTRA, height), bf16),
            pltpu.VMEM((tasks, type_count, width), f32),
            pltpu.VMEM((type_count, LANES), f32),
            pltpu.VMEM((halves, height, width), bf16),
            pltpu.VMEM((halves, height, width), bf16),
            pltpu.VMEM((height, LANES), f32),
            pltpu.VMEM((height, LANES), f32),
            pltpu.VMEM((pairs, halves, stride, width), bf16),
            pltpu.VMEM((halves, end_rows, width), bf16),
            pltpu.VMEM(tower_in.shape, f32),
            pltpu.VMEM(tower_bias.shape, f32),
            pltpu.VMEM(tower_out.shape, f32),
            pltpu.SemaphoreType.DMA((pairs, halves)),
            pltpu.SemaphoreType.DMA((pairs, halves)),
            pltpu.SemaphoreType.DMA((halves, groups)),
            pltpu.SemaphoreType.DMA((7,)),
        ],
        compiler_params=kernel_params(58),
        cost_estimate=pl.CostEstimate(
            flops=14 * experts * height * width * width,
            bytes_accessed=experts * 8 * width * width + 16 * height * width,
            transcendentals=experts * height * width,
        ),
    )(place, *operands, *pieces)


def backward_kernel(places, pieces, each, held, tasks, *refs):
    refs = list(refs)
    take = lambda count: [refs.pop(0) for _ in range(count)]
    x_ref, type_ref, across_types_ref, stream_ref, gate_slope_ref, value_ref, hidden_ref, slope_ref = take(8)
    last_value_ref, last_low_ref, last_across_ref, last_share_ref, last_end_ref = take(5)
    last_refs, last_weight_refs = take(3), take(each)
    weight_refs = take(pieces)
    stream_out_ref = take(1)[0]
    groups = len(places) // each // held
    out_refs = take(1 + groups * (each - 1))
    last_out_refs = take(each)
    x_low, across, low, share, table, before_grads, result_grads, gate_lanes, buffer, ready, ends = take(11)
    x_wide, gate_slopes, last_table, dots, kept, last_weights, last_ready = take(7)
    sems, store_sem, end_sem, last_sem, last_store_sem, late_sem = take(6)
    step = pl.program_id(0)
    slot = lax.rem(step, 2)
    experts = len(places)
    types = type_ref.shape[1]
    stride = buffer.shape[2]
    scratch = (before_grads, result_grads)
    weights = fetch_weights([(weight_refs[piece], at) for piece, at in places], buffer, sems, each)

    late = [
        (None, pltpu.make_async_copy(source, target, late_sem.at[at]))
        for at, (source, target) in enumerate(((x_ref, x_wide), (gate_slope_ref, gate_slopes)))
    ]

    def last_loads(unit):
        copies = [
            pltpu.make_async_copy(last_refs[which].at[unit], kept.at[which, unit], last_sem.at[unit, which])
            for which in range(3)
        ]
        for half in range(each):
            source, sem = last_weight_refs[half].at[unit], last_sem.at[unit, 3 + half]
            copies.append(pltpu.make_async_copy(source, last_weights.at[unit, half], sem))
        return [(None, copy) for copy in copies]

    def last_stores():
        copies = []
        for half, ref in enumerate(last_out_refs):
            for unit in range(held):
                rows = pl.ds(unit * stride, stride)
                copies.append(
                    pltpu.make_async_copy(last_ready.at[unit, half], ref.at[rows], last_store_sem.at[half, unit])
                )
            rows = pl.ds(held * stride, last_end_ref.shape[1])
            copies.append(pltpu.make_async_copy(last_end_ref.at[half], ref.at[rows], last_store_sem.at[half, held]))
        return [(None, copy) for copy in copies]

    @pl.when(step == 0)
    def _():
        for unit in range(held):
            for_each(last_loads(unit), start)
        for_each(late, start)
        stream_out_ref[...] = stream_ref[...]
        last_table[...] = jnp.zeros_like(last_table)
        dots[...] = jnp.zeros_like(dots)

        def last_pair(unit, carry):
            for_each(last_loads(unit), wait)
            backward_step(
                [last_weights.at[unit, i] for i in range(each)],
                last_value_ref.at[unit],
                [kept.at[0, unit, i] for i in range(each)],
                [kept.at[1, unit, i] for i in range(each)],
                [last_ready.at[unit, i] for i in range(each)],
                unit,
                experts,
                type_ref,
                across_types_ref,
                last_low_ref,
                stream_out_ref,
                last_across_ref,
                last_share_ref,
                last_table,
                scratch,
                None,
                [kept.at[2, unit, i] for i in range(each)],
                dots,
            )
            return carry

        lax.fori_loop(0, held, last_pair, 0)
        for_each(last_stores(), start)
        last_table[...] += by_type(across_types_ref, dots)
        dots[...] = jnp.zeros_like(dots)
        for_each(late[:1], wait)
        x_low[...] = x_wide[...].astype(bf16)
        low[0] = stream_out_ref[...].astype(bf16)
        table[...] = jnp.zeros_like(table)
        gate_lanes[...] = jnp.zeros_like(gate_lanes)
        backward_start(x_low, across_types_ref, low, across, share)

    def stores(pair):
        at = lax.rem(pair, 2)
        return store_copies(ready.at[at], pair, held, out_refs, store_sem.at[at])

    @pl.when(step >= 2)
    def _():
        for_each(stores(step - 2), wait)

    backward_step(
        weights,
        value_ref.at[0],
        [hidden_ref.at[0, i] for i in range(each)],
        [slope_ref.at[0, i] for i in range(each)],
        [ready.at[slot, i] for i in range(each)],
        step,
        experts,
        type_ref,
        across_types_ref,
        low,
        stream_out_ref,
        across,
        share,
        table,
        scratch,
        None,
        None,
        dots,
        gate_lanes,
    )

    for_each(stores(step), start)

    @pl.when(step == pl.num_programs(0) - 1)
    def _():
        for_each(late[1:], wait)
        gate = gate_lanes[...]
        found = 0.5 * by_type(across_types_ref, dots) / jnp.where(gate > 0.0, gate, 1.0)
        table[...] += jnp.where(gate > 0.0, found, 0.0)
        both = ((table, 0), (last_table, types))
        small = [through_gates(part, gate_slopes.at[:, pl.ds(at, types)], experts, tasks) for part, at in both]
        for half in range(each):
            ends[half] = jnp.concatenate(small)
        for_each(end_copies(ends, out_refs, end_sem), start)
        for_each(stores(step - 1), wait)
        for_each(stores(step), wait)
        for_each(end_copies(ends, out_refs, end_sem), wait)
        for_each(last_stores(), wait)


def backward_call(x, types, across_types, stream, gate_slopes, values, stash, pieces, places, held, tasks, last):
    height, width = x.shape
    pairs, type_count, lanes = values.shape
    each = lanes // LANES
    groups = pairs // held
    stride = 2 * width + EXTRA
    last_values, last_weights, *last_kept, last_low, last_across, last_share, last_ends = last
    operands = [x, types, across_types, stream, gate_slopes, values, *stash]
    specs = [FAR, *[whole_spec(a.shape) for a in operands[1:4]], FAR]
    specs.append(pl.BlockSpec((1, type_count, lanes), lambda i: (i, 0, 0)))
    specs += [pl.BlockSpec((1, each, height, width), lambda i: (i, 0, 0, 0))] * 2
    near = [last_low, last_across, last_share, last_ends]
    operands += [last_values, *near, *last_kept, *last_weights]
    specs.append(pl.BlockSpec((held, *last_values.shape[1:]), lambda i: (0, 0, 0)))
    specs += [whole_spec(a.shape) for a in near]
    specs += [FAR] * (len(last_kept) + each)
    rows = held * stride + type_count
    mine = jax.ShapeDtypeStruct((groups, rows, width), bf16)
    others = [jax.ShapeDtypeStruct((rows, width), bf16)] * (groups * (each - 1))
    others += [jax.ShapeDtypeStruct((held * stride + last_ends.shape[1], width), bf16)] * each
    number = pairs * each
    return pl.pallas_call(
        functools.partial(backward_kernel, places, len(pieces), each, held, tasks),
        grid=(pairs,),
        out_shape=[jax.ShapeDtypeStruct(stream.shape, f32), mine, *others],
        in_specs=specs + [FAR] * len(pieces),
        out_specs=[whole_spec(stream.shape)] + [FAR] * (1 + len(others)),
        scratch_shapes=[
            pltpu.VMEM((height, width), bf16),
            pltpu.VMEM((width + EXTRA, height), bf16),
            pltpu.VMEM((1, height, width), bf16),
            pltpu.VMEM((1, type_count, width), f32),
            pltpu.VMEM((type_count, LANES), f32),
            pltpu.VMEM((each, height, width), bf16),
            pltpu.VMEM((each, height, width), bf16),
            pltpu.VMEM((type_count, LANES), f32),
            pltpu.VMEM((2, each, stride, width), bf16),
            pltpu.VMEM((2, each, stride, width), bf16),
            pltpu.VMEM((each, type_count, width), bf16),
            pltpu.VMEM((height, width), f32),
            pltpu.VMEM(gate_slopes.shape, f32),
            pltpu.VMEM((type_count, LANES), f32),
            pltpu.VMEM((height, LANES), f32),
            pltpu.VMEM((3, held, each, height, width), bf16),
            pltpu.VMEM((held, each, stride, width), bf16),
            pltpu.VMEM((held, each, stride, width), bf16),
            pltpu.SemaphoreType.DMA((2, each)),
            pltpu.SemaphoreType.DMA((2, each)),
            pltpu.SemaphoreType.DMA((each, groups)),
            pltpu.SemaphoreType.DMA((held, 3 + each)),
            pltpu.SemaphoreType.DMA((each, held + 1)),
            pltpu.SemaphoreType.DMA((2,)),
        ],
        compiler_params=kernel_params(58),
        cost_estimate=pl.CostEstimate(
            flops=10 * number * height * width * width,
            bytes_accessed=number * (8 * width * width + 4 * height * width) + 16 * height * width,
            transcendentals=0,
        ),
    )(*operands, *pieces)


def finish_kernel(names, held, rows, first, *refs):
    place_ref, *refs = refs
    sources, refs = refs[: len(names)], refs[len(names) :]
    in_ref, out_ref, in_bias_out_ref, out_bias_out_ref, ready, sems = refs[-6:]
    in_bias_out_ref[...] = jnp.zeros_like(in_bias_out_ref) if first else refs[2][...]
    out_bias_out_ref[...] = jnp.zeros_like(out_bias_out_ref) if first else refs[3][...]
    copies = []
    for at, ((layer_at, half), source) in enumerate(zip(names, sources)):
        for unit in range(held):
            base = unit * (2 * rows + EXTRA)
            where = held * (place_ref[2] ^ half) + unit
            for which, ref in enumerate((in_ref, out_ref)):
                begin = base + which * rows
                ready[at, unit, which] = source[begin : begin + rows].astype(f32)
                copy = pltpu.make_async_copy(
                    ready.at[at, unit, which], ref.at[layer_at, where], sems.at[at, unit, which]
                )
                copy.start()
                copies.append(copy)
            tail = source[base + 2 * rows : base + 2 * rows + EXTRA].astype(f32)
            in_bias_out_ref[layer_at, pl.ds(where, 1)] = tail[0:1]
            out_bias_out_ref[layer_at, pl.ds(where, 1)] = tail[1:2]
    for copy in copies:
        copy.wait()


def finish_call(place, named, held_arrays, held, shape):
    rows, width = shape[2:]
    names, sources = tuple(named), list(named.values())
    outs = [jax.ShapeDtypeStruct(shape, f32)] * 2
    outs += [jax.ShapeDtypeStruct((*shape[:2], width), f32)] * 2
    first = held_arrays is None
    number = len(names)
    return pl.pallas_call(
        functools.partial(finish_kernel, names, held, rows, first),
        out_shape=outs,
        in_specs=[SCALARS] + [NEAR] * number + ([] if first else [FAR, FAR, NEAR, NEAR]),
        out_specs=[FAR, FAR, NEAR, NEAR],
        scratch_shapes=[
            pltpu.VMEM((number, held, 2, rows, width), f32),
            pltpu.SemaphoreType.DMA((number, held, 2)),
        ],
        input_output_aliases={} if first else {1 + number: 0, 2 + number: 1},
        compiler_params=kernel_params(12),
        cost_estimate=pl.CostEstimate(flops=0, bytes_accessed=number * held * 12 * rows * width, transcendentals=0),
    )(place, *sources, *([] if first else held_arrays))


def flip(array, axis, bits):
    size = lax.axis_size(axis)
    return lax.ppermute(array, axis, [(i, i ^ bits) for i in range(size)])


def add_low(*arrays):
    level = [a.astype(f32) for a in arrays]
    while len(level) > 1:
        level = [level[i] + level[i + 1] for i in range(0, len(level), 2)]
    return level[0].astype(bf16)


def after(arrays, others):
    return lax.optimization_barrier((arrays, others))[0]


def near(mine, groups):
    if groups == 4 and mine.shape[0] == 2:
        return {1: [flip(mine, "expert", 1)], 2: [flip(mine, "expert", 2)]}
    return {ro: [flip(mine, "expert", ro)] for ro in range(1, groups)}


def relay(arrived, groups, held):
    if groups == 4 and held == 2:
        return {3: [flip(arrived[1][0][:1], "expert", 2), flip(arrived[2][0][1:], "expert", 1)]}
    return {}


def crossed(parts, halves):
    return [] if halves == 1 else [flip(part, "rows", 1) for part in parts]


def body(
    rows_in,
    pred_grad,
    lengths,
    session_type,
    expert_in,
    expert_in_bias,
    expert_out,
    expert_out_bias,
    selector_logits,
    selector_mix,
    tower_in,
    tower_bias,
    tower_out,
):
    height, width = rows_in.shape
    layers, owned = expert_in.shape[:2]
    type_count, tasks = selector_logits.shape[1:3]
    selectors, bits = selector_logits.shape[3:]
    groups = lax.axis_size("expert")
    halves = 2 if owned % 2 == 0 else 1
    held = owned // halves
    stride = 2 * width + EXTRA
    me, row_at = lax.axis_index("expert"), lax.axis_index("rows")
    core = row_at % 2 if halves == 2 else jnp.int32(0)
    place = jnp.stack([(row_at * groups + me) * height, me, core]).astype(jnp.int32)

    def rows_of(layer_at, first):
        cut = lambda a: lax.dynamic_slice(a, (layer_at, first) + (0,) * (a.ndim - 2), (1, held) + a.shape[2:])[0]
        half = lambda a: a * jnp.asarray(0.5, a.dtype)
        tail = []
        for bias in (half(cut(expert_in_bias)), cut(expert_out_bias)):
            high = bias.astype(bf16)
            tail += [high, (bias - high.astype(f32)).astype(bf16)]
        tail = jnp.pad(jnp.stack(tail, axis=1), ((0, 0), (0, EXTRA - len(tail)), (0, 0)))
        return jnp.concatenate([half(cut(expert_in)), cut(expert_out), tail], axis=1)

    first = rows_of(0, held * core)
    asked = near(first, groups)
    sizes = (owned, halves, held, selectors, bits, tasks)
    types, across_types, gate_slopes, *values = prepare_call(
        place, lengths, session_type, selector_logits, selector_mix, height, sizes
    )

    later = after((expert_in, expert_in_bias, expert_out, expert_out_bias), types)
    expert_in, expert_in_bias, expert_out, expert_out_bias = later
    own = [[rows_of(layer_at, held * (core ^ half)) for half in range(halves)] for layer_at in range(layers)]
    own[0][0] = first

    def parts_of(got, across):
        pieces, places = [], {}
        for ro in got:
            spots = []
            for parts in (got[ro], across[ro]):
                here = []
                for part in parts:
                    here += [(len(pieces), at) for at in range(part.shape[0])]
                    pieces.append(part)
                if here:
                    spots.append(here)
            places[ro] = [[spots[half][unit] for half in range(halves)] for unit in range(held)]
        return pieces, places

    def pair_order(places, units):
        return tuple(spot for ro in sorted(places) for unit in units for spot in places[ro][unit])

    streams, stashes, weights = [rows_in], [], []
    for layer_at in range(layers):
        last = layer_at == layers - 1
        got = near(own[layer_at][0], groups) if layer_at else after(asked, (types, own[0][1:], own[1:]))
        far = relay(got, groups, held)
        across = {ro: crossed(got[ro], halves) for ro in got}
        got = {0: own[layer_at][:1], **got}
        across[0] = own[layer_at][1:]
        if not last:
            pieces, places = parts_of(got, across)
            total, stash = forward_call(
                streams[-1], types, values[layer_at], None, None, pieces, pair_order(places, range(held)), 0
            )
            far = after(far, total)
        elif streams[1:]:
            far = after(far, streams[-1])
        far_across = {ro: crossed(far[ro], halves) for ro in far}
        if not last:
            if far:
                pieces, places = parts_of(far, far_across)
                base = held * min(far)
                order = pair_order(places, range(held))
                total, stash = forward_call(
                    streams[-1], types, values[layer_at], total, stash, pieces, order, base
                )
            streams.append(total[0])
            stashes.append(stash)
        weights.append(parts_of({**got, **far}, {**across, **far_across}))

    pieces, places = weights[-1]
    predictions, stream, *payload = middle_call(
        place,
        streams[-1],
        types,
        across_types,
        values[-1],
        gate_slopes,
        (pred_grad.T, tower_in, tower_bias, tower_out),
        pieces,
        pair_order(places, range(held)),
        groups,
        halves,
        held,
    )

    shards = lax.axis_size("rows")
    paired = shards > 2
    hops = ["share"] + [4 << at for at in range(shards.bit_length() - 3)] + ["join"] if paired else []
    upper = (row_at & 2) > 0

    class Moving:
        def __init__(self, layer_at, mine, others):
            self.layer_at, self.mine, self.own = layer_at, mine, None
            self.got = [flip(part, "rows", 1) for part in others]
            self.sums, self.parts, self.total, self.hops = None, None, None, -2

        def ask(self, token):
            if self.hops == -1:
                sums, own = after((self.sums, self.own), token)
                ros = range(1, groups) if self.parts is None else ()
                self.got = [flip(sums[ro - 1], "expert", ro) for ro in ros]
                self.got += [] if own is None else [flip(own[1], "rows", 1)]
                return
            total = after(self.total, token)
            if self.hops == len(hops):
                self.got = [total] + ([flip(total, "rows", 1)] if halves == 2 else [])
            elif hops[self.hops] == "share":
                cut = total.shape[0] // 2
                self.got = [
                    jnp.where(upper, total[cut:], total[:cut]),
                    flip(jnp.where(upper, total[:cut], total[cut:]), "rows", 2),
                ]
            else:
                self.got = [total, flip(total, "rows", 2 if hops[self.hops] == "join" else hops[self.hops])]

        def add(self):
            if self.hops == -2:
                self.sums = [add_low(*pair) for pair in zip(self.mine, self.got)]
            elif self.hops == -1:
                got = self.got
                if self.parts is None:
                    self.parts = []
                    while len(got) >= 1 << len(self.parts) and (1 << len(self.parts)) < groups:
                        size = 1 << len(self.parts)
                        level, got = got[:size], got[size:]
                        while len(level) > 1:
                            level = [add_low(*level[i : i + 2]) for i in range(0, len(level), 2)]
                        self.parts += level
                if self.own is None:
                    return
                self.total = functools.reduce(add_low, self.parts, add_low(self.own[0], got[0]))
            elif hops[self.hops] != "join":
                self.total = add_low(*self.got)
            else:
                here, there = self.got
                self.total = jnp.concatenate([jnp.where(upper, there, here), jnp.where(upper, here, there)])
            self.hops += 1

    def arrive(entries, others):
        got, others = lax.optimization_barrier(([entry.got for entry in entries], others))
        for entry, what in zip(entries, got):
            entry.got = what
            entry.add()
        there = [[x for x in (entry.total, entry.parts, entry.sums) if x is not None][0] for entry in entries]
        return there, others

    assert layers == 2
    mine, left = payload[0], payload[-7:]
    mine = [mine[ro] for ro in range(groups - 1)]
    later = Moving(1, mine, payload[1:-7] or mine)
    token = arrive([later], ())
    stream = after(stream, token)
    later.ask(token)
    pieces, places = weights[0]
    stream, mine, *others = backward_call(
        streams[0],
        types,
        across_types,
        stream,
        gate_slopes,
        values[0],
        stashes[0],
        pieces,
        pair_order(places, range(held)),
        held,
        tasks,
        (values[1], own[1], *left),
    )
    token = arrive([later], stream)
    others, last_own = others[:-halves], others[-halves:]
    mine = [mine[ro] for ro in range(groups)]
    others = others or mine
    earlier = Moving(0, mine[1:], others[1:])
    earlier.own = (mine[0], others[0])
    later.own = (last_own[0], last_own[-1])
    later.ask(())
    token = arrive([earlier, later], token)
    moving = [later, earlier]

    whole = {}
    arrays, tower_sums = None, ()

    def ask(*entries):
        nonlocal arrays, tower_sums
        for entry in entries:
            entry.ask(token)
        for entry in entries:
            if entry.hops < len(hops):
                continue
            moving.remove(entry)
            layer_at, got = entry.layer_at, entry.got
            whole[layer_at] = got
            if layer_at == layers - 1:
                end = got[0][held * stride + type_count // 2 :].astype(f32)
                tower_rows = [array[held * stride + type_count // 2 + EXTRA :].astype(f32) for array in got]
                if halves == 2:
                    tower_rows = [jnp.where(core == 0, *tower_rows), jnp.where(core == 0, *tower_rows[::-1])]
                wide = jnp.concatenate(tower_rows).reshape(tasks, -1, width)
                narrow = tower_in.shape[2]
                parts = [wide[:, :, at : at + narrow] for at in range(0, width, narrow)]
                tower_sums = (
                    jnp.concatenate(parts, axis=1),
                    end[0].reshape(tower_bias.shape),
                    end[1].reshape(tower_out.shape),
                )
            if moving:
                sources = {(layer_at, half): array for half, array in enumerate(got)}
                arrays = finish_call(place, sources, arrays, held, expert_in.shape)

    if len(hops) == 3:
        ask(earlier, later)
        token = arrive([later], ())
        ask(later)
        token = arrive([earlier, later], ())
        ask(earlier)
        token = arrive([earlier], ())
        ask(earlier, later)
        token = arrive([earlier, later], ())
    while moving:
        ask(*moving)
        if moving:
            token = arrive(moving, (arrays, tower_sums))
    ends = [whole[layer_at][0][held * stride : held * stride + type_count].astype(f32) for layer_at in range(layers)]
    cut = type_count // 2
    gate_grads = [ends[0][:cut], ends[1][:cut] + ends[0][cut:]]
    quantities = selectors * (bits + 1)
    small = jnp.stack(gate_grads)
    small = jnp.concatenate([small[..., :LANES], small[..., LANES:]], axis=1)[..., : tasks * quantities]
    small = small.reshape(layers, type_count, tasks, quantities)
    logits_grad = small[..., : selectors * bits].reshape(selector_logits.shape)
    smalls = (logits_grad, small[..., selectors * bits :], *tower_sums)
    got, (arrays, smalls) = lax.optimization_barrier((whole[0], (arrays, smalls)))
    arrays = finish_call(place, {(0, half): array for half, array in enumerate(got)}, arrays, held, expert_in.shape)
    return (
        predictions.T,
        stream,
        arrays[0],
        arrays[2],
        arrays[1],
        arrays[3],
        *smalls,
    )


def solution(mesh):
    in_specs = (
        P(("rows", "expert"), None),
        P(("rows", "expert"), None),
        P(),
        P(),
        P(None, "expert", None, None),
        P(None, "expert", None),
        P(None, "expert", None, None),
        P(None, "expert", None),
        P(),
        P(),
        P(),
        P(),
        P(),
    )
    out_specs = (
        P(("rows", "expert"), None),
        P(("rows", "expert"), None),
        P(None, "expert", None, None),
        P(None, "expert", None),
        P(None, "expert", None, None),
        P(None, "expert", None),
        P(),
        P(),
        P(),
        P(),
        P(),
    )
    return jax.shard_map(body, mesh=mesh, in_specs=in_specs, out_specs=out_specs, check_vma=False)
```

```python
import functools
import math

import jax
import jax.numpy as jnp
import numpy as np
from jax import lax
from jax.experimental import pallas as pl
from jax.experimental.pallas import tpu as pltpu
from jax.sharding import PartitionSpec as P

SHARPNESS = 10.0
EXACT = lax.Precision.HIGHEST
bf16 = jnp.bfloat16
f32 = jnp.float32
INNER = math.sqrt(2.0 / math.pi)
CUBE = 0.044715 * INNER
TILE = 1024
TOWER_TILE = 512
LANES = 128
EXTRA = 16


def mm(a, b):
    return jnp.dot(a, b, preferred_element_type=f32)


def mm_exact(a, b):
    return jnp.dot(a, b, precision=EXACT, preferred_element_type=f32)


def mm_nt(a, b):
    return lax.dot_general(a, b, (((1,), (1,)), ((), ())), preferred_element_type=f32)


def mm_tn(a, b):
    return lax.dot_general(a, b, (((0,), (0,)), ((), ())), preferred_element_type=f32)


def gelu_both(v):
    square = v * v
    half = 0.5 + 0.5 * jnp.tanh(v * (INNER + CUBE * square))
    value = v * half
    slope = half + value * (1.0 - half) * (2.0 * INNER + 6.0 * CUBE * square)
    return value, slope


def gelu_parts(v):
    bend = 2.0 * INNER + 8.0 * CUBE * (v * v)
    twice_share = 1.0 + jnp.tanh(v * bend)
    return v * twice_share, bend, twice_share


def gelu_slope(value, bend, twice_share):
    rise = 3.0 * bend - 4.0 * INNER
    return twice_share + value * (2.0 - twice_share) * rise


FAR = pl.BlockSpec(memory_space=pl.ANY)
NEAR = pl.BlockSpec(memory_space=pltpu.VMEM)
SCALARS = pl.BlockSpec(memory_space=pltpu.SMEM)


def kernel_params(mebibytes):
    return pltpu.CompilerParams(vmem_limit_bytes=mebibytes * 2**20)


def whole_spec(shape):
    zeros = (0,) * len(shape)
    return pl.BlockSpec(shape, lambda i: zeros)


def prepare_kernel(sizes, place_ref, length_ref, kind_ref, logit_ref, mix_ref, spread_logit_ref, spread_mix_ref, *outs):
    owned, halves, held, selectors, bits, tasks = sizes
    type_ref, across_ref, slope_ref, *value_refs = outs
    height, type_count = type_ref.shape
    experts = 2**bits
    sessions = length_ref.shape[1]
    chunk = min(256, sessions)
    position = (place_ref[0] + lax.broadcasted_iota(jnp.int32, (height, 1), 0)).astype(f32)
    earlier = lax.broadcasted_iota(jnp.int32, (chunk, chunk), 0) < lax.broadcasted_iota(jnp.int32, (chunk, chunk), 1)
    earlier = jnp.where(earlier, 1.0, 0.0).astype(bf16)
    kinds = lax.broadcasted_iota(jnp.int32, (type_count, chunk), 0)
    before = jnp.zeros((1, 1), f32)
    types = jnp.zeros((height, type_count), f32)
    across = jnp.zeros((type_count, height), f32)
    for at in range(0, sessions, chunk):
        lengths = length_ref[:, at : at + chunk].astype(f32)
        begin = before + mm(jnp.broadcast_to(lengths.astype(bf16), (EXTRA, chunk)), earlier)[0:1]
        before += jnp.sum(lengths, axis=1, keepdims=True)
        member = jnp.where((position >= begin) & (position < begin + lengths), 1.0, 0.0).astype(bf16)
        of_type = jnp.where(kinds == kind_ref[:, at : at + chunk], 1.0, 0.0).astype(bf16)
        types += mm_nt(member, of_type)
        across += mm_nt(of_type, member)
    type_ref[...] = types.astype(bf16)
    across_ref[...] = across.astype(bf16)

    rows = logit_ref.shape[0]
    place = lax.broadcasted_iota(jnp.int32, (rows, LANES), 1) % experts
    expert = (
        owned * ((place // owned) ^ place_ref[1])
        + held * ((place % halves) ^ place_ref[2])
        + (place // halves) % held
    )
    logits = mm_exact(logit_ref[...], spread_logit_ref[...])
    mixes = mm_exact(mix_ref[...], spread_mix_ref[...])
    mixes = [mixes[:, k * LANES : (k + 1) * LANES] for k in range(selectors)]
    top = functools.reduce(jnp.maximum, mixes)
    shares = [jnp.exp(mix - top) for mix in mixes]
    whole = functools.reduce(jnp.add, shares)
    shares = [share / whole for share in shares]
    value = jnp.zeros((rows, LANES), f32)
    reaches = []
    for k in range(selectors):
        factors, signed = [], []
        for bit in range(bits):
            at = (k * bits + bit) * LANES
            logit = logits[:, at : at + LANES]
            cubic = (-2.0 / SHARPNESS**3) * logit * logit * logit + (1.5 / SHARPNESS) * logit + 0.5
            step = jnp.where(logit <= -SHARPNESS / 2, 0.0, jnp.where(logit >= SHARPNESS / 2, 1.0, cubic))
            slope = (-6.0 / SHARPNESS**3) * logit * logit + 1.5 / SHARPNESS
            slope = jnp.where((logit > -SHARPNESS / 2) & (logit < SHARPNESS / 2), slope, 0.0)
            on = (expert >> bit) & 1 == 1
            factors.append(jnp.where(on, step, 1.0 - step))
            signed.append(jnp.where(on, slope, -slope))
        reaches.append(functools.reduce(jnp.multiply, factors))
        value += shares[k] * reaches[k]
        for bit in range(bits):
            others = [factors[b] for b in range(bits) if b != bit]
            slope_ref[k * bits + bit] = shares[k] * signed[bit] * functools.reduce(jnp.multiply, others)
    for k in range(selectors):
        slope_ref[selectors * bits + k] = shares[k] * (reaches[k] - value)

    value = value.astype(bf16).astype(f32)
    for layer_at, ref in enumerate(value_refs):
        table = value[layer_at * type_count : (layer_at + 1) * type_count]
        columns = [table[:, t * experts : (t + 1) * experts] for t in range(tasks)]
        if layer_at < len(value_refs) - 1:
            columns = [functools.reduce(jnp.add, columns) / tasks]
        for pair in range(ref.shape[0]):
            lanes = []
            for half in range(halves):
                at = pair * halves + half
                lanes += [jnp.broadcast_to(c[:, at : at + 1], (type_count, LANES)) for c in columns]
            ref[pair] = jnp.concatenate(lanes, axis=1).astype(bf16)


def prepare_call(place, lengths, session_type, logits, mixing, height, sizes):
    owned, halves, held, selectors, bits, tasks = sizes
    layers, type_count = logits.shape[:2]
    experts = 2**bits
    rows = layers * type_count
    lane = np.arange(LANES)
    source = np.arange(tasks * selectors * bits)
    task, number = source // (selectors * bits), source % (selectors * bits)
    mine = (lane[None, :] // experts == task[:, None])[:, None, :]
    spread_logit = mine & (number[:, None, None] == np.arange(selectors * bits)[None, :, None])
    source = np.arange(tasks * selectors)
    mine = (lane[None, :] // experts == (source // selectors)[:, None])[:, None, :]
    spread_mix = mine & ((source % selectors)[:, None, None] == np.arange(selectors)[None, :, None])
    spread_logit = spread_logit.reshape(spread_logit.shape[0], -1).astype(np.float32)
    spread_mix = spread_mix.reshape(spread_mix.shape[0], -1).astype(np.float32)
    outs = [
        jax.ShapeDtypeStruct((height, type_count), bf16),
        jax.ShapeDtypeStruct((type_count, height), bf16),
        jax.ShapeDtypeStruct((selectors * (bits + 1), rows, LANES), f32),
    ]
    for layer_at in range(layers):
        each = tasks if layer_at == layers - 1 else 1
        outs.append(jax.ShapeDtypeStruct((experts // halves, type_count, halves * each * LANES), bf16))
    return pl.pallas_call(
        functools.partial(prepare_kernel, sizes),
        out_shape=outs,
        in_specs=[SCALARS] + [NEAR] * 6,
        out_specs=[NEAR] * len(outs),
        compiler_params=kernel_params(58),
        cost_estimate=pl.CostEstimate(flops=2 * height * lengths.size * 64, bytes_accessed=2**21, transcendentals=2**16),
    )(
        place,
        lengths.reshape(1, -1),
        session_type.reshape(1, -1),
        logits.reshape(rows, -1),
        mixing.reshape(rows, -1),
        spread_logit,
        spread_mix,
    )


def bias_rows(weights, width):
    rows = weights[2 * width : 2 * width + EXTRA].astype(f32)
    return rows[0:1] + rows[1:2], rows[2:3] + rows[3:4]


def twice(a):
    return jnp.concatenate([a, a], axis=1)


def tiles(height, most):
    tile = min(most, height)
    return [pl.ds(at, tile) for at in range(0, height, tile)]


def joined(parts, axis):
    return parts[0] if len(parts) == 1 else jnp.concatenate(parts, axis=axis)


def gates_of(types, value_ref, count):
    gates = mm(types, value_ref[...]).astype(bf16)
    return [gates[:, at * LANES : (at + 1) * LANES] for at in range(count)]


def forward_step(weights, value_ref, x_low, type_ref, total_ref, biases, keep, keep_gate=None, keep_result=None):
    height, width = x_low.shape
    kinds = total_ref.shape[0]
    bias_in, bias_out = zip(*(bias_rows(w, width) for w in weights))
    second = joined([w[width : 2 * width] for w in weights], 0)
    for rows in tiles(height, TILE // 2):
        gates = gates_of(type_ref[rows], value_ref, len(weights) * kinds)
        if keep_gate is not None:
            for at, gate in enumerate(gates):
                keep_gate(at, rows, gate)
        scaled = [[] for _ in range(kinds)]
        for i, w in enumerate(weights):
            before = mm(x_low[rows], w[0:width]) + bias_in[i]
            hidden, bend, twice_share = gelu_parts(before)
            hidden = hidden.astype(bf16)
            keep(i, rows, hidden, gelu_slope(hidden, bend.astype(bf16), twice_share.astype(bf16)))
            if keep_result is not None:
                result = mm(hidden, w[width : 2 * width]).astype(bf16)
                keep_result(i, rows, result)
            for t in range(kinds):
                scaled[t].append(twice(gates[i * kinds + t]) * (hidden if keep_result is None else result))
        for t in range(kinds):
            if keep_result is None:
                total_ref[t, rows] += mm(joined(scaled[t], 1), second)
            else:
                total_ref[t, rows] += functools.reduce(jnp.add, scaled[t]).astype(f32)
    for i in range(len(weights)):
        for t in range(kinds):
            at = (i * kinds + t) * LANES
            biases[t] += twice(value_ref[:, at : at + LANES].astype(f32)) * bias_out[i]


def forward_end(type_ref, total_ref, biases):
    for t in range(total_ref.shape[0]):
        high = biases[t].astype(bf16)
        rest = (biases[t] - high.astype(f32)).astype(bf16)
        for rows in tiles(total_ref.shape[1], TILE):
            total_ref[t, rows] += mm(twice(type_ref[rows]), jnp.concatenate([high, rest], axis=0))


def backward_start(x_low, type_across, low, across, share):
    width = x_low.shape[1]
    across[0:width] = x_low[...].T
    ones = lax.broadcasted_iota(jnp.int32, (EXTRA, x_low.shape[0]), 0) == 0
    across[width:] = jnp.where(ones, 1.0, 0.0).astype(bf16)
    for t in range(low.shape[0]):
        share[t] = mm(type_across[...], low[t])


def backward_step(weights, value_ref, hiddens, slopes, outs, pair, experts, type_ref, type_across, low, stream_ref, across, share, table, scratch, kept_gates=None, results=None, dots=None, gate_lanes=None):
    before_grads, result_grads = scratch
    kinds, height, width = low.shape
    count = len(weights)
    first = joined([w[0:width] for w in weights], 1)
    for rows in tiles(height, TILE):
        if kept_gates is None:
            gates = gates_of(type_ref[rows], value_ref, count * kinds)
        else:
            gates = [kept_gates[at, rows] for at in range(count * kinds)]
        gates = [twice(gate) for gate in gates]
        befores = []
        for i, w in enumerate(weights):
            hidden, slope = hiddens[i][rows], slopes[i][rows]
            second = w[width : 2 * width]
            result_grad = gates[i * kinds] * low[0, rows]
            for t in range(1, kinds):
                result_grad += gates[i * kinds + t] * low[t, rows]
            hidden_grad = mm_nt(result_grad, second).astype(bf16)
            for t in range(kinds):
                product = hidden * hidden_grad if results is None else results[i][rows] * low[t, rows]
                product = functools.reduce(
                    jnp.add, [product[:, lane : lane + LANES] for lane in range(0, width, LANES)]
                )
                found = jnp.sum(product.astype(f32), axis=1, keepdims=True)
                lanes = lax.broadcasted_iota(jnp.int32, (1, LANES), 1)
                place = pair * count + i
                chosen = lanes % experts == place if kinds == 1 else lanes == t * experts + place
                dots[rows] = jnp.where(chosen, found, dots[rows])
            before = slope * hidden_grad
            before_grads[i, rows] = before
            result_grads[i, rows] = result_grad
            befores.append(before)
        stream_ref[rows] += mm_nt(joined(befores, 1), first)
    lanes = lax.broadcasted_iota(jnp.int32, (type_ref.shape[1], LANES), 1)
    for i, w in enumerate(weights):
        _, bias_out = bias_rows(w, width)
        first_grad = 0.5 * mm(across[...], before_grads[i])
        outs[i][0:width] = first_grad[0:width].astype(bf16)
        outs[i][width : 2 * width] = mm_tn(hiddens[i][...], result_grads[i]).astype(bf16)
        out_bias = jnp.zeros((1, width), f32)
        place = pair * count + i
        for t in range(kinds):
            at = (i * kinds + t) * LANES
            gate = value_ref[:, at : at + LANES].astype(f32)
            out_bias += jnp.sum(twice(gate) * share[t], axis=0, keepdims=True)
            bias_part = jnp.sum(share[t] * bias_out, axis=1, keepdims=True)
            if kinds == 1:
                table[...] = jnp.where(lanes % experts == place, 0.5 * bias_part, table[...])
                gate_lanes[...] = jnp.where(lanes % experts == place, gate, gate_lanes[...])
            else:
                table[...] = jnp.where(lanes == t * experts + place, bias_part, table[...])
        tail = jnp.concatenate([first_grad[width : width + 1], out_bias, jnp.zeros((EXTRA - 2, width), f32)])
        outs[i][2 * width : 2 * width + EXTRA] = tail.astype(bf16)


def by_type(type_across, dots):
    high = dots[...].astype(bf16)
    rest = (dots[...] - high.astype(f32)).astype(bf16)
    return mm(type_across[...], high) + mm(type_across[...], rest)


def through_gates(table, gate_slope_ref, experts, tasks):
    quantities, type_count = gate_slope_ref.shape[:2]
    lanes = lax.broadcasted_iota(jnp.int32, (type_count, LANES), 1)
    small = jnp.zeros((type_count, LANES), f32)
    for q in range(quantities):
        product = gate_slope_ref[q] * table[...]
        for t in range(tasks):
            part = jnp.sum(jnp.where(lanes // experts == t, product, 0.0), axis=1, keepdims=True)
            small = jnp.where(lanes == t * quantities + q, part, small)
    half = type_count // 2
    return jnp.concatenate([small[:half], small[half:]], axis=1).astype(bf16)


def store_copies(ready, pair, held, out_refs, sems):
    group, unit = pair // held, lax.rem(pair, held)
    rows = pl.ds(pl.multiple_of(unit * ready.shape[1], EXTRA), ready.shape[1])
    copies = [(None, pltpu.make_async_copy(ready.at[0], out_refs[0].at[group, rows], sems.at[0]))]
    for at, ref in enumerate(out_refs[1:]):
        copies.append((group == at, pltpu.make_async_copy(ready.at[1], ref.at[rows], sems.at[1])))
    return copies


def end_copies(ends, out_refs, sems):
    rows = out_refs[0].shape[1]
    last = pl.ds(rows - ends.shape[1], ends.shape[1])
    groups = out_refs[0].shape[0]
    copies = [pltpu.make_async_copy(ends.at[0], out_refs[0].at[at, last], sems.at[0, at]) for at in range(groups)]
    copies += [
        pltpu.make_async_copy(ends.at[1], ref.at[last], sems.at[1, at]) for at, ref in enumerate(out_refs[1:])
    ]
    return [(None, copy) for copy in copies]


def for_each(copies, act):
    for condition, copy in copies:
        if condition is None:
            act(copy)
        else:
            pl.when(condition)(functools.partial(act, copy))


def start(copy):
    copy.start()


def wait(copy):
    copy.wait()


def fetch_weights(places, buffer, sems, each):
    step = pl.program_id(0)
    for of in range(len(places) // each):

        @pl.when(step == max(of - 1, 0))
        def _(of=of):
            for i, (ref, at) in enumerate(places[of * each : (of + 1) * each]):
                pltpu.make_async_copy(ref.at[at], buffer.at[of % 2, i], sems.at[of % 2, i]).start()

    slot = lax.rem(step, 2)
    for i in range(each):
        ref, at = places[0]
        pltpu.make_async_copy(ref.at[at], buffer.at[slot, i], sems.at[slot, i]).wait()
    return [buffer.at[slot, i] for i in range(each)]


def forward_kernel(places, pieces, each, first, *refs):
    refs = list(refs)
    take = lambda count: [refs.pop(0) for _ in range(count)]
    x_ref, type_ref, value_ref = take(3)
    if not first:
        total_ref, _, _ = take(3)
    weight_refs = take(pieces)
    out_ref, hidden_ref, slope_ref, x_low, biases, buffer, sems = take(7)
    step = pl.program_id(0)
    weights = fetch_weights([(weight_refs[piece], at) for piece, at in places], buffer, sems, each)

    @pl.when(step == 0)
    def _():
        x_low[...] = x_ref[...].astype(bf16)
        biases[...] = jnp.zeros_like(biases)
        out_ref[0] = x_ref[...] if first else total_ref[0]

    def keep(i, rows, hidden, slope):
        hidden_ref[0, i, rows] = hidden
        slope_ref[0, i, rows] = slope

    forward_step(weights, value_ref.at[0], x_low, type_ref, out_ref, biases, keep)

    @pl.when(step == pl.num_programs(0) - 1)
    def _():
        forward_end(type_ref, out_ref, biases)


def forward_call(x, types, values, total, stash, pieces, places, base):
    height, width = x.shape
    pairs, type_count, lanes = values.shape
    each = lanes // LANES
    operands = [x, types, values]
    specs = [whole_spec(x.shape), whole_spec(types.shape)]
    specs.append(pl.BlockSpec((1, type_count, lanes), lambda i: (base + i, 0, 0)))
    aliases = {}
    if total is not None:
        operands += [total, *stash]
        specs += [whole_spec(total.shape), FAR, FAR]
        aliases = {4: 1, 5: 2}
    summed = jax.ShapeDtypeStruct((1, height, width), f32)
    kept = jax.ShapeDtypeStruct((pairs, each, height, width), bf16)
    kept_spec = pl.BlockSpec((1, each, height, width), lambda i: (base + i, 0, 0, 0))
    number = len(places)
    results = pl.pallas_call(
        functools.partial(forward_kernel, places, len(pieces), each, total is None),
        grid=(number // each,),
        out_shape=[summed, kept, kept],
        in_specs=specs + [whole_spec(piece.shape) for piece in pieces],
        out_specs=[whole_spec(summed.shape), kept_spec, kept_spec],
        scratch_shapes=[
            pltpu.VMEM((height, width), bf16),
            pltpu.VMEM((1, type_count, width), f32),
            pltpu.VMEM((2, each, *pieces[0].shape[1:]), bf16),
            pltpu.SemaphoreType.DMA((2, each)),
        ],
        input_output_aliases=aliases,
        compiler_params=kernel_params(58),
        cost_estimate=pl.CostEstimate(
            flops=4 * number * height * width * width,
            bytes_accessed=number * (4 * width * width + 4 * height * width) + 8 * height * width,
            transcendentals=number * height * width,
        ),
    )(*operands, *pieces)
    return results[0], results[1:]


def middle_kernel(places, pieces, groups, halves, held, *refs):
    refs = list(refs)
    take = lambda count: [refs.pop(0) for _ in range(count)]
    place_ref, x_ref, type_ref, across_types_ref, value_ref, gate_slope_ref, pred_grad_ref = take(7)
    tower_in_ref, tower_bias_ref, tower_out_ref = take(3)
    weight_refs = take(pieces)
    pred_ref, stream_ref = take(2)
    out_refs = take(1 + (groups - 1) * (halves - 1))
    left_refs = take(7)
    x_low, weights, hidden_all, slope_all, result_all, gates_all, total, biases, low, across, share, table = take(12)
    before_grads, result_grads, dots, cotangents, ready, ends, in_grad, bias_grad, out_grad, load_sem, store_sem, end_sem, left_sem = take(13)
    height, width = x_ref.shape
    pairs = value_ref.shape[0]
    experts = pairs * halves
    tasks = total.shape[0]

    def load(pair, i, ref, at):
        return pltpu.make_async_copy(ref.at[at], weights.at[pair, i], load_sem.at[pair, i])

    for j, (piece, at) in enumerate(places):
        load(j // halves, j % halves, weight_refs[piece], at).start()
    x_low[...] = x_ref[...].astype(bf16)
    biases[...] = jnp.zeros_like(biases)
    for t in range(tasks):
        total[t] = x_ref[...]

    def forward_pair(pair, carry):
        for i in range(halves):
            load(pair, i, weight_refs[0], 0).wait()

        def keep(i, rows, hidden, slope):
            hidden_all[pair, i, rows] = hidden
            slope_all[pair, i, rows] = slope

        def keep_gate(at, rows, gate):
            gates_all[pair, at, rows] = gate

        def keep_result(i, rows, result):
            result_all[pair, i, rows] = result

        forward_step(
            [weights.at[pair, i] for i in range(halves)],
            value_ref.at[pair],
            x_low,
            type_ref,
            total,
            biases,
            keep,
            keep_gate,
            keep_result,
        )
        return carry

    lax.fori_loop(0, pairs, forward_pair, 0)
    forward_end(type_ref, total, biases)

    def left(at, source):
        return pltpu.make_async_copy(source, left_refs[at], left_sem.at[at])

    own = [kept.at[0:held] for kept in (hidden_all, slope_all, result_all)]
    for at, source in enumerate(own):
        left(at, source).start()

    cotangents[...] = jnp.concatenate(
        [pred_grad_ref[...], jnp.zeros((cotangents.shape[1] - tasks, height), f32)]
    ).T
    in_grad[...] = jnp.zeros_like(in_grad)
    bias_grad[...] = jnp.zeros_like(bias_grad)
    out_grad[...] = jnp.zeros_like(out_grad)
    for rows in tiles(height, TOWER_TILE):
        summed = None
        predicted = []
        for t in range(tasks):
            closing_low = total[t, rows].astype(bf16)
            act, slope = gelu_both(mm(closing_low, tower_in_ref[t]) + tower_bias_ref[t : t + 1])
            vector = tower_out_ref[t : t + 1]
            predicted.append(jnp.sum(act * vector, axis=1, keepdims=True))
            cotangent = cotangents[rows, t : t + 1]
            out_grad[t : t + 1] += jnp.sum(act * cotangent, axis=0, keepdims=True)
            before_grad = (slope * (cotangent * vector)).astype(bf16)
            bias_grad[t : t + 1] += jnp.sum(before_grad.astype(f32), axis=0, keepdims=True)
            in_grad[t] += mm_tn(closing_low, before_grad)
            closing_grad = mm_nt(before_grad, tower_in_ref[t])
            low[t, rows] = closing_grad.astype(bf16)
            summed = closing_grad if summed is None else summed + closing_grad
        stream_ref[rows] = summed
        blank = jnp.zeros((predicted[0].shape[0], cotangents.shape[1] - tasks), f32)
        pred_ref[:, rows] = jnp.concatenate([*predicted, blank], axis=1).T[0:tasks]
    narrow = in_grad.shape[2]
    tall = width * narrow // width
    begin = type_ref.shape[1] // 2 + EXTRA
    for t in range(tasks):
        wide = jnp.concatenate([in_grad[t, :tall], in_grad[t, tall:]], axis=1).astype(bf16)
        if halves == 2:
            ends[place_ref[2] ^ t, begin:] = wide
        else:
            ends[0, begin + t * tall : begin + (t + 1) * tall] = wide
    vectors = [jnp.concatenate([ref[0:1], ref[1:2]], axis=1) for ref in (bias_grad, out_grad)]
    vectors = jnp.concatenate([*vectors, jnp.zeros((EXTRA - 2, width), f32)]).astype(bf16)
    for half in range(halves):
        ends[half, begin - EXTRA : begin] = vectors

    left(3, low).start()
    backward_start(x_low, across_types_ref, low, across, share)
    left(4, across).start()
    left(5, share).start()
    table[...] = jnp.zeros_like(table)
    dots[...] = jnp.zeros_like(dots)

    def stores(pair):
        return store_copies(ready.at[pair], pair - held, held, out_refs, store_sem.at[pair])

    def backward_pair(pair, carry):
        backward_step(
            [weights.at[pair, i] for i in range(halves)],
            value_ref.at[pair],
            [hidden_all.at[pair, i] for i in range(halves)],
            [slope_all.at[pair, i] for i in range(halves)],
            [ready.at[pair, i] for i in range(halves)],
            pair,
            experts,
            type_ref,
            across_types_ref,
            low,
            stream_ref,
            across,
            share,
            table,
            (before_grads, result_grads),
            gates_all.at[pair],
            [result_all.at[pair, i] for i in range(halves)],
            dots,
        )
        for_each(stores(pair), start)
        return carry

    lax.fori_loop(held, pairs, backward_pair, 0)
    table[...] += by_type(across_types_ref, dots)
    small = through_gates(table, gate_slope_ref, experts, tasks)
    for half in range(halves):
        ends[half, 0 : small.shape[0]] = small
    left(6, ends).start()
    for_each(end_copies(ends, out_refs, end_sem), start)

    def drain(pair, carry):
        for_each(stores(pair), wait)
        return carry

    lax.fori_loop(held, pairs, drain, 0)
    for_each(end_copies(ends, out_refs, end_sem), wait)
    for at, source in enumerate([*own, low, across, share, ends]):
        left(at, source).wait()


def middle_call(place, x, types, across_types, values, gate_slopes, tower, pieces, places, groups, halves, held):
    height, width = x.shape
    pairs, type_count, lanes = values.shape
    pred_grad, tower_in, tower_bias, tower_out = tower
    tasks = tower_in.shape[0]
    stride = 2 * width + EXTRA
    experts = pairs * halves
    outs = [jax.ShapeDtypeStruct(shape, f32) for shape in (pred_grad.shape, (height, width))]
    near = len(outs)
    end_rows = type_count // 2 + EXTRA + tower_in.size // width // halves
    rows = held * stride + end_rows
    outs.append(jax.ShapeDtypeStruct((groups - 1, rows, width), bf16))
    outs += [jax.ShapeDtypeStruct((rows, width), bf16)] * ((groups - 1) * (halves - 1))
    outs += [jax.ShapeDtypeStruct((held, halves, height, width), bf16)] * 3
    outs.append(jax.ShapeDtypeStruct((tasks, height, width), bf16))
    outs.append(jax.ShapeDtypeStruct((width + EXTRA, height), bf16))
    outs.append(jax.ShapeDtypeStruct((tasks, type_count, width), f32))
    outs.append(jax.ShapeDtypeStruct((halves, end_rows, width), bf16))
    layer_at = gate_slopes.shape[1] // type_count - 1
    slope_spec = pl.BlockSpec((gate_slopes.shape[0], type_count, LANES), lambda i: (0, layer_at, 0))
    kept = pltpu.VMEM((pairs, halves, height, width), bf16)
    operands = [x, types, across_types, values, gate_slopes, *tower]
    specs = [whole_spec(a.shape) for a in operands]
    specs[4] = slope_spec
    return pl.pallas_call(
        functools.partial(middle_kernel, places, len(pieces), groups, halves, held),
        grid=(1,),
        out_shape=outs,
        in_specs=[SCALARS] + specs + [whole_spec(a.shape) for a in pieces[:halves]] + [FAR] * (len(pieces) - halves),
        out_specs=[whole_spec(out.shape) for out in outs[:near]] + [FAR] * (len(outs) - near),
        scratch_shapes=[
            pltpu.VMEM((height, width), bf16),
            pltpu.VMEM((pairs, halves, stride, width), bf16),
            kept,
            kept,
            kept,
            pltpu.VMEM((pairs, halves * tasks, height, LANES), bf16),
            pltpu.VMEM((tasks, height, width), f32),
            pltpu.VMEM((tasks, type_count, width), f32),
            pltpu.VMEM((tasks, height, width), bf16),
            pltpu.VMEM((width + EXTRA, height), bf16),
            pltpu.VMEM((tasks, type_count, width), f32),
            pltpu.VMEM((type_count, LANES), f32),
            pltpu.VMEM((halves, height, width), bf16),
            pltpu.VMEM((halves, height, width), bf16),
            pltpu.VMEM((height, LANES), f32),
            pltpu.VMEM((height, LANES), f32),
            pltpu.VMEM((pairs, halves, stride, width), bf16),
            pltpu.VMEM((halves, end_rows, width), bf16),
            pltpu.VMEM(tower_in.shape, f32),
            pltpu.VMEM(tower_bias.shape, f32),
            pltpu.VMEM(tower_out.shape, f32),
            pltpu.SemaphoreType.DMA((pairs, halves)),
            pltpu.SemaphoreType.DMA((pairs, halves)),
            pltpu.SemaphoreType.DMA((halves, groups)),
            pltpu.SemaphoreType.DMA((7,)),
        ],
        compiler_params=kernel_params(58),
        cost_estimate=pl.CostEstimate(
            flops=14 * experts * height * width * width,
            bytes_accessed=experts * 8 * width * width + 16 * height * width,
            transcendentals=experts * height * width,
        ),
    )(place, *operands, *pieces)


def backward_kernel(places, pieces, each, held, tasks, *refs):
    refs = list(refs)
    take = lambda count: [refs.pop(0) for _ in range(count)]
    x_ref, type_ref, across_types_ref, stream_ref, gate_slope_ref, value_ref, hidden_ref, slope_ref = take(8)
    last_value_ref, last_low_ref, last_across_ref, last_share_ref, last_end_ref = take(5)
    last_refs, last_weight_refs = take(3), take(each)
    weight_refs = take(pieces)
    stream_out_ref = take(1)[0]
    groups = len(places) // each // held
    out_refs = take(1 + groups * (each - 1))
    last_out_refs = take(each)
    x_low, across, low, share, table, before_grads, result_grads, gate_lanes, buffer, ready, ends = take(11)
    x_wide, gate_slopes, last_table, dots, kept, last_weights, last_ready = take(7)
    sems, store_sem, end_sem, last_sem, last_store_sem, late_sem = take(6)
    step = pl.program_id(0)
    slot = lax.rem(step, 2)
    experts = len(places)
    types = type_ref.shape[1]
    stride = buffer.shape[2]
    scratch = (before_grads, result_grads)
    weights = fetch_weights([(weight_refs[piece], at) for piece, at in places], buffer, sems, each)

    late = [
        (None, pltpu.make_async_copy(source, target, late_sem.at[at]))
        for at, (source, target) in enumerate(((x_ref, x_wide), (gate_slope_ref, gate_slopes)))
    ]

    def last_loads(unit):
        copies = [
            pltpu.make_async_copy(last_refs[which].at[unit], kept.at[which, unit], last_sem.at[unit, which])
            for which in range(3)
        ]
        for half in range(each):
            source, sem = last_weight_refs[half].at[unit], last_sem.at[unit, 3 + half]
            copies.append(pltpu.make_async_copy(source, last_weights.at[unit, half], sem))
        return [(None, copy) for copy in copies]

    def last_stores():
        copies = []
        for half, ref in enumerate(last_out_refs):
            for unit in range(held):
                rows = pl.ds(unit * stride, stride)
                copies.append(
                    pltpu.make_async_copy(last_ready.at[unit, half], ref.at[rows], last_store_sem.at[half, unit])
                )
            rows = pl.ds(held * stride, last_end_ref.shape[1])
            copies.append(pltpu.make_async_copy(last_end_ref.at[half], ref.at[rows], last_store_sem.at[half, held]))
        return [(None, copy) for copy in copies]

    @pl.when(step == 0)
    def _():
        for unit in range(held):
            for_each(last_loads(unit), start)
        for_each(late, start)
        stream_out_ref[...] = stream_ref[...]
        last_table[...] = jnp.zeros_like(last_table)
        dots[...] = jnp.zeros_like(dots)

        def last_pair(unit, carry):
            for_each(last_loads(unit), wait)
            backward_step(
                [last_weights.at[unit, i] for i in range(each)],
                last_value_ref.at[unit],
                [kept.at[0, unit, i] for i in range(each)],
                [kept.at[1, unit, i] for i in range(each)],
                [last_ready.at[unit, i] for i in range(each)],
                unit,
                experts,
                type_ref,
                across_types_ref,
                last_low_ref,
                stream_out_ref,
                last_across_ref,
                last_share_ref,
                last_table,
                scratch,
                None,
                [kept.at[2, unit, i] for i in range(each)],
                dots,
            )
            return carry

        lax.fori_loop(0, held, last_pair, 0)
        for_each(last_stores(), start)
        last_table[...] += by_type(across_types_ref, dots)
        dots[...] = jnp.zeros_like(dots)
        for_each(late[:1], wait)
        x_low[...] = x_wide[...].astype(bf16)
        low[0] = stream_out_ref[...].astype(bf16)
        table[...] = jnp.zeros_like(table)
        gate_lanes[...] = jnp.zeros_like(gate_lanes)
        backward_start(x_low, across_types_ref, low, across, share)

    def stores(pair):
        at = lax.rem(pair, 2)
        return store_copies(ready.at[at], pair, held, out_refs, store_sem.at[at])

    @pl.when(step >= 2)
    def _():
        for_each(stores(step - 2), wait)

    backward_step(
        weights,
        value_ref.at[0],
        [hidden_ref.at[0, i] for i in range(each)],
        [slope_ref.at[0, i] for i in range(each)],
        [ready.at[slot, i] for i in range(each)],
        step,
        experts,
        type_ref,
        across_types_ref,
        low,
        stream_out_ref,
        across,
        share,
        table,
        scratch,
        None,
        None,
        dots,
        gate_lanes,
    )

    for_each(stores(step), start)

    @pl.when(step == pl.num_programs(0) - 1)
    def _():
        for_each(late[1:], wait)
        gate = gate_lanes[...]
        found = 0.5 * by_type(across_types_ref, dots) / jnp.where(gate > 0.0, gate, 1.0)
        table[...] += jnp.where(gate > 0.0, found, 0.0)
        both = ((table, 0), (last_table, types))
        small = [through_gates(part, gate_slopes.at[:, pl.ds(at, types)], experts, tasks) for part, at in both]
        for half in range(each):
            ends[half] = jnp.concatenate(small)
        for_each(end_copies(ends, out_refs, end_sem), start)
        for_each(stores(step - 1), wait)
        for_each(stores(step), wait)
        for_each(end_copies(ends, out_refs, end_sem), wait)
        for_each(last_stores(), wait)


def backward_call(x, types, across_types, stream, gate_slopes, values, stash, pieces, places, held, tasks, last):
    height, width = x.shape
    pairs, type_count, lanes = values.shape
    each = lanes // LANES
    groups = pairs // held
    stride = 2 * width + EXTRA
    last_values, last_weights, *last_kept, last_low, last_across, last_share, last_ends = last
    operands = [x, types, across_types, stream, gate_slopes, values, *stash]
    specs = [FAR, *[whole_spec(a.shape) for a in operands[1:4]], FAR]
    specs.append(pl.BlockSpec((1, type_count, lanes), lambda i: (i, 0, 0)))
    specs += [pl.BlockSpec((1, each, height, width), lambda i: (i, 0, 0, 0))] * 2
    near = [last_low, last_across, last_share, last_ends]
    operands += [last_values, *near, *last_kept, *last_weights]
    specs.append(pl.BlockSpec((held, *last_values.shape[1:]), lambda i: (0, 0, 0)))
    specs += [whole_spec(a.shape) for a in near]
    specs += [FAR] * (len(last_kept) + each)
    rows = held * stride + type_count
    mine = jax.ShapeDtypeStruct((groups, rows, width), bf16)
    others = [jax.ShapeDtypeStruct((rows, width), bf16)] * (groups * (each - 1))
    others += [jax.ShapeDtypeStruct((held * stride + last_ends.shape[1], width), bf16)] * each
    number = pairs * each
    return pl.pallas_call(
        functools.partial(backward_kernel, places, len(pieces), each, held, tasks),
        grid=(pairs,),
        out_shape=[jax.ShapeDtypeStruct(stream.shape, f32), mine, *others],
        in_specs=specs + [FAR] * len(pieces),
        out_specs=[whole_spec(stream.shape)] + [FAR] * (1 + len(others)),
        scratch_shapes=[
            pltpu.VMEM((height, width), bf16),
            pltpu.VMEM((width + EXTRA, height), bf16),
            pltpu.VMEM((1, height, width), bf16),
            pltpu.VMEM((1, type_count, width), f32),
            pltpu.VMEM((type_count, LANES), f32),
            pltpu.VMEM((each, height, width), bf16),
            pltpu.VMEM((each, height, width), bf16),
            pltpu.VMEM((type_count, LANES), f32),
            pltpu.VMEM((2, each, stride, width), bf16),
            pltpu.VMEM((2, each, stride, width), bf16),
            pltpu.VMEM((each, type_count, width), bf16),
            pltpu.VMEM((height, width), f32),
            pltpu.VMEM(gate_slopes.shape, f32),
            pltpu.VMEM((type_count, LANES), f32),
            pltpu.VMEM((height, LANES), f32),
            pltpu.VMEM((3, held, each, height, width), bf16),
            pltpu.VMEM((held, each, stride, width), bf16),
            pltpu.VMEM((held, each, stride, width), bf16),
            pltpu.SemaphoreType.DMA((2, each)),
            pltpu.SemaphoreType.DMA((2, each)),
            pltpu.SemaphoreType.DMA((each, groups)),
            pltpu.SemaphoreType.DMA((held, 3 + each)),
            pltpu.SemaphoreType.DMA((each, held + 1)),
            pltpu.SemaphoreType.DMA((2,)),
        ],
        compiler_params=kernel_params(58),
        cost_estimate=pl.CostEstimate(
            flops=10 * number * height * width * width,
            bytes_accessed=number * (8 * width * width + 4 * height * width) + 16 * height * width,
            transcendentals=0,
        ),
    )(*operands, *pieces)


def finish_kernel(names, held, rows, first, *refs):
    place_ref, *refs = refs
    sources, refs = refs[: len(names)], refs[len(names) :]
    in_ref, out_ref, in_bias_out_ref, out_bias_out_ref, ready, sems = refs[-6:]
    in_bias_out_ref[...] = jnp.zeros_like(in_bias_out_ref) if first else refs[2][...]
    out_bias_out_ref[...] = jnp.zeros_like(out_bias_out_ref) if first else refs[3][...]
    copies = []
    for at, ((layer_at, half), source) in enumerate(zip(names, sources)):
        for unit in range(held):
            base = unit * (2 * rows + EXTRA)
            where = held * (place_ref[2] ^ half) + unit
            for which, ref in enumerate((in_ref, out_ref)):
                begin = base + which * rows
                ready[at, unit, which] = source[begin : begin + rows].astype(f32)
                copy = pltpu.make_async_copy(
                    ready.at[at, unit, which], ref.at[layer_at, where], sems.at[at, unit, which]
                )
                copy.start()
                copies.append(copy)
            tail = source[base + 2 * rows : base + 2 * rows + EXTRA].astype(f32)
            in_bias_out_ref[layer_at, pl.ds(where, 1)] = tail[0:1]
            out_bias_out_ref[layer_at, pl.ds(where, 1)] = tail[1:2]
    for copy in copies:
        copy.wait()


def finish_call(place, named, held_arrays, held, shape):
    rows, width = shape[2:]
    names, sources = tuple(named), list(named.values())
    outs = [jax.ShapeDtypeStruct(shape, f32)] * 2
    outs += [jax.ShapeDtypeStruct((*shape[:2], width), f32)] * 2
    first = held_arrays is None
    number = len(names)
    return pl.pallas_call(
        functools.partial(finish_kernel, names, held, rows, first),
        out_shape=outs,
        in_specs=[SCALARS] + [NEAR] * number + ([] if first else [FAR, FAR, NEAR, NEAR]),
        out_specs=[FAR, FAR, NEAR, NEAR],
        scratch_shapes=[
            pltpu.VMEM((number, held, 2, rows, width), f32),
            pltpu.SemaphoreType.DMA((number, held, 2)),
        ],
        input_output_aliases={} if first else {1 + number: 0, 2 + number: 1},
        compiler_params=kernel_params(12),
        cost_estimate=pl.CostEstimate(flops=0, bytes_accessed=number * held * 12 * rows * width, transcendentals=0),
    )(place, *sources, *([] if first else held_arrays))


def flip(array, axis, bits):
    size = lax.axis_size(axis)
    return lax.ppermute(array, axis, [(i, i ^ bits) for i in range(size)])


def add_low(*arrays):
    level = [a.astype(f32) for a in arrays]
    while len(level) > 1:
        level = [level[i] + level[i + 1] for i in range(0, len(level), 2)]
    return level[0].astype(bf16)


def after(arrays, others):
    return lax.optimization_barrier((arrays, others))[0]


def near(mine, groups):
    if groups == 4 and mine.shape[0] == 2:
        return {1: [flip(mine, "expert", 1)], 2: [flip(mine, "expert", 2)]}
    return {ro: [flip(mine, "expert", ro)] for ro in range(1, groups)}


def relay(arrived, groups, held):
    if groups == 4 and held == 2:
        return {3: [flip(arrived[1][0][:1], "expert", 2), flip(arrived[2][0][1:], "expert", 1)]}
    return {}


def crossed(parts, halves):
    return [] if halves == 1 else [flip(part, "rows", 1) for part in parts]


def body(
    rows_in,
    pred_grad,
    lengths,
    session_type,
    expert_in,
    expert_in_bias,
    expert_out,
    expert_out_bias,
    selector_logits,
    selector_mix,
    tower_in,
    tower_bias,
    tower_out,
):
    height, width = rows_in.shape
    layers, owned = expert_in.shape[:2]
    type_count, tasks = selector_logits.shape[1:3]
    selectors, bits = selector_logits.shape[3:]
    groups = lax.axis_size("expert")
    halves = 2 if owned % 2 == 0 else 1
    held = owned // halves
    stride = 2 * width + EXTRA
    me, row_at = lax.axis_index("expert"), lax.axis_index("rows")
    core = row_at % 2 if halves == 2 else jnp.int32(0)
    place = jnp.stack([(row_at * groups + me) * height, me, core]).astype(jnp.int32)

    def rows_of(layer_at, first):
        cut = lambda a: lax.dynamic_slice(a, (layer_at, first) + (0,) * (a.ndim - 2), (1, held) + a.shape[2:])[0]
        half = lambda a: a * jnp.asarray(0.5, a.dtype)
        tail = []
        for bias in (half(cut(expert_in_bias)), cut(expert_out_bias)):
            high = bias.astype(bf16)
            tail += [high, (bias - high.astype(f32)).astype(bf16)]
        tail = jnp.pad(jnp.stack(tail, axis=1), ((0, 0), (0, EXTRA - len(tail)), (0, 0)))
        return jnp.concatenate([half(cut(expert_in)), cut(expert_out), tail], axis=1)

    first = rows_of(0, held * core)
    asked = near(first, groups)
    sizes = (owned, halves, held, selectors, bits, tasks)
    types, across_types, gate_slopes, *values = prepare_call(
        place, lengths, session_type, selector_logits, selector_mix, height, sizes
    )

    later = after((expert_in, expert_in_bias, expert_out, expert_out_bias), types)
    expert_in, expert_in_bias, expert_out, expert_out_bias = later
    own = [[rows_of(layer_at, held * (core ^ half)) for half in range(halves)] for layer_at in range(layers)]
    own[0][0] = first

    def parts_of(got, across):
        pieces, places = [], {}
        for ro in got:
            spots = []
            for parts in (got[ro], across[ro]):
                here = []
                for part in parts:
                    here += [(len(pieces), at) for at in range(part.shape[0])]
                    pieces.append(part)
                if here:
                    spots.append(here)
            places[ro] = [[spots[half][unit] for half in range(halves)] for unit in range(held)]
        return pieces, places

    def pair_order(places, units):
        return tuple(spot for ro in sorted(places) for unit in units for spot in places[ro][unit])

    streams, stashes, weights = [rows_in], [], []
    for layer_at in range(layers):
        last = layer_at == layers - 1
        got = near(own[layer_at][0], groups) if layer_at else after(asked, (types, own[0][1:], own[1:]))
        far = relay(got, groups, held)
        across = {ro: crossed(got[ro], halves) for ro in got}
        got = {0: own[layer_at][:1], **got}
        across[0] = own[layer_at][1:]
        if not last:
            pieces, places = parts_of(got, across)
            total, stash = forward_call(
                streams[-1], types, values[layer_at], None, None, pieces, pair_order(places, range(held)), 0
            )
            far = after(far, total)
        elif streams[1:]:
            far = after(far, streams[-1])
        far_across = {ro: crossed(far[ro], halves) for ro in far}
        if not last:
            if far:
                pieces, places = parts_of(far, far_across)
                base = held * min(far)
                order = pair_order(places, range(held))
                total, stash = forward_call(
                    streams[-1], types, values[layer_at], total, stash, pieces, order, base
                )
            streams.append(total[0])
            stashes.append(stash)
        weights.append(parts_of({**got, **far}, {**across, **far_across}))

    pieces, places = weights[-1]
    predictions, stream, *payload = middle_call(
        place,
        streams[-1],
        types,
        across_types,
        values[-1],
        gate_slopes,
        (pred_grad.T, tower_in, tower_bias, tower_out),
        pieces,
        pair_order(places, range(held)),
        groups,
        halves,
        held,
    )

    shards = lax.axis_size("rows")
    paired = shards > 2
    hops = ["share"] + [4 << at for at in range(shards.bit_length() - 3)] + ["join"] if paired else []
    upper = (row_at & 2) > 0

    class Moving:
        def __init__(self, layer_at, mine, others):
            self.layer_at, self.mine, self.own = layer_at, mine, None
            self.got = [flip(part, "rows", 1) for part in others]
            self.sums, self.parts, self.total, self.hops = None, None, None, -2

        def ask(self, token):
            if self.hops == -1:
                sums, own = after((self.sums, self.own), token)
                ros = range(1, groups) if self.parts is None else ()
                self.got = [flip(sums[ro - 1], "expert", ro) for ro in ros]
                self.got += [] if own is None else [flip(own[1], "rows", 1)]
                return
            total = after(self.total, token)
            if self.hops == len(hops):
                self.got = [total] + ([flip(total, "rows", 1)] if halves == 2 else [])
            elif hops[self.hops] == "share":
                cut = total.shape[0] // 2
                self.got = [
                    jnp.where(upper, total[cut:], total[:cut]),
                    flip(jnp.where(upper, total[:cut], total[cut:]), "rows", 2),
                ]
            else:
                self.got = [total, flip(total, "rows", 2 if hops[self.hops] == "join" else hops[self.hops])]

        def add(self):
            if self.hops == -2:
                self.sums = [add_low(*pair) for pair in zip(self.mine, self.got)]
            elif self.hops == -1:
                got = self.got
                if self.parts is None:
                    self.parts = []
                    while len(got) >= 1 << len(self.parts) and (1 << len(self.parts)) < groups:
                        size = 1 << len(self.parts)
                        level, got = got[:size], got[size:]
                        while len(level) > 1:
                            level = [add_low(*level[i : i + 2]) for i in range(0, len(level), 2)]
                        self.parts += level
                if self.own is None:
                    return
                self.total = functools.reduce(add_low, self.parts, add_low(self.own[0], got[0]))
            elif hops[self.hops] != "join":
                self.total = add_low(*self.got)
            else:
                here, there = self.got
                self.total = jnp.concatenate([jnp.where(upper, there, here), jnp.where(upper, here, there)])
            self.hops += 1

    def arrive(entries, others):
        got, others = lax.optimization_barrier(([entry.got for entry in entries], others))
        for entry, what in zip(entries, got):
            entry.got = what
            entry.add()
        there = [[x for x in (entry.total, entry.parts, entry.sums) if x is not None][0] for entry in entries]
        return there, others

    assert layers == 2
    mine, left = payload[0], payload[-7:]
    mine = [mine[ro] for ro in range(groups - 1)]
    later = Moving(1, mine, payload[1:-7] or mine)
    token = arrive([later], ())
    stream = after(stream, token)
    later.ask(token)
    pieces, places = weights[0]
    stream, mine, *others = backward_call(
        streams[0],
        types,
        across_types,
        stream,
        gate_slopes,
        values[0],
        stashes[0],
        pieces,
        pair_order(places, range(held)),
        held,
        tasks,
        (values[1], own[1], *left),
    )
    token = arrive([later], stream)
    others, last_own = others[:-halves], others[-halves:]
    mine = [mine[ro] for ro in range(groups)]
    others = others or mine
    earlier = Moving(0, mine[1:], others[1:])
    earlier.own = (mine[0], others[0])
    later.own = (last_own[0], last_own[-1])
    later.ask(())
    token = arrive([earlier, later], token)
    moving = [later, earlier]

    whole = {}
    arrays, tower_sums = None, ()

    def ask(*entries):
        nonlocal arrays, tower_sums
        for entry in entries:
            entry.ask(token)
        for entry in entries:
            if entry.hops < len(hops):
                continue
            moving.remove(entry)
            layer_at, got = entry.layer_at, entry.got
            whole[layer_at] = got
            if layer_at == layers - 1:
                end = got[0][held * stride + type_count // 2 :].astype(f32)
                tower_rows = [array[held * stride + type_count // 2 + EXTRA :].astype(f32) for array in got]
                if halves == 2:
                    tower_rows = [jnp.where(core == 0, *tower_rows), jnp.where(core == 0, *tower_rows[::-1])]
                wide = jnp.concatenate(tower_rows).reshape(tasks, -1, width)
                narrow = tower_in.shape[2]
                parts = [wide[:, :, at : at + narrow] for at in range(0, width, narrow)]
                tower_sums = (
                    jnp.concatenate(parts, axis=1),
                    end[0].reshape(tower_bias.shape),
                    end[1].reshape(tower_out.shape),
                )
            if moving:
                sources = {(layer_at, half): array for half, array in enumerate(got)}
                arrays = finish_call(place, sources, arrays, held, expert_in.shape)

    if len(hops) == 3:
        ask(earlier, later)
        token = arrive([later], ())
        ask(later)
        token = arrive([earlier, later], ())
        ask(earlier)
        token = arrive([earlier], ())
        ask(earlier, later)
        token = arrive([earlier, later], ())
    while moving:
        ask(*moving)
        if moving:
            token = arrive(moving, (arrays, tower_sums))
    ends = [whole[layer_at][0][held * stride : held * stride + type_count].astype(f32) for layer_at in range(layers)]
    cut = type_count // 2
    gate_grads = [ends[0][:cut], ends[1][:cut] + ends[0][cut:]]
    quantities = selectors * (bits + 1)
    small = jnp.stack(gate_grads)
    small = jnp.concatenate([small[..., :LANES], small[..., LANES:]], axis=1)[..., : tasks * quantities]
    small = small.reshape(layers, type_count, tasks, quantities)
    logits_grad = small[..., : selectors * bits].reshape(selector_logits.shape)
    smalls = (logits_grad, small[..., selectors * bits :], *tower_sums)
    got, (arrays, smalls) = lax.optimization_barrier((whole[0], (arrays, smalls)))
    arrays = finish_call(place, {(0, half): array for half, array in enumerate(got)}, arrays, held, expert_in.shape)
    return (
        predictions.T,
        stream,
        arrays[0],
        arrays[2],
        arrays[1],
        arrays[3],
        *smalls,
    )


def solution(mesh):
    in_specs = (
        P(("rows", "expert"), None),
        P(("rows", "expert"), None),
        P(),
        P(),
        P(None, "expert", None, None),
        P(None, "expert", None),
        P(None, "expert", None, None),
        P(None, "expert", None),
        P(),
        P(),
        P(),
        P(),
        P(),
    )
    out_specs = (
        P(("rows", "expert"), None),
        P(("rows", "expert"), None),
        P(None, "expert", None, None),
        P(None, "expert", None),
        P(None, "expert", None, None),
        P(None, "expert", None),
        P(),
        P(),
        P(),
        P(),
        P(),
    )
    return jax.shard_map(body, mesh=mesh, in_specs=in_specs, out_specs=out_specs, check_vma=False)
```
